32 devices in a mesh: dp: 4 (over y, core), seq: 8 (over z, x).
Axes of the slice: x: 2, y: 2, z: 4, core: 2. Of those that a mesh axis runs over, the one named last changes fastest.
Arguments:
- source: bfloat16 [32, 1024, 768], P('dp', 'seq'), may hold values from -6 to 6
- target: bfloat16 [32, 512, 768], P('dp', 'seq'), may hold values from -6 to 6
- source_segments: int32 [32, 1024], P('dp'), may hold values from 0 to 3, as said below
- target_segments: int32 [32, 512], P('dp'), may hold values from 0 to 3, as said below
- cotangent: bfloat16 [32, 512, 768], P('dp', 'seq'), may hold values from -6 to 6
- enc_qkv: bfloat16 [768, 2304], replicated, may hold values from -0.21875 to 0.21875
- enc_out: bfloat16 [768, 768], replicated, may hold values from -6 to 6
- enc_up: bfloat16 [768, 3072], replicated, may hold values from -0.21875 to 0.21875
- enc_down: bfloat16 [3072, 768], replicated, may hold values from -0.109375 to 0.109375
- dec_qkv: bfloat16 [768, 2304], replicated, may hold values from -0.21875 to 0.21875
- dec_out: bfloat16 [768, 768], replicated, may hold values from -2.5 to 2.5
- cross_q: bfloat16 [768, 768], replicated, may hold values from -0.21875 to 0.21875
- cross_kv: bfloat16 [768, 1536], replicated, may hold values from -0.21875 to 0.21875
- cross_out: bfloat16 [768, 768], replicated, may hold values from -6 to 6
- dec_up: bfloat16 [768, 3072], replicated, may hold values from -0.21875 to 0.21875
- dec_down: bfloat16 [3072, 768], replicated, may hold values from -0.109375 to 0.109375
- enc_prefix: bfloat16 [30, 768], replicated, may hold values from -6 to 6
- enc_prefix_in: bfloat16 [768, 512], replicated, may hold values from -0.21875 to 0.21875
- enc_prefix_out: bfloat16 [512, 1536], replicated, may hold values from -0.375 to 0.375
- enc_adapter_down: bfloat16 [768, 512], replicated, may hold values from -0.21875 to 0.21875
- enc_adapter_up: bfloat16 [512, 768], replicated, may hold values from -0.125 to 0.125
- dec_prefix: bfloat16 [30, 768], replicated, may hold values from -6 to 6
- dec_prefix_in: bfloat16 [768, 512], replicated, may hold values from -0.21875 to 0.21875
- dec_prefix_out: bfloat16 [512, 1536], replicated, may hold values from -0.375 to 0.375
- dec_adapter_down: bfloat16 [768, 512], replicated, may hold values from -0.21875 to 0.21875
- dec_adapter_up: bfloat16 [512, 768], replicated, may hold values from -0.125 to 0.125
Outputs:
- out_hidden: bfloat16 [32, 512, 768], P('dp', 'seq')
- source_grad: float32 [32, 1024, 768], P('dp', 'seq')
- target_grad: float32 [32, 512, 768], P('dp', 'seq')
- enc_prefix_grad: float32 [30, 768], P(None, 'seq')
- enc_prefix_in_grad: float32 [768, 512], P('seq')
- enc_prefix_out_grad: float32 [512, 1536], P('seq')
- enc_adapter_down_grad: float32 [768, 512], P('seq')
- enc_adapter_up_grad: float32 [512, 768], P('seq')
- dec_prefix_grad: float32 [30, 768], P(None, 'seq')
- dec_prefix_in_grad: float32 [768, 512], P('seq')
- dec_prefix_out_grad: float32 [512, 1536], P('seq')
- dec_adapter_down_grad: float32 [768, 512], P('seq')
- dec_adapter_up_grad: float32 [512, 768], P('seq')
The draws below stay inside these ranges and needn't reach their ends.
Inputs may be any that keep to these rules, and one draw needn't show every extreme that they name: `source_segments`: in every row the positions carry the document numbers 0, 1, 2, 3 in this order, never falling, each document at least one position long; document k of a target row belongs to document k of the source row with the same index. `target_segments`: as for source_segments; the longest document of a target row has the number of the longest document of its source row.
All inputs are finite; a program needn't handle non-finite values.
Results may differ from the reference program's by a relative error of at most 0.03.
Values may be sent and summed in bfloat16 or wider, within the bound.
A program may use at most 320 MiB of HBM per device.

```python
import math
import jax
import jax.numpy as jnp
from jax import lax

D = 768
HEADS = 12
HEAD = 64
FF = 3072
ADP = 512
PMLP = 512
PRE = 30
SRC_LEN = 1024
TGT_LEN = 512
ROWS = 32


def layout_parts(key):
    short_most = max(SRC_LEN // 64, 1)
    key_short, key_long = jax.random.split(key)
    short_sizes = jax.random.randint(key_short, (ROWS, 3), 1, short_most + 1)
    long_slot = jax.random.randint(key_long, (ROWS, 1), 0, 4)
    return (short_sizes, long_slot)


def document_ids(short_sizes, long_slot, length):
    slots = jnp.arange(4)[None, :]
    before = jnp.concatenate([short_sizes, short_sizes[:, :1]], axis=1)
    after = jnp.concatenate([short_sizes[:, :1], short_sizes], axis=1)
    long_size = length - jnp.sum(short_sizes, axis=1, keepdims=True)
    sizes = jnp.where(slots < long_slot, before, jnp.where(slots == long_slot, long_size, after))
    ends = jnp.cumsum(sizes, axis=1)
    positions = jnp.arange(length)
    return jnp.sum((positions[None, :, None] >= ends[:, None, :3]).astype(jnp.int32), axis=2).astype(jnp.int32)


def draw_source_segments(key, part):
    short_sizes, long_slot = layout_parts(key)
    return document_ids(short_sizes, long_slot, SRC_LEN)


def draw_target_segments(key, part):
    short_sizes, long_slot = layout_parts(key)
    target_short = jnp.maximum(short_sizes * TGT_LEN // SRC_LEN, 1)
    return document_ids(target_short, long_slot, TGT_LEN)


def block_levels(key, extent, cuts, smallest, largest):
    gain = 1.0
    for position, parts in cuts:
        heights = jax.random.uniform(jax.random.fold_in(jax.random.fold_in(key, 6), position), (parts,), jnp.float32, smallest / len(cuts), largest / len(cuts))
        gain = gain * jnp.repeat(jnp.exp(heights), extent[position] // parts).reshape((-1,) + (1,) * (len(extent) - 1 - position))
    return gain


def centred(key, dims, deviation, most, pieces=(), kind=jnp.bfloat16):
    array = jax.random.normal(key, dims, jnp.float32) * deviation
    if len(pieces) > 0:
        array = block_levels(key, dims, pieces, -0.22, 0.18) * array
    return jnp.clip(array, min=-most, max=most).astype(kind)


def setup_inputs(seed: int = 0) -> dict:
    seeds = jax.random.split(jax.random.key(seed), 27)
    source = centred(seeds[0], (ROWS, SRC_LEN, D), 1.0, 6.0, ((0, 4), (1, 8)))
    target = centred(seeds[1], (ROWS, TGT_LEN, D), 1.0, 6.0, ((0, 4), (1, 8)))
    source_segments = draw_source_segments(jax.random.fold_in(seeds[26], 71), 0)
    target_segments = draw_target_segments(jax.random.fold_in(seeds[26], 71), 0)
    cotangent = centred(seeds[4], (ROWS, TGT_LEN, D), 1.0, 6.0, ((0, 4), (1, 8)))
    enc_qkv = centred(seeds[5], (D, 3 * D), D ** -0.5, 0.21875)
    enc_out = centred(seeds[6], (D, D), (max(D // 512, 1)) ** -0.5, 6.0)
    enc_up = centred(seeds[7], (D, FF), D ** -0.5, 0.21875)
    enc_down = centred(seeds[8], (FF, D), FF ** -0.5, 0.109375)
    dec_qkv = centred(seeds[9], (D, 3 * D), D ** -0.5, 0.21875)
    dec_out = centred(seeds[10], (D, D), (max(D // 128, 1)) ** -0.5, 2.5)
    cross_q = centred(seeds[11], (D, D), D ** -0.5, 0.21875)
    cross_kv = centred(seeds[12], (D, 2 * D), D ** -0.5, 0.21875)
    cross_out = centred(seeds[13], (D, D), (max(D // 512, 1)) ** -0.5, 6.0)
    dec_up = centred(seeds[14], (D, FF), D ** -0.5, 0.21875)
    dec_down = centred(seeds[15], (FF, D), FF ** -0.5, 0.109375)
    enc_prefix = centred(seeds[16], (PRE, D), 1.0, 6.0)
    enc_prefix_in = centred(seeds[17], (D, PMLP), D ** -0.5, 0.21875)
    enc_prefix_out = centred(seeds[18], (PMLP, 2 * D), (PMLP // 2) ** -0.5, 0.375)
    enc_adapter_down = centred(seeds[19], (D, ADP), D ** -0.5, 0.21875)
    enc_adapter_up = centred(seeds[20], (ADP, D), (4 * ADP) ** -0.5, 0.125)
    dec_prefix = centred(seeds[21], (PRE, D), 1.0, 6.0)
    dec_prefix_in = centred(seeds[22], (D, PMLP), D ** -0.5, 0.21875)
    dec_prefix_out = centred(seeds[23], (PMLP, 2 * D), (PMLP // 2) ** -0.5, 0.375)
    dec_adapter_down = centred(seeds[24], (D, ADP), D ** -0.5, 0.21875)
    dec_adapter_up = centred(seeds[25], (ADP, D), (4 * ADP) ** -0.5, 0.125)
    return dict(source=source, target=target, source_segments=source_segments, target_segments=target_segments, cotangent=cotangent, enc_qkv=enc_qkv, enc_out=enc_out, enc_up=enc_up, enc_down=enc_down, dec_qkv=dec_qkv, dec_out=dec_out, cross_q=cross_q, cross_kv=cross_kv, cross_out=cross_out, dec_up=dec_up, dec_down=dec_down, enc_prefix=enc_prefix, enc_prefix_in=enc_prefix_in, enc_prefix_out=enc_prefix_out, enc_adapter_down=enc_adapter_down, enc_adapter_up=enc_adapter_up, dec_prefix=dec_prefix, dec_prefix_in=dec_prefix_in, dec_prefix_out=dec_prefix_out, dec_adapter_down=dec_adapter_down, dec_adapter_up=dec_adapter_up)


@jax.custom_vjp
def low(v):
    return lax.optimization_barrier(v.astype(jnp.bfloat16)).astype(jnp.float32)

@jax.custom_vjp
def low_back(v):
    return v

def low_keep(v):
    return (low(v), None)

def low_pass(kept, grad):
    return (grad,)

def back_keep(v):
    return (v, None)

def back_low(kept, grad):
    return (low(grad),)
low.defvjp(low_keep, low_pass)
low_back.defvjp(back_keep, back_low)

def rounded_both(value):
    return low(low_back(value))

def matmul(left, right):
    return jnp.matmul(left, right, precision=lax.Precision.HIGHEST)

def normalize(value):
    centered = value - lax.optimization_barrier(jnp.mean(value, axis=-1, keepdims=True))
    return centered * lax.rsqrt(lax.optimization_barrier(jnp.mean(centered * centered, axis=-1, keepdims=True)) + 1e-05)

def gelu_act(value):
    return jax.nn.gelu(value, approximate=True)

def attend_row(query_rows, key_rows, value_rows, allowed, prefix_keys, prefix_values):
    score_scale = 1.0 / math.sqrt(HEAD)
    length = query_rows.shape[0]
    query_heads = query_rows.reshape(length, HEADS, HEAD)
    key_heads = jnp.concatenate([prefix_keys, key_rows], axis=0).reshape(-1, HEADS, HEAD)
    value_heads = jnp.concatenate([prefix_values, value_rows], axis=0).reshape(-1, HEADS, HEAD)
    opened = jnp.concatenate([jnp.ones((length, prefix_keys.shape[0]), jnp.bool_), allowed], axis=1)
    scores = low_back(jnp.einsum('qhe,khe->hqk', query_heads, key_heads, precision=lax.Precision.HIGHEST) * score_scale)
    scores = jnp.where(opened[None], scores, -1e+30)
    weights = jnp.exp(scores - lax.optimization_barrier(jnp.max(scores, axis=-1, keepdims=True)))
    probabilities = weights / lax.optimization_barrier(jnp.sum(weights, axis=-1, keepdims=True))
    context = jnp.einsum('hqk,khe->qhe', low(probabilities), value_heads, precision=lax.Precision.HIGHEST)
    return context.reshape(length, HEADS * HEAD)

def attend_rows(queries, key_rows, values, mask_rows, prefix_keys, prefix_values):
    row_attend = jax.checkpoint(attend_row)

    def one_row(row_items):
        return row_attend(row_items[0], row_items[1], row_items[2], row_items[3], prefix_keys, prefix_values)
    return lax.map(one_row, (queries, key_rows, values, mask_rows))

def self_block(hidden, qkv_weight, out_weight, prefix, prefix_in, prefix_out, mask_rows):
    model_width = hidden.shape[-1]
    prefix_pairs = low(matmul(jnp.tanh(matmul(prefix, prefix_in)), prefix_out))
    qkv_rows = rounded_both(matmul(low(hidden), qkv_weight))
    context = attend_rows(qkv_rows[..., :model_width], qkv_rows[..., model_width:2 * model_width], qkv_rows[..., 2 * model_width:], mask_rows, prefix_pairs[:, :model_width], prefix_pairs[:, model_width:])
    branch = low_back(matmul(rounded_both(context), out_weight))
    return normalize(hidden + branch)

def cross_block(hidden, memory, query_weight, pair_weight, out_weight, mask_rows):
    model_width = hidden.shape[-1]
    queries = rounded_both(matmul(low(hidden), query_weight))
    memory_pairs = rounded_both(matmul(low(memory), pair_weight))
    no_prefix = jnp.zeros((0, model_width), jnp.float32)
    context = attend_rows(queries, memory_pairs[..., :model_width], memory_pairs[..., model_width:], mask_rows, no_prefix, no_prefix)
    branch = low_back(matmul(rounded_both(context), out_weight))
    return normalize(hidden + branch)

def feed_block(hidden, up_weight, down_weight, adapter_down, adapter_up):
    hidden_low = low(hidden)
    inner_pre = low_back(matmul(hidden_low, up_weight))
    main_branch = low_back(matmul(low(gelu_act(inner_pre)), down_weight))
    narrow = low_back(matmul(hidden_low, adapter_down))
    side_branch = 4.0 * low_back(matmul(low(gelu_act(narrow)), adapter_up))
    return normalize(hidden + main_branch + side_branch)

def forward(source, target, trainable, frozen, mask_rows):
    enc_qkv, enc_out, enc_up, enc_down, dec_qkv, dec_out, cross_q, cross_kv, cross_out, dec_up, dec_down = frozen
    enc_prefix, enc_prefix_in, enc_prefix_out, enc_adapter_down, enc_adapter_up, dec_prefix, dec_prefix_in, dec_prefix_out, dec_adapter_down, dec_adapter_up = trainable
    enc_mask, dec_mask, cross_mask = mask_rows
    encoded_mid = self_block(source, enc_qkv, enc_out, enc_prefix, enc_prefix_in, enc_prefix_out, enc_mask)
    memory = feed_block(encoded_mid, enc_up, enc_down, enc_adapter_down, enc_adapter_up)
    decoded_mid = self_block(target, dec_qkv, dec_out, dec_prefix, dec_prefix_in, dec_prefix_out, dec_mask)
    crossed = cross_block(decoded_mid, memory, cross_q, cross_kv, cross_out, cross_mask)
    return feed_block(crossed, dec_up, dec_down, dec_adapter_down, dec_adapter_up)

def reference(source, target, source_segments, target_segments, cotangent, enc_qkv, enc_out, enc_up, enc_down, dec_qkv, dec_out, cross_q, cross_kv, cross_out, dec_up, dec_down, enc_prefix, enc_prefix_in, enc_prefix_out, enc_adapter_down, enc_adapter_up, dec_prefix, dec_prefix_in, dec_prefix_out, dec_adapter_down, dec_adapter_up):
    places = jnp.arange(TGT_LEN)
    enc_mask = source_segments[:, :, None] == source_segments[:, None, :]
    dec_mask = (target_segments[:, :, None] == target_segments[:, None, :]) & (places[None, None, :] <= places[None, :, None])
    cross_mask = target_segments[:, :, None] == source_segments[:, None, :]
    frozen = tuple((weight.astype(jnp.float32) for weight in (enc_qkv, enc_out, enc_up, enc_down, dec_qkv, dec_out, cross_q, cross_kv, cross_out, dec_up, dec_down)))
    trainable = tuple((weight.astype(jnp.float32) for weight in (enc_prefix, enc_prefix_in, enc_prefix_out, enc_adapter_down, enc_adapter_up, dec_prefix, dec_prefix_in, dec_prefix_out, dec_adapter_down, dec_adapter_up)))

    def run_layers(source_wide, target_wide, weight_set):
        return forward(source_wide, target_wide, weight_set, frozen, (enc_mask, dec_mask, cross_mask))
    output, pullback = jax.vjp(run_layers, source.astype(jnp.float32), target.astype(jnp.float32), trainable)
    source_grad, target_grad, weight_grads = pullback(cotangent.astype(jnp.float32))
    return (output.astype(jnp.bfloat16), source_grad, target_grad, weight_grads[0], weight_grads[1], weight_grads[2], weight_grads[3], weight_grads[4], weight_grads[5], weight_grads[6], weight_grads[7], weight_grads[8], weight_grads[9])
```

```python
import functools
import math

import jax
import jax.numpy as jnp
from jax import lax
from jax.experimental import pallas as pl
from jax.experimental.pallas import tpu as pltpu
from jax.sharding import PartitionSpec as P

HEAD = 64
GROUP = 4
PAD = 32
BIG = 2.0**100
LOG2E = math.log2(math.e)
QUERY_SCALE = LOG2E / math.sqrt(HEAD)
VMEM_BYTES = 60 * 2**20
LOW = jnp.bfloat16
WIDE = jnp.float32


def contract(left, right, left_dim, right_dim):
    return lax.dot_general(
        left, right, (((left_dim,), (right_dim,)), ((), ())), preferred_element_type=WIDE
    )


def project(left, right):
    return jnp.dot(left, right, preferred_element_type=WIDE)


def project_wide(weight, rows):
    return jnp.einsum("io,ti->ot", weight, rows, preferred_element_type=WIDE)


def back_through(gradient, weight):
    return jnp.einsum("ln,dn->ld", gradient, weight, preferred_element_type=WIDE)


def weight_grad(inputs, gradient):
    return jnp.einsum("la,lb->ab", inputs, gradient, preferred_element_type=WIDE)


def normalize(value):
    centered = value - jnp.mean(value, axis=-1, keepdims=True)
    inverse = lax.rsqrt(jnp.mean(centered * centered, axis=-1, keepdims=True) + 1e-05)
    return (centered * inverse, inverse)


def normalize_back(gradient, normed, inverse):
    return (
        gradient
        - jnp.mean(gradient, axis=-1, keepdims=True)
        - normed * jnp.mean(gradient * normed, axis=-1, keepdims=True)
    ) * inverse


def gelu_act(value):
    return jax.nn.gelu(value, approximate=True)


def gelu_back(value, gradient):
    return jax.vjp(gelu_act, value)[1](gradient)[0]


def rows_at(head, size):
    return pl.ds(pl.multiple_of(head * size, size), size)


def split_three(value):
    high = value.astype(LOW).astype(WIDE)
    rest = value - high
    middle = rest.astype(LOW).astype(WIDE)
    return (high, middle, rest - middle)


def place_rows(parts, first, shape):
    row = lax.broadcasted_iota(jnp.int32, shape, 0)
    out = jnp.zeros(shape, WIDE)
    for offset, part in enumerate(parts):
        out = jnp.where(row == first + offset, part, out)
    return out


def document_rows(segments, shape, is_key):
    row = lax.broadcasted_iota(jnp.int32, shape, 0)
    same = row == segments
    if is_key:
        return jnp.where(row < 4, jnp.where(same, 0.0, -BIG), 0.0)
    return jnp.where(same & (row < 4), 1.0, 0.0)


def column_peak(scores, peak):
    for start in range(0, scores.shape[0], 8):
        peak = jnp.maximum(peak, scores[start : start + 8])
    return peak


def attend_kernel(tile, causal, prefix, *refs):
    if prefix:
        q_ref, k_ref, v_ref, qseg_ref, kseg_ref, pk_ref, pv_ref = refs[:7]
        refs = refs[7:]
    else:
        q_ref, k_ref, v_ref, qseg_ref, kseg_ref = refs[:5]
        refs = refs[5:]
    out_ref, lse_ref, qx_ref, kx_ref, s_ref, sp_ref, peak_ref = refs
    width, queries = q_ref.shape
    keys = k_ref.shape[1]
    heads = width // HEAD
    tiles = keys // tile
    qx_ref[...] = document_rows(qseg_ref[...], qx_ref.shape, False).astype(LOW)
    kx_ref[...] = document_rows(kseg_ref[...], kx_ref.shape, True).astype(LOW)
    start_peak = jnp.full((8, queries), -4.0 * BIG, WIDE)

    def query_of(head):
        return jnp.concatenate([q_ref[rows_at(head, HEAD), :], qx_ref[...]], 0)

    def tile_scores(head, part, query):
        cut = slice(part * tile, (part + 1) * tile)
        key = jnp.concatenate([k_ref[rows_at(head, HEAD), cut], kx_ref[:, cut]], 0)
        scores = contract(key, query, 0, 0)
        if causal:
            place = lax.broadcasted_iota(jnp.int32, scores.shape, 0) + part * tile
            scores = jnp.where(
                place <= lax.broadcasted_iota(jnp.int32, scores.shape, 1), scores, -BIG
            )
        return scores

    def prefix_scores(head, slot):
        if not prefix:
            return start_peak
        scores = contract(pk_ref[rows_at(head, HEAD), :], q_ref[rows_at(head, HEAD), :], 0, 0)
        row = lax.broadcasted_iota(jnp.int32, scores.shape, 0)
        scores = jnp.where(row < prefix, scores, -BIG)
        sp_ref[slot] = scores
        return column_peak(scores, start_peak)

    def score_tile(head, part, query, slot, peak):
        scores = tile_scores(head, part, query)
        s_ref[slot, part * tile : (part + 1) * tile, :] = scores
        return column_peak(scores, peak)

    def step(head, following, slot):
        other = 1 - slot
        query = query_of(following)
        peak = jnp.max(peak_ref[slot], 0, keepdims=True)
        next_peak = prefix_scores(following, other)
        context = jnp.zeros((HEAD + 16, queries), WIDE)
        if prefix:
            weights = jnp.exp2(sp_ref[slot] - peak).astype(LOW)
            value = jnp.concatenate(
                [pv_ref[rows_at(head, HEAD), :], jnp.ones((16, PAD), LOW)], 0
            )
            context = contract(value, weights, 1, 0)
        for part in range(tiles):
            next_peak = score_tile(following, part, query, other, next_peak)
            cut = slice(part * tile, (part + 1) * tile)
            weights = jnp.exp2(s_ref[slot, cut, :] - peak).astype(LOW)
            value = jnp.concatenate(
                [v_ref[rows_at(head, HEAD), cut], jnp.ones((16, tile), LOW)], 0
            )
            context = context + contract(value, weights, 1, 0)
        peak_ref[other] = next_peak
        total = context[HEAD : HEAD + 1]
        out_ref[rows_at(head, HEAD), :] = (context[:HEAD] * (1.0 / total)).astype(LOW)
        lse_ref[pl.ds(head, 1), :] = peak + jnp.log2(total)

    first = query_of(0)
    peak = prefix_scores(0, 0)
    for part in range(tiles):
        peak = score_tile(0, part, first, 0, peak)
    peak_ref[0] = peak

    def pair(index, carry):
        step(2 * index, 2 * index + 1, 0)
        step(2 * index + 1, jnp.minimum(2 * index + 2, heads - 1), 1)
        return carry

    lax.fori_loop(0, heads // 2, pair, 0)


def whole(shape):
    return pl.BlockSpec(shape, lambda step: (0,) * len(shape))


def third(width, tokens, index):
    return pl.BlockSpec((width, tokens), lambda step: (index, 0))


def attend(q_all, kv_all, places, q_segments, k_segments, prefix_pairs, causal):
    queries, keys = q_all.shape[1], kv_all.shape[1]
    width = q_all.shape[0] if places[0] == 0 and q_all is not kv_all else q_all.shape[0] // 3
    tile = min(256, keys)
    operands = [q_all, kv_all, kv_all, q_segments, k_segments]
    specs = [
        third(width, queries, places[0]),
        third(width, keys, places[1]),
        third(width, keys, places[2]),
        whole((1, queries)),
        whole((1, keys)),
    ]
    count = 0
    if prefix_pairs is not None:
        count = prefix_pairs.shape[0]
        padded = jnp.pad(prefix_pairs, ((0, PAD - count), (0, 0))).T
        operands += [padded, padded]
        specs += [third(width, PAD, 0), third(width, PAD, 1)]
    lse_rows = -(-(width // HEAD) // 8) * 8
    return pl.pallas_call(
        functools.partial(attend_kernel, tile, causal, count),
        grid=(1,),
        out_shape=(
            jax.ShapeDtypeStruct((width, queries), LOW),
            jax.ShapeDtypeStruct((lse_rows, queries), WIDE),
        ),
        in_specs=specs,
        out_specs=(whole((width, queries)), whole((lse_rows, queries))),
        scratch_shapes=[
            pltpu.VMEM((16, queries), LOW),
            pltpu.VMEM((16, keys), LOW),
            pltpu.VMEM((2, keys, queries), WIDE),
            pltpu.VMEM((2, PAD, queries), WIDE),
            pltpu.VMEM((2, 8, queries), WIDE),
        ],
        compiler_params=pltpu.CompilerParams(vmem_limit_bytes=VMEM_BYTES),
        name="attend",
    )(*operands)


def attend_back_kernel(tile, causal, prefix, *refs):
    q_ref, k_ref, v_ref, dc_ref, ctx_ref, lse_ref, qseg_ref, kseg_ref = refs[:8]
    refs = refs[8:]
    if prefix:
        pk_ref, pv_ref, dq_out, dk_out, dv_out, dpk_out, dpv_out = refs[:7]
        refs = refs[7:]
    else:
        dq_out, dk_out, dv_out = refs[:3]
        refs = refs[3:]
    qx_ref, kx_ref, dx_ref, vx_ref, delta_ref, dq_ref, p_ref, ds_ref = refs
    width, queries = q_ref.shape
    keys = k_ref.shape[1]
    heads = width // HEAD
    tiles = keys // tile
    scale = 1.0 / math.sqrt(HEAD)
    row = lax.broadcasted_iota(jnp.int32, (16, keys), 0)
    kx_ref[...] = jnp.where(
        (row >= 4) & (row < 7), 1.0, document_rows(kseg_ref[...], (16, keys), True)
    ).astype(LOW)
    vx_ref[...] = jnp.where(row < 3, 1.0, 0.0).astype(LOW)
    documents = document_rows(qseg_ref[...], (16, queries), False)

    def prepare(head, carry):
        delta = jnp.sum(
            dc_ref[rows_at(head, HEAD), :].astype(WIDE) * ctx_ref[rows_at(head, HEAD), :].astype(WIDE),
            axis=0,
            keepdims=True,
        )
        delta_ref[pl.ds(head, 1), :] = delta
        dx_ref[rows_at(head, 16), :] = place_rows(split_three(-delta), 0, (16, queries)).astype(LOW)
        minus = split_three(-lse_ref[pl.ds(head, 1), :])
        qx_ref[rows_at(head, 16), :] = (
            documents + place_rows(minus, 4, (16, queries))
        ).astype(LOW)
        return carry

    lax.fori_loop(0, heads, prepare, 0)

    if prefix:
        for group in range(heads // GROUP):
            wide = slice(group * GROUP * HEAD, (group + 1) * GROUP * HEAD)
            tall = slice(group * GROUP * PAD, (group + 1) * GROUP * PAD)
            scores = contract(pk_ref[tall, :], q_ref[wide, :], 1, 0)
            gains = contract(pv_ref[tall, :], dc_ref[wide, :], 1, 0)
            chances, changes = [], []
            for member in range(GROUP):
                head = group * GROUP + member
                part = slice(member * PAD, (member + 1) * PAD)
                chance = jnp.exp2(scores[part] - lse_ref[head : head + 1, :])
                place = lax.broadcasted_iota(jnp.int32, chance.shape, 0)
                chance = jnp.where(place < prefix, chance, 0.0)
                chances.append(chance.astype(LOW))
                changes.append((chance * (gains[part] - delta_ref[head : head + 1, :])).astype(LOW))
            chances = jnp.concatenate(chances, 0)
            changes = jnp.concatenate(changes, 0)
            dq_ref[wide, :] = contract(pk_ref[tall, :], changes, 0, 0)
            dpk_out[tall, :] = contract(changes, q_ref[wide, :], 1, 1) * (1.0 / LOG2E)
            dpv_out[tall, :] = contract(chances, dc_ref[wide, :], 1, 1)
    else:
        dq_ref[...] = jnp.zeros(dq_ref.shape, WIDE)

    def front(head, part, slot):
        cut = slice(part * tile, (part + 1) * tile)
        query = jnp.concatenate([q_ref[rows_at(head, HEAD), :], qx_ref[rows_at(head, 16), :]], 0)
        key = jnp.concatenate([k_ref[rows_at(head, HEAD), cut], kx_ref[:, cut]], 0)
        scores = contract(query, key, 0, 0)
        if causal:
            place = lax.broadcasted_iota(jnp.int32, scores.shape, 1) + part * tile
            scores = jnp.where(
                place <= lax.broadcasted_iota(jnp.int32, scores.shape, 0), scores, -BIG
            )
        grad = jnp.concatenate([dc_ref[rows_at(head, HEAD), :], dx_ref[rows_at(head, 16), :]], 0)
        value = jnp.concatenate([v_ref[rows_at(head, HEAD), cut], vx_ref[:, cut]], 0)
        gains = contract(grad, value, 0, 0)
        chance = jnp.exp2(scores)
        p_ref[slot] = chance.astype(LOW)
        ds_ref[slot] = (chance * gains).astype(LOW)

    def back(head, part, slot):
        cut = slice(part * tile, (part + 1) * tile)
        rows = rows_at(head, HEAD)
        dv_out[rows, cut] = contract(dc_ref[rows, :], p_ref[slot], 1, 0).astype(LOW)
        dk_out[rows, cut] = (contract(q_ref[rows, :], ds_ref[slot], 1, 0) * (1.0 / LOG2E)).astype(LOW)
        dq_ref[rows, :] += contract(k_ref[rows, cut], ds_ref[slot], 1, 1)

    def one_head(head, carry):
        for part in range(tiles):
            last = part == tiles - 1
            front(
                jnp.minimum(head + 1, heads - 1) if last else head,
                0 if last else part + 1,
                (part + 1) % 2,
            )
            back(head, part, part % 2)
        dq_out[rows_at(head, HEAD), :] = (dq_ref[rows_at(head, HEAD), :] * scale).astype(LOW)
        return carry

    front(0, 0, 0)
    lax.fori_loop(0, heads, one_head, 0)


def block_diagonal(pairs, width):
    count = pairs.shape[0]
    heads = width // HEAD
    padded = jnp.pad(pairs, ((0, PAD - count), (0, 0))).reshape(PAD, heads // GROUP, GROUP, HEAD)
    spread = jnp.einsum("pgae,ab->gapbe", padded, jnp.eye(GROUP, dtype=pairs.dtype))
    return spread.reshape(heads * PAD, GROUP * HEAD)


def from_block_diagonal(grads, count):
    rows, columns = grads.shape
    heads = rows // PAD
    spread = grads.reshape(heads // GROUP, GROUP, PAD, GROUP, HEAD)
    own = jnp.einsum("gapae->pgae", spread)
    return own.reshape(PAD, heads * HEAD)[:count]


def attend_back(
    q_all, kv_all, places, context_grad, context, row_lse, q_segments, k_segments, prefix_pairs, causal
):
    width, queries = context.shape
    keys = kv_all.shape[1]
    tile = min(256, keys // 2)
    lse_rows = row_lse.shape[0]
    heads = width // HEAD
    operands = [q_all, kv_all, kv_all, context_grad, context, row_lse, q_segments, k_segments]
    specs = [
        third(width, queries, places[0]),
        third(width, keys, places[1]),
        third(width, keys, places[2]),
        whole((width, queries)),
        whole((width, queries)),
        whole((lse_rows, queries)),
        whole((1, queries)),
        whole((1, keys)),
    ]
    outs = [
        jax.ShapeDtypeStruct((width, queries), LOW),
        jax.ShapeDtypeStruct((width, keys), LOW),
        jax.ShapeDtypeStruct((width, keys), LOW),
    ]
    count = 0
    if prefix_pairs is not None:
        count = prefix_pairs.shape[0]
        block = (heads * PAD, GROUP * HEAD)
        operands += [
            block_diagonal(prefix_pairs[:, :width], width),
            block_diagonal(prefix_pairs[:, width:], width),
        ]
        specs += [whole(block), whole(block)]
        outs += [jax.ShapeDtypeStruct(block, WIDE)] * 2
    results = pl.pallas_call(
        functools.partial(attend_back_kernel, tile, causal, count),
        grid=(1,),
        out_shape=tuple(outs),
        in_specs=specs,
        out_specs=tuple(whole(out.shape) for out in outs),
        scratch_shapes=[
            pltpu.VMEM((heads * 16, queries), LOW),
            pltpu.VMEM((16, keys), LOW),
            pltpu.VMEM((heads * 16, queries), LOW),
            pltpu.VMEM((16, keys), LOW),
            pltpu.VMEM((lse_rows, queries), WIDE),
            pltpu.VMEM((width, queries), WIDE),
            pltpu.VMEM((2, queries, tile), LOW),
            pltpu.VMEM((2, queries, tile), LOW),
        ],
        compiler_params=pltpu.CompilerParams(vmem_limit_bytes=VMEM_BYTES),
        name="attend_back",
    )(*operands)
    if prefix_pairs is None:
        return (results[0], results[1], results[2], None)
    pair_grad = jnp.concatenate(
        [from_block_diagonal(results[3], count), from_block_diagonal(results[4], count)], axis=1
    )
    return (results[0], results[1], results[2], pair_grad)


def prefix_forward(prefix, prefix_in, prefix_out):
    hidden = jnp.tanh(jnp.dot(prefix, prefix_in, preferred_element_type=WIDE))
    pair_rows = jnp.dot(hidden, prefix_out.astype(WIDE), precision=lax.Precision.HIGHEST)
    return (hidden, pair_rows.astype(LOW))


def prefix_backward(prefix, prefix_in, prefix_out, hidden, pair_grad, place, count):
    def share(value, axis):
        size = value.shape[axis] // count
        return lax.dynamic_slice_in_dim(value, place * size, size, axis).astype(WIDE)

    exact = functools.partial(jnp.matmul, precision=lax.Precision.HIGHEST)
    out_grad = exact(share(hidden, 1).T, pair_grad)
    hidden_grad = exact(pair_grad, prefix_out.astype(WIDE).T) * (1.0 - hidden * hidden)
    in_grad = exact(share(prefix, 1).T, hidden_grad)
    embed_grad = exact(hidden_grad, share(prefix_in, 0).T)
    return (embed_grad, in_grad, out_grad)


def scaled_queries(rows, width):
    row = lax.broadcasted_iota(jnp.int32, (rows.shape[0], 1), 0)
    return (rows * jnp.where(row < width, QUERY_SCALE, 1.0)).astype(LOW)


def self_forward(hidden, qkv_weight, out_weight, prefix_pairs, segments, causal):
    width = hidden.shape[1]
    qkv = scaled_queries(project_wide(qkv_weight, hidden), width)
    context, row_lse = attend(qkv, qkv, (0, 1, 2), segments, segments, prefix_pairs, causal)
    branch = jnp.einsum("it,io->to", context, out_weight, preferred_element_type=WIDE)
    normed, inverse = normalize(hidden.astype(WIDE) + branch)
    return (normed, (qkv, context, row_lse, normed, inverse))


def self_backward(gradient, stored, qkv_weight, out_weight, prefix_pairs, segments, causal):
    qkv, context, row_lse, normed, inverse = stored
    summed_grad = normalize_back(gradient, normed, inverse)
    context_grad = jnp.einsum(
        "io,to->it", out_weight, summed_grad.astype(LOW), preferred_element_type=WIDE
    ).astype(LOW)
    query_grad, key_grad, value_grad, pair_grad = attend_back(
        qkv, qkv, (0, 1, 2), context_grad, context, row_lse, segments, segments, prefix_pairs, causal
    )
    qkv_grad = jnp.concatenate([query_grad, key_grad, value_grad], axis=0)
    hidden_grad = summed_grad + jnp.einsum(
        "ot,io->ti", qkv_grad, qkv_weight, preferred_element_type=WIDE
    )
    return (hidden_grad, pair_grad)


def feed_forward(hidden, up_weight, down_weight, adapter_down, adapter_up):
    hidden_low = hidden.astype(LOW)
    inner_pre = project(hidden_low, up_weight)
    active = gelu_act(inner_pre).astype(LOW)
    narrow = project(hidden_low, adapter_down)
    narrow_act = gelu_act(narrow).astype(LOW)
    summed = hidden + project(active, down_weight) + 4.0 * project(narrow_act, adapter_up)
    normed, inverse = normalize(summed)
    return (normed, (hidden_low, inner_pre, narrow, narrow_act, normed, inverse))


def feed_backward(gradient, stored, up_weight, down_weight, adapter_down, adapter_up):
    hidden_low, inner_pre, narrow, narrow_act, normed, inverse = stored
    summed_grad = normalize_back(gradient, normed, inverse)
    main_grad = summed_grad.astype(LOW)
    side_grad = (4.0 * summed_grad).astype(LOW)
    adapter_up_grad = weight_grad(narrow_act, side_grad)
    narrow_grad = gelu_back(narrow, back_through(side_grad, adapter_up)).astype(LOW)
    adapter_down_grad = weight_grad(hidden_low, narrow_grad)
    inner_grad = gelu_back(inner_pre, back_through(main_grad, down_weight)).astype(LOW)
    hidden_grad = (
        summed_grad + back_through(inner_grad, up_weight) + back_through(narrow_grad, adapter_down)
    )
    return (hidden_grad, adapter_down_grad, adapter_up_grad)


def one_row(
    source,
    target,
    source_segments,
    target_segments,
    cotangent,
    weights,
    enc_pairs,
    dec_pairs,
):
    (
        enc_qkv,
        enc_out,
        enc_up,
        enc_down,
        dec_qkv,
        dec_out,
        cross_q,
        cross_kv,
        cross_out,
        dec_up,
        dec_down,
        enc_adapter_down,
        enc_adapter_up,
        dec_adapter_down,
        dec_adapter_up,
    ) = weights
    width = source.shape[1]
    encoded_mid, encoded_stored = self_forward(
        source, enc_qkv, enc_out, enc_pairs, source_segments, False
    )
    memory, memory_stored = feed_forward(
        encoded_mid, enc_up, enc_down, enc_adapter_down, enc_adapter_up
    )
    decoded_mid, decoded_stored = self_forward(
        target, dec_qkv, dec_out, dec_pairs, target_segments, True
    )
    cross_query = scaled_queries(project_wide(cross_q, decoded_mid.astype(LOW)), width)
    memory_pairs = project_wide(cross_kv, memory.astype(LOW)).astype(LOW)
    cross_context, cross_lse = attend(
        cross_query, memory_pairs, (0, 0, 1), target_segments, source_segments, None, False
    )
    crossed, crossed_inverse = normalize(
        decoded_mid
        + jnp.einsum("it,io->to", cross_context, cross_out, preferred_element_type=WIDE)
    )
    output_wide, output_stored = feed_forward(
        crossed, dec_up, dec_down, dec_adapter_down, dec_adapter_up
    )
    crossed_grad, dec_adapter_down_grad, dec_adapter_up_grad = feed_backward(
        cotangent.astype(WIDE), output_stored, dec_up, dec_down, dec_adapter_down, dec_adapter_up
    )
    cross_sum_grad = normalize_back(crossed_grad, crossed, crossed_inverse)
    context_grad = jnp.einsum(
        "io,to->it", cross_out, cross_sum_grad.astype(LOW), preferred_element_type=WIDE
    ).astype(LOW)
    query_grad, key_grad, value_grad, _ = attend_back(
        cross_query,
        memory_pairs,
        (0, 0, 1),
        context_grad,
        cross_context,
        cross_lse,
        target_segments,
        source_segments,
        None,
        False,
    )
    pair_grad = jnp.concatenate([key_grad, value_grad], axis=0)
    memory_grad = jnp.einsum("ot,io->ti", pair_grad, cross_kv, preferred_element_type=WIDE)
    decoded_grad = cross_sum_grad + jnp.einsum(
        "ot,io->ti", query_grad, cross_q, preferred_element_type=WIDE
    )
    target_grad, dec_pair_grad = self_backward(
        decoded_grad, decoded_stored, dec_qkv, dec_out, dec_pairs, target_segments, True
    )
    encoded_grad, enc_adapter_down_grad, enc_adapter_up_grad = feed_backward(
        memory_grad, memory_stored, enc_up, enc_down, enc_adapter_down, enc_adapter_up
    )
    source_grad, enc_pair_grad = self_backward(
        encoded_grad, encoded_stored, enc_qkv, enc_out, enc_pairs, source_segments, False
    )
    activations = (output_wide.astype(LOW), source_grad.astype(LOW), target_grad.astype(LOW))
    adapter_grads = (
        enc_adapter_down_grad,
        enc_adapter_up_grad,
        dec_adapter_down_grad,
        dec_adapter_up_grad,
    )
    return (activations, adapter_grads, (enc_pair_grad, dec_pair_grad))


def total(values):
    return functools.reduce(lambda left, right: left + right, values)


def shards(
    source,
    target,
    source_segments,
    target_segments,
    cotangent,
    enc_qkv,
    enc_out,
    enc_up,
    enc_down,
    dec_qkv,
    dec_out,
    cross_q,
    cross_kv,
    cross_out,
    dec_up,
    dec_down,
    enc_prefix,
    enc_prefix_in,
    enc_prefix_out,
    enc_adapter_down,
    enc_adapter_up,
    dec_prefix,
    dec_prefix_in,
    dec_prefix_out,
    dec_adapter_down,
    dec_adapter_up,
    *,
    count,
):
    place = lax.axis_index("seq")
    rows = source.shape[0]
    copies = max(count // rows, 1)
    own = max(rows // count, 1)

    def bring(value):
        return lax.all_to_all(jnp.repeat(value, copies, axis=0), "seq", 0, 1, tiled=True)

    def send_back(value):
        return lax.all_to_all(value, "seq", 1, 0, tiled=True)[::copies]

    def own_rows(segments):
        return lax.dynamic_slice_in_dim(segments, place // copies * own, own, 0)

    source_rows, target_rows, cotangent_rows = bring(source), bring(target), bring(cotangent)
    source_marks, target_marks = own_rows(source_segments), own_rows(target_segments)
    enc_hidden, enc_pairs = prefix_forward(enc_prefix, enc_prefix_in, enc_prefix_out)
    dec_hidden, dec_pairs = prefix_forward(dec_prefix, dec_prefix_in, dec_prefix_out)
    weights = (
        enc_qkv,
        enc_out,
        enc_up,
        enc_down,
        dec_qkv,
        dec_out,
        cross_q,
        cross_kv,
        cross_out,
        dec_up,
        dec_down,
        enc_adapter_down,
        enc_adapter_up,
        dec_adapter_down,
        dec_adapter_up,
    )
    results = [
        one_row(
            source_rows[row],
            target_rows[row],
            source_marks[row : row + 1],
            target_marks[row : row + 1],
            cotangent_rows[row],
            weights,
            enc_pairs,
            dec_pairs,
        )
        for row in range(own)
    ]
    activations = [send_back(jnp.stack(parts)) for parts in zip(*(result[0] for result in results))]
    share = 1.0 / copies
    adapters = [total(parts) * share for parts in zip(*(result[1] for result in results))]
    adapters = [
        lax.psum(
            lax.psum_scatter(grad.astype(LOW), "seq", scatter_dimension=0, tiled=True), "dp"
        ).astype(WIDE)
        for grad in adapters
    ]
    pair_grads = [total(parts) * share for parts in zip(*(result[2] for result in results))]
    enc_pair_grad, dec_pair_grad = lax.psum(tuple(pair_grads), ("dp", "seq"))
    enc_prefix_grads = prefix_backward(
        enc_prefix, enc_prefix_in, enc_prefix_out, enc_hidden, enc_pair_grad, place, count
    )
    dec_prefix_grads = prefix_backward(
        dec_prefix, dec_prefix_in, dec_prefix_out, dec_hidden, dec_pair_grad, place, count
    )
    return (
        activations[0],
        activations[1].astype(WIDE),
        activations[2].astype(WIDE),
        *enc_prefix_grads,
        adapters[0],
        adapters[1],
        *dec_prefix_grads,
        adapters[2],
        adapters[3],
    )


def solution(mesh):
    rows = P("dp", "seq", None)
    marks = P("dp", None)
    in_specs = (rows, rows, marks, marks, rows) + (P(),) * 21
    across, down = P(None, "seq"), P("seq", None)
    layer = (across, down, down, down, down)
    return jax.shard_map(
        functools.partial(shards, count=mesh.shape["seq"]),
        mesh=mesh,
        in_specs=in_specs,
        out_specs=(rows, rows, rows) + layer + layer,
        check_vma=False,
    )
```

```python
import functools
import math
from types import SimpleNamespace

import jax
import jax.numpy as jnp
from jax import lax
from jax.experimental import pallas as pl
from jax.experimental.pallas import tpu as pltpu
from jax.sharding import PartitionSpec as P

HEAD = 64
GROUP = 4
PAD = 32
BIG = 2.0**100
LOG2E = math.log2(math.e)
SCALE = 1.0 / math.sqrt(HEAD)
VMEM_BYTES = 60 * 2**20
CHUNK = 256
INNER = 512
LOW = jnp.bfloat16
WIDE = jnp.float32


def contract(left, right, left_dim, right_dim):
    return lax.dot_general(
        left, right, (((left_dim,), (right_dim,)), ((), ())), preferred_element_type=WIDE
    )


def rows_at(index, size, base=0):
    return pl.ds(pl.multiple_of(base + index * size, size), size)


def chunks(size, step):
    step = min(step, size)
    return [slice(start, start + step) for start in range(0, size, step)]


def normalize(value):
    centered = value - jnp.mean(value, axis=-1, keepdims=True)
    inverse = lax.rsqrt(jnp.mean(centered * centered, axis=-1, keepdims=True) + 1e-05)
    return (centered * inverse, inverse)


def normalize_back(gradient, normed, inverse):
    return (
        gradient
        - jnp.mean(gradient, axis=-1, keepdims=True)
        - normed * jnp.mean(gradient * normed, axis=-1, keepdims=True)
    ) * inverse


def gelu_both(value):
    scale = math.sqrt(2.0 / math.pi)
    square = value * value
    half = 0.5 + 0.5 * jnp.tanh(value * (scale + (scale * 0.044715) * square))
    active = value * half
    slope = half + active * (1.0 - half) * (2.0 * scale + (6.0 * scale * 0.044715) * square)
    return (active, slope)


class Mover:
    def __init__(self, semaphores):
        self.semaphores = semaphores
        self.used = 0

    def start(self, origin, goal):
        copy = pltpu.make_async_copy(origin, goal, self.semaphores.at[self.used])
        self.used += 1
        copy.start()
        return copy


def run_kernel(body, name, near, far, near_outs, far_outs, scratch, flops, links=0, collective=None):
    in_names = list(near) + list(far)
    out_names = list(near_outs) + list(far_outs)
    names = in_names + out_names + list(scratch) + ["semaphores"]
    link_scratch = []
    remote = {}
    if collective is not None:
        names += ["sent", "arrived"]
        link_scratch = [pltpu.SemaphoreType.DMA((links,)), pltpu.SemaphoreType.DMA((links,))]
        remote = dict(collective_id=collective, has_side_effects=True)

    def kernel(*refs):
        body(SimpleNamespace(**dict(zip(names, refs))))

    near_spec = pl.BlockSpec(memory_space=pltpu.VMEM)
    far_spec = pl.BlockSpec(memory_space=pl.ANY)
    results = pl.pallas_call(
        kernel,
        out_shape=tuple(
            jax.ShapeDtypeStruct(*out) for out in (*near_outs.values(), *far_outs.values())
        ),
        in_specs=[near_spec] * len(near) + [far_spec] * len(far),
        out_specs=tuple([near_spec] * len(near_outs) + [far_spec] * len(far_outs)),
        scratch_shapes=[pltpu.VMEM(*shape) for shape in scratch.values()]
        + [pltpu.SemaphoreType.DMA((40,))]
        + link_scratch,
        compiler_params=pltpu.CompilerParams(vmem_limit_bytes=VMEM_BYTES, **remote),
        cost_estimate=pl.CostEstimate(flops=flops, bytes_accessed=2**24, transcendentals=0),
        name=name,
    )(*near.values(), *far.values())
    return SimpleNamespace(**dict(zip(out_names, results)))


class Links:
    def __init__(self, sent, arrived, groups):
        self.sent, self.arrived = sent, arrived
        self.used = 0
        self.place = {axis: lax.axis_index(axis) for axis in ("dp", "seq")}
        self.sizes = groups
        barrier = pltpu.get_barrier_semaphore()
        peers = 0
        for axis, size in groups.items():
            for shift in range(1, size):
                pl.semaphore_signal(
                    barrier, inc=1, device_id=self.device(axis, shift), device_id_type=pl.DeviceIdType.MESH
                )
                peers += 1
        pl.semaphore_wait(barrier, peers)

    def peer(self, axis, shift):
        return lax.rem(self.place[axis] + shift, self.sizes[axis])

    def device(self, axis, shift):
        index = self.peer(axis, shift)
        return (index, self.place["seq"]) if axis == "dp" else (self.place["dp"], index)

    def start(self, axis, shift, origin, goal):
        copy = pltpu.make_async_remote_copy(
            src_ref=origin,
            dst_ref=goal,
            send_sem=self.sent.at[self.used],
            recv_sem=self.arrived.at[self.used],
            device_id=self.device(axis, shift),
            device_id_type=pl.DeviceIdType.MESH,
        )
        self.used += 1
        copy.start()
        return copy

    def scatter(self, axis, pick, goal):
        return [
            self.start(axis, shift, pick(self.peer(axis, shift)), goal)
            for shift in range(1, self.sizes[axis])
        ]


def split_three(value):
    high = value.astype(LOW).astype(WIDE)
    rest = value - high
    middle = rest.astype(LOW).astype(WIDE)
    return (high, middle, rest - middle)


def place_rows(parts, first, shape):
    row = lax.broadcasted_iota(jnp.int32, shape, 0)
    out = jnp.zeros(shape, WIDE)
    for offset, part in enumerate(parts):
        out = jnp.where(row == first + offset, part, out)
    return out


def document_rows(segments, tokens, is_key):
    row = lax.broadcasted_iota(jnp.int32, (16, tokens), 0)
    same = row == segments
    if is_key:
        return jnp.where(row < 4, jnp.where(same, 0.0, -BIG), 0.0)
    return jnp.where(same & (row < 4), 1.0, 0.0)


def column_peak(scores, peak):
    for start in range(0, scores.shape[0], 8):
        peak = jnp.maximum(peak, scores[start : start + 8])
    return peak


def from_column(value, low):
    if low == 0:
        return value
    return jnp.concatenate([jnp.zeros((value.shape[0], low), value.dtype), value], 1)


def attend(a, causal, prefix):
    queries, keys = a.q.shape[1], a.k.shape[1]
    width = a.context.shape[0]
    heads = width // HEAD
    tile = min(256, keys)
    tiles = keys // tile
    a.qx[:16, :queries] = document_rows(a.q_marks, queries, False).astype(LOW)
    a.kx[:, :keys] = document_rows(a.k_marks, keys, True).astype(LOW)
    start_peak = jnp.full((8, queries), -4.0 * BIG, WIDE)

    def query_of(head):
        return jnp.concatenate([a.q[rows_at(head, HEAD, a.q0), :], a.qx[:16, :queries]], 0)

    def prefix_scores(head, slot):
        if not prefix:
            return start_peak
        scores = contract(a.pair_keys[rows_at(head, HEAD), :], a.q[rows_at(head, HEAD, a.q0), :], 0, 0)
        row = lax.broadcasted_iota(jnp.int32, scores.shape, 0)
        scores = jnp.where(row < prefix, scores, -BIG)
        a.pair_scores[slot, :, :queries] = scores
        return column_peak(scores, start_peak)

    def score_tile(head, part, query, slot, peak):
        cut = slice(part * tile, (part + 1) * tile)
        low = part * tile if causal else 0
        key = jnp.concatenate([a.k[rows_at(head, HEAD, a.k0), cut], a.kx[:, cut]], 0)
        scores = contract(key, query[:, low:], 0, 0)
        if causal:
            place = lax.broadcasted_iota(jnp.int32, scores.shape, 0)
            scores = jnp.where(place <= lax.broadcasted_iota(jnp.int32, scores.shape, 1), scores, -BIG)
        a.scores[slot, cut, low:queries] = scores
        new = column_peak(scores, peak[:, low:])
        return new if low == 0 else jnp.concatenate([peak[:, :low], new], 1)

    def step(head, following, slot):
        other = 1 - slot
        query = query_of(following)
        peak = jnp.max(a.peak[slot, :, :queries], 0, keepdims=True)
        next_peak = prefix_scores(following, other)
        context = jnp.zeros((HEAD + 16, queries), WIDE)
        if prefix:
            weights = jnp.exp2(a.pair_scores[slot, :, :queries] - peak).astype(LOW)
            value = jnp.concatenate(
                [a.pair_values[rows_at(head, HEAD), :], jnp.ones((16, PAD), LOW)], 0
            )
            context = contract(value, weights, 1, 0)
        for part in range(tiles):
            next_peak = score_tile(following, part, query, other, next_peak)
            cut = slice(part * tile, (part + 1) * tile)
            low = part * tile if causal else 0
            weights = jnp.exp2(a.scores[slot, cut, low:queries] - peak[:, low:]).astype(LOW)
            value = jnp.concatenate(
                [a.v[rows_at(head, HEAD, a.v0), cut], jnp.ones((16, tile), LOW)], 0
            )
            context = context + from_column(contract(value, weights, 1, 0), low)
        a.peak[other, :, :queries] = next_peak
        total = context[HEAD : HEAD + 1]
        a.context[rows_at(head, HEAD), :] = (context[:HEAD] * (1.0 / total)).astype(LOW)
        a.lse[pl.ds(head, 1), :] = peak + jnp.log2(total)

    first = query_of(0)
    peak = prefix_scores(0, 0)
    for part in range(tiles):
        peak = score_tile(0, part, first, 0, peak)
    a.peak[0, :, :queries] = peak

    def pair(index, carry):
        step(2 * index, 2 * index + 1, 0)
        step(2 * index + 1, jnp.minimum(2 * index + 2, heads - 1), 1)
        return carry

    lax.fori_loop(0, heads // 2, pair, 0)


def block_diagonal(pairs, group, first):
    wide = GROUP * HEAD
    rows = pairs[:, first + group * wide : first + (group + 1) * wide]
    column = lax.broadcasted_iota(jnp.int32, rows.shape, 1)
    parts = [
        jnp.where((column >= member * HEAD) & (column < (member + 1) * HEAD), rows.astype(WIDE), 0.0)
        for member in range(GROUP)
    ]
    return jnp.concatenate(parts, 0).astype(LOW)


def own_columns(grads):
    column = lax.broadcasted_iota(jnp.int32, (PAD, GROUP * HEAD), 1)
    out = jnp.zeros((PAD, GROUP * HEAD), WIDE)
    for member in range(GROUP):
        own = (column >= member * HEAD) & (column < (member + 1) * HEAD)
        out = jnp.where(own, grads[member * PAD : (member + 1) * PAD], out)
    return out


def attend_back(a, causal, prefix):
    queries, keys = a.q.shape[1], a.k.shape[1]
    width = a.context.shape[0]
    heads = width // HEAD
    tile = min(256, keys // 2)
    tiles = keys // tile
    row = lax.broadcasted_iota(jnp.int32, (16, keys), 0)
    a.kx[:, :keys] = jnp.where(
        (row >= 4) & (row < 7), 1.0, document_rows(a.k_marks, keys, True)
    ).astype(LOW)
    a.vx[:, :keys] = jnp.where(row < 3, 1.0, 0.0).astype(LOW)
    documents = document_rows(a.q_marks, queries, False)

    def prepare(head, carry):
        rows = rows_at(head, HEAD)
        delta = jnp.sum(
            a.d_context[rows, :].astype(WIDE) * a.context[rows, :].astype(WIDE),
            axis=0,
            keepdims=True,
        )
        a.delta[pl.ds(head, 1), :queries] = delta
        a.dx[rows_at(head, 16), :queries] = place_rows(
            split_three(-delta), 0, (16, queries)
        ).astype(LOW)
        minus = split_three(-a.lse[pl.ds(head, 1), :])
        a.qx[rows_at(head, 16), :queries] = (
            documents + place_rows(minus, 4, (16, queries))
        ).astype(LOW)
        return carry

    lax.fori_loop(0, heads, prepare, 0)

    if prefix:
        for group in range(heads // GROUP):
            start = group * GROUP * HEAD
            own = slice(start, start + GROUP * HEAD)
            query = a.q[a.q0 + start : a.q0 + start + GROUP * HEAD, :]
            grad = a.d_context[own, :]
            pair_keys = block_diagonal(a.pairs[...], group, 0)
            pair_values = block_diagonal(a.pairs[...], group, width)
            scores = contract(pair_keys, query, 1, 0)
            gains = contract(pair_values, grad, 1, 0)
            chances, changes = [], []
            for member in range(GROUP):
                head = group * GROUP + member
                part = slice(member * PAD, (member + 1) * PAD)
                chance = jnp.exp2(scores[part] - a.lse[head : head + 1, :])
                place = lax.broadcasted_iota(jnp.int32, chance.shape, 0)
                chance = jnp.where(place < prefix, chance, 0.0)
                chances.append(chance)
                changes.append(chance * (gains[part] - a.delta[head : head + 1, :queries]))
            chances = jnp.concatenate(chances, 0).astype(LOW)
            changes = jnp.concatenate(changes, 0).astype(LOW)
            a.dq_sum[own, :queries] = contract(pair_keys, changes, 0, 0)
            a.d_pairs[:, own] = own_columns(contract(changes, query, 1, 1)) * (1.0 / LOG2E)
            a.d_pairs[:, width + start : width + start + GROUP * HEAD] = own_columns(
                contract(chances, grad, 1, 1)
            )
    else:
        a.dq_sum[:, :queries] = jnp.zeros((width, queries), WIDE)

    def front(head, part, slot):
        cut = slice(part * tile, (part + 1) * tile)
        low = part * tile if causal else 0
        query = jnp.concatenate(
            [a.q[rows_at(head, HEAD, a.q0), low:], a.qx[rows_at(head, 16), low:queries]], 0
        )
        key = jnp.concatenate([a.k[rows_at(head, HEAD, a.k0), cut], a.kx[:, cut]], 0)
        scores = contract(query, key, 0, 0)
        if causal:
            place = lax.broadcasted_iota(jnp.int32, scores.shape, 1)
            scores = jnp.where(place <= lax.broadcasted_iota(jnp.int32, scores.shape, 0), scores, -BIG)
        grad = jnp.concatenate(
            [a.d_context[rows_at(head, HEAD), low:], a.dx[rows_at(head, 16), low:queries]], 0
        )
        value = jnp.concatenate([a.v[rows_at(head, HEAD, a.v0), cut], a.vx[:, cut]], 0)
        gains = contract(grad, value, 0, 0)
        chance = jnp.exp2(scores)
        a.chances[slot, low:queries, :tile] = chance.astype(LOW)
        a.changes[slot, low:queries, :tile] = (chance * gains).astype(LOW)

    def back(head, part, slot):
        cut = slice(part * tile, (part + 1) * tile)
        low = part * tile if causal else 0
        chances = a.chances[slot, low:queries, :tile]
        changes = a.changes[slot, low:queries, :tile]
        a.dv[rows_at(head, HEAD, a.dv0), cut] = contract(
            a.d_context[rows_at(head, HEAD), low:], chances, 1, 0
        ).astype(LOW)
        a.dk[rows_at(head, HEAD, a.dk0), cut] = (
            contract(a.q[rows_at(head, HEAD, a.q0), low:], changes, 1, 0) * (1.0 / LOG2E)
        ).astype(LOW)
        a.dq_sum[rows_at(head, HEAD), low:queries] += contract(
            a.k[rows_at(head, HEAD, a.k0), cut], changes, 1, 1
        )

    def one_head(head, carry):
        for part in range(tiles):
            last = part == tiles - 1
            front(
                jnp.minimum(head + 1, heads - 1) if last else head,
                0 if last else part + 1,
                (part + 1) % 2,
            )
            back(head, part, part % 2)
        a.dq[rows_at(head, HEAD, a.dq0), :] = (
            a.dq_sum[rows_at(head, HEAD), :queries] * SCALE
        ).astype(LOW)
        return carry

    front(0, 0, 0)
    lax.fori_loop(0, heads, one_head, 0)


def project_wide(out, weight, rows, scaled, place=slice(None)):
    for cut in chunks(weight.shape[1], 256):
        result = contract(weight[:, cut], rows, 0, 1)
        if cut.start < scaled:
            result = result * (SCALE * LOG2E)
        out[cut, place] = result.astype(LOW)


def add_and_normalize(hidden, context, weight, normed, inverse):
    for cut in chunks(hidden.shape[0], CHUNK):
        summed = hidden[cut, :].astype(WIDE) + contract(context[:, cut], weight[...], 0, 0)
        result, scale = normalize(summed)
        normed[cut, :] = result.astype(LOW)
        inverse[cut, :] = scale


def feed_forward(hidden, up, down, adapter_down, adapter_up, total, slopes_of, store, narrow):
    cuts = chunks(hidden.shape[0], CHUNK)

    def block(index, first, second, factor, is_first):
        place = slopes_of(index)
        value = contract(hidden[cuts[0], :], first(), 1, 0)
        for number, cut in enumerate(cuts):
            following = None
            if number + 1 < len(cuts):
                following = contract(hidden[cuts[number + 1], :], first(), 1, 0)
            active, slope = gelu_both(value)
            place[cut, :] = slope.astype(LOW)
            if factor != 1.0:
                narrow[cut, :] = active.astype(LOW)
                active = active * factor
            product = contract(active.astype(LOW), second(), 1, 0)
            if is_first:
                total[cut, :] = hidden[cut, :].astype(WIDE) + product
            else:
                total[cut, :] += product
            value = following
        store(index)

    count = up.shape[1] // INNER
    block(0, lambda: adapter_down[...], lambda: adapter_up[...], 4.0, True)

    def main(index, carry):
        columns = rows_at(index, INNER)
        block(index + 1, lambda: up[:, columns], lambda: down[columns, :], 1.0, False)
        return carry

    lax.fori_loop(0, count, main, 0)


def finish_forward(total, normed, inverse):
    for cut in chunks(total.shape[0], CHUNK):
        result, scale = normalize(total[cut, :])
        normed[cut, :] = result.astype(LOW)
        inverse[cut, :] = scale


def feed_back(f):
    tokens = f.hidden.shape[0]
    cuts = chunks(tokens, CHUNK)
    for cut in cuts:
        value = f.grad[cut, :]
        f.low[cut, :] = value.astype(LOW)
        f.side[cut, :] = (4.0 * value).astype(LOW)

    def block(index, origin, first, second, keep):
        place = f.slopes(index)
        value = contract(origin[cuts[0], :], first(), 1, 1)
        for number, cut in enumerate(cuts):
            following = None
            if number + 1 < len(cuts):
                following = contract(origin[cuts[number + 1], :], first(), 1, 1)
            change = (value * place[cut, :].astype(WIDE)).astype(LOW)
            if keep is not None:
                keep[cut, :] = change
            f.grad[cut, :] += contract(change, second(), 1, 1)
            value = following

    block(0, f.side, lambda: f.adapter_up[...], lambda: f.adapter_down[...], f.d_narrow)
    f.d_adapter_up[...] = contract(f.narrow[...], f.side[...], 0, 0).astype(LOW)
    f.d_adapter_down[...] = contract(f.hidden[...], f.d_narrow[...], 0, 0).astype(LOW)

    def main(index, carry):
        columns = rows_at(index, INNER)
        block(index + 1, f.low, lambda: f.down[columns, :], lambda: f.up[:, columns], None)
        return carry

    lax.fori_loop(0, f.up.shape[1] // INNER, main, 0)


def normalize_back_all(grad, normed, inverse, out):
    for cut in chunks(grad.shape[0], CHUNK):
        out[cut, :] = normalize_back(
            grad[cut, :].astype(WIDE), normed[cut, :].astype(WIDE), inverse[cut, :]
        ).astype(out.dtype)


def context_back(out, weight, grad):
    value = grad[...].astype(LOW)
    for cut in chunks(weight.shape[0], 256):
        out[cut, :] = contract(weight[cut, :], value, 1, 1).astype(LOW)


def prefix_pairs(prefix, first, second, hidden, pairs, pairs_wide):
    count = prefix.shape[0]
    hidden[...] = jnp.zeros(hidden.shape, WIDE)
    hidden[:count, :] = jnp.tanh(contract(prefix[...], first[...], 1, 0))
    parts = [part.astype(LOW) for part in split_three(hidden[...])]
    pairs[...] = total_of([contract(part, second[...], 1, 0) for part in parts]).astype(LOW)
    pairs_wide[...] = total_of([contract(second[...], part, 0, 1) for part in parts]).astype(LOW)


def encoder_forward(w, group, copies):
    width = w.source.shape[2]
    share, later_share = w.source.shape[1], w.target.shape[1]
    tokens, later_tokens = share * group, later_share * group
    inner = w.enc_up.shape[1]
    narrow = w.enc_adapter_down.shape[1]
    units = w.enc_prefix_in.shape[1]
    count = w.enc_prefix.shape[0]
    blocks = 1 + inner // INNER

    def body(r):
        move = Mover(r.semaphores)
        weights = [move.start(r.enc_qkv, r.qkv_weight)]
        enc_first, dec_first = r.mid_v.at[:width, :units], r.memory_v.at[:width, :units]
        enc_second, dec_second = r.up.at[:units, : 2 * width], r.up.at[:units, 2 * width : 4 * width]
        weights.append(move.start(r.enc_prefix_in, enc_first))
        weights.append(move.start(r.enc_prefix_out, enc_second))
        weights.append(move.start(r.dec_prefix_in, dec_first))
        weights.append(move.start(r.dec_prefix_out, dec_second))
        links = Links(r.sent, r.arrived, {"seq": group})
        me = links.place["seq"]
        row = me // copies

        def tokens_of(place, size):
            return pl.ds(pl.multiple_of(place * size, size), size)

        def bring(origin, goal, size):
            own = tokens_of(me, size)
            copies_out = links.scatter("seq", lambda peer: origin.at[peer // copies], goal.at[own, :])
            return (move.start(origin.at[row], goal.at[own, :]), copies_out)

        here, sources = bring(r.source, r.x, share)
        out_weight = move.start(r.enc_out, r.out_weight)
        adapters = [
            move.start(r.enc_adapter_down, r.a_down),
            move.start(r.enc_adapter_up, r.a_up),
        ]
        pair_weight = move.start(r.cross_kv, r.pair_weight)
        for copy in weights:
            copy.wait()
        prefix_pairs(r.enc_prefix, enc_first, enc_second, r.enc_hidden, r.enc_pairs, r.enc_pairs_wide)
        prefix_pairs(r.dec_prefix, dec_first, dec_second, r.dec_hidden, r.dec_pairs, r.dec_pairs_wide)
        ups = [move.start(r.enc_up, r.up), move.start(r.enc_down, r.down)]
        here.wait()
        if share % 128 == 0:
            place = tokens_of(me, share)
            project_wide(r.qkv_v, r.qkv_weight, r.x[place, :], width, place)
            for shift, copy in enumerate(sources, 1):
                copy.wait()
                place = tokens_of(lax.rem(me + group - shift, group), share)
                project_wide(r.qkv_v, r.qkv_weight, r.x[place, :], width, place)
        else:
            for copy in sources:
                copy.wait()
            project_wide(r.qkv_v, r.qkv_weight, r.x[...], width)
        later = [
            bring(r.target, r.target_rows, later_share),
            bring(r.cotangent, r.cotangent_rows, later_share),
        ]
        outs = [move.start(r.qkv_v, r.qkv)]
        marks = r.marks[pl.ds(row, 1), :]
        attend(
            SimpleNamespace(
                q=r.qkv_v, k=r.qkv_v, v=r.qkv_v, q0=0, k0=width, v0=2 * width,
                q_marks=marks, k_marks=marks, pair_keys=r.enc_pairs_wide.at[:width],
                pair_values=r.enc_pairs_wide.at[width:],
                context=r.context_v, lse=r.lse, qx=r.qx, kx=r.kx, scores=r.scores,
                pair_scores=r.pair_scores, peak=r.peak,
            ),
            False,
            count,
        )
        outs.append(move.start(r.context_v, r.context))
        out_weight.wait()
        add_and_normalize(r.x, r.context_v, r.out_weight, r.mid_v, r.mid_inverse)
        outs.append(move.start(r.mid_v, r.mid))
        for copy in adapters + ups:
            copy.wait()
        feed_forward(
            r.mid_v, r.up, r.down, r.a_down, r.a_up, r.total,
            lambda index: r.slopes_v.at[index], lambda index: None, r.narrow_v,
        )
        outs.append(move.start(r.slopes_v, r.slopes))
        outs.append(move.start(r.narrow_v, r.narrow))
        finish_forward(r.total, r.memory_v, r.memory_inverse)
        outs.append(move.start(r.memory_v, r.memory))
        pair_weight.wait()
        project_wide(r.pairs_v, r.pair_weight, r.memory_v[...], 0)
        outs.append(move.start(r.pairs_v, r.memory_pairs))
        for own, remote in later:
            own.wait()
            for copy in remote:
                copy.wait()
        for copy in outs:
            copy.wait()

    return run_kernel(
        body,
        "encoder_forward",
        near=dict(marks=w.source_segments, enc_prefix=w.enc_prefix, dec_prefix=w.dec_prefix),
        far=dict(
            source=w.source, target=w.target, cotangent=w.cotangent, enc_qkv=w.enc_qkv,
            enc_out=w.enc_out, enc_up=w.enc_up, enc_down=w.enc_down,
            enc_adapter_down=w.enc_adapter_down, enc_adapter_up=w.enc_adapter_up,
            cross_kv=w.cross_kv, enc_prefix_in=w.enc_prefix_in, enc_prefix_out=w.enc_prefix_out,
            dec_prefix_in=w.dec_prefix_in, dec_prefix_out=w.dec_prefix_out,
        ),
        near_outs=dict(
            lse=((16, tokens), WIDE), mid_inverse=((tokens, 1), WIDE),
            memory_inverse=((tokens, 1), WIDE),
            enc_hidden=((PAD, units), WIDE), enc_pairs=((PAD, 2 * width), LOW),
            dec_hidden=((PAD, units), WIDE), dec_pairs=((PAD, 2 * width), LOW),
            dec_pairs_wide=((2 * width, PAD), LOW),
        ),
        far_outs=dict(
            qkv=((3 * width, tokens), LOW), context=((width, tokens), LOW), mid=((tokens, width), LOW),
            slopes=((blocks, tokens, INNER), LOW), narrow=((tokens, narrow), LOW),
            memory=((tokens, width), LOW), memory_pairs=((2 * width, tokens), LOW),
            target_rows=((later_tokens, width), LOW), cotangent_rows=((later_tokens, width), LOW),
        ),
        scratch=dict(
            x=((tokens, width), LOW), qkv_weight=((width, 3 * width), LOW),
            enc_pairs_wide=((2 * width, PAD), LOW),
            out_weight=((width, width), LOW), a_down=((width, narrow), LOW),
            a_up=((narrow, width), LOW), up=((width, inner), LOW), down=((inner, width), LOW),
            pair_weight=((width, 2 * width), LOW), qkv_v=((3 * width, tokens), LOW),
            context_v=((width, tokens), LOW), mid_v=((tokens, width), LOW),
            slopes_v=((blocks, tokens, INNER), LOW), narrow_v=((tokens, narrow), LOW),
            memory_v=((tokens, width), LOW), pairs_v=((2 * width, tokens), LOW),
            total=((tokens, width), WIDE), qx=((16, tokens), LOW), kx=((16, tokens), LOW),
            scores=((2, tokens, tokens), WIDE), pair_scores=((2, PAD, tokens), WIDE),
            peak=((2, 8, tokens), WIDE),
        ),
        flops=2 * tokens * width * 11776 + 4 * tokens * tokens * width,
        links=3 * (group - 1),
        collective=0,
    )


def decoder(forward, w, copies):
    tokens, width = forward.target_rows.shape
    keys = forward.memory_pairs.shape[1]
    count = w.dec_prefix.shape[0]
    inner = w.dec_up.shape[1]
    narrow = w.dec_adapter_down.shape[1]
    blocks = 1 + inner // INNER
    heads = width // HEAD

    def body(r):
        move = Mover(r.semaphores)
        ins = [move.start(r.target, r.x), move.start(r.dec_qkv, r.qkv_weight)]
        for copy in ins:
            copy.wait()
        out_weight = move.start(r.dec_out, r.out_weight)
        crosses = [
            move.start(r.cross_q, r.query_weight),
            move.start(r.memory_pairs, r.pairs_v),
            move.start(r.cross_out, r.cross_out_weight),
        ]
        adapters = [
            move.start(r.dec_adapter_down, r.a_down),
            move.start(r.dec_adapter_up, r.a_up),
        ]
        ups = [move.start(r.dec_up, r.up), move.start(r.dec_down, r.down)]
        cotangents = move.start(r.cotangent, r.cotangent_v)
        project_wide(r.qkv, r.qkv_weight, r.x[...], width)
        row = pl.ds(lax.axis_index("seq") // copies, 1)
        marks, source_marks = r.marks[row, :], r.source_marks[row, :]
        shared = dict(
            qx=r.qx, kx=r.kx, scores=r.scores, pair_scores=r.pair_scores, peak=r.peak, dx=r.dx,
            vx=r.vx, delta=r.delta, dq_sum=r.dq_sum, chances=r.chances, changes=r.changes,
            d_context=r.d_context,
        )
        self_part = SimpleNamespace(
            q=r.qkv, k=r.qkv, v=r.qkv, q0=0, k0=width, v0=2 * width,
            q_marks=marks, k_marks=marks, pair_keys=r.pairs_wide.at[:width],
            pair_values=r.pairs_wide.at[width:], pairs=r.pairs, context=r.context, lse=r.lse,
            dq=r.d_qkv, dk=r.d_qkv, dv=r.d_qkv, dq0=0, dk0=width, dv0=2 * width,
            d_pairs=r.d_pairs, **shared,
        )
        attend(self_part, True, count)
        out_weight.wait()
        add_and_normalize(r.x, r.context, r.out_weight, r.mid, r.mid_inverse)
        for copy in crosses:
            copy.wait()
        project_wide(r.query, r.query_weight, r.mid[...], width)
        cross_part = SimpleNamespace(
            q=r.query, k=r.pairs_v, v=r.pairs_v, q0=0, k0=0, v0=width,
            q_marks=marks, k_marks=source_marks, context=r.cross_context, lse=r.cross_lse,
            dq=r.d_query, dk=r.d_pairs_v, dv=r.d_pairs_v, dq0=0, dk0=0, dv0=width, **shared,
        )
        attend(cross_part, False, 0)
        add_and_normalize(r.mid, r.cross_context, r.cross_out_weight, r.crossed, r.crossed_inverse)
        for copy in adapters + ups + [cotangents]:
            copy.wait()
        feed_forward(
            r.crossed, r.up, r.down, r.a_down, r.a_up, r.total,
            lambda index: r.slopes.at[index], lambda index: None, r.narrow,
        )
        finish_forward(r.total, r.out_v, r.out_inverse)
        outs = [move.start(r.out_v, r.out)]
        normalize_back_all(r.cotangent_v, r.out_v, r.out_inverse, r.total)
        feed_back(
            SimpleNamespace(
                grad=r.total, low=r.low, side=r.side, hidden=r.crossed, narrow=r.narrow, up=r.up,
                down=r.down, adapter_down=r.a_down, adapter_up=r.a_up,
                slopes=lambda index: r.slopes.at[index], d_adapter_down=r.d_a_down,
                d_adapter_up=r.d_a_up, d_narrow=r.d_narrow,
            )
        )
        outs.append(move.start(r.d_a_down, r.adapter_down_grad))
        outs.append(move.start(r.d_a_up, r.adapter_up_grad))
        normalize_back_all(r.total, r.crossed, r.crossed_inverse, r.total)
        context_back(r.d_context, r.cross_out_weight, r.total)
        attend_back(cross_part, False, 0)
        outs.append(move.start(r.d_pairs_v, r.memory_pairs_grad))
        for cut in chunks(tokens, CHUNK):
            r.total[cut, :] += contract(r.d_query[:, cut], r.query_weight[...], 0, 1)
        normalize_back_all(r.total, r.mid, r.mid_inverse, r.total)
        context_back(r.d_context, r.out_weight, r.total)
        attend_back(self_part, True, count)
        for cut in chunks(tokens, CHUNK):
            r.x[cut, :] = (
                r.total[cut, :] + contract(r.d_qkv[:, cut], r.qkv_weight[...], 0, 1)
            ).astype(LOW)
        outs.append(move.start(r.x, r.target_grad))
        for copy in outs:
            copy.wait()

    return run_kernel(
        body,
        "decoder",
        near=dict(
            marks=w.target_segments, source_marks=w.source_segments,
            pairs_wide=forward.dec_pairs_wide, pairs=forward.dec_pairs,
        ),
        far=dict(
            target=forward.target_rows, cotangent=forward.cotangent_rows,
            memory_pairs=forward.memory_pairs, dec_qkv=w.dec_qkv,
            dec_out=w.dec_out, cross_q=w.cross_q, cross_out=w.cross_out, dec_up=w.dec_up,
            dec_down=w.dec_down, dec_adapter_down=w.dec_adapter_down,
            dec_adapter_up=w.dec_adapter_up,
        ),
        near_outs=dict(d_pairs=((PAD, 2 * width), WIDE)),
        far_outs=dict(
            out=((tokens, width), LOW), target_grad=((tokens, width), LOW),
            memory_pairs_grad=((2 * width, keys), LOW), adapter_down_grad=((width, narrow), LOW),
            adapter_up_grad=((narrow, width), LOW),
        ),
        scratch=dict(
            x=((tokens, width), LOW), cotangent_v=((tokens, width), LOW),
            qkv_weight=((width, 3 * width), LOW), out_weight=((width, width), LOW),
            query_weight=((width, width), LOW), cross_out_weight=((width, width), LOW),
            pairs_v=((2 * width, keys), LOW), a_down=((width, narrow), LOW),
            a_up=((narrow, width), LOW), up=((width, inner), LOW), down=((inner, width), LOW),
            qkv=((3 * width, tokens), LOW), context=((width, tokens), LOW),
            mid=((tokens, width), LOW), mid_inverse=((tokens, 1), WIDE),
            query=((width, tokens), LOW), cross_context=((width, tokens), LOW),
            crossed=((tokens, width), LOW), crossed_inverse=((tokens, 1), WIDE),
            out_v=((tokens, width), LOW), out_inverse=((tokens, 1), WIDE),
            slopes=((blocks, tokens, INNER), LOW), narrow=((tokens, narrow), LOW),
            low=((tokens, width), LOW), side=((tokens, width), LOW), d_narrow=((tokens, narrow), LOW),
            d_a_down=((width, narrow), LOW), d_a_up=((narrow, width), LOW),
            total=((tokens, width), WIDE), lse=((16, tokens), WIDE), cross_lse=((16, tokens), WIDE),
            d_context=((width, tokens), LOW), d_query=((width, tokens), LOW),
            d_pairs_v=((2 * width, keys), LOW), d_qkv=((3 * width, tokens), LOW),
            qx=((heads * 16, tokens), LOW), kx=((16, keys), LOW),
            scores=((2, keys, tokens), WIDE), pair_scores=((2, PAD, tokens), WIDE),
            peak=((2, 8, tokens), WIDE), dx=((heads * 16, tokens), LOW), vx=((16, keys), LOW),
            delta=((16, tokens), WIDE), dq_sum=((width, tokens), WIDE),
            chances=((2, tokens, 256), LOW), changes=((2, tokens, 256), LOW),
        ),
        flops=4 * tokens * width * 11776 + 14 * tokens * (keys + tokens) * width,
    )


def encoder_feed_back(dec, forward, w, group):
    tokens, width = forward.memory.shape
    inner = w.enc_up.shape[1]
    narrow = w.enc_adapter_down.shape[1]
    blocks = 1 + inner // INNER

    def body(r):
        move = Mover(r.semaphores)
        firsts = [
            move.start(r.memory_pairs_grad, r.d_pairs),
            move.start(r.cross_kv, r.pair_weight),
            move.start(r.memory, r.memory_v),
        ]
        adapters = [
            move.start(r.enc_adapter_down, r.a_down),
            move.start(r.enc_adapter_up, r.a_up),
            move.start(r.narrow, r.narrow_v),
            move.start(r.mid, r.mid_v),
        ]
        ups = [
            move.start(r.slopes, r.slopes_v),
            move.start(r.enc_down, r.down),
            move.start(r.enc_up, r.up),
            move.start(r.enc_out, r.out_weight),
        ]
        links = Links(r.sent, r.arrived, {"seq": group})
        me = links.place["seq"]
        crossing = []
        for origin, goal in ((r.out, r.out_all), (r.target_grad, r.target_grad_all)):
            crossing += links.scatter("seq", lambda peer: origin.at[peer], goal.at[me])
            crossing.append(move.start(origin.at[me], goal.at[me]))
        for copy in firsts:
            copy.wait()
        for cut in chunks(tokens, CHUNK):
            grad = contract(r.d_pairs[:, cut], r.pair_weight[...], 0, 1)
            r.total[cut, :] = normalize_back(
                grad, r.memory_v[cut, :].astype(WIDE), r.memory_inverse[cut, :]
            )
        for copy in adapters + ups:
            copy.wait()
        feed_back(
            SimpleNamespace(
                grad=r.total, low=r.low, side=r.side, hidden=r.mid_v, narrow=r.narrow_v, up=r.up,
                down=r.down, adapter_down=r.a_down, adapter_up=r.a_up,
                slopes=lambda index: r.slopes_v.at[index], d_adapter_down=r.d_a_down,
                d_adapter_up=r.d_a_up, d_narrow=r.d_narrow,
            )
        )
        outs = [
            move.start(r.d_a_down, r.adapter_down_grad),
            move.start(r.d_a_up, r.adapter_up_grad),
        ]
        normalize_back_all(r.total, r.mid_v, r.mid_inverse, r.low)
        outs.append(move.start(r.low, r.summed_grad))
        context_back(r.d_context_v, r.out_weight, r.low)
        outs.append(move.start(r.d_context_v, r.d_context))
        for copy in outs + crossing:
            copy.wait()

    return run_kernel(
        body,
        "encoder_feed_back",
        near=dict(mid_inverse=forward.mid_inverse, memory_inverse=forward.memory_inverse),
        far=dict(
            out=dec.out.reshape(group, -1, width), target_grad=dec.target_grad.reshape(group, -1, width),
            memory_pairs_grad=dec.memory_pairs_grad, memory=forward.memory, mid=forward.mid,
            slopes=forward.slopes, narrow=forward.narrow, cross_kv=w.cross_kv,
            enc_out=w.enc_out, enc_up=w.enc_up, enc_down=w.enc_down,
            enc_adapter_down=w.enc_adapter_down, enc_adapter_up=w.enc_adapter_up,
        ),
        near_outs={},
        far_outs=dict(
            summed_grad=((tokens, width), LOW), d_context=((width, tokens), LOW),
            adapter_down_grad=((width, narrow), LOW), adapter_up_grad=((narrow, width), LOW),
            out_all=((group, dec.out.shape[0] // group, width), LOW),
            target_grad_all=((group, dec.out.shape[0] // group, width), LOW),
        ),
        scratch=dict(
            d_pairs=((2 * width, tokens), LOW), pair_weight=((width, 2 * width), LOW),
            memory_v=((tokens, width), LOW), mid_v=((tokens, width), LOW),
            slopes_v=((blocks, tokens, INNER), LOW), narrow_v=((tokens, narrow), LOW),
            out_weight=((width, width), LOW), a_down=((width, narrow), LOW),
            a_up=((narrow, width), LOW), up=((width, inner), LOW), down=((inner, width), LOW),
            low=((tokens, width), LOW), side=((tokens, width), LOW), d_narrow=((tokens, narrow), LOW),
            d_a_down=((width, narrow), LOW), d_a_up=((narrow, width), LOW),
            total=((tokens, width), WIDE), d_context_v=((width, tokens), LOW),
        ),
        flops=2 * tokens * width * 9728,
        links=2 * (group - 1),
        collective=1,
    )


def encoder_attend_back(feed, forward, w, group, copies):
    tokens, width = feed.summed_grad.shape
    share = tokens // group
    count = w.enc_prefix.shape[0]
    heads = width // HEAD

    def body(r):
        move = Mover(r.semaphores)
        firsts = [
            move.start(r.qkv, r.qkv_v),
            move.start(r.d_context, r.d_context_v),
            move.start(r.context, r.context_v),
        ]
        lasts = [move.start(r.enc_qkv, r.qkv_weight), move.start(r.summed_grad, r.summed_v)]
        links = Links(r.sent, r.arrived, {"seq": group})
        me = links.place["seq"]
        marks = r.marks[pl.ds(me // copies, 1), :]
        for copy in firsts:
            copy.wait()
        attend_back(
            SimpleNamespace(
                q=r.qkv_v, k=r.qkv_v, v=r.qkv_v, q0=0, k0=width, v0=2 * width,
                q_marks=marks, k_marks=marks, pairs=r.pairs, context=r.context_v, lse=r.lse,
                d_context=r.d_context_v, dq=r.d_qkv, dk=r.d_qkv, dv=r.d_qkv, dq0=0, dk0=width,
                dv0=2 * width, d_pairs=r.d_pairs, qx=r.qx, kx=r.kx, dx=r.dx, vx=r.vx,
                delta=r.delta, dq_sum=r.dq_sum, chances=r.chances, changes=r.changes,
            ),
            False,
            count,
        )
        for copy in lasts:
            copy.wait()
        for cut in chunks(tokens, CHUNK):
            r.summed_v[cut, :] = (
                r.summed_v[cut, :].astype(WIDE)
                + contract(r.d_qkv[:, cut], r.qkv_weight[...], 0, 1)
            ).astype(LOW)

        def tokens_of(place):
            return r.summed_v.at[pl.ds(pl.multiple_of(place * share, share), share), :]

        crossing = links.scatter("seq", tokens_of, r.source_grad.at[me])
        crossing.append(move.start(tokens_of(me), r.source_grad.at[me]))
        for copy in crossing:
            copy.wait()

    return run_kernel(
        body,
        "encoder_attend_back",
        near=dict(marks=w.source_segments, pairs=forward.enc_pairs, lse=forward.lse),
        far=dict(
            qkv=forward.qkv, d_context=feed.d_context, context=forward.context,
            enc_qkv=w.enc_qkv, summed_grad=feed.summed_grad,
        ),
        near_outs=dict(d_pairs=((PAD, 2 * width), WIDE)),
        far_outs=dict(source_grad=((group, share, width), LOW)),
        scratch=dict(
            qkv_v=((3 * width, tokens), LOW), d_context_v=((width, tokens), LOW),
            context_v=((width, tokens), LOW), qkv_weight=((width, 3 * width), LOW),
            summed_v=((tokens, width), LOW), d_qkv=((3 * width, tokens), LOW),
            qx=((heads * 16, tokens), LOW), kx=((16, tokens), LOW),
            dx=((heads * 16, tokens), LOW), vx=((16, tokens), LOW), delta=((16, tokens), WIDE),
            dq_sum=((width, tokens), WIDE), chances=((2, tokens, 256), LOW),
            changes=((2, tokens, 256), LOW),
        ),
        flops=2 * tokens * width * 2304 + 20 * tokens * tokens * width,
        links=group - 1,
        collective=2,
    )


def prefix_backward(prefix, prefix_in, prefix_out, hidden, pair_grad, place, count):
    def share(value, axis):
        size = value.shape[axis] // count
        return lax.dynamic_slice_in_dim(value, place * size, size, axis).astype(WIDE)

    exact = functools.partial(jnp.matmul, precision=lax.Precision.HIGHEST)
    out_grad = exact(share(hidden, 1).T, pair_grad)
    hidden_grad = exact(pair_grad, prefix_out.astype(WIDE).T) * (1.0 - hidden * hidden)
    in_grad = exact(share(prefix, 1).T, hidden_grad)
    embed_grad = exact(hidden_grad, share(prefix_in, 0).T)
    return (embed_grad, in_grad, out_grad)


def total_of(values):
    return functools.reduce(lambda left, right: left + right, values)


NAMES = (
    "source",
    "target",
    "source_segments",
    "target_segments",
    "cotangent",
    "enc_qkv",
    "enc_out",
    "enc_up",
    "enc_down",
    "dec_qkv",
    "dec_out",
    "cross_q",
    "cross_kv",
    "cross_out",
    "dec_up",
    "dec_down",
    "enc_prefix",
    "enc_prefix_in",
    "enc_prefix_out",
    "enc_adapter_down",
    "enc_adapter_up",
    "dec_prefix",
    "dec_prefix_in",
    "dec_prefix_out",
    "dec_adapter_down",
    "dec_adapter_up",
)


def shards(*operands, count):
    w = SimpleNamespace(**dict(zip(NAMES, operands)))
    place = lax.axis_index("seq")
    copies = count // w.source.shape[0]
    forward = encoder_forward(w, count, copies)
    dec = decoder(forward, w, copies)
    feed = encoder_feed_back(dec, forward, w, count)
    attended = encoder_attend_back(feed, forward, w, count, copies)
    share = 1.0 / copies

    def gathered(grad):
        grad = (grad.astype(WIDE) * share).astype(LOW)
        return lax.psum(lax.psum_scatter(grad, "seq", scatter_dimension=0, tiled=True), "dp").astype(WIDE)

    adapters = [
        gathered(grad)
        for grad in (
            feed.adapter_down_grad, feed.adapter_up_grad, dec.adapter_down_grad, dec.adapter_up_grad
        )
    ]
    used = w.enc_prefix.shape[0]
    enc_pair_grad, dec_pair_grad = lax.psum(
        (attended.d_pairs[:used] * share, dec.d_pairs[:used] * share), ("dp", "seq")
    )
    enc_prefix_grads = prefix_backward(
        w.enc_prefix, w.enc_prefix_in, w.enc_prefix_out, forward.enc_hidden[:used], enc_pair_grad, place, count
    )
    dec_prefix_grads = prefix_backward(
        w.dec_prefix, w.dec_prefix_in, w.dec_prefix_out, forward.dec_hidden[:used], dec_pair_grad, place, count
    )
    return (
        feed.out_all[::copies],
        attended.source_grad[::copies].astype(WIDE),
        feed.target_grad_all[::copies].astype(WIDE),
        *enc_prefix_grads,
        adapters[0],
        adapters[1],
        *dec_prefix_grads,
        adapters[2],
        adapters[3],
    )


def solution(mesh):
    rows = P("dp", "seq", None)
    marks = P("dp", None)
    in_specs = (rows, rows, marks, marks, rows) + (P(),) * 21
    across, down = P(None, "seq"), P("seq", None)
    layer = (across, down, down, down, down)
    return jax.shard_map(
        functools.partial(shards, count=mesh.shape["seq"]),
        mesh=mesh,
        in_specs=in_specs,
        out_specs=(rows, rows, rows) + layer + layer,
        check_vma=False,
    )
```

```python
import functools
import math
from types import SimpleNamespace

import jax
import jax.numpy as jnp
from jax import lax
from jax.experimental import pallas as pl
from jax.experimental.pallas import tpu as pltpu
from jax.sharding import PartitionSpec as P

HEAD = 64
GROUP = 4
PAD = 32
BIG = 2.0**100
LOG2E = math.log2(math.e)
SCALE = 1.0 / math.sqrt(HEAD)
VMEM_BYTES = 60 * 2**20
CHUNK = 256
INNER = 512
LOW = jnp.bfloat16
WIDE = jnp.float32


def contract(left, right, left_dim, right_dim):
    return lax.dot_general(
        left, right, (((left_dim,), (right_dim,)), ((), ())), preferred_element_type=WIDE
    )


def rows_at(index, size, base=0):
    return pl.ds(pl.multiple_of(base + index * size, size), size)


def chunks(size, step):
    step = min(step, size)
    return [slice(start, start + step) for start in range(0, size, step)]


def total_of(values):
    return functools.reduce(lambda left, right: left + right, values)


def normalize(value):
    centered = value - jnp.mean(value, axis=-1, keepdims=True)
    inverse = lax.rsqrt(jnp.mean(centered * centered, axis=-1, keepdims=True) + 1e-05)
    return (centered * inverse, inverse)


def normalize_back(gradient, normed, inverse):
    return (
        gradient
        - jnp.mean(gradient, axis=-1, keepdims=True)
        - normed * jnp.mean(gradient * normed, axis=-1, keepdims=True)
    ) * inverse


def gelu_both(value):
    scale = math.sqrt(2.0 / math.pi)
    square = value * value
    half = 0.5 + 0.5 * jnp.tanh(value * (scale + (scale * 0.044715) * square))
    active = value * half
    slope = half + active * (1.0 - half) * (2.0 * scale + (6.0 * scale * 0.044715) * square)
    return (active, slope)


class Mover:
    def __init__(self, semaphores):
        self.semaphores = semaphores
        self.used = 0

    def start(self, origin, goal):
        copy = pltpu.make_async_copy(origin, goal, self.semaphores.at[self.used])
        self.used += 1
        copy.start()
        return copy


def run_kernel(body, name, near, far, near_outs, far_outs, scratch, flops, links=0, collective=None):
    in_names = list(near) + list(far)
    out_names = list(near_outs) + list(far_outs)
    names = in_names + out_names + list(scratch) + ["semaphores"]
    link_scratch = []
    remote = {}
    if collective is not None:
        names += ["sent", "arrived"]
        link_scratch = [pltpu.SemaphoreType.DMA((links,)), pltpu.SemaphoreType.DMA((links,))]
        remote = dict(collective_id=collective, has_side_effects=True)

    def kernel(*refs):
        body(SimpleNamespace(**dict(zip(names, refs))))

    near_spec = pl.BlockSpec(memory_space=pltpu.VMEM)
    far_spec = pl.BlockSpec(memory_space=pl.ANY)
    results = pl.pallas_call(
        kernel,
        out_shape=tuple(
            jax.ShapeDtypeStruct(*out) for out in (*near_outs.values(), *far_outs.values())
        ),
        in_specs=[near_spec] * len(near) + [far_spec] * len(far),
        out_specs=tuple([near_spec] * len(near_outs) + [far_spec] * len(far_outs)),
        scratch_shapes=[pltpu.VMEM(*shape) for shape in scratch.values()]
        + [pltpu.SemaphoreType.DMA((64,))]
        + link_scratch,
        compiler_params=pltpu.CompilerParams(vmem_limit_bytes=VMEM_BYTES, **remote),
        cost_estimate=pl.CostEstimate(flops=flops, bytes_accessed=2**24, transcendentals=0),
        name=name,
    )(*near.values(), *far.values())
    return SimpleNamespace(**dict(zip(out_names, results)))


class Links:
    def __init__(self, sent, arrived, groups):
        self.sent, self.arrived = sent, arrived
        self.used = 0
        self.place = {axis: lax.axis_index(axis) for axis in ("dp", "seq")}
        self.sizes = groups
        barrier = pltpu.get_barrier_semaphore()
        peers = 0
        for axis, size in groups.items():
            for shift in range(1, size):
                pl.semaphore_signal(
                    barrier, inc=1, device_id=self.device(axis, shift), device_id_type=pl.DeviceIdType.MESH
                )
                peers += 1
        pl.semaphore_wait(barrier, peers)

    def peer(self, axis, shift):
        return lax.rem(self.place[axis] + shift, self.sizes[axis])

    def device(self, axis, shift):
        index = self.peer(axis, shift)
        return (index, self.place["seq"]) if axis == "dp" else (self.place["dp"], index)

    def start(self, axis, shift, origin, goal):
        copy = pltpu.make_async_remote_copy(
            src_ref=origin,
            dst_ref=goal,
            send_sem=self.sent.at[self.used],
            recv_sem=self.arrived.at[self.used],
            device_id=self.device(axis, shift),
            device_id_type=pl.DeviceIdType.MESH,
        )
        self.used += 1
        copy.start()
        return copy

    def scatter(self, axis, pick, goal):
        return [
            self.start(axis, shift, pick(self.peer(axis, shift)), goal)
            for shift in range(1, self.sizes[axis])
        ]


def split_three(value):
    high = value.astype(LOW).astype(WIDE)
    rest = value - high
    middle = rest.astype(LOW).astype(WIDE)
    return (high, middle, rest - middle)


def place_rows(parts, first, shape):
    row = lax.broadcasted_iota(jnp.int32, shape, 0)
    out = jnp.zeros(shape, WIDE)
    for offset, part in enumerate(parts):
        out = jnp.where(row == first + offset, part, out)
    return out


def document_rows(segments, tokens, is_key):
    row = lax.broadcasted_iota(jnp.int32, (16, tokens), 0)
    same = row == segments
    if is_key:
        return jnp.where(row < 4, jnp.where(same, 0.0, -BIG), 0.0)
    return jnp.where(same & (row < 4), 1.0, 0.0)


def column_peak(scores, peak):
    for start in range(0, scores.shape[0], 8):
        peak = jnp.maximum(peak, scores[start : start + 8])
    return peak


def from_column(value, low):
    if low == 0:
        return value
    return jnp.concatenate([jnp.zeros((value.shape[0], low), value.dtype), value], 1)


def attend(a, causal, prefix):
    queries, keys = a.q.shape[1], a.k.shape[1]
    width = a.context.shape[0]
    heads = width // HEAD
    tile = min(256, keys)
    tiles = keys // tile
    a.qx[:16, :queries] = document_rows(a.q_marks, queries, False).astype(LOW)
    a.kx[:, :keys] = document_rows(a.k_marks, keys, True).astype(LOW)
    start_peak = jnp.full((8, queries), -4.0 * BIG, WIDE)

    def query_of(head):
        return jnp.concatenate([a.q[rows_at(head, HEAD, a.q0), :], a.qx[:16, :queries]], 0)

    def prefix_scores(head, slot):
        if not prefix:
            return start_peak
        scores = contract(a.pair_keys[rows_at(head, HEAD), :], a.q[rows_at(head, HEAD, a.q0), :], 0, 0)
        row = lax.broadcasted_iota(jnp.int32, scores.shape, 0)
        scores = jnp.where(row < prefix, scores, -BIG)
        a.pair_scores[slot, :, :queries] = scores
        return column_peak(scores, start_peak)

    def score_tile(head, part, query, slot, peak):
        cut = slice(part * tile, (part + 1) * tile)
        low = part * tile if causal else 0
        key = jnp.concatenate([a.k[rows_at(head, HEAD, a.k0), cut], a.kx[:, cut]], 0)
        scores = contract(key, query[:, low:], 0, 0)
        if causal:
            place = lax.broadcasted_iota(jnp.int32, scores.shape, 0)
            scores = jnp.where(place <= lax.broadcasted_iota(jnp.int32, scores.shape, 1), scores, -BIG)
        a.scores[slot, cut, low:queries] = scores
        new = column_peak(scores, peak[:, low:])
        return new if low == 0 else jnp.concatenate([peak[:, :low], new], 1)

    def step(head, following, slot):
        other = 1 - slot
        query = query_of(following)
        peak = jnp.max(a.peak[slot, :, :queries], 0, keepdims=True)
        next_peak = prefix_scores(following, other)
        context = jnp.zeros((HEAD + 16, queries), WIDE)
        if prefix:
            weights = jnp.exp2(a.pair_scores[slot, :, :queries] - peak).astype(LOW)
            value = jnp.concatenate(
                [a.pair_values[rows_at(head, HEAD), :], jnp.ones((16, PAD), LOW)], 0
            )
            context = contract(value, weights, 1, 0)
        for part in range(tiles):
            next_peak = score_tile(following, part, query, other, next_peak)
            cut = slice(part * tile, (part + 1) * tile)
            low = part * tile if causal else 0
            weights = jnp.exp2(a.scores[slot, cut, low:queries] - peak[:, low:]).astype(LOW)
            value = jnp.concatenate(
                [a.v[rows_at(head, HEAD, a.v0), cut], jnp.ones((16, tile), LOW)], 0
            )
            context = context + from_column(contract(value, weights, 1, 0), low)
        a.peak[other, :, :queries] = next_peak
        total = context[HEAD : HEAD + 1]
        a.context[rows_at(head, HEAD), :] = (context[:HEAD] * (1.0 / total)).astype(LOW)
        a.lse[pl.ds(head, 1), :] = peak + jnp.log2(total)

    first = query_of(0)
    peak = prefix_scores(0, 0)
    for part in range(tiles):
        peak = score_tile(0, part, first, 0, peak)
    a.peak[0, :, :queries] = peak

    def pair(index, carry):
        step(2 * index, 2 * index + 1, 0)
        step(2 * index + 1, jnp.minimum(2 * index + 2, heads - 1), 1)
        return carry

    lax.fori_loop(0, heads // 2, pair, 0)


def block_diagonal(pairs, group, first):
    wide = GROUP * HEAD
    rows = pairs[:, first + group * wide : first + (group + 1) * wide]
    column = lax.broadcasted_iota(jnp.int32, rows.shape, 1)
    parts = [
        jnp.where((column >= member * HEAD) & (column < (member + 1) * HEAD), rows.astype(WIDE), 0.0)
        for member in range(GROUP)
    ]
    return jnp.concatenate(parts, 0).astype(LOW)


def own_columns(grads):
    column = lax.broadcasted_iota(jnp.int32, (PAD, GROUP * HEAD), 1)
    out = jnp.zeros((PAD, GROUP * HEAD), WIDE)
    for member in range(GROUP):
        own = (column >= member * HEAD) & (column < (member + 1) * HEAD)
        out = jnp.where(own, grads[member * PAD : (member + 1) * PAD], out)
    return out


def attend_back(a, causal, prefix, pauses=()):
    queries, keys = a.q.shape[1], a.k.shape[1]
    width = a.context.shape[0]
    heads = width // HEAD
    tile = min(256, keys // 2)
    tiles = keys // tile
    row = lax.broadcasted_iota(jnp.int32, (16, keys), 0)
    a.kx[:, :keys] = jnp.where(
        (row >= 4) & (row < 7), 1.0, document_rows(a.k_marks, keys, True)
    ).astype(LOW)
    a.vx[:, :keys] = jnp.where(row < 3, 1.0, 0.0).astype(LOW)
    documents = document_rows(a.q_marks, queries, False)

    def prepare(head, carry):
        rows = rows_at(head, HEAD)
        delta = jnp.sum(
            a.d_context[rows, :].astype(WIDE) * a.context[rows, :].astype(WIDE),
            axis=0,
            keepdims=True,
        )
        a.delta[pl.ds(head, 1), :queries] = delta
        a.dx[rows_at(head, 16), :queries] = place_rows(
            split_three(-delta), 0, (16, queries)
        ).astype(LOW)
        minus = split_three(-a.lse[pl.ds(head, 1), :])
        a.qx[rows_at(head, 16), :queries] = (
            documents + place_rows(minus, 4, (16, queries))
        ).astype(LOW)
        return carry

    lax.fori_loop(0, heads, prepare, 0)

    if prefix:
        for group in range(heads // GROUP):
            start = group * GROUP * HEAD
            own = slice(start, start + GROUP * HEAD)
            query = a.q[a.q0 + start : a.q0 + start + GROUP * HEAD, :]
            grad = a.d_context[own, :]
            pair_keys = block_diagonal(a.pairs[...], group, 0)
            pair_values = block_diagonal(a.pairs[...], group, width)
            scores = contract(pair_keys, query, 1, 0)
            gains = contract(pair_values, grad, 1, 0)
            chances, changes = [], []
            for member in range(GROUP):
                head = group * GROUP + member
                part = slice(member * PAD, (member + 1) * PAD)
                chance = jnp.exp2(scores[part] - a.lse[head : head + 1, :])
                place = lax.broadcasted_iota(jnp.int32, chance.shape, 0)
                chance = jnp.where(place < prefix, chance, 0.0)
                chances.append(chance)
                changes.append(chance * (gains[part] - a.delta[head : head + 1, :queries]))
            chances = jnp.concatenate(chances, 0).astype(LOW)
            changes = jnp.concatenate(changes, 0).astype(LOW)
            a.dq_sum[own, :queries] = contract(pair_keys, changes, 0, 0)
            a.d_pairs[:, own] = own_columns(contract(changes, query, 1, 1)) * (a.factor / LOG2E)
            a.d_pairs[:, width + start : width + start + GROUP * HEAD] = (
                own_columns(contract(chances, grad, 1, 1)) * a.factor
            )
    else:
        a.dq_sum[:, :queries] = jnp.zeros((width, queries), WIDE)
    if pauses:
        pauses[0]()

    def front(head, part, slot):
        cut = slice(part * tile, (part + 1) * tile)
        low = part * tile if causal else 0
        query = jnp.concatenate(
            [a.q[rows_at(head, HEAD, a.q0), low:], a.qx[rows_at(head, 16), low:queries]], 0
        )
        key = jnp.concatenate([a.k[rows_at(head, HEAD, a.k0), cut], a.kx[:, cut]], 0)
        scores = contract(query, key, 0, 0)
        if causal:
            place = lax.broadcasted_iota(jnp.int32, scores.shape, 1)
            scores = jnp.where(place <= lax.broadcasted_iota(jnp.int32, scores.shape, 0), scores, -BIG)
        grad = jnp.concatenate(
            [a.d_context[rows_at(head, HEAD), low:], a.dx[rows_at(head, 16), low:queries]], 0
        )
        value = jnp.concatenate([a.v[rows_at(head, HEAD, a.v0), cut], a.vx[:, cut]], 0)
        gains = contract(grad, value, 0, 0)
        chance = jnp.exp2(scores)
        a.chances[slot, low:queries, :tile] = chance.astype(LOW)
        a.changes[slot, low:queries, :tile] = (chance * gains).astype(LOW)

    def back(head, part, slot):
        cut = slice(part * tile, (part + 1) * tile)
        low = part * tile if causal else 0
        chances = a.chances[slot, low:queries, :tile]
        changes = a.changes[slot, low:queries, :tile]
        a.dv[rows_at(head, HEAD, a.dv0), cut] = contract(
            a.d_context[rows_at(head, HEAD), low:], chances, 1, 0
        ).astype(LOW)
        a.dk[rows_at(head, HEAD, a.dk0), cut] = (
            contract(a.q[rows_at(head, HEAD, a.q0), low:], changes, 1, 0) * (1.0 / LOG2E)
        ).astype(LOW)
        a.dq_sum[rows_at(head, HEAD), low:queries] += contract(
            a.k[rows_at(head, HEAD, a.k0), cut], changes, 1, 1
        )

    def one_head(head, carry):
        for part in range(tiles):
            last = part == tiles - 1
            front(
                jnp.minimum(head + 1, heads - 1) if last else head,
                0 if last else part + 1,
                (part + 1) % 2,
            )
            back(head, part, part % 2)
        a.dq[rows_at(head, HEAD, a.dq0), :] = (
            a.dq_sum[rows_at(head, HEAD), :queries] * SCALE
        ).astype(LOW)
        return carry

    front(0, 0, 0)
    steps = max(len(pauses), 1)
    for number in range(steps):
        lax.fori_loop(heads * number // steps, heads * (number + 1) // steps, one_head, 0)
        if number + 1 < steps:
            pauses[number + 1]()


def project_wide(out, weight, rows, scaled, place=slice(None)):
    for cut in chunks(weight.shape[1], 256):
        result = contract(weight[:, cut], rows, 0, 1)
        if cut.start < scaled:
            result = result * (SCALE * LOG2E)
        out[cut, place] = result.astype(LOW)


def add_and_normalize(hidden, context, weight, normed, inverse):
    for cut in chunks(hidden.shape[0], CHUNK):
        summed = hidden[cut, :].astype(WIDE) + contract(context[:, cut], weight[...], 0, 0)
        result, scale = normalize(summed)
        normed[cut, :] = result.astype(LOW)
        inverse[cut, :] = scale


def feed_forward(hidden, up, down, adapter_down, adapter_up, total, slopes_of, store, narrow):
    cuts = chunks(hidden.shape[0], CHUNK)

    def block(index, first, second, factor, is_first):
        place = slopes_of(index)
        value = contract(hidden[cuts[0], :], first(), 1, 0)
        for number, cut in enumerate(cuts):
            following = None
            if number + 1 < len(cuts):
                following = contract(hidden[cuts[number + 1], :], first(), 1, 0)
            active, slope = gelu_both(value)
            place[cut, :] = slope.astype(LOW)
            if factor != 1.0:
                narrow[cut, :] = active.astype(LOW)
                active = active * factor
            product = contract(active.astype(LOW), second(), 1, 0)
            if is_first:
                total[cut, :] = hidden[cut, :].astype(WIDE) + product
            else:
                total[cut, :] += product
            value = following
        store(index)

    count = up.shape[1] // INNER
    block(0, lambda: adapter_down[...], lambda: adapter_up[...], 4.0, True)

    def main(index, carry):
        columns = rows_at(index, INNER)
        block(index + 1, lambda: up[:, columns], lambda: down[columns, :], 1.0, False)
        return carry

    lax.fori_loop(0, count, main, 0)


def finish_forward(total, normed, inverse):
    for cut in chunks(total.shape[0], CHUNK):
        result, scale = normalize(total[cut, :])
        normed[cut, :] = result.astype(LOW)
        inverse[cut, :] = scale


def spread(parts, value):
    size = parts.shape[2]
    for part in range(parts.shape[0]):
        parts[part] = value[:, part * size : (part + 1) * size].astype(parts.dtype)


def feed_back(f):
    tokens = f.hidden.shape[0]
    cuts = chunks(tokens, CHUNK)
    for cut in cuts:
        value = f.grad[cut, :]
        f.low[cut, :] = value.astype(LOW)
        f.side[cut, :] = (4.0 * value).astype(LOW)

    def block(index, origin, first, second, keep):
        place = f.slopes(index)
        value = contract(origin[cuts[0], :], first(), 1, 1)
        for number, cut in enumerate(cuts):
            following = None
            if number + 1 < len(cuts):
                following = contract(origin[cuts[number + 1], :], first(), 1, 1)
            change = (value * place[cut, :].astype(WIDE)).astype(LOW)
            if keep is not None:
                keep[cut, :] = change
            f.grad[cut, :] += contract(change, second(), 1, 1)
            value = following

    block(0, f.side, lambda: f.adapter_up[...], lambda: f.adapter_down[...], f.d_narrow)
    spread(f.d_adapter_up, contract(f.narrow[...], f.side[...], 0, 0) * f.factor)
    spread(f.d_adapter_down, contract(f.hidden[...], f.d_narrow[...], 0, 0) * f.factor)

    def main(index, carry):
        columns = rows_at(index, INNER)
        block(index + 1, f.low, lambda: f.down[columns, :], lambda: f.up[:, columns], None)
        return carry

    lax.fori_loop(0, f.up.shape[1] // INNER, main, 0)


def normalize_back_all(grad, normed, inverse, out):
    for cut in chunks(grad.shape[0], CHUNK):
        out[cut, :] = normalize_back(
            grad[cut, :].astype(WIDE), normed[cut, :].astype(WIDE), inverse[cut, :]
        ).astype(out.dtype)


def context_back(out, weight, grad):
    value = grad[...].astype(LOW)
    for cut in chunks(weight.shape[0], 256):
        out[cut, :] = contract(weight[cut, :], value, 1, 1).astype(LOW)


def prefix_pairs(prefix, first, second, hidden, pairs, pairs_wide):
    count = prefix.shape[0]
    hidden[...] = jnp.zeros(hidden.shape, WIDE)
    hidden[:count, :] = jnp.tanh(contract(prefix[...], first[...], 1, 0))
    parts = [part.astype(LOW) for part in split_three(hidden[...])]
    pairs[...] = total_of([contract(part, second[...], 1, 0) for part in parts]).astype(LOW)
    pairs_wide[...] = total_of([contract(second[...], part, 0, 1) for part in parts]).astype(LOW)


def encoder_forward(w, group, copies):
    width = w.source.shape[2]
    share, later_share = w.source.shape[1], w.target.shape[1]
    tokens, later_tokens = share * group, later_share * group
    inner = w.enc_up.shape[1]
    narrow = w.enc_adapter_down.shape[1]
    units = w.enc_prefix_in.shape[1]
    count = w.enc_prefix.shape[0]
    blocks = 1 + inner // INNER

    def body(r):
        move = Mover(r.semaphores)
        weights = [move.start(r.enc_qkv, r.qkv_weight)]
        enc_first, dec_first = r.mid_v.at[:width, :units], r.memory_v.at[:width, :units]
        enc_second, dec_second = r.up.at[:units, : 2 * width], r.up.at[:units, 2 * width : 4 * width]
        weights.append(move.start(r.enc_prefix_in, enc_first))
        weights.append(move.start(r.enc_prefix_out, enc_second))
        weights.append(move.start(r.dec_prefix_in, dec_first))
        weights.append(move.start(r.dec_prefix_out, dec_second))
        links = Links(r.sent, r.arrived, {"seq": group})
        me = links.place["seq"]
        row = me // copies

        def tokens_of(place, size):
            return pl.ds(pl.multiple_of(place * size, size), size)

        def bring(origin, goal, size, via=None):
            own = tokens_of(me, size)
            copies_out = links.scatter("seq", lambda peer: origin.at[peer // copies], goal.at[own, :])
            if via is None:
                return (move.start(origin.at[row], goal.at[own, :]), copies_out)
            move.start(origin.at[row], via).wait()
            return (move.start(via, goal.at[own, :]), copies_out)

        here, sources = bring(r.source, r.x, share)
        out_weight = move.start(r.enc_out, r.out_weight)
        adapters = [
            move.start(r.enc_adapter_down, r.a_down),
            move.start(r.enc_adapter_up, r.a_up),
        ]
        pair_weight = move.start(r.cross_kv, r.pair_weight)
        for copy in weights:
            copy.wait()
        prefix_pairs(r.enc_prefix, enc_first, enc_second, r.enc_hidden, r.enc_pairs, r.enc_pairs_wide)
        prefix_pairs(r.dec_prefix, dec_first, dec_second, r.dec_hidden, r.dec_pairs, r.dec_pairs_wide)
        ups = [move.start(r.enc_up, r.up), move.start(r.enc_down, r.down)]
        here.wait()
        if share % 128 == 0:
            place = tokens_of(me, share)
            project_wide(r.qkv_v, r.qkv_weight, r.x[place, :], width, place)
            for shift, copy in enumerate(sources, 1):
                copy.wait()
                place = tokens_of(lax.rem(me + group - shift, group), share)
                project_wide(r.qkv_v, r.qkv_weight, r.x[place, :], width, place)
        else:
            for copy in sources:
                copy.wait()
            project_wide(r.qkv_v, r.qkv_weight, r.x[...], width)
        later = [
            bring(r.target, r.target_rows, later_share, r.own_target),
            bring(r.cotangent, r.cotangent_rows, later_share, r.own_cotangent),
        ]
        outs = [move.start(r.qkv_v, r.qkv)]
        marks = r.marks[pl.ds(row, 1), :]
        attend(
            SimpleNamespace(
                q=r.qkv_v, k=r.qkv_v, v=r.qkv_v, q0=0, k0=width, v0=2 * width,
                q_marks=marks, k_marks=marks, pair_keys=r.enc_pairs_wide.at[:width],
                pair_values=r.enc_pairs_wide.at[width:],
                context=r.context_v, lse=r.lse, qx=r.qx, kx=r.kx, scores=r.scores,
                pair_scores=r.pair_scores, peak=r.peak,
            ),
            False,
            count,
        )
        outs.append(move.start(r.context_v, r.context))
        out_weight.wait()
        add_and_normalize(r.x, r.context_v, r.out_weight, r.mid_v, r.mid_inverse)
        outs.append(move.start(r.mid_v, r.mid))
        for copy in adapters + ups:
            copy.wait()
        feed_forward(
            r.mid_v, r.up, r.down, r.a_down, r.a_up, r.total,
            lambda index: r.slopes_v.at[index], lambda index: None, r.narrow_v,
        )
        outs.append(move.start(r.slopes_v, r.slopes))
        outs.append(move.start(r.narrow_v, r.narrow))
        finish_forward(r.total, r.memory_v, r.memory_inverse)
        outs.append(move.start(r.memory_v, r.memory))
        pair_weight.wait()
        project_wide(r.pairs_v, r.pair_weight, r.memory_v[...], 0)
        outs.append(move.start(r.pairs_v, r.memory_pairs))
        for own, remote in later:
            own.wait()
            for copy in remote:
                copy.wait()
        for copy in outs:
            copy.wait()

    return run_kernel(
        body,
        "encoder_forward",
        near=dict(marks=w.source_segments, enc_prefix=w.enc_prefix, dec_prefix=w.dec_prefix),
        far=dict(
            source=w.source, target=w.target, cotangent=w.cotangent, enc_qkv=w.enc_qkv,
            enc_out=w.enc_out, enc_up=w.enc_up, enc_down=w.enc_down,
            enc_adapter_down=w.enc_adapter_down, enc_adapter_up=w.enc_adapter_up,
            cross_kv=w.cross_kv, enc_prefix_in=w.enc_prefix_in, enc_prefix_out=w.enc_prefix_out,
            dec_prefix_in=w.dec_prefix_in, dec_prefix_out=w.dec_prefix_out,
        ),
        near_outs=dict(
            lse=((16, tokens), WIDE), mid_inverse=((tokens, 1), WIDE),
            memory_inverse=((tokens, 1), WIDE),
            enc_hidden=((PAD, units), WIDE), enc_pairs=((PAD, 2 * width), LOW),
            dec_hidden=((PAD, units), WIDE), dec_pairs=((PAD, 2 * width), LOW),
            dec_pairs_wide=((2 * width, PAD), LOW),
        ),
        far_outs=dict(
            qkv=((3 * width, tokens), LOW), context=((width, tokens), LOW), mid=((tokens, width), LOW),
            slopes=((blocks, tokens, INNER), LOW), narrow=((tokens, narrow), LOW),
            memory=((tokens, width), LOW), memory_pairs=((2 * width, tokens), LOW),
            target_rows=((later_tokens, width), LOW), cotangent_rows=((later_tokens, width), LOW),
        ),
        scratch=dict(
            x=((tokens, width), LOW), qkv_weight=((width, 3 * width), LOW),
            own_target=((later_share, width), LOW), own_cotangent=((later_share, width), LOW),
            enc_pairs_wide=((2 * width, PAD), LOW),
            out_weight=((width, width), LOW), a_down=((width, narrow), LOW),
            a_up=((narrow, width), LOW), up=((width, inner), LOW), down=((inner, width), LOW),
            pair_weight=((width, 2 * width), LOW), qkv_v=((3 * width, tokens), LOW),
            context_v=((width, tokens), LOW), mid_v=((tokens, width), LOW),
            slopes_v=((blocks, tokens, INNER), LOW), narrow_v=((tokens, narrow), LOW),
            memory_v=((tokens, width), LOW), pairs_v=((2 * width, tokens), LOW),
            total=((tokens, width), WIDE), qx=((16, tokens), LOW), kx=((16, tokens), LOW),
            scores=((2, tokens, tokens), WIDE), pair_scores=((2, PAD, tokens), WIDE),
            peak=((2, 8, tokens), WIDE),
        ),
        flops=2 * tokens * width * 11776 + 4 * tokens * tokens * width,
        links=3 * (group - 1),
        collective=0,
    )


def decoder(forward, w, copies, replicas):
    tokens, width = forward.target_rows.shape
    keys = forward.memory_pairs.shape[1]
    count = w.dec_prefix.shape[0]
    inner = w.dec_up.shape[1]
    narrow = w.dec_adapter_down.shape[1]
    blocks = 1 + inner // INNER
    heads = width // HEAD

    def body(r):
        move = Mover(r.semaphores)
        ins = [move.start(r.target, r.x), move.start(r.dec_qkv, r.qkv_weight)]
        for copy in ins:
            copy.wait()
        out_weight = move.start(r.dec_out, r.out_weight)
        crosses = [
            move.start(r.cross_q, r.query_weight),
            move.start(r.memory_pairs, r.pairs_v),
            move.start(r.cross_out, r.cross_out_weight),
        ]
        adapters = [
            move.start(r.dec_adapter_down, r.a_down),
            move.start(r.dec_adapter_up, r.a_up),
        ]
        ups = [move.start(r.dec_up, r.up), move.start(r.dec_down, r.down)]
        cotangents = move.start(r.cotangent, r.cotangent_v)
        project_wide(r.qkv, r.qkv_weight, r.x[...], width)
        row = pl.ds(lax.axis_index("seq") // copies, 1)
        marks, source_marks = r.marks[row, :], r.source_marks[row, :]
        shared = dict(
            qx=r.qx, kx=r.kx, scores=r.scores, pair_scores=r.pair_scores, peak=r.peak, dx=r.dx,
            vx=r.vx, delta=r.delta, dq_sum=r.dq_sum, chances=r.chances, changes=r.changes,
            d_context=r.d_context,
        )
        self_part = SimpleNamespace(
            q=r.qkv, k=r.qkv, v=r.qkv, q0=0, k0=width, v0=2 * width,
            q_marks=marks, k_marks=marks, pair_keys=r.pairs_wide.at[:width],
            pair_values=r.pairs_wide.at[width:], pairs=r.pairs, context=r.context, lse=r.lse,
            dq=r.d_qkv, dk=r.d_qkv, dv=r.d_qkv, dq0=0, dk0=width, dv0=2 * width,
            d_pairs=r.d_pairs, factor=1.0 / copies, **shared,
        )
        attend(self_part, True, count)
        out_weight.wait()
        add_and_normalize(r.x, r.context, r.out_weight, r.mid, r.mid_inverse)
        for copy in crosses:
            copy.wait()
        project_wide(r.query, r.query_weight, r.mid[...], width)
        cross_part = SimpleNamespace(
            q=r.query, k=r.pairs_v, v=r.pairs_v, q0=0, k0=0, v0=width,
            q_marks=marks, k_marks=source_marks, context=r.cross_context, lse=r.cross_lse,
            dq=r.d_query, dk=r.d_pairs_v, dv=r.d_pairs_v, dq0=0, dk0=0, dv0=width, **shared,
        )
        attend(cross_part, False, 0)
        add_and_normalize(r.mid, r.cross_context, r.cross_out_weight, r.crossed, r.crossed_inverse)
        for copy in adapters + ups + [cotangents]:
            copy.wait()
        feed_forward(
            r.crossed, r.up, r.down, r.a_down, r.a_up, r.total,
            lambda index: r.slopes.at[index], lambda index: None, r.narrow,
        )
        finish_forward(r.total, r.out_v, r.out_inverse)
        outs = [move.start(r.out_v, r.out)]
        normalize_back_all(r.cotangent_v, r.out_v, r.out_inverse, r.total)
        feed_back(
            SimpleNamespace(
                grad=r.total, low=r.low, side=r.side, hidden=r.crossed, narrow=r.narrow, up=r.up,
                down=r.down, adapter_down=r.a_down, adapter_up=r.a_up,
                slopes=lambda index: r.slopes.at[index], d_adapter_down=r.d_a_down,
                d_adapter_up=r.d_a_up, d_narrow=r.d_narrow, factor=1.0 / copies,
            )
        )
        outs.append(move.start(r.d_a_down, r.adapter_down_grad))
        outs.append(move.start(r.d_a_up, r.adapter_up_grad))
        normalize_back_all(r.total, r.crossed, r.crossed_inverse, r.total)
        context_back(r.d_context, r.cross_out_weight, r.total)
        attend_back(cross_part, False, 0)
        outs.append(move.start(r.d_pairs_v, r.memory_pairs_grad))
        for cut in chunks(tokens, CHUNK):
            r.total[cut, :] += contract(r.d_query[:, cut], r.query_weight[...], 0, 1)
        normalize_back_all(r.total, r.mid, r.mid_inverse, r.total)
        context_back(r.d_context, r.out_weight, r.total)
        attend_back(self_part, True, count)
        for cut in chunks(tokens, CHUNK):
            r.x[cut, :] = (
                r.total[cut, :] + contract(r.d_qkv[:, cut], r.qkv_weight[...], 0, 1)
            ).astype(LOW)
        outs.append(move.start(r.x, r.target_grad))
        for copy in outs:
            copy.wait()

    return run_kernel(
        body,
        "decoder",
        near=dict(
            marks=w.target_segments, source_marks=w.source_segments,
            pairs_wide=forward.dec_pairs_wide, pairs=forward.dec_pairs,
        ),
        far=dict(
            target=forward.target_rows, cotangent=forward.cotangent_rows,
            memory_pairs=forward.memory_pairs, dec_qkv=w.dec_qkv,
            dec_out=w.dec_out, cross_q=w.cross_q, cross_out=w.cross_out, dec_up=w.dec_up,
            dec_down=w.dec_down, dec_adapter_down=w.dec_adapter_down,
            dec_adapter_up=w.dec_adapter_up,
        ),
        near_outs=dict(d_pairs=((PAD, 2 * width), WIDE)),
        far_outs=dict(
            out=((tokens, width), LOW), target_grad=((tokens, width), LOW),
            memory_pairs_grad=((2 * width, keys), LOW),
            adapter_down_grad=((replicas, width, narrow // replicas), LOW),
            adapter_up_grad=((replicas, narrow, width // replicas), LOW),
        ),
        scratch=dict(
            x=((tokens, width), LOW), cotangent_v=((tokens, width), LOW),
            qkv_weight=((width, 3 * width), LOW), out_weight=((width, width), LOW),
            query_weight=((width, width), LOW), cross_out_weight=((width, width), LOW),
            pairs_v=((2 * width, keys), LOW), a_down=((width, narrow), LOW),
            a_up=((narrow, width), LOW), up=((width, inner), LOW), down=((inner, width), LOW),
            qkv=((3 * width, tokens), LOW), context=((width, tokens), LOW),
            mid=((tokens, width), LOW), mid_inverse=((tokens, 1), WIDE),
            query=((width, tokens), LOW), cross_context=((width, tokens), LOW),
            crossed=((tokens, width), LOW), crossed_inverse=((tokens, 1), WIDE),
            out_v=((tokens, width), LOW), out_inverse=((tokens, 1), WIDE),
            slopes=((blocks, tokens, INNER), LOW), narrow=((tokens, narrow), LOW),
            low=((tokens, width), LOW), side=((tokens, width), LOW), d_narrow=((tokens, narrow), LOW),
            d_a_down=((replicas, width, narrow // replicas), LOW),
            d_a_up=((replicas, narrow, width // replicas), LOW),
            total=((tokens, width), WIDE), lse=((16, tokens), WIDE), cross_lse=((16, tokens), WIDE),
            d_context=((width, tokens), LOW), d_query=((width, tokens), LOW),
            d_pairs_v=((2 * width, keys), LOW), d_qkv=((3 * width, tokens), LOW),
            qx=((heads * 16, tokens), LOW), kx=((16, keys), LOW),
            scores=((2, keys, tokens), WIDE), pair_scores=((2, PAD, tokens), WIDE),
            peak=((2, 8, tokens), WIDE), dx=((heads * 16, tokens), LOW), vx=((16, keys), LOW),
            delta=((16, tokens), WIDE), dq_sum=((width, tokens), WIDE),
            chances=((2, tokens, 256), LOW), changes=((2, tokens, 256), LOW),
        ),
        flops=4 * tokens * width * 11776 + 14 * tokens * (keys + tokens) * width,
    )


def encoder_feed_back(dec, forward, w, group, copies, replicas):
    tokens, width = forward.memory.shape
    inner = w.enc_up.shape[1]
    narrow = w.enc_adapter_down.shape[1]
    blocks = 1 + inner // INNER

    def body(r):
        move = Mover(r.semaphores)
        firsts = [
            move.start(r.memory_pairs_grad, r.d_pairs),
            move.start(r.cross_kv, r.pair_weight),
            move.start(r.memory, r.memory_v),
        ]
        adapters = [
            move.start(r.enc_adapter_down, r.a_down),
            move.start(r.enc_adapter_up, r.a_up),
            move.start(r.narrow, r.narrow_v),
            move.start(r.mid, r.mid_v),
        ]
        ups = [
            move.start(r.slopes, r.slopes_v),
            move.start(r.enc_down, r.down),
            move.start(r.enc_up, r.up),
            move.start(r.enc_out, r.out_weight),
        ]
        links = Links(r.sent, r.arrived, {"seq": group, "dp": replicas})
        me, replica = links.place["seq"], links.place["dp"]
        crossing, relays = [], []
        for origin, goal, via in (
            (r.dec_adapter_down_grad, r.dec_down_parts, r.own_down),
            (r.dec_adapter_up_grad, r.dec_up_parts, r.own_up),
        ):
            crossing += links.scatter("dp", lambda peer: origin.at[peer], goal.at[replica])
            relays.append((move.start(origin.at[replica], via), via, goal.at[replica]))
        for origin, goal, via in (
            (r.out, r.out_all, r.own_out), (r.target_grad, r.target_grad_all, r.own_target)
        ):
            crossing += links.scatter("seq", lambda peer: origin.at[peer], goal.at[me])
            relays.append((move.start(origin.at[me], via), via, goal.at[me]))
        for copy in firsts:
            copy.wait()
        for copy, via, goal in relays:
            copy.wait()
            crossing.append(move.start(via, goal))
        for cut in chunks(tokens, CHUNK):
            grad = contract(r.d_pairs[:, cut], r.pair_weight[...], 0, 1)
            r.total[cut, :] = normalize_back(
                grad, r.memory_v[cut, :].astype(WIDE), r.memory_inverse[cut, :]
            )
        for copy in adapters + ups:
            copy.wait()
        feed_back(
            SimpleNamespace(
                grad=r.total, low=r.low, side=r.side, hidden=r.mid_v, narrow=r.narrow_v, up=r.up,
                down=r.down, adapter_down=r.a_down, adapter_up=r.a_up,
                slopes=lambda index: r.slopes_v.at[index], d_adapter_down=r.d_a_down,
                d_adapter_up=r.d_a_up, d_narrow=r.d_narrow, factor=1.0 / copies,
            )
        )
        outs = [
            move.start(r.d_a_down, r.adapter_down_grad),
            move.start(r.d_a_up, r.adapter_up_grad),
        ]
        normalize_back_all(r.total, r.mid_v, r.mid_inverse, r.low)
        outs.append(move.start(r.low, r.summed_grad))
        context_back(r.d_context_v, r.out_weight, r.low)
        outs.append(move.start(r.d_context_v, r.d_context))
        for copy in outs + crossing:
            copy.wait()

    return run_kernel(
        body,
        "encoder_feed_back",
        near=dict(mid_inverse=forward.mid_inverse, memory_inverse=forward.memory_inverse),
        far=dict(
            out=dec.out.reshape(group, -1, width), target_grad=dec.target_grad.reshape(group, -1, width),
            dec_adapter_down_grad=dec.adapter_down_grad, dec_adapter_up_grad=dec.adapter_up_grad,
            memory_pairs_grad=dec.memory_pairs_grad, memory=forward.memory, mid=forward.mid,
            slopes=forward.slopes, narrow=forward.narrow, cross_kv=w.cross_kv,
            enc_out=w.enc_out, enc_up=w.enc_up, enc_down=w.enc_down,
            enc_adapter_down=w.enc_adapter_down, enc_adapter_up=w.enc_adapter_up,
        ),
        near_outs={},
        far_outs=dict(
            summed_grad=((tokens, width), LOW), d_context=((width, tokens), LOW),
            adapter_down_grad=((replicas, width, narrow // replicas), LOW),
            adapter_up_grad=((replicas, narrow, width // replicas), LOW),
            dec_down_parts=((replicas, width, narrow // replicas), LOW),
            dec_up_parts=((replicas, narrow, width // replicas), LOW),
            out_all=((group, dec.out.shape[0] // group, width), LOW),
            target_grad_all=((group, dec.out.shape[0] // group, width), LOW),
        ),
        scratch=dict(
            own_down=((width, narrow // replicas), LOW), own_up=((narrow, width // replicas), LOW),
            own_out=((dec.out.shape[0] // group, width), LOW),
            own_target=((dec.out.shape[0] // group, width), LOW),
            d_pairs=((2 * width, tokens), LOW), pair_weight=((width, 2 * width), LOW),
            memory_v=((tokens, width), LOW), mid_v=((tokens, width), LOW),
            slopes_v=((blocks, tokens, INNER), LOW), narrow_v=((tokens, narrow), LOW),
            out_weight=((width, width), LOW), a_down=((width, narrow), LOW),
            a_up=((narrow, width), LOW), up=((width, inner), LOW), down=((inner, width), LOW),
            low=((tokens, width), LOW), side=((tokens, width), LOW), d_narrow=((tokens, narrow), LOW),
            d_a_down=((replicas, width, narrow // replicas), LOW),
            d_a_up=((replicas, narrow, width // replicas), LOW),
            total=((tokens, width), WIDE), d_context_v=((width, tokens), LOW),
        ),
        flops=2 * tokens * width * 9728,
        links=2 * (group - 1) + 2 * (replicas - 1),
        collective=1,
    )


def split_product(left, right, left_dim, right_dim):
    return total_of(
        [contract(part.astype(LOW), right, left_dim, right_dim) for part in split_three(left)]
    )


def prefix_back(p):
    count, group = p.prefix.shape[0], p.group
    d_pairs, hidden = p.d_pairs, p.hidden[...]
    units, width = hidden.shape[1], p.prefix.shape[1]
    p.tall_hidden[...] = hidden.T
    share = units // group
    own = p.tall_hidden[pl.ds(pl.multiple_of(p.place * share, share), share), :]
    parts = split_three(d_pairs)
    p.out_grad[...] = total_of(
        [split_product(own, part.astype(LOW), 1, 0) for part in parts]
    )
    d_hidden = split_product(d_pairs, p.second[...], 1, 1) * (1.0 - hidden * hidden)
    p.wide_prefix[...] = jnp.zeros(p.wide_prefix.shape, WIDE)
    p.wide_prefix[:count, :] = p.prefix[...].astype(WIDE)
    p.tall_prefix[...] = p.wide_prefix[...].T
    share = width // group
    own = p.tall_prefix[pl.ds(pl.multiple_of(p.place * share, share), share), :].astype(LOW)
    p.in_grad[...] = total_of([contract(own, part.astype(LOW), 1, 0) for part in split_three(d_hidden)])
    p.embed_grad[...] = split_product(d_hidden, p.first_share[...], 1, 1)[:count]


def encoder_attend_back(feed, dec, forward, w, group, copies, replicas):
    tokens, width = feed.summed_grad.shape
    share = tokens // group
    count = w.enc_prefix.shape[0]
    narrow, units = w.enc_adapter_down.shape[1], w.enc_prefix_in.shape[1]
    down_part, up_part = (width, narrow // replicas), (narrow, width // replicas)
    down_piece, up_piece = (width // group, narrow // replicas), (narrow // group, width // replicas)
    heads = width // HEAD
    pair_rows = 2 * PAD // group
    layers = ("enc", "dec")

    def body(r):
        move = Mover(r.semaphores)
        firsts = [
            move.start(r.qkv, r.qkv_v),
            move.start(r.d_context, r.d_context_v),
            move.start(r.context, r.context_v),
        ]
        parts_in = [
            move.start(r.dec_down_parts, r.dec_downs), move.start(r.dec_up_parts, r.dec_ups)
        ]
        links = Links(r.sent, r.arrived, {"seq": group, "dp": replicas})
        me, replica = links.place["seq"], links.place["dp"]
        marks = r.marks[pl.ds(me // copies, 1), :]
        waits = {}

        def exchange(name, axis, pick, goal, own):
            copies_out = links.scatter(axis, pick, goal)
            copies_out.append(move.start(own, goal))
            waits[name] = copies_out

        def arrive(name):
            for copy in waits.pop(name):
                copy.wait()

        def sum_of(parts):
            return total_of([parts[part].astype(WIDE) for part in range(parts.shape[0])])

        def piece(ref):
            size = ref.shape[0] // group
            return lambda place: ref.at[pl.ds(pl.multiple_of(place * size, size), size), :]

        for name, origin, goal in (
            ("enc_down", r.enc_down_grad, r.enc_downs), ("enc_up", r.enc_up_grad, r.enc_ups)
        ):
            exchange(name, "dp", lambda peer: origin.at[peer], goal.at[replica], origin.at[replica])
        lasts = [
            move.start(r.enc_qkv, r.qkv_weight), move.start(r.summed_grad, r.summed_v),
            move.start(r.enc_prefix_out, r.enc_second), move.start(r.dec_prefix_out, r.dec_second),
        ]
        size = width // group
        first_rows = pl.ds(pl.multiple_of(me * size, size), size)
        lasts.append(move.start(r.enc_prefix_in.at[first_rows, :], r.enc_first))
        lasts.append(move.start(r.dec_prefix_in.at[first_rows, :], r.dec_first))

        def send_pieces(layer, kind):
            parts, summed = getattr(r, f"{layer}_{kind}s"), getattr(r, f"{layer}_{kind}_sum")
            goal = getattr(r, f"{layer}_{kind}_pieces")
            summed[...] = sum_of(parts).astype(LOW)
            cut = piece(summed)
            exchange(f"{layer}_{kind}", "seq", cut, goal.at[me], cut(me))

        def send_totals(layer, kind):
            pieces, mine = getattr(r, f"{layer}_{kind}_pieces"), getattr(r, f"{layer}_{kind}_mine")
            goal = getattr(r, f"{layer}_{kind}_total")
            mine[...] = sum_of(pieces).astype(LOW)
            exchange(f"{layer}_{kind}", "dp", lambda peer: mine, goal.at[replica], mine)

        def first_pause():
            both = jnp.concatenate([r.enc_d_pairs[...], r.dec_d_pairs[...]], 0)
            for part in range(group):
                r.pair_out[part] = both[part * pair_rows : (part + 1) * pair_rows]
            exchange("pairs", "seq", lambda peer: r.pair_out.at[peer], r.pair_pieces.at[me], r.pair_out.at[me])
            for copy in parts_in:
                copy.wait()
            send_pieces("dec", "down")
            send_pieces("dec", "up")

        def second_pause():
            arrive("pairs")
            r.pair_sum[...] = sum_of(r.pair_pieces)
            exchange("pairs", "dp", lambda peer: r.pair_sum, r.pair_parts.at[replica], r.pair_sum)
            for kind in ("down", "up"):
                arrive(f"enc_{kind}")
                send_pieces("enc", kind)

        def third_pause():
            arrive("pairs")
            r.pair_mine[...] = sum_of(r.pair_parts)
            exchange("pairs", "seq", lambda peer: r.pair_mine, r.pair_total.at[me], r.pair_mine)
            for kind in ("down", "up"):
                arrive(f"dec_{kind}")
                send_totals("dec", kind)

        def fourth_pause():
            for kind in ("down", "up"):
                arrive(f"enc_{kind}")
                send_totals("enc", kind)

        for copy in firsts:
            copy.wait()
        attend_back(
            SimpleNamespace(
                q=r.qkv_v, k=r.qkv_v, v=r.qkv_v, q0=0, k0=width, v0=2 * width,
                q_marks=marks, k_marks=marks, pairs=r.enc_pairs, context=r.context_v, lse=r.lse,
                d_context=r.d_context_v, dq=r.d_qkv, dk=r.d_qkv, dv=r.d_qkv, dq0=0, dk0=width,
                dv0=2 * width, d_pairs=r.enc_d_pairs, factor=1.0 / copies, qx=r.qx, kx=r.kx, dx=r.dx,
                vx=r.vx, delta=r.delta, dq_sum=r.dq_sum, chances=r.chances, changes=r.changes,
            ),
            False,
            count,
            [first_pause, second_pause, third_pause, fourth_pause],
        )
        for copy in lasts:
            copy.wait()
        for cut in chunks(tokens, CHUNK):
            r.summed_v[cut, :] = (
                r.summed_v[cut, :].astype(WIDE)
                + contract(r.d_qkv[:, cut], r.qkv_weight[...], 0, 1)
            ).astype(LOW)
        cut = piece(r.summed_v)
        exchange("source", "seq", cut, r.source_grad.at[me], cut(me))
        arrive("pairs")
        whole = jnp.concatenate([r.pair_total[part] for part in range(group)], 0)
        for number, layer in enumerate(layers):
            prefix_back(
                SimpleNamespace(
                    d_pairs=whole[number * PAD : (number + 1) * PAD], group=group, place=me,
                    hidden=getattr(r, f"{layer}_hidden"), prefix=getattr(r, f"{layer}_prefix"),
                    second=getattr(r, f"{layer}_second"), first_share=getattr(r, f"{layer}_first"),
                    tall_hidden=r.tall_hidden, tall_prefix=r.tall_prefix, wide_prefix=r.wide_prefix,
                    embed_grad=getattr(r, f"{layer}_embed"), in_grad=getattr(r, f"{layer}_in"),
                    out_grad=getattr(r, f"{layer}_out_grad"),
                )
            )
            for kind in ("down", "up"):
                arrive(f"{layer}_{kind}")
                total, out = getattr(r, f"{layer}_{kind}_total"), getattr(r, f"{layer}_{kind}_grad_all")
                out[...] = jnp.concatenate([total[part].astype(WIDE) for part in range(replicas)], 1)
        arrive("source")

    near_outs = {}
    for layer in layers:
        near_outs[f"{layer}_embed"] = ((count, width // group), WIDE)
        near_outs[f"{layer}_in"] = ((width // group, units), WIDE)
        near_outs[f"{layer}_out_grad"] = ((units // group, 2 * width), WIDE)
        near_outs[f"{layer}_down_grad_all"] = ((width // group, narrow), WIDE)
        near_outs[f"{layer}_up_grad_all"] = ((narrow // group, width), WIDE)
    scratch = {}
    for layer in layers:
        for kind, part, own in (("down", down_part, down_piece), ("up", up_part, up_piece)):
            scratch[f"{layer}_{kind}s"] = ((replicas, *part), LOW)
            scratch[f"{layer}_{kind}_sum"] = (part, LOW)
            scratch[f"{layer}_{kind}_pieces"] = ((group, *own), LOW)
            scratch[f"{layer}_{kind}_mine"] = (own, LOW)
            scratch[f"{layer}_{kind}_total"] = ((replicas, *own), LOW)
        scratch[f"{layer}_second"] = ((units, 2 * width), LOW)
        scratch[f"{layer}_first"] = ((width // group, units), LOW)
    for name in ("pair_out", "pair_pieces", "pair_total"):
        scratch[name] = ((group, pair_rows, 2 * width), WIDE)
    scratch["pair_parts"] = ((replicas, pair_rows, 2 * width), WIDE)
    scratch["pair_sum"] = scratch["pair_mine"] = ((pair_rows, 2 * width), WIDE)
    scratch["enc_d_pairs"] = ((PAD, 2 * width), WIDE)
    scratch["tall_hidden"] = ((units, PAD), WIDE)
    scratch["wide_prefix"] = ((PAD, width), WIDE)
    scratch["tall_prefix"] = ((width, PAD), WIDE)
    return run_kernel(
        body,
        "encoder_attend_back",
        near=dict(
            marks=w.source_segments, enc_pairs=forward.enc_pairs, lse=forward.lse,
            dec_d_pairs=dec.d_pairs, enc_hidden=forward.enc_hidden, dec_hidden=forward.dec_hidden,
            enc_prefix=w.enc_prefix, dec_prefix=w.dec_prefix,
        ),
        far=dict(
            qkv=forward.qkv, d_context=feed.d_context, context=forward.context,
            enc_qkv=w.enc_qkv, summed_grad=feed.summed_grad,
            dec_down_parts=feed.dec_down_parts, dec_up_parts=feed.dec_up_parts,
            enc_down_grad=feed.adapter_down_grad, enc_up_grad=feed.adapter_up_grad,
            enc_prefix_in=w.enc_prefix_in, enc_prefix_out=w.enc_prefix_out,
            dec_prefix_in=w.dec_prefix_in, dec_prefix_out=w.dec_prefix_out,
        ),
        near_outs=near_outs,
        far_outs=dict(source_grad=((group, share, width), LOW)),
        scratch=dict(
            qkv_v=((3 * width, tokens), LOW), d_context_v=((width, tokens), LOW),
            context_v=((width, tokens), LOW), qkv_weight=((width, 3 * width), LOW),
            summed_v=((tokens, width), LOW), d_qkv=((3 * width, tokens), LOW),
            qx=((heads * 16, tokens), LOW), kx=((16, tokens), LOW),
            dx=((heads * 16, tokens), LOW), vx=((16, tokens), LOW), delta=((16, tokens), WIDE),
            dq_sum=((width, tokens), WIDE), chances=((2, tokens, 256), LOW),
            changes=((2, tokens, 256), LOW), **scratch,
        ),
        flops=2 * tokens * width * 2304 + 20 * tokens * tokens * width,
        links=7 * (group - 1) + 5 * (replicas - 1) + group - 1,
        collective=2,
    )


def finish(attended, feed, copies):
    small = [name for name in vars(attended) if name != "source_grad"]
    shape = attended.source_grad.shape
    later = feed.out_all.shape

    def body(r):
        move = Mover(r.semaphores)
        ins = [
            move.start(r.source_grad, r.source_v),
            move.start(r.target_grad, r.target_v),
        ]
        outs = []
        relays = [
            (move.start(r.out_all.at[place * copies], r.out_v.at[place]), r.out_v.at[place], r.out.at[place])
            for place in range(later[0] // copies)
        ]
        for name in small:
            via = getattr(r, name + "_v")
            relays.append((move.start(getattr(r, name + "_in"), via), via, getattr(r, name)))
        for copy, via, goal in relays:
            copy.wait()
            outs.append(move.start(via, goal))
        for copy, origin, wide, goal in (
            (ins[0], r.source_v, r.source_w, r.source_out), (ins[1], r.target_v, r.target_w, r.target_out)
        ):
            copy.wait()
            for place in range(wide.shape[0]):
                wide[place] = origin[place * copies].astype(WIDE)
                outs.append(move.start(wide.at[place], goal.at[place]))
        for copy in outs:
            copy.wait()

    rows = shape[0] // copies
    return run_kernel(
        body,
        "finish",
        near={},
        far=dict(
            source_grad=attended.source_grad, target_grad=feed.target_grad_all, out_all=feed.out_all,
            **{name + "_in": getattr(attended, name) for name in small},
        ),
        near_outs={},
        far_outs=dict(
            out=((rows, *later[1:]), LOW), source_out=((rows, *shape[1:]), WIDE),
            target_out=((rows, *later[1:]), WIDE),
            **{name: (getattr(attended, name).shape, WIDE) for name in small},
        ),
        scratch=dict(
            source_v=(shape, LOW), source_w=((rows, *shape[1:]), WIDE), target_v=(later, LOW),
            target_w=((rows, *later[1:]), WIDE), out_v=((rows, *later[1:]), LOW),
            **{name + "_v": (getattr(attended, name).shape, WIDE) for name in small},
        ),
        flops=0,
    )


NAMES = (
    "source",
    "target",
    "source_segments",
    "target_segments",
    "cotangent",
    "enc_qkv",
    "enc_out",
    "enc_up",
    "enc_down",
    "dec_qkv",
    "dec_out",
    "cross_q",
    "cross_kv",
    "cross_out",
    "dec_up",
    "dec_down",
    "enc_prefix",
    "enc_prefix_in",
    "enc_prefix_out",
    "enc_adapter_down",
    "enc_adapter_up",
    "dec_prefix",
    "dec_prefix_in",
    "dec_prefix_out",
    "dec_adapter_down",
    "dec_adapter_up",
)


def shards(*operands, group, replicas):
    w = SimpleNamespace(**dict(zip(NAMES, operands)))
    copies = group // w.source.shape[0]
    forward = encoder_forward(w, group, copies)
    dec = decoder(forward, w, copies, replicas)
    feed = encoder_feed_back(dec, forward, w, group, copies, replicas)
    attended = encoder_attend_back(feed, dec, forward, w, group, copies, replicas)
    done = finish(attended, feed, copies)
    results = [done.out, done.source_out, done.target_out]
    for layer in ("enc", "dec"):
        for name in ("embed", "in", "out_grad", "down_grad_all", "up_grad_all"):
            results.append(getattr(done, f"{layer}_{name}"))
    return tuple(results)


def solution(mesh):
    rows = P("dp", "seq", None)
    marks = P("dp", None)
    in_specs = (rows, rows, marks, marks, rows) + (P(),) * 21
    across, down = P(None, "seq"), P("seq", None)
    layer = (across, down, down, down, down)
    return jax.shard_map(
        functools.partial(shards, group=mesh.shape["seq"], replicas=mesh.shape["dp"]),
        mesh=mesh,
        in_specs=in_specs,
        out_specs=(rows, rows, rows) + layer + layer,
        check_vma=False,
    )
```

```python
import functools
import math
from types import SimpleNamespace

import jax
import jax.numpy as jnp
from jax import lax
from jax.experimental import pallas as pl
from jax.experimental.pallas import tpu as pltpu
from jax.sharding import PartitionSpec as P

HEAD = 64
GROUP = 4
PAD = 32
BIG = 2.0**100
LOG2E = math.log2(math.e)
SCALE = 1.0 / math.sqrt(HEAD)
VMEM_BYTES = 60 * 2**20
CHUNK = 256
TILE = 256
COLUMNS = 512
INNER = 512
LOW = jnp.bfloat16
WIDE = jnp.float32


def contract(left, right, left_dim, right_dim):
    return lax.dot_general(
        left, right, (((left_dim,), (right_dim,)), ((), ())), preferred_element_type=WIDE
    )


def rows_at(index, size, base=0):
    return pl.ds(pl.multiple_of(base + index * size, size), size)


def chunks(size, step):
    step = min(step, size)
    return [slice(start, start + step) for start in range(0, size, step)]


def total_of(values):
    return functools.reduce(lambda left, right: left + right, values)


def normalize(value):
    centered = value - jnp.mean(value, axis=-1, keepdims=True)
    inverse = lax.rsqrt(jnp.mean(centered * centered, axis=-1, keepdims=True) + 1e-05)
    return (centered * inverse, inverse)


def normalize_back(gradient, normed, inverse):
    return (
        gradient
        - jnp.mean(gradient, axis=-1, keepdims=True)
        - normed * jnp.mean(gradient * normed, axis=-1, keepdims=True)
    ) * inverse


def gelu_both(value):
    scale = math.sqrt(2.0 / math.pi)
    square = value * value
    half = 0.5 + 0.5 * jnp.tanh(value * (scale + (scale * 0.044715) * square))
    active = value * half
    slope = half + active * (1.0 - half) * (2.0 * scale + (6.0 * scale * 0.044715) * square)
    return (active, slope)


class Mover:
    def __init__(self, semaphores):
        self.semaphores = semaphores
        self.used = 0

    def start(self, origin, goal):
        copy = pltpu.make_async_copy(origin, goal, self.semaphores.at[self.used])
        self.used += 1
        copy.start()
        return copy


def run_kernel(body, name, near, far, near_outs, far_outs, scratch, flops, links=0, collective=None):
    in_names = list(near) + list(far)
    out_names = list(near_outs) + list(far_outs)
    names = in_names + out_names + list(scratch) + ["semaphores"]
    link_scratch = []
    remote = {}
    if collective is not None:
        names += ["sent", "arrived"]
        link_scratch = [pltpu.SemaphoreType.DMA((links,)), pltpu.SemaphoreType.DMA((links,))]
        remote = dict(collective_id=collective, has_side_effects=True)

    def kernel(*refs):
        body(SimpleNamespace(**dict(zip(names, refs))))

    near_spec = pl.BlockSpec(memory_space=pltpu.VMEM)
    far_spec = pl.BlockSpec(memory_space=pl.ANY)
    results = pl.pallas_call(
        kernel,
        out_shape=tuple(
            jax.ShapeDtypeStruct(*out) for out in (*near_outs.values(), *far_outs.values())
        ),
        in_specs=[near_spec] * len(near) + [far_spec] * len(far),
        out_specs=tuple([near_spec] * len(near_outs) + [far_spec] * len(far_outs)),
        scratch_shapes=[pltpu.VMEM(*shape) for shape in scratch.values()]
        + [pltpu.SemaphoreType.DMA((80,))]
        + link_scratch,
        compiler_params=pltpu.CompilerParams(vmem_limit_bytes=VMEM_BYTES, **remote),
        cost_estimate=pl.CostEstimate(flops=flops, bytes_accessed=2**24, transcendentals=0),
        name=name,
    )(*near.values(), *far.values())
    return SimpleNamespace(**dict(zip(out_names, results)))


class Links:
    def __init__(self, sent, arrived, groups):
        self.sent, self.arrived = sent, arrived
        self.used = 0
        self.place = {axis: lax.axis_index(axis) for axis in ("dp", "seq")}
        self.sizes = groups
        barrier = pltpu.get_barrier_semaphore()
        peers = 0
        for axis, size in groups.items():
            for shift in range(1, size):
                pl.semaphore_signal(
                    barrier, inc=1, device_id=self.device(axis, shift), device_id_type=pl.DeviceIdType.MESH
                )
                peers += 1
        pl.semaphore_wait(barrier, peers)

    def peer(self, axis, shift):
        return lax.rem(self.place[axis] + shift, self.sizes[axis])

    def device(self, axis, shift):
        return self.device_at(axis, self.peer(axis, shift))

    def device_at(self, axis, index):
        return (index, self.place["seq"]) if axis == "dp" else (self.place["dp"], index)

    def start(self, axis, shift, origin, goal):
        return self.start_to(axis, self.peer(axis, shift), origin, goal)

    def start_to(self, axis, index, origin, goal):
        copy = pltpu.make_async_remote_copy(
            src_ref=origin,
            dst_ref=goal,
            send_sem=self.sent.at[self.used],
            recv_sem=self.arrived.at[self.used],
            device_id=self.device_at(axis, index),
            device_id_type=pl.DeviceIdType.MESH,
        )
        self.used += 1
        copy.start()
        return copy

    def scatter(self, axis, pick, goal):
        return [
            self.start(axis, shift, pick(self.peer(axis, shift)), goal)
            for shift in range(1, self.sizes[axis])
        ]


class Exchange:
    def __init__(self, move, links):
        self.move, self.links = move, links
        self.place, self.sizes = links.place, links.sizes
        self.open = {}

    def start(self, name, axis, pick, goal, via=None):
        mine = self.place[axis]
        copies = self.links.scatter(axis, pick, goal.at[mine])
        if via is None:
            copies.append(self.move.start(pick(mine), goal.at[mine]))
        else:
            self.move.start(pick(mine), via).wait()
            copies.append(self.move.start(via, goal.at[mine]))
        self.open[name] = copies

    def end(self, *names):
        for name in names:
            for copy in self.open.pop(name):
                copy.wait()


def sum_parts(parts):
    return total_of([parts[part].astype(WIDE) for part in range(parts.shape[0])])


def rows_for(ref, count):
    size = ref.shape[0] // count
    return lambda place: ref.at[pl.ds(pl.multiple_of(place * size, size), size), :]


def split_three(value):
    high = value.astype(LOW).astype(WIDE)
    rest = value - high
    middle = rest.astype(LOW).astype(WIDE)
    return (high, middle, rest - middle)


def place_rows(parts, first, shape):
    row = lax.broadcasted_iota(jnp.int32, shape, 0)
    out = jnp.zeros(shape, WIDE)
    for offset, part in enumerate(parts):
        out = jnp.where(row == first + offset, part, out)
    return out


def document_rows(segments, tokens, is_key):
    row = lax.broadcasted_iota(jnp.int32, (16, tokens), 0)
    same = row == segments
    if is_key:
        return jnp.where(row < 4, jnp.where(same, 0.0, -BIG), 0.0)
    return jnp.where(same & (row < 4), 1.0, 0.0)


def column_peak(scores, peak):
    for start in range(0, scores.shape[0], 8):
        peak = jnp.maximum(peak, scores[start : start + 8])
    return peak


def from_column(value, low):
    if low == 0:
        return value
    return jnp.concatenate([jnp.zeros((value.shape[0], low), value.dtype), value], 1)


def attend(a, causal, prefix):
    queries, keys = a.q.shape[1], a.k.shape[1]
    width = a.context.shape[0]
    heads = width // HEAD
    tile = min(256, keys)
    tiles = keys // tile
    a.qx[:16, :queries] = document_rows(a.q_marks, queries, False).astype(LOW)
    a.kx[:, :keys] = document_rows(a.k_marks, keys, True).astype(LOW)
    columns = chunks(queries, COLUMNS)

    def front(head, slot, own, work):
        start = own.start
        query = jnp.concatenate([a.q[rows_at(head, HEAD, a.q0), own], a.qx[:16, own]], 0)
        peak = jnp.full((8, own.stop - start), -4.0 * BIG, WIDE)
        if prefix:
            scores = contract(a.pair_keys[rows_at(head, HEAD), :], query[:HEAD], 0, 0)
            row = lax.broadcasted_iota(jnp.int32, scores.shape, 0)
            scores = jnp.where(row < prefix, scores, -BIG)
            a.pair_scores[slot, :, own] = scores
            peak = column_peak(scores, peak)
        for part in range(tiles):
            if not (causal and part * tile >= own.stop):
                cut = slice(part * tile, (part + 1) * tile)
                key = jnp.concatenate([a.k[rows_at(head, HEAD, a.k0), cut], a.kx[:, cut]], 0)
                scores = contract(key, query, 0, 0)
                if causal and cut.stop > start:
                    place = lax.broadcasted_iota(jnp.int32, scores.shape, 0) + (cut.start - start)
                    scores = jnp.where(
                        place <= lax.broadcasted_iota(jnp.int32, scores.shape, 1), scores, -BIG
                    )
                a.scores[slot, cut, own] = scores
                peak = column_peak(scores, peak)
            work(part)
        a.peak[slot, :, own] = peak

    def step(head, following, slot):
        for own in columns:
            peak = jnp.max(a.peak[slot, :, own], 0, keepdims=True)
            context = []
            if prefix:
                weights = jnp.exp2(a.pair_scores[slot, :, own] - peak).astype(LOW)
                value = jnp.concatenate(
                    [a.pair_values[rows_at(head, HEAD), :], jnp.ones((16, PAD), LOW)], 0
                )
                context.append(contract(value, weights, 1, 0))

            def work(part):
                if causal and part * tile >= own.stop:
                    return
                cut = slice(part * tile, (part + 1) * tile)
                weights = jnp.exp2(a.scores[slot, cut, own] - peak).astype(LOW)
                value = jnp.concatenate(
                    [a.v[rows_at(head, HEAD, a.v0), cut], jnp.ones((16, tile), LOW)], 0
                )
                context.append(contract(value, weights, 1, 0))

            front(following, 1 - slot, own, work)
            summed = total_of(context)
            total = summed[HEAD : HEAD + 1]
            a.context[rows_at(head, HEAD), own] = (summed[:HEAD] * (1.0 / total)).astype(LOW)
            a.lse[pl.ds(head, 1), own] = peak + jnp.log2(total)

    for own in columns:
        front(0, 0, own, lambda part: None)

    def pair(index, carry):
        step(2 * index, 2 * index + 1, 0)
        step(2 * index + 1, jnp.minimum(2 * index + 2, heads - 1), 1)
        return carry

    lax.fori_loop(0, heads // 2, pair, 0)


def block_diagonal(pairs, group, first):
    wide = GROUP * HEAD
    rows = pairs[:, first + group * wide : first + (group + 1) * wide]
    column = lax.broadcasted_iota(jnp.int32, rows.shape, 1)
    parts = [
        jnp.where((column >= member * HEAD) & (column < (member + 1) * HEAD), rows.astype(WIDE), 0.0)
        for member in range(GROUP)
    ]
    return jnp.concatenate(parts, 0).astype(LOW)


def own_columns(grads):
    column = lax.broadcasted_iota(jnp.int32, (PAD, GROUP * HEAD), 1)
    out = jnp.zeros((PAD, GROUP * HEAD), WIDE)
    for member in range(GROUP):
        own = (column >= member * HEAD) & (column < (member + 1) * HEAD)
        out = jnp.where(own, grads[member * PAD : (member + 1) * PAD], out)
    return out


def attend_back(a, causal, prefix, ready=None, staged=None):
    queries, keys = a.q.shape[1], a.k.shape[1]
    width = a.context.shape[0]
    heads = width // HEAD
    tiles = keys // TILE
    row = lax.broadcasted_iota(jnp.int32, (16, keys), 0)
    a.kx[:, :keys] = jnp.where(
        (row >= 4) & (row < 7), 1.0, document_rows(a.k_marks, keys, True)
    ).astype(LOW)
    a.vx[:, :keys] = jnp.where(row < 3, 1.0, 0.0).astype(LOW)
    documents = document_rows(a.q_marks, queries, False)

    def prepare(head, carry):
        rows = rows_at(head, HEAD)
        delta = jnp.sum(
            a.d_context[rows, :].astype(WIDE) * a.context[rows, :].astype(WIDE),
            axis=0,
            keepdims=True,
        )
        a.delta[pl.ds(head, 1), :queries] = delta
        a.dx[rows_at(head, 16), :queries] = place_rows(
            split_three(-delta), 0, (16, queries)
        ).astype(LOW)
        minus = split_three(-a.lse[pl.ds(head, 1), :])
        a.qx[rows_at(head, 16), :queries] = (
            documents + place_rows(minus, 4, (16, queries))
        ).astype(LOW)
        return carry

    lax.fori_loop(0, heads, prepare, 0)

    if prefix:
        for group in range(heads // GROUP):
            start = group * GROUP * HEAD
            own = slice(start, start + GROUP * HEAD)
            query = a.q[a.q0 + start : a.q0 + start + GROUP * HEAD, :]
            grad = a.d_context[own, :]
            pair_keys = block_diagonal(a.pairs[...], group, 0)
            pair_values = block_diagonal(a.pairs[...], group, width)
            scores = contract(pair_keys, query, 1, 0)
            gains = contract(pair_values, grad, 1, 0)
            chances, changes = [], []
            for member in range(GROUP):
                head = group * GROUP + member
                part = slice(member * PAD, (member + 1) * PAD)
                chance = jnp.exp2(scores[part] - a.lse[head : head + 1, :])
                place = lax.broadcasted_iota(jnp.int32, chance.shape, 0)
                chance = jnp.where(place < prefix, chance, 0.0)
                chances.append(chance)
                changes.append(chance * (gains[part] - a.delta[head : head + 1, :queries]))
            chances = jnp.concatenate(chances, 0).astype(LOW)
            changes = jnp.concatenate(changes, 0).astype(LOW)
            a.dq_sum[own, :queries] = contract(pair_keys, changes, 0, 0)
            a.d_pairs[:, own] = own_columns(contract(changes, query, 1, 1)) * (a.factor / LOG2E)
            a.d_pairs[:, width + start : width + start + GROUP * HEAD] = (
                own_columns(contract(chances, grad, 1, 1)) * a.factor
            )
    else:
        a.dq_sum[:, :queries] = jnp.zeros((width, queries), WIDE)
    if ready is not None:
        ready(0)


    def span(part):
        return slice(part * TILE, (part + 1) * TILE)

    def front(head, own, cut, slot, number):
        query = jnp.concatenate([a.q[rows_at(head, HEAD, a.q0), own], a.qx[rows_at(head, 16), own]], 0)
        key = jnp.concatenate([a.k[rows_at(head, HEAD, a.k0), cut], a.kx[:, cut]], 0)
        scores = contract(query, key, 0, 0)
        if causal and own == cut:
            place = lax.broadcasted_iota(jnp.int32, scores.shape, 1)
            scores = jnp.where(place <= lax.broadcasted_iota(jnp.int32, scores.shape, 0), scores, -BIG)
        grad = jnp.concatenate([a.d_context[rows_at(head, HEAD), own], a.dx[rows_at(head, 16), own]], 0)
        value = jnp.concatenate([a.v[rows_at(head, HEAD, a.v0), cut], a.vx[:, cut]], 0)
        gains = contract(grad, value, 0, 0)
        chance = jnp.exp2(scores)
        a.chances[slot, number] = chance.astype(LOW)
        a.changes[slot, number] = (chance * gains).astype(LOW)

    def run(pieces, together, add):
        unit = [(offset, own, cut) for offset in range(together) for own, cut in pieces]

        def begin(index, slot, number):
            offset, own, cut = unit[number]
            front(index * together + offset, own, cut, slot, number)

        def mix(index, slot, following):
            by_key, by_query = {}, {}
            for number, (offset, own, cut) in enumerate(unit):
                head = index * together + offset
                rows = rows_at(head, HEAD)
                left = unit[number + 1 :]
                chances, changes = a.chances[slot, number], a.changes[slot, number]
                pair = by_key.setdefault((offset, cut.start), [])
                d_value = contract(a.d_context[rows, own], chances, 1, 0)
                pair.append((contract(a.q[rows_at(head, HEAD, a.q0), own], changes, 1, 0), d_value))
                begin(following, 1 - slot, number)
                d_query = by_query.setdefault((offset, own.start), [])
                d_query.append(contract(a.k[rows_at(head, HEAD, a.k0), cut], changes, 1, 1))
                if not any((other, keys_.start) == (offset, cut.start) for other, _, keys_ in left):
                    add(head, cut, *(total_of(parts) for parts in zip(*pair)))
                if not any((other, queries_.start) == (offset, own.start) for other, queries_, _ in left):
                    a.dq_sum[rows, own] += total_of(d_query)

        def two(index, carry):
            mix(2 * index, 0, 2 * index + 1)
            mix(2 * index + 1, 1, jnp.minimum(2 * index + 2, count - 1))
            return carry

        count = heads // together
        for number in range(len(unit)):
            begin(0, 0, number)
        return two, count // 2

    if staged is not None:
        for stage in range(tiles):
            pieces = [(span(other), span(stage)) for other in range(stage + 1, tiles)]
            pieces += [(span(stage), span(other)) for other in range(stage, tiles)]

            def add(head, cut, d_key, d_value):
                rows = rows_at(head, HEAD)
                if stage == 0:
                    a.dk_sum[rows, cut] = d_key
                    a.dv_sum[rows, cut] = d_value
                else:
                    a.dk_sum[rows, cut] += d_key
                    a.dv_sum[rows, cut] += d_value

            step, steps = run(pieces, {1: heads // 2, 3: 2}.get(len(pieces), 1), add)
            cuts = [0, steps // 3, 2 * steps // 3, steps] if stage == 0 else [0, steps]
            for number in range(len(cuts) - 1):
                lax.fori_loop(cuts[number], cuts[number + 1], step, 0)
                if number + 2 < len(cuts):
                    ready(number + 1)
            staged(stage, span(stage))
        return

    def add(head, cut, d_key, d_value):
        a.dk[rows_at(head, HEAD, a.dk0), cut] = (d_key * (1.0 / LOG2E)).astype(LOW)
        a.dv[rows_at(head, HEAD, a.dv0), cut] = d_value.astype(LOW)

    pieces = [
        (span(own), span(part))
        for part in range(tiles)
        for own in range(part if causal else 0, queries // TILE)
    ]
    step, steps = run(pieces, 2 if len(pieces) < 4 else 1, add)
    lax.fori_loop(0, steps, step, 0)
    a.dq[rows_at(0, width, a.dq0), :] = (a.dq_sum[:, :queries] * SCALE).astype(LOW)


def project_wide(out, weight, rows, scaled, place=slice(None)):
    for cut in chunks(weight.shape[1], 256):
        result = contract(weight[:, cut], rows, 0, 1)
        if cut.start < scaled:
            result = result * (SCALE * LOG2E)
        out[cut, place] = result.astype(LOW)


def add_and_normalize(hidden, context, weight, normed, inverse):
    for cut in chunks(hidden.shape[0], CHUNK):
        summed = hidden[cut, :].astype(WIDE) + contract(context[:, cut], weight[...], 0, 0)
        result, scale = normalize(summed)
        normed[cut, :] = result.astype(LOW)
        inverse[cut, :] = scale


def feed_forward(hidden, up, down, adapter_down, adapter_up, total, slopes_of, ahead, narrow):
    cuts = chunks(hidden.shape[0], CHUNK)
    count = up.shape[1] // INNER

    def block(index, second, factor, first, following, is_first):
        place = slopes_of(index)
        value = ahead[...]
        for number, cut in enumerate(cuts):
            if number + 1 < len(cuts):
                coming = contract(hidden[cuts[number + 1], :], first(), 1, 0)
            else:
                coming = contract(hidden[cuts[0], :], following(), 1, 0)
            active, slope = gelu_both(value)
            place[cut, :] = slope.astype(LOW)
            if factor != 1.0:
                narrow[cut, :] = active.astype(LOW)
                active = active * factor
            product = contract(active.astype(LOW), second(), 1, 0)
            if is_first:
                total[cut, :] = hidden[cut, :].astype(WIDE) + product
            else:
                total[cut, :] += product
            value = coming
        ahead[...] = value

    def first_of(index):
        return lambda: up[:, rows_at(jnp.minimum(index, count - 1), INNER)]

    ahead[...] = contract(hidden[cuts[0], :], adapter_down[...], 1, 0)
    block(0, lambda: adapter_up[...], 4.0, lambda: adapter_down[...], first_of(0), True)

    def main(index, carry):
        block(
            index + 1, lambda: down[rows_at(index, INNER), :], 1.0, first_of(index), first_of(index + 1), False
        )
        return carry

    lax.fori_loop(0, count, main, 0)


def finish_forward(total, normed, inverse):
    for cut in chunks(total.shape[0], CHUNK):
        result, scale = normalize(total[cut, :])
        normed[cut, :] = result.astype(LOW)
        inverse[cut, :] = scale


def pack(flat, value, first):
    size = value.shape[0] // flat.shape[0]
    for place in range(flat.shape[0]):
        for block in range(value.shape[1] // 128):
            goal = slice(first + block * size, first + (block + 1) * size)
            flat[place, goal, :] = value[
                place * size : (place + 1) * size, block * 128 : (block + 1) * 128
            ].astype(flat.dtype)


def unpack(rows, first, shape):
    parts = [
        rows[first + block * shape[0] : first + (block + 1) * shape[0]] for block in range(shape[1] // 128)
    ]
    return jnp.concatenate(parts, 1)


def flat_shapes(width, narrow, group, replicas):
    second = width // group * (narrow // 128)
    rows = second + narrow // group * (width // 128)
    return second, (group, rows, 128), (group, rows // replicas, 128)


def columns_for(flat, replicas):
    size = flat.shape[1] // replicas
    return lambda place: flat.at[:, pl.ds(pl.multiple_of(place * size, size), size), :]


def feed_back(f, send=None):
    tokens = f.hidden.shape[0]
    cuts = chunks(tokens, CHUNK)
    for cut in cuts:
        value = f.grad[cut, :]
        f.low[cut, :] = value.astype(LOW)
        f.side[cut, :] = (4.0 * value).astype(LOW)

    count = f.up.shape[1] // INNER

    def block(index, origin, first, second, keep, next_origin, following):
        place = f.slopes(index)
        value = f.ahead[...]
        for number, cut in enumerate(cuts):
            if number + 1 < len(cuts):
                coming = contract(origin[cuts[number + 1], :], first(), 1, 1)
            else:
                coming = contract(next_origin[cuts[0], :], following(), 1, 1)
            change = (value * place[cut, :].astype(WIDE)).astype(LOW)
            if keep is not None:
                keep[cut, :] = change
            f.grad[cut, :] += contract(change, second(), 1, 1)
            value = coming
        f.ahead[...] = value

    def first_of(index):
        return lambda: f.down[rows_at(jnp.minimum(index, count - 1), INNER), :]

    f.ahead[...] = contract(f.side[cuts[0], :], f.adapter_up[...], 1, 1)
    block(
        0, f.side, lambda: f.adapter_up[...], lambda: f.adapter_down[...], f.d_narrow, f.low, first_of(0)
    )
    pack(f.flat, contract(f.hidden[...], f.d_narrow[...], 0, 0) * f.factor, 0)
    pack(f.flat, contract(f.narrow[...], f.side[...], 0, 0) * f.factor, f.second)
    if send is not None:
        send()

    def main(index, carry):
        block(
            index + 1, f.low, first_of(index), lambda: f.up[:, rows_at(index, INNER)], None, f.low,
            first_of(index + 1),
        )
        return carry

    lax.fori_loop(0, count, main, 0)


def normalize_back_all(grad, normed, inverse, out):
    for cut in chunks(grad.shape[0], CHUNK):
        out[cut, :] = normalize_back(
            grad[cut, :].astype(WIDE), normed[cut, :].astype(WIDE), inverse[cut, :]
        ).astype(out.dtype)


def context_back(out, weight, grad):
    value = grad[...].astype(LOW)
    for cut in chunks(weight.shape[0], 256):
        out[cut, :] = contract(weight[cut, :], value, 1, 1).astype(LOW)


def prefix_pairs(prefix, first, second, hidden, pairs, pairs_wide):
    count = prefix.shape[0]
    hidden[...] = jnp.zeros(hidden.shape, WIDE)
    hidden[:count, :] = jnp.tanh(contract(prefix[...], first[...], 1, 0))
    parts = [part.astype(LOW) for part in split_three(hidden[...])]
    pairs[...] = total_of([contract(part, second[...], 1, 0) for part in parts]).astype(LOW)
    pairs_wide[...] = total_of([contract(second[...], part, 0, 1) for part in parts]).astype(LOW)


def encoder_forward(w, group, copies):
    width = w.source.shape[2]
    share, later_share = w.source.shape[1], w.target.shape[1]
    tokens, later_tokens = share * group, later_share * group
    inner = w.enc_up.shape[1]
    narrow = w.enc_adapter_down.shape[1]
    units = w.enc_prefix_in.shape[1]
    count = w.enc_prefix.shape[0]
    blocks = 1 + inner // INNER

    def body(r):
        move = Mover(r.semaphores)
        weights = [move.start(r.enc_qkv, r.qkv_weight)]
        enc_first, dec_first = r.mid_v.at[:width, :units], r.memory_v.at[:width, :units]
        enc_second, dec_second = r.up.at[:units, : 2 * width], r.up.at[:units, 2 * width : 4 * width]
        weights.append(move.start(r.enc_prefix_in, enc_first))
        weights.append(move.start(r.enc_prefix_out, enc_second))
        weights.append(move.start(r.dec_prefix_in, dec_first))
        weights.append(move.start(r.dec_prefix_out, dec_second))
        links = Links(r.sent, r.arrived, {"seq": group})
        me = links.place["seq"]
        row = me // copies

        def tokens_of(place, size):
            return pl.ds(pl.multiple_of(place * size, size), size)

        def bring(origin, goal, size, via=None):
            own = tokens_of(me, size)
            copies_out = links.scatter("seq", lambda peer: origin.at[peer // copies], goal.at[own, :])
            if via is None:
                return (move.start(origin.at[row], goal.at[own, :]), copies_out)
            move.start(origin.at[row], via).wait()
            return (move.start(via, goal.at[own, :]), copies_out)

        here, sources = bring(r.source, r.x, share)
        out_weight = move.start(r.enc_out, r.out_weight)
        adapters = [
            move.start(r.enc_adapter_down, r.a_down),
            move.start(r.enc_adapter_up, r.a_up),
        ]
        pair_weight = move.start(r.cross_kv, r.pair_weight)
        for copy in weights:
            copy.wait()
        prefix_pairs(r.enc_prefix, enc_first, enc_second, r.enc_hidden, r.enc_pairs, r.enc_pairs_wide)
        prefix_pairs(r.dec_prefix, dec_first, dec_second, r.dec_hidden, r.dec_pairs, r.dec_pairs_wide)
        ups = [move.start(r.enc_up, r.up), move.start(r.enc_down, r.down)]
        here.wait()
        if share % 128 == 0:
            place = tokens_of(me, share)
            project_wide(r.qkv_v, r.qkv_weight, r.x[place, :], width, place)
            for shift, copy in enumerate(sources, 1):
                copy.wait()
                place = tokens_of(lax.rem(me + group - shift, group), share)
                project_wide(r.qkv_v, r.qkv_weight, r.x[place, :], width, place)
        else:
            for copy in sources:
                copy.wait()
            project_wide(r.qkv_v, r.qkv_weight, r.x[...], width)
        later = [
            bring(r.target, r.target_rows, later_share, r.own_target),
            bring(r.cotangent, r.cotangent_rows, later_share, r.own_cotangent),
        ]
        outs = [move.start(r.qkv_v, r.qkv)]
        marks = r.marks[pl.ds(row, 1), :]
        attend(
            SimpleNamespace(
                q=r.qkv_v, k=r.qkv_v, v=r.qkv_v, q0=0, k0=width, v0=2 * width,
                q_marks=marks, k_marks=marks, pair_keys=r.enc_pairs_wide.at[:width],
                pair_values=r.enc_pairs_wide.at[width:],
                context=r.context_v, lse=r.lse, qx=r.qx, kx=r.kx, scores=r.scores,
                pair_scores=r.pair_scores, peak=r.peak,
            ),
            False,
            count,
        )
        outs.append(move.start(r.context_v, r.context))
        out_weight.wait()
        add_and_normalize(r.x, r.context_v, r.out_weight, r.mid_v, r.mid_inverse)
        outs.append(move.start(r.mid_v, r.mid))
        for copy in adapters + ups:
            copy.wait()
        feed_forward(
            r.mid_v, r.up, r.down, r.a_down, r.a_up, r.total,
            lambda index: r.slopes_v.at[index], r.ahead, r.narrow_v,
        )
        outs.append(move.start(r.slopes_v, r.slopes))
        outs.append(move.start(r.narrow_v, r.narrow))
        finish_forward(r.total, r.memory_v, r.memory_inverse)
        outs.append(move.start(r.memory_v, r.memory))
        pair_weight.wait()
        project_wide(r.pairs_v, r.pair_weight, r.memory_v[...], 0)
        outs.append(move.start(r.pairs_v, r.memory_pairs))
        for own, remote in later:
            own.wait()
            for copy in remote:
                copy.wait()
        for copy in outs:
            copy.wait()

    return run_kernel(
        body,
        "encoder_forward",
        near=dict(marks=w.source_segments, enc_prefix=w.enc_prefix, dec_prefix=w.dec_prefix),
        far=dict(
            source=w.source, target=w.target, cotangent=w.cotangent, enc_qkv=w.enc_qkv,
            enc_out=w.enc_out, enc_up=w.enc_up, enc_down=w.enc_down,
            enc_adapter_down=w.enc_adapter_down, enc_adapter_up=w.enc_adapter_up,
            cross_kv=w.cross_kv, enc_prefix_in=w.enc_prefix_in, enc_prefix_out=w.enc_prefix_out,
            dec_prefix_in=w.dec_prefix_in, dec_prefix_out=w.dec_prefix_out,
        ),
        near_outs=dict(
            lse=((16, tokens), WIDE), mid_inverse=((tokens, 1), WIDE),
            memory_inverse=((tokens, 1), WIDE),
            enc_hidden=((PAD, units), WIDE), enc_pairs=((PAD, 2 * width), LOW),
            dec_hidden=((PAD, units), WIDE), dec_pairs=((PAD, 2 * width), LOW),
            dec_pairs_wide=((2 * width, PAD), LOW),
        ),
        far_outs=dict(
            qkv=((3 * width, tokens), LOW), context=((width, tokens), LOW), mid=((tokens, width), LOW),
            slopes=((blocks, tokens, INNER), LOW), narrow=((tokens, narrow), LOW),
            memory=((tokens, width), LOW), memory_pairs=((2 * width, tokens), LOW),
            target_rows=((later_tokens, width), LOW), cotangent_rows=((later_tokens, width), LOW),
        ),
        scratch=dict(
            x=((tokens, width), LOW), qkv_weight=((width, 3 * width), LOW),
            own_target=((later_share, width), LOW), own_cotangent=((later_share, width), LOW),
            enc_pairs_wide=((2 * width, PAD), LOW),
            out_weight=((width, width), LOW), a_down=((width, narrow), LOW),
            a_up=((narrow, width), LOW), up=((width, inner), LOW), down=((inner, width), LOW),
            pair_weight=((width, 2 * width), LOW), qkv_v=((3 * width, tokens), LOW),
            context_v=((width, tokens), LOW), mid_v=((tokens, width), LOW),
            slopes_v=((blocks, tokens, INNER), LOW), narrow_v=((tokens, narrow), LOW),
            memory_v=((tokens, width), LOW), pairs_v=((2 * width, tokens), LOW),
            ahead=((CHUNK, INNER), WIDE), total=((tokens, width), WIDE), qx=((16, tokens), LOW), kx=((16, tokens), LOW),
            scores=((2, tokens, tokens), WIDE), pair_scores=((2, PAD, tokens), WIDE),
            peak=((2, 8, tokens), WIDE),
        ),
        flops=2 * tokens * width * 11776 + 4 * tokens * tokens * width,
        links=3 * (group - 1),
        collective=0,
    )


def decoder(forward, w, group, copies, replicas):
    tokens, width = forward.target_rows.shape
    share = tokens // group
    keys = forward.memory_pairs.shape[1]
    count = w.dec_prefix.shape[0]
    second, flat, part = flat_shapes(width, w.dec_adapter_down.shape[1], group, replicas)
    inner = w.dec_up.shape[1]
    narrow = w.dec_adapter_down.shape[1]
    blocks = 1 + inner // INNER
    heads = width // HEAD

    def body(r):
        move = Mover(r.semaphores)
        ins = [move.start(r.target, r.x), move.start(r.dec_qkv, r.qkv_weight)]
        for copy in ins:
            copy.wait()
        out_weight = move.start(r.dec_out, r.out_weight)
        crosses = [
            move.start(r.cross_q, r.query_weight),
            move.start(r.memory_pairs, r.pairs_v),
            move.start(r.cross_out, r.cross_out_weight),
        ]
        adapters = [
            move.start(r.dec_adapter_down, r.a_down),
            move.start(r.dec_adapter_up, r.a_up),
        ]
        ups = [move.start(r.dec_up, r.up), move.start(r.dec_down, r.down)]
        d_qkv = r.slopes.at[: 3 * width, :tokens]

        def slope_of(index):
            return r.slopes.at[rows_at(index, tokens), :]

        links = Links(r.sent, r.arrived, {"seq": group, "dp": replicas})
        exchange = Exchange(move, links)
        project_wide(r.qkv, r.qkv_weight, r.x[...], width)
        row = pl.ds(links.place["seq"] // copies, 1)
        marks, source_marks = r.marks[row, :], r.source_marks[row, :]
        shared = dict(
            qx=r.qx, kx=r.kx, scores=r.scores, pair_scores=r.pair_scores, peak=r.peak, dx=r.dx,
            vx=r.vx, delta=r.delta, dq_sum=r.dq_sum, chances=r.chances, changes=r.changes,
            d_context=r.d_context,
        )
        self_part = SimpleNamespace(
            q=r.qkv, k=r.qkv, v=r.qkv, q0=0, k0=width, v0=2 * width,
            q_marks=marks, k_marks=marks, pair_keys=r.pairs_wide.at[:width],
            pair_values=r.pairs_wide.at[width:], pairs=r.pairs, context=r.context, lse=r.lse,
            dq=d_qkv, dk=d_qkv, dv=d_qkv, dq0=0, dk0=width, dv0=2 * width,
            d_pairs=r.d_pairs, factor=1.0 / copies, **shared,
        )
        attend(self_part, True, count)
        out_weight.wait()
        add_and_normalize(r.x, r.context, r.out_weight, r.mid, r.mid_inverse)
        cotangents = move.start(r.cotangent, r.x)
        for copy in crosses:
            copy.wait()
        project_wide(r.query, r.query_weight, r.mid[...], width)
        cross_part = SimpleNamespace(
            q=r.query, k=r.pairs_v, v=r.pairs_v, q0=0, k0=0, v0=width,
            q_marks=marks, k_marks=source_marks, context=r.cross_context, lse=r.cross_lse,
            dq=r.d_query, dk=r.d_pairs_v, dv=r.d_pairs_v, dq0=0, dk0=0, dv0=width, **shared,
        )
        attend(cross_part, False, 0)
        add_and_normalize(r.mid, r.cross_context, r.cross_out_weight, r.crossed, r.crossed_inverse)
        for copy in adapters + ups + [cotangents]:
            copy.wait()
        feed_forward(
            r.crossed, r.up, r.down, r.a_down, r.a_up, r.total,
            slope_of, r.ahead, r.narrow,
        )
        finish_forward(r.total, r.out_v, r.out_inverse)
        exchange.start("out", "seq", rows_for(r.out_v, group), r.out_all)
        outs = []
        normalize_back_all(r.x, r.out_v, r.out_inverse, r.total)
        feed_back(
            SimpleNamespace(
                grad=r.total, low=r.low, side=r.side, hidden=r.crossed, narrow=r.narrow, up=r.up,
                down=r.down, adapter_down=r.a_down, adapter_up=r.a_up,
                slopes=slope_of, flat=r.flat, second=second,
                d_narrow=r.d_narrow, factor=1.0 / copies, ahead=r.ahead,
            )
        )
        exchange.start("flat", "dp", columns_for(r.flat, replicas), r.parts)
        normalize_back_all(r.total, r.crossed, r.crossed_inverse, r.total)
        context_back(r.d_context, r.cross_out_weight, r.total)
        attend_back(cross_part, False, 0)
        outs.append(move.start(r.d_pairs_v, r.memory_pairs_grad))
        exchange.end("flat")
        r.flat_sum[...] = sum_parts(r.parts).astype(LOW)
        exchange.start("flat", "seq", lambda peer: r.flat_sum.at[peer], r.flat_own)
        for cut in chunks(tokens, CHUNK):
            r.total[cut, :] += contract(r.d_query[:, cut], r.query_weight[...], 0, 1)
        normalize_back_all(r.total, r.mid, r.mid_inverse, r.total)
        context_back(r.d_context, r.out_weight, r.total)
        attend_back(self_part, True, count)
        for cut in chunks(tokens, CHUNK):
            r.x[cut, :] = (
                r.total[cut, :] + contract(d_qkv[:, cut], r.qkv_weight[...], 0, 1)
            ).astype(LOW)
        outs.append(move.start(r.x, r.target_grad))
        for copy in outs:
            copy.wait()
        exchange.end("out", "flat")

    return run_kernel(
        body,
        "decoder",
        near=dict(
            marks=w.target_segments, source_marks=w.source_segments,
            pairs_wide=forward.dec_pairs_wide, pairs=forward.dec_pairs,
        ),
        far=dict(
            target=forward.target_rows, cotangent=forward.cotangent_rows,
            memory_pairs=forward.memory_pairs, dec_qkv=w.dec_qkv,
            dec_out=w.dec_out, cross_q=w.cross_q, cross_out=w.cross_out, dec_up=w.dec_up,
            dec_down=w.dec_down, dec_adapter_down=w.dec_adapter_down,
            dec_adapter_up=w.dec_adapter_up,
        ),
        near_outs=dict(d_pairs=((PAD, 2 * width), WIDE)),
        far_outs=dict(
            out_all=((group, share, width), LOW), target_grad=((tokens, width), LOW),
            memory_pairs_grad=((2 * width, keys), LOW),
            flat_own=(part, LOW),
        ),
        scratch=dict(
            flat=(flat, LOW), parts=((replicas, *part), LOW), flat_sum=(part, LOW),
            x=((tokens, width), LOW),
            qkv_weight=((width, 3 * width), LOW), out_weight=((width, width), LOW),
            query_weight=((width, width), LOW), cross_out_weight=((width, width), LOW),
            pairs_v=((2 * width, keys), LOW), a_down=((width, narrow), LOW),
            a_up=((narrow, width), LOW), up=((width, inner), LOW), down=((inner, width), LOW),
            qkv=((3 * width, tokens), LOW), context=((width, tokens), LOW),
            mid=((tokens, width), LOW), mid_inverse=((tokens, 1), WIDE),
            query=((width, tokens), LOW), cross_context=((width, tokens), LOW),
            crossed=((tokens, width), LOW), crossed_inverse=((tokens, 1), WIDE),
            out_v=((tokens, width), LOW), out_inverse=((tokens, 1), WIDE),
            slopes=((blocks * tokens, INNER), LOW), narrow=((tokens, narrow), LOW),
            low=((tokens, width), LOW), side=((tokens, width), LOW), d_narrow=((tokens, narrow), LOW),
            ahead=((CHUNK, INNER), WIDE), total=((tokens, width), WIDE), lse=((16, tokens), WIDE), cross_lse=((16, tokens), WIDE),
            d_context=((width, tokens), LOW), d_query=((width, tokens), LOW),
            d_pairs_v=((2 * width, keys), LOW),
            qx=((heads * 16, tokens), LOW), kx=((16, keys), LOW),
            scores=((2, keys, tokens), WIDE), pair_scores=((2, PAD, tokens), WIDE),
            peak=((2, 8, tokens), WIDE), dx=((heads * 16, tokens), LOW), vx=((16, keys), LOW),
            delta=((16, tokens), WIDE), dq_sum=((width, tokens), WIDE),
            chances=((2, 8, TILE, TILE), LOW), changes=((2, 8, TILE, TILE), LOW),
        ),
        flops=4 * tokens * width * 11776 + 14 * tokens * (keys + tokens) * width,
        links=2 * (group - 1) + replicas - 1,
        collective=3,
    )


def encoder_feed_back(dec, forward, w, group, copies, replicas):
    tokens, width = forward.memory.shape
    inner = w.enc_up.shape[1]
    narrow = w.enc_adapter_down.shape[1]
    blocks = 1 + inner // INNER
    second, flat, part = flat_shapes(width, narrow, group, replicas)
    later = dec.target_grad.shape[0] // group

    def body(r):
        move = Mover(r.semaphores)
        firsts = [
            move.start(r.memory_pairs_grad, r.d_pairs),
            move.start(r.cross_kv, r.pair_weight),
            move.start(r.memory, r.memory_v),
        ]
        adapters = [
            move.start(r.enc_adapter_down, r.a_down),
            move.start(r.enc_adapter_up, r.a_up),
            move.start(r.narrow, r.narrow_v),
            move.start(r.mid, r.mid_v),
        ]
        ups = [
            move.start(r.slopes, r.slopes_v),
            move.start(r.enc_down, r.down),
            move.start(r.enc_up, r.up),
            move.start(r.enc_out, r.out_weight),
        ]
        links = Links(r.sent, r.arrived, {"seq": group, "dp": replicas})
        exchange = Exchange(move, links)
        exchange.start("target", "seq", lambda peer: r.target_grad.at[peer], r.target_grad_all, r.own_target)
        for copy in firsts:
            copy.wait()
        for cut in chunks(tokens, CHUNK):
            grad = contract(r.d_pairs[:, cut], r.pair_weight[...], 0, 1)
            r.total[cut, :] = normalize_back(
                grad, r.memory_v[cut, :].astype(WIDE), r.memory_inverse[cut, :]
            )
        for copy in adapters + ups:
            copy.wait()

        def send():
            exchange.start("flat", "dp", columns_for(r.flat, replicas), r.parts)

        feed_back(
            SimpleNamespace(
                grad=r.total, low=r.low, side=r.side, hidden=r.mid_v, narrow=r.narrow_v, up=r.up,
                down=r.down, adapter_down=r.a_down, adapter_up=r.a_up,
                slopes=lambda index: r.slopes_v.at[index], flat=r.flat, second=second,
                d_narrow=r.d_narrow, factor=1.0 / copies, ahead=r.ahead,
            ),
            send,
        )
        normalize_back_all(r.total, r.mid_v, r.mid_inverse, r.low)
        outs = [move.start(r.low, r.summed_grad)]
        context_back(r.d_context_v, r.out_weight, r.low)
        outs.append(move.start(r.d_context_v, r.d_context))
        for copy in outs:
            copy.wait()
        exchange.end("target", "flat")

    return run_kernel(
        body,
        "encoder_feed_back",
        near=dict(mid_inverse=forward.mid_inverse, memory_inverse=forward.memory_inverse),
        far=dict(
            target_grad=dec.target_grad.reshape(group, -1, width),
            memory_pairs_grad=dec.memory_pairs_grad, memory=forward.memory, mid=forward.mid,
            slopes=forward.slopes, narrow=forward.narrow, cross_kv=w.cross_kv,
            enc_out=w.enc_out, enc_up=w.enc_up, enc_down=w.enc_down,
            enc_adapter_down=w.enc_adapter_down, enc_adapter_up=w.enc_adapter_up,
        ),
        near_outs={},
        far_outs=dict(
            summed_grad=((tokens, width), LOW), d_context=((width, tokens), LOW),
            parts=((replicas, *part), LOW),
            target_grad_all=((group, later, width), LOW),
        ),
        scratch=dict(
            own_target=((later, width), LOW),
            flat=(flat, LOW), d_pairs=((2 * width, tokens), LOW), pair_weight=((width, 2 * width), LOW),
            memory_v=((tokens, width), LOW), mid_v=((tokens, width), LOW),
            slopes_v=((blocks, tokens, INNER), LOW), narrow_v=((tokens, narrow), LOW),
            out_weight=((width, width), LOW), a_down=((width, narrow), LOW),
            a_up=((narrow, width), LOW), up=((width, inner), LOW), down=((inner, width), LOW),
            low=((tokens, width), LOW), side=((tokens, width), LOW), d_narrow=((tokens, narrow), LOW),
            ahead=((CHUNK, INNER), WIDE), total=((tokens, width), WIDE), d_context_v=((width, tokens), LOW),
        ),
        flops=2 * tokens * width * 9728,
        links=group - 1 + replicas - 1,
        collective=1,
    )


def split_product(left, right, left_dim, right_dim):
    return total_of(
        [contract(part.astype(LOW), right, left_dim, right_dim) for part in split_three(left)]
    )


def prefix_back(p):
    count, group = p.prefix.shape[0], p.group
    d_pairs, hidden = p.d_pairs, p.hidden[...]
    units, width = hidden.shape[1], p.prefix.shape[1]
    p.tall_hidden[...] = hidden.T
    share = units // group
    own = p.tall_hidden[pl.ds(pl.multiple_of(p.place * share, share), share), :]
    parts = split_three(d_pairs)
    p.out_grad[...] = total_of(
        [split_product(own, part.astype(LOW), 1, 0) for part in parts]
    )
    d_hidden = split_product(d_pairs, p.second[...], 1, 1) * (1.0 - hidden * hidden)
    p.wide_prefix[...] = jnp.zeros(p.wide_prefix.shape, WIDE)
    p.wide_prefix[:count, :] = p.prefix[...].astype(WIDE)
    p.tall_prefix[...] = p.wide_prefix[...].T
    share = width // group
    own = p.tall_prefix[pl.ds(pl.multiple_of(p.place * share, share), share), :].astype(LOW)
    p.in_grad[...] = total_of([contract(own, part.astype(LOW), 1, 0) for part in split_three(d_hidden)])
    p.embed_grad[...] = split_product(d_hidden, p.first_share[...], 1, 1)[:count]


def block_order(place, count):
    if count == 4:
        return [lax.rem(place + 2, 4), 3 - place, place + 1 - 2 * lax.rem(place, 2), place]
    return [lax.rem(place + step + 1, count) for step in range(count)]


def encoder_attend_back(feed, dec, forward, w, group, copies, replicas):
    tokens, width = feed.summed_grad.shape
    share = tokens // group
    count = w.enc_prefix.shape[0]
    narrow, units = w.enc_adapter_down.shape[1], w.enc_prefix_in.shape[1]
    second, _, part = flat_shapes(width, narrow, group, replicas)
    heads = width // HEAD
    tile = TILE
    blocks, per = tokens // tile, tile // share
    grains = [
        (layer, 8 * row, 128 * column)
        for layer in range(2) for column in range(2 * width // 128) for row in range(PAD // 8)
    ]
    depth = -(-len(grains) // (group * replicas))

    def grain_place(number):
        device, inside = number // depth, number % depth
        return (device // group, device % group, slice(8 * inside, 8 * inside + 8))
    layers = ("enc", "dec")

    def body(r):
        move = Mover(r.semaphores)
        links = Links(r.sent, r.arrived, {"seq": group, "dp": replicas})
        exchange = Exchange(move, links)
        me = links.place["seq"]
        order = [pl.multiple_of(block * tile, tile) for block in block_order(me // per, blocks)]
        firsts, lasts = [], []
        for stage, begin in enumerate(order):
            goal, origin = slice(stage * tile, (stage + 1) * tile), pl.ds(begin, tile)
            firsts.append(move.start(r.qkv.at[:, origin], r.qkv_v.at[:, goal]))
            firsts.append(move.start(r.d_context.at[:, origin], r.d_context_v.at[:, goal]))
            firsts.append(move.start(r.context.at[:, origin], r.context_v.at[:, goal]))
            lasts.append(move.start(r.summed_grad.at[origin, :], r.summed_v.at[goal, :]))
            r.lse_v[:, goal] = r.lse[:, origin]
        sums = move.start(r.enc_parts, r.enc_parts_v)
        totals = move.start(r.dec_own, r.dec_own_v)
        row = pl.ds(me // copies, 1)
        marks = jnp.concatenate([r.marks[row, pl.ds(begin, tile)] for begin in order], 1)
        lasts += [
            move.start(r.enc_qkv, r.qkv_weight),
            move.start(r.enc_prefix_out, r.enc_second), move.start(r.dec_prefix_out, r.dec_second),
        ]
        size = width // group
        first_rows = pl.ds(pl.multiple_of(me * size, size), size)
        lasts.append(move.start(r.enc_prefix_in.at[first_rows, :], r.enc_first))
        lasts.append(move.start(r.dec_prefix_in.at[first_rows, :], r.dec_first))

        def send_total(name, own, mine, total):
            mine[...] = sum_parts(own).astype(LOW)
            exchange.start(name, "dp", lambda peer: mine, total)

        def ready(step):
            if step == 0:
                r.pair_out[...] = jnp.zeros(r.pair_out.shape, WIDE)
                for number, (layer, row, column) in enumerate(grains):
                    origin = (r.enc_d_pairs, r.dec_d_pairs)[layer]
                    r.pair_out[grain_place(number)] = origin[row : row + 8, column : column + 128]
                exchange.start("pairs", "dp", lambda peer: r.pair_out.at[peer], r.pair_parts)
                totals.wait()
                send_total("dec", r.dec_own_v, r.dec_mine, r.dec_total)
            elif step == 1:
                exchange.end("pairs")
                r.pair_sum[...] = sum_parts(r.pair_parts)
                exchange.start("pairs", "seq", lambda peer: r.pair_sum.at[peer], r.pair_own)
            else:
                exchange.end("pairs")
                r.pair_mine[...] = sum_parts(r.pair_own)
                exchange.start("pairs", "seq", lambda peer: r.pair_mine, r.pair_row)

        sent = []

        def staged(stage, cut):
            r.d_qkv[:width, :] = (r.dq_sum[:, cut] * SCALE).astype(LOW)
            r.d_qkv[width : 2 * width, :] = (r.dk_sum[:, cut] * (1.0 / LOG2E)).astype(LOW)
            r.d_qkv[2 * width :, :] = r.dv_sum[:, cut].astype(LOW)
            if stage == 0:
                for copy in lasts:
                    copy.wait()
            r.summed_v[cut, :] = (
                r.summed_v[cut, :].astype(WIDE) + contract(r.d_qkv[...], r.qkv_weight[...], 0, 1)
            ).astype(LOW)
            inside = lax.rem(me, per)
            last = stage == blocks - 1
            for turn in range(per):
                number = lax.rem(inside + turn, per)
                origin = r.summed_v.at[
                    pl.ds(pl.multiple_of(stage * tile + number * share, share), share), :
                ]
                if last and turn == 0:
                    sent.append(move.start(origin, r.source_grad.at[me]))
                else:
                    target = order[stage] // share + number
                    sent.append(links.start_to("seq", target, origin, r.source_grad.at[me]))
            if stage == 0:
                exchange.end("enc", "pairs")
                send_total("enc", r.enc_own, r.enc_mine, r.enc_total)
                exchange.start("pairs", "dp", lambda peer: r.pair_row, r.pair_total)

        sums.wait()
        r.enc_sum[...] = sum_parts(r.enc_parts_v).astype(LOW)
        exchange.start("enc", "seq", lambda peer: r.enc_sum.at[peer], r.enc_own)
        for copy in firsts:
            copy.wait()
        attend_back(
            SimpleNamespace(
                q=r.qkv_v, k=r.qkv_v, v=r.qkv_v, q0=0, k0=width, v0=2 * width,
                q_marks=marks, k_marks=marks, pairs=r.enc_pairs, context=r.context_v, lse=r.lse_v,
                d_context=r.d_context_v, d_pairs=r.enc_d_pairs, factor=1.0 / copies, qx=r.qx, kx=r.kx,
                dx=r.dx, vx=r.vx, delta=r.delta, dq_sum=r.dq_sum, dk_sum=r.dk_sum, dv_sum=r.dv_sum,
                chances=r.chances, changes=r.changes,
            ),
            False,
            count,
            ready,
            staged,
        )
        exchange.end("pairs")
        for number, (layer, row, column) in enumerate(grains):
            r.whole[layer, row : row + 8, column : column + 128] = r.pair_total[grain_place(number)]
        for number, layer in enumerate(layers):
            prefix_back(
                SimpleNamespace(
                    d_pairs=r.whole[number], group=group, place=me,
                    hidden=getattr(r, f"{layer}_hidden"), prefix=getattr(r, f"{layer}_prefix"),
                    second=getattr(r, f"{layer}_second"), first_share=getattr(r, f"{layer}_first"),
                    tall_hidden=r.tall_hidden, tall_prefix=r.tall_prefix, wide_prefix=r.wide_prefix,
                    embed_grad=getattr(r, f"{layer}_embed"), in_grad=getattr(r, f"{layer}_in"),
                    out_grad=getattr(r, f"{layer}_out_grad"),
                )
            )
            exchange.end(layer)
            total = getattr(r, f"{layer}_total")
            total = jnp.concatenate([total[place].astype(WIDE) for place in range(replicas)], 0)
            for kind, first in (("down", 0), ("up", second)):
                out = getattr(r, f"{layer}_{kind}_grad_all")
                out[...] = unpack(total, first, out.shape)
        for copy in sent:
            copy.wait()

    near_outs = {}
    for layer in layers:
        near_outs[f"{layer}_embed"] = ((count, width // group), WIDE)
        near_outs[f"{layer}_in"] = ((width // group, units), WIDE)
        near_outs[f"{layer}_out_grad"] = ((units // group, 2 * width), WIDE)
        near_outs[f"{layer}_down_grad_all"] = ((width // group, narrow), WIDE)
        near_outs[f"{layer}_up_grad_all"] = ((narrow // group, width), WIDE)
    scratch = {}
    scratch["enc_parts_v"] = ((replicas, *part), LOW)
    scratch["enc_sum"] = scratch["enc_own"] = scratch["dec_own_v"] = (part, LOW)
    for layer in layers:
        scratch[f"{layer}_mine"] = (part[1:], LOW)
        scratch[f"{layer}_total"] = ((replicas, *part[1:]), LOW)
        scratch[f"{layer}_second"] = ((units, 2 * width), LOW)
        scratch[f"{layer}_first"] = ((width // group, units), LOW)
    own = (group, 8 * depth, 128)
    for name in ("pair_out", "pair_parts", "pair_total"):
        scratch[name] = ((replicas, *own), WIDE)
    for name in ("pair_sum", "pair_own", "pair_row"):
        scratch[name] = (own, WIDE)
    scratch["pair_mine"] = (own[1:], WIDE)
    scratch["whole"] = ((2, PAD, 2 * width), WIDE)
    scratch["enc_d_pairs"] = ((PAD, 2 * width), WIDE)
    scratch["tall_hidden"] = ((units, PAD), WIDE)
    scratch["wide_prefix"] = ((PAD, width), WIDE)
    scratch["tall_prefix"] = ((width, PAD), WIDE)
    for name in ("dq_sum", "dk_sum", "dv_sum"):
        scratch[name] = ((width, tokens), WIDE)
    return run_kernel(
        body,
        "encoder_attend_back",
        near=dict(
            marks=w.source_segments, enc_pairs=forward.enc_pairs, lse=forward.lse,
            dec_d_pairs=dec.d_pairs, enc_hidden=forward.enc_hidden, dec_hidden=forward.dec_hidden,
            enc_prefix=w.enc_prefix, dec_prefix=w.dec_prefix,
        ),
        far=dict(
            qkv=forward.qkv, d_context=feed.d_context, context=forward.context,
            enc_qkv=w.enc_qkv, summed_grad=feed.summed_grad,
            enc_parts=feed.parts, dec_own=dec.flat_own,
            enc_prefix_in=w.enc_prefix_in, enc_prefix_out=w.enc_prefix_out,
            dec_prefix_in=w.dec_prefix_in, dec_prefix_out=w.dec_prefix_out,
        ),
        near_outs=near_outs,
        far_outs=dict(source_grad=((group, share, width), LOW)),
        scratch=dict(
            qkv_v=((3 * width, tokens), LOW), d_context_v=((width, tokens), LOW),
            context_v=((width, tokens), LOW), qkv_weight=((width, 3 * width), LOW),
            summed_v=((tokens, width), LOW), d_qkv=((3 * width, tile), LOW), lse_v=((16, tokens), WIDE),
            qx=((heads * 16, tokens), LOW), kx=((16, tokens), LOW),
            dx=((heads * 16, tokens), LOW), vx=((16, tokens), LOW), delta=((16, tokens), WIDE),
            chances=((2, 7, TILE, TILE), LOW), changes=((2, 7, TILE, TILE), LOW), **scratch,
        ),
        flops=2 * tokens * width * 2304 + 20 * tokens * tokens * width,
        links=3 * (group - 1) + 4 * (replicas - 1) + group - 1,
        collective=2,
    )


def finish(attended, feed, dec, copies):
    small = [name for name in vars(attended) if name != "source_grad"]
    shape = attended.source_grad.shape
    later = dec.out_all.shape

    def body(r):
        move = Mover(r.semaphores)
        ins = [
            move.start(r.source_grad, r.source_v),
            move.start(r.target_grad, r.target_v),
        ]
        outs = []
        relays = [
            (move.start(r.out_all.at[place * copies], r.out_v.at[place]), r.out_v.at[place], r.out.at[place])
            for place in range(later[0] // copies)
        ]
        for name in small:
            via = getattr(r, name + "_v")
            relays.append((move.start(getattr(r, name + "_in"), via), via, getattr(r, name)))
        for copy, via, goal in relays:
            copy.wait()
            outs.append(move.start(via, goal))
        for copy, origin, wide, goal in (
            (ins[0], r.source_v, r.source_w, r.source_out), (ins[1], r.target_v, r.target_w, r.target_out)
        ):
            copy.wait()
            for place in range(wide.shape[0]):
                wide[place] = origin[place * copies].astype(WIDE)
                outs.append(move.start(wide.at[place], goal.at[place]))
        for copy in outs:
            copy.wait()

    rows = shape[0] // copies
    return run_kernel(
        body,
        "finish",
        near={},
        far=dict(
            source_grad=attended.source_grad, target_grad=feed.target_grad_all, out_all=dec.out_all,
            **{name + "_in": getattr(attended, name) for name in small},
        ),
        near_outs={},
        far_outs=dict(
            out=((rows, *later[1:]), LOW), source_out=((rows, *shape[1:]), WIDE),
            target_out=((rows, *later[1:]), WIDE),
            **{name: (getattr(attended, name).shape, WIDE) for name in small},
        ),
        scratch=dict(
            source_v=(shape, LOW), source_w=((rows, *shape[1:]), WIDE), target_v=(later, LOW),
            target_w=((rows, *later[1:]), WIDE), out_v=((rows, *later[1:]), LOW),
            **{name + "_v": (getattr(attended, name).shape, WIDE) for name in small},
        ),
        flops=0,
    )


NAMES = (
    "source",
    "target",
    "source_segments",
    "target_segments",
    "cotangent",
    "enc_qkv",
    "enc_out",
    "enc_up",
    "enc_down",
    "dec_qkv",
    "dec_out",
    "cross_q",
    "cross_kv",
    "cross_out",
    "dec_up",
    "dec_down",
    "enc_prefix",
    "enc_prefix_in",
    "enc_prefix_out",
    "enc_adapter_down",
    "enc_adapter_up",
    "dec_prefix",
    "dec_prefix_in",
    "dec_prefix_out",
    "dec_adapter_down",
    "dec_adapter_up",
)


def shards(*operands, group, replicas):
    w = SimpleNamespace(**dict(zip(NAMES, operands)))
    copies = group // w.source.shape[0]
    forward = encoder_forward(w, group, copies)
    dec = decoder(forward, w, group, copies, replicas)
    feed = encoder_feed_back(dec, forward, w, group, copies, replicas)
    attended = encoder_attend_back(feed, dec, forward, w, group, copies, replicas)
    done = finish(attended, feed, dec, copies)
    results = [done.out, done.source_out, done.target_out]
    for layer in ("enc", "dec"):
        for name in ("embed", "in", "out_grad", "down_grad_all", "up_grad_all"):
            results.append(getattr(done, f"{layer}_{name}"))
    return tuple(results)


def solution(mesh):
    rows = P("dp", "seq", None)
    marks = P("dp", None)
    in_specs = (rows, rows, marks, marks, rows) + (P(),) * 21
    across, down = P(None, "seq"), P("seq", None)
    layer = (across, down, down, down, down)
    return jax.shard_map(
        functools.partial(shards, group=mesh.shape["seq"], replicas=mesh.shape["dp"]),
        mesh=mesh,
        in_specs=in_specs,
        out_specs=(rows, rows, rows) + layer + layer,
        check_vma=False,
    )
```

```python
import functools
import math
from types import SimpleNamespace

import jax
import jax.numpy as jnp
from jax import lax
from jax.experimental import pallas as pl
from jax.experimental.pallas import tpu as pltpu
from jax.sharding import PartitionSpec as P

HEAD = 64
GROUP = 4
PAD = 32
BIG = 2.0**100
LOG2E = math.log2(math.e)
SCALE = 1.0 / math.sqrt(HEAD)
VMEM_BYTES = 60 * 2**20
CHUNK = 256
TILE = 256
COLUMNS = 512
INNER = 512
LOW = jnp.bfloat16
WIDE = jnp.float32


def contract(left, right, left_dim, right_dim):
    return lax.dot_general(
        left, right, (((left_dim,), (right_dim,)), ((), ())), preferred_element_type=WIDE
    )


def rows_at(index, size, base=0):
    return pl.ds(pl.multiple_of(base + index * size, size), size)


def chunks(size, step):
    step = min(step, size)
    return [slice(start, start + step) for start in range(0, size, step)]


def total_of(values):
    return functools.reduce(lambda left, right: left + right, values)


def normalize(value):
    centered = value - jnp.mean(value, axis=-1, keepdims=True)
    inverse = lax.rsqrt(jnp.mean(centered * centered, axis=-1, keepdims=True) + 1e-05)
    return (centered * inverse, inverse)


def normalize_back(gradient, normed, inverse):
    return (
        gradient
        - jnp.mean(gradient, axis=-1, keepdims=True)
        - normed * jnp.mean(gradient * normed, axis=-1, keepdims=True)
    ) * inverse


def gelu_both(value):
    scale = math.sqrt(2.0 / math.pi)
    square = value * value
    half = 0.5 + 0.5 * jnp.tanh(value * (scale + (scale * 0.044715) * square))
    active = value * half
    slope = half + active * (1.0 - half) * (2.0 * scale + (6.0 * scale * 0.044715) * square)
    return (active, slope)


class Mover:
    def __init__(self, semaphores):
        self.semaphores = semaphores
        self.used = 0

    def start(self, origin, goal):
        copy = pltpu.make_async_copy(origin, goal, self.semaphores.at[self.used])
        self.used += 1
        copy.start()
        return copy


def run_kernel(body, name, near, far, near_outs, far_outs, scratch, flops, links=0, collective=None):
    in_names = list(near) + list(far)
    out_names = list(near_outs) + list(far_outs)
    names = in_names + out_names + list(scratch) + ["semaphores"]
    link_scratch = []
    remote = {}
    if collective is not None:
        names += ["sent", "arrived"]
        link_scratch = [pltpu.SemaphoreType.DMA((links,)), pltpu.SemaphoreType.DMA((links,))]
        remote = dict(collective_id=collective, has_side_effects=True)

    def kernel(*refs):
        body(SimpleNamespace(**dict(zip(names, refs))))

    near_spec = pl.BlockSpec(memory_space=pltpu.VMEM)
    far_spec = pl.BlockSpec(memory_space=pl.ANY)
    results = pl.pallas_call(
        kernel,
        out_shape=tuple(
            jax.ShapeDtypeStruct(*out) for out in (*near_outs.values(), *far_outs.values())
        ),
        in_specs=[near_spec] * len(near) + [far_spec] * len(far),
        out_specs=tuple([near_spec] * len(near_outs) + [far_spec] * len(far_outs)),
        scratch_shapes=[pltpu.VMEM(*shape) for shape in scratch.values()]
        + [pltpu.SemaphoreType.DMA((80,))]
        + link_scratch,
        compiler_params=pltpu.CompilerParams(vmem_limit_bytes=VMEM_BYTES, **remote),
        cost_estimate=pl.CostEstimate(flops=flops, bytes_accessed=2**24, transcendentals=0),
        name=name,
    )(*near.values(), *far.values())
    return SimpleNamespace(**dict(zip(out_names, results)))


class Links:
    def __init__(self, sent, arrived, groups):
        self.sent, self.arrived = sent, arrived
        self.used = 0
        self.place = {axis: lax.axis_index(axis) for axis in ("dp", "seq")}
        self.sizes = groups
        barrier = pltpu.get_barrier_semaphore()
        peers = 0
        for axis, size in groups.items():
            for shift in range(1, size):
                pl.semaphore_signal(
                    barrier, inc=1, device_id=self.device(axis, shift), device_id_type=pl.DeviceIdType.MESH
                )
                peers += 1
        pl.semaphore_wait(barrier, peers)

    def peer(self, axis, shift):
        return lax.rem(self.place[axis] + shift, self.sizes[axis])

    def device(self, axis, shift):
        return self.device_at(axis, self.peer(axis, shift))

    def device_at(self, axis, index):
        return (index, self.place["seq"]) if axis == "dp" else (self.place["dp"], index)

    def start(self, axis, shift, origin, goal):
        return self.start_to(axis, self.peer(axis, shift), origin, goal)

    def start_to(self, axis, index, origin, goal):
        copy = self.plan(axis, index, origin, goal)
        copy.start()
        return copy

    def plan(self, axis, index, origin, goal):
        copy = pltpu.make_async_remote_copy(
            src_ref=origin,
            dst_ref=goal,
            send_sem=self.sent.at[self.used],
            recv_sem=self.arrived.at[self.used],
            device_id=self.device_at(axis, index),
            device_id_type=pl.DeviceIdType.MESH,
        )
        self.used += 1
        return copy

    def scatter(self, axis, pick, goal):
        return [
            self.start(axis, shift, pick(self.peer(axis, shift)), goal)
            for shift in range(1, self.sizes[axis])
        ]


class Exchange:
    def __init__(self, move, links):
        self.move, self.links = move, links
        self.place, self.sizes = links.place, links.sizes
        self.open = {}

    def start(self, name, axis, pick, goal, via=None):
        mine = self.place[axis]
        copies = self.links.scatter(axis, pick, goal.at[mine])
        if via is None:
            copies.append(self.move.start(pick(mine), goal.at[mine]))
        else:
            self.move.start(pick(mine), via).wait()
            copies.append(self.move.start(via, goal.at[mine]))
        self.open[name] = copies

    def end(self, *names):
        for name in names:
            for copy in self.open.pop(name):
                copy.wait()


def sum_parts(parts):
    return total_of([parts[part].astype(WIDE) for part in range(parts.shape[0])])


def rows_for(ref, count):
    size = ref.shape[0] // count
    return lambda place: ref.at[pl.ds(pl.multiple_of(place * size, size), size), :]


def split_three(value):
    high = value.astype(LOW).astype(WIDE)
    rest = value - high
    middle = rest.astype(LOW).astype(WIDE)
    return (high, middle, rest - middle)


def place_rows(parts, first, shape):
    row = lax.broadcasted_iota(jnp.int32, shape, 0)
    out = jnp.zeros(shape, WIDE)
    for offset, part in enumerate(parts):
        out = jnp.where(row == first + offset, part, out)
    return out


def document_rows(segments, tokens, is_key):
    row = lax.broadcasted_iota(jnp.int32, (16, tokens), 0)
    same = row == segments
    if is_key:
        return jnp.where(row < 4, jnp.where(same, 0.0, -BIG), 0.0)
    return jnp.where(same & (row < 4), 1.0, 0.0)


def column_peak(scores, peak):
    for start in range(0, scores.shape[0], 8):
        peak = jnp.maximum(peak, scores[start : start + 8])
    return peak


def from_column(value, low):
    if low == 0:
        return value
    return jnp.concatenate([jnp.zeros((value.shape[0], low), value.dtype), value], 1)


def attend(a, causal, prefix):
    queries, keys = a.q.shape[1], a.k.shape[1]
    width = a.context.shape[0]
    heads = width // HEAD
    tile = min(256, keys)
    tiles = keys // tile
    a.qx[:16, :queries] = document_rows(a.q_marks, queries, False).astype(LOW)
    a.kx[:, :keys] = document_rows(a.k_marks, keys, True).astype(LOW)
    columns = chunks(queries, COLUMNS)

    def front(head, slot, own, work):
        start = own.start
        query = jnp.concatenate([a.q[rows_at(head, HEAD, a.q0), own], a.qx[:16, own]], 0)
        peak = jnp.full((8, own.stop - start), -4.0 * BIG, WIDE)
        if prefix:
            scores = contract(a.pair_keys[rows_at(head, HEAD), :], query[:HEAD], 0, 0)
            row = lax.broadcasted_iota(jnp.int32, scores.shape, 0)
            scores = jnp.where(row < prefix, scores, -BIG)
            a.pair_scores[slot, :, own] = scores
            peak = column_peak(scores, peak)
        for part in range(tiles):
            if not (causal and part * tile >= own.stop):
                cut = slice(part * tile, (part + 1) * tile)
                key = jnp.concatenate([a.k[rows_at(head, HEAD, a.k0), cut], a.kx[:, cut]], 0)
                scores = contract(key, query, 0, 0)
                if causal and cut.stop > start:
                    place = lax.broadcasted_iota(jnp.int32, scores.shape, 0) + (cut.start - start)
                    scores = jnp.where(
                        place <= lax.broadcasted_iota(jnp.int32, scores.shape, 1), scores, -BIG
                    )
                a.scores[slot, cut, own] = scores
                peak = column_peak(scores, peak)
            work(part)
        a.peak[slot, :, own] = peak

    def step(head, following, slot):
        for own in columns:
            peak = jnp.max(a.peak[slot, :, own], 0, keepdims=True)
            context = []
            if prefix:
                weights = jnp.exp2(a.pair_scores[slot, :, own] - peak).astype(LOW)
                value = jnp.concatenate(
                    [a.pair_values[rows_at(head, HEAD), :], jnp.ones((16, PAD), LOW)], 0
                )
                context.append(contract(value, weights, 1, 0))

            def work(part):
                if causal and part * tile >= own.stop:
                    return
                cut = slice(part * tile, (part + 1) * tile)
                weights = jnp.exp2(a.scores[slot, cut, own] - peak).astype(LOW)
                value = jnp.concatenate(
                    [a.v[rows_at(head, HEAD, a.v0), cut], jnp.ones((16, tile), LOW)], 0
                )
                context.append(contract(value, weights, 1, 0))

            front(following, 1 - slot, own, work)
            summed = total_of(context)
            total = summed[HEAD : HEAD + 1]
            a.context[rows_at(head, HEAD), own] = (summed[:HEAD] * (1.0 / total)).astype(LOW)
            a.lse[pl.ds(head, 1), own] = peak + jnp.log2(total)

    for own in columns:
        front(0, 0, own, lambda part: None)

    def pair(index, carry):
        step(2 * index, 2 * index + 1, 0)
        step(2 * index + 1, jnp.minimum(2 * index + 2, heads - 1), 1)
        return carry

    lax.fori_loop(0, heads // 2, pair, 0)


def block_diagonal(pairs, group, first):
    wide = GROUP * HEAD
    rows = pairs[:, first + group * wide : first + (group + 1) * wide]
    column = lax.broadcasted_iota(jnp.int32, rows.shape, 1)
    parts = [
        jnp.where((column >= member * HEAD) & (column < (member + 1) * HEAD), rows.astype(WIDE), 0.0)
        for member in range(GROUP)
    ]
    return jnp.concatenate(parts, 0).astype(LOW)


def own_columns(grads):
    column = lax.broadcasted_iota(jnp.int32, (PAD, GROUP * HEAD), 1)
    out = jnp.zeros((PAD, GROUP * HEAD), WIDE)
    for member in range(GROUP):
        own = (column >= member * HEAD) & (column < (member + 1) * HEAD)
        out = jnp.where(own, grads[member * PAD : (member + 1) * PAD], out)
    return out


def attend_back(a, causal, prefix, ready=None, staged=None):
    queries, keys = a.q.shape[1], a.k.shape[1]
    width = a.context.shape[0]
    heads = width // HEAD
    tiles = keys // TILE
    row = lax.broadcasted_iota(jnp.int32, (16, keys), 0)
    a.kx[:, :keys] = jnp.where(
        (row >= 4) & (row < 7), 1.0, document_rows(a.k_marks, keys, True)
    ).astype(LOW)
    a.vx[:, :keys] = jnp.where(row < 3, 1.0, 0.0).astype(LOW)
    documents = document_rows(a.q_marks, queries, False)

    def prepare(head, carry):
        rows = rows_at(head, HEAD)
        delta = jnp.sum(
            a.d_context[rows, :].astype(WIDE) * a.context[rows, :].astype(WIDE),
            axis=0,
            keepdims=True,
        )
        a.delta[pl.ds(head, 1), :queries] = delta
        a.dx[rows_at(head, 16), :queries] = place_rows(
            split_three(-delta), 0, (16, queries)
        ).astype(LOW)
        minus = split_three(-a.lse[pl.ds(head, 1), :])
        a.qx[rows_at(head, 16), :queries] = (
            documents + place_rows(minus, 4, (16, queries))
        ).astype(LOW)
        return carry

    lax.fori_loop(0, heads, prepare, 0)

    if prefix:
        for group in range(heads // GROUP):
            start = group * GROUP * HEAD
            own = slice(start, start + GROUP * HEAD)
            query = a.q[a.q0 + start : a.q0 + start + GROUP * HEAD, :]
            grad = a.d_context[own, :]
            pair_keys = block_diagonal(a.pairs[...], group, 0)
            pair_values = block_diagonal(a.pairs[...], group, width)
            scores = contract(pair_keys, query, 1, 0)
            gains = contract(pair_values, grad, 1, 0)
            chances, changes = [], []
            for member in range(GROUP):
                head = group * GROUP + member
                part = slice(member * PAD, (member + 1) * PAD)
                chance = jnp.exp2(scores[part] - a.lse[head : head + 1, :])
                place = lax.broadcasted_iota(jnp.int32, chance.shape, 0)
                chance = jnp.where(place < prefix, chance, 0.0)
                chances.append(chance)
                changes.append(chance * (gains[part] - a.delta[head : head + 1, :queries]))
            chances = jnp.concatenate(chances, 0).astype(LOW)
            changes = jnp.concatenate(changes, 0).astype(LOW)
            a.dq_sum[own, :queries] = contract(pair_keys, changes, 0, 0)
            a.d_pairs[:, own] = own_columns(contract(changes, query, 1, 1)) * (a.factor / LOG2E)
            a.d_pairs[:, width + start : width + start + GROUP * HEAD] = (
                own_columns(contract(chances, grad, 1, 1)) * a.factor
            )
    else:
        a.dq_sum[:, :queries] = jnp.zeros((width, queries), WIDE)
    if ready is not None:
        ready(0)


    def span(part):
        return slice(part * TILE, (part + 1) * TILE)

    def place_of(number, kind):
        return span(2 * number + kind)

    def front(head, own, cut, slot, number):
        query = jnp.concatenate([a.q[rows_at(head, HEAD, a.q0), own], a.qx[rows_at(head, 16), own]], 0)
        key = jnp.concatenate([a.k[rows_at(head, HEAD, a.k0), cut], a.kx[:, cut]], 0)
        scores = contract(query, key, 0, 0)
        if causal and own == cut:
            place = lax.broadcasted_iota(jnp.int32, scores.shape, 1)
            scores = jnp.where(place <= lax.broadcasted_iota(jnp.int32, scores.shape, 0), scores, -BIG)
        grad = jnp.concatenate([a.d_context[rows_at(head, HEAD), own], a.dx[rows_at(head, 16), own]], 0)
        value = jnp.concatenate([a.v[rows_at(head, HEAD, a.v0), cut], a.vx[:, cut]], 0)
        gains = contract(grad, value, 0, 0)
        chance = jnp.exp2(scores)
        a.work[slot, :, place_of(number, 0)] = chance.astype(LOW)
        a.work[slot, :, place_of(number, 1)] = (chance * gains).astype(LOW)

    def run(pieces, together, add):
        unit = [(offset, own, cut) for offset in range(together) for own, cut in pieces]

        def begin(index, slot, number):
            offset, own, cut = unit[number]
            front(index * together + offset, own, cut, slot, number)

        def mix(index, slot, following):
            by_key, by_query = {}, {}
            for number, (offset, own, cut) in enumerate(unit):
                head = index * together + offset
                rows = rows_at(head, HEAD)
                left = unit[number + 1 :]
                chances = a.work[slot, :, place_of(number, 0)]
                changes = a.work[slot, :, place_of(number, 1)]
                pair = by_key.setdefault((offset, cut.start), [])
                d_value = contract(a.d_context[rows, own], chances, 1, 0)
                pair.append((contract(a.q[rows_at(head, HEAD, a.q0), own], changes, 1, 0), d_value))
                begin(following, 1 - slot, number)
                d_query = by_query.setdefault((offset, own.start), [])
                d_query.append(contract(a.k[rows_at(head, HEAD, a.k0), cut], changes, 1, 1))
                if not any((other, keys_.start) == (offset, cut.start) for other, _, keys_ in left):
                    add(head, cut, *(total_of(parts) for parts in zip(*pair)))
                if not any((other, queries_.start) == (offset, own.start) for other, queries_, _ in left):
                    a.dq_sum[rows, own] += total_of(d_query)

        def two(index, carry):
            mix(2 * index, 0, 2 * index + 1)
            mix(2 * index + 1, 1, jnp.minimum(2 * index + 2, count - 1))
            return carry

        count = heads // together
        for number in range(len(unit)):
            begin(0, 0, number)
        return two, count // 2

    if staged is not None:
        for stage in range(tiles):
            pieces = [(span(other), span(stage)) for other in range(stage + 1, tiles)]
            pieces += [(span(stage), span(other)) for other in range(stage, tiles)]

            def add(head, cut, d_key, d_value):
                rows = rows_at(head, HEAD)
                if stage == 0:
                    a.dk_sum[rows, cut] = d_key
                    a.dv_sum[rows, cut] = d_value
                else:
                    a.dk_sum[rows, cut] += d_key
                    a.dv_sum[rows, cut] += d_value

            step, steps = run(pieces, {1: heads // 2, 3: 2}.get(len(pieces), 1), add)
            cuts = [0, steps // 3, 2 * steps // 3, steps] if stage == 0 else [0, steps]
            for number in range(len(cuts) - 1):
                lax.fori_loop(cuts[number], cuts[number + 1], step, 0)
                if number + 2 < len(cuts):
                    ready(number + 1)
            staged(stage, span(stage))
        return

    def add(head, cut, d_key, d_value):
        a.dk[rows_at(head, HEAD, a.dk0), cut] = (d_key * (1.0 / LOG2E)).astype(LOW)
        a.dv[rows_at(head, HEAD, a.dv0), cut] = d_value.astype(LOW)

    pieces = [
        (span(own), span(part))
        for part in range(tiles)
        for own in range(part if causal else 0, queries // TILE)
    ]
    step, steps = run(pieces, 2 if len(pieces) < 4 else 1, add)
    lax.fori_loop(0, steps, step, 0)
    a.dq[rows_at(0, width, a.dq0), :] = (a.dq_sum[:, :queries] * SCALE).astype(LOW)


def project_wide(out, weight, rows, scaled, place=slice(None)):
    for cut in chunks(weight.shape[1], 256):
        result = contract(weight[:, cut], rows, 0, 1)
        if cut.start < scaled:
            result = result * (SCALE * LOG2E)
        out[cut, place] = result.astype(LOW)


def add_and_normalize(hidden, context, weight, normed, inverse):
    for cut in chunks(hidden.shape[0], CHUNK):
        summed = hidden[cut, :].astype(WIDE) + contract(context[:, cut], weight[...], 0, 0)
        result, scale = normalize(summed)
        normed[cut, :] = result.astype(LOW)
        inverse[cut, :] = scale


def chunk_pipeline(tokens, make, use, steps, uses):
    count = tokens // CHUNK

    def rows_of(index):
        return rows_at(index, CHUNK)

    def body(index, slot, following):
        done = 0
        for step in range(steps):
            if following is not None:
                make(rows_of(following), 1 - slot, step)
            while done < uses and done * steps <= step * uses:
                use(rows_of(index), slot, done)
                done += 1
        while done < uses:
            use(rows_of(index), slot, done)
            done += 1

    def two(index, carry):
        body(2 * index, 0, 2 * index + 1)
        body(2 * index + 1, 1, 2 * index + 2)
        return carry

    for step in range(steps):
        make(rows_of(0), 0, step)
    if count > 2:
        lax.fori_loop(0, count // 2 - 1, two, 0)
    body(count - 2, 0, count - 1)
    body(count - 1, 1, None)


def feed_forward(hidden, up, down, adapter_down, adapter_up, total, slopes_of, active_of, narrow):
    inner = up.shape[1]
    count = inner // INNER

    def make(rows, slot, step):
        if step < count:
            cut = slice(step * INNER, (step + 1) * INNER)
            active, slope = gelu_both(contract(hidden[rows, :], up[:, cut], 1, 0))
            slopes_of(step + 1)[rows, :] = slope.astype(LOW)
        else:
            cut = slice(inner, inner + INNER)
            active, slope = gelu_both(contract(hidden[rows, :], adapter_down[...], 1, 0))
            slopes_of(0)[rows, :] = slope.astype(LOW)
            narrow[rows, :] = active.astype(LOW)
            active = 4.0 * active
        active_of(slot)[:, cut] = active.astype(LOW)

    def use(rows, slot, number):
        active = active_of(slot)
        total[rows, :] = (
            hidden[rows, :].astype(WIDE)
            + contract(active[:, :inner], down[...], 1, 0)
            + contract(active[:, inner : inner + INNER], adapter_up[...], 1, 0)
        )

    chunk_pipeline(hidden.shape[0], make, use, count + 1, 1)


def finish_forward(total, normed, inverse):
    for cut in chunks(total.shape[0], CHUNK):
        result, scale = normalize(total[cut, :])
        normed[cut, :] = result.astype(LOW)
        inverse[cut, :] = scale


def pack(flat, value, first):
    size = value.shape[0] // flat.shape[0]
    for place in range(flat.shape[0]):
        for block in range(value.shape[1] // 128):
            goal = slice(first + block * size, first + (block + 1) * size)
            flat[place, goal, :] = value[
                place * size : (place + 1) * size, block * 128 : (block + 1) * 128
            ].astype(flat.dtype)


def unpack(rows, first, shape):
    parts = [
        rows[first + block * shape[0] : first + (block + 1) * shape[0]] for block in range(shape[1] // 128)
    ]
    return jnp.concatenate(parts, 1)


def flat_shapes(width, narrow, group, replicas):
    second = width // group * (narrow // 128)
    rows = second + narrow // group * (width // 128)
    return second, (group, rows, 128), (group, rows // replicas, 128)


def columns_for(flat, replicas):
    size = flat.shape[1] // replicas
    return lambda place: flat.at[:, pl.ds(pl.multiple_of(place * size, size), size), :]


def feed_back(f, send=None):
    tokens = f.hidden.shape[0]
    cuts = chunks(tokens, CHUNK)
    for cut in cuts:
        value = f.grad[cut, :]
        f.low[cut, :] = value.astype(LOW)
        f.side[cut, :] = (4.0 * value).astype(LOW)

    for cut in cuts:
        change = contract(f.side[cut, :], f.adapter_up[...], 1, 1) * f.slopes(0)[cut, :].astype(WIDE)
        f.d_narrow[cut, :] = change.astype(LOW)
    pack(f.flat, contract(f.hidden[...], f.d_narrow[...], 0, 0) * f.factor, 0)
    pack(f.flat, contract(f.narrow[...], f.side[...], 0, 0) * f.factor, f.second)
    if send is not None:
        send()

    def make(rows, slot, step):
        cut = slice(step * INNER, (step + 1) * INNER)
        change = contract(f.low[rows, :], f.down[cut, :], 1, 1) * f.slopes(step + 1)[rows, :].astype(WIDE)
        f.active(slot)[:, cut] = change.astype(LOW)

    def use(rows, slot, number):
        f.grad[rows, :] += contract(f.active(slot)[:, : f.up.shape[1]], f.up[...], 1, 1) + contract(
            f.d_narrow[rows, :], f.adapter_down[...], 1, 1
        )

    chunk_pipeline(tokens, make, use, f.up.shape[1] // INNER, 1)


def normalize_back_all(grad, normed, inverse, out):
    for cut in chunks(grad.shape[0], CHUNK):
        out[cut, :] = normalize_back(
            grad[cut, :].astype(WIDE), normed[cut, :].astype(WIDE), inverse[cut, :]
        ).astype(out.dtype)


def context_back(out, weight, grad):
    value = grad[...].astype(LOW)
    for cut in chunks(weight.shape[0], 256):
        out[cut, :] = contract(weight[cut, :], value, 1, 1).astype(LOW)


def prefix_pairs(prefix, first, second, hidden, pairs, pairs_wide):
    count = prefix.shape[0]
    hidden[...] = jnp.zeros(hidden.shape, WIDE)
    hidden[:count, :] = jnp.tanh(contract(prefix[...], first[...], 1, 0))
    parts = [part.astype(LOW) for part in split_three(hidden[...])]
    pairs[...] = total_of([contract(part, second[...], 1, 0) for part in parts]).astype(LOW)
    pairs_wide[...] = total_of([contract(second[...], part, 0, 1) for part in parts]).astype(LOW)


def encoder_forward(w, group, copies):
    width = w.source.shape[2]
    share, later_share = w.source.shape[1], w.target.shape[1]
    tokens, later_tokens = share * group, later_share * group
    inner = w.enc_up.shape[1]
    narrow = w.enc_adapter_down.shape[1]
    units = w.enc_prefix_in.shape[1]
    count = w.enc_prefix.shape[0]
    blocks = 1 + inner // INNER

    def body(r):
        move = Mover(r.semaphores)
        weights = [move.start(r.enc_qkv, r.qkv_weight)]
        enc_first, dec_first = r.mid_v.at[:width, :units], r.memory_v.at[:width, :units]
        enc_second, dec_second = r.up.at[:units, : 2 * width], r.up.at[:units, 2 * width : 4 * width]
        weights.append(move.start(r.enc_prefix_in, enc_first))
        weights.append(move.start(r.enc_prefix_out, enc_second))
        weights.append(move.start(r.dec_prefix_in, dec_first))
        weights.append(move.start(r.dec_prefix_out, dec_second))
        links = Links(r.sent, r.arrived, {"seq": group})
        me = links.place["seq"]
        row = me // copies

        def tokens_of(place, size):
            return pl.ds(pl.multiple_of(place * size, size), size)

        def bring(origin, goal, size, via=None):
            own = tokens_of(me, size)
            copies_out = links.scatter("seq", lambda peer: origin.at[peer // copies], goal.at[own, :])
            if via is None:
                return (move.start(origin.at[row], goal.at[own, :]), copies_out)
            move.start(origin.at[row], via).wait()
            return (move.start(via, goal.at[own, :]), copies_out)

        here, sources = bring(r.source, r.x, share)
        out_weight = move.start(r.enc_out, r.out_weight)
        adapters = [
            move.start(r.enc_adapter_down, r.a_down),
            move.start(r.enc_adapter_up, r.a_up),
        ]
        pair_weight = move.start(r.cross_kv, r.pair_weight)
        for copy in weights:
            copy.wait()
        prefix_pairs(r.enc_prefix, enc_first, enc_second, r.enc_hidden, r.enc_pairs, r.enc_pairs_wide)
        prefix_pairs(r.dec_prefix, dec_first, dec_second, r.dec_hidden, r.dec_pairs, r.dec_pairs_wide)
        ups = [move.start(r.enc_up, r.up), move.start(r.enc_down, r.down)]
        here.wait()
        if share % 128 == 0:
            place = tokens_of(me, share)
            project_wide(r.qkv_v, r.qkv_weight, r.x[place, :], width, place)
            for shift, copy in enumerate(sources, 1):
                copy.wait()
                place = tokens_of(lax.rem(me + group - shift, group), share)
                project_wide(r.qkv_v, r.qkv_weight, r.x[place, :], width, place)
        else:
            for copy in sources:
                copy.wait()
            project_wide(r.qkv_v, r.qkv_weight, r.x[...], width)
        later = [bring(r.target, r.target_rows, later_share, r.own_target)]
        outs = [move.start(r.qkv_v, r.qkv)]
        marks = r.marks[pl.ds(row, 1), :]
        attend(
            SimpleNamespace(
                q=r.qkv_v, k=r.qkv_v, v=r.qkv_v, q0=0, k0=width, v0=2 * width,
                q_marks=marks, k_marks=marks, pair_keys=r.enc_pairs_wide.at[:width],
                pair_values=r.enc_pairs_wide.at[width:],
                context=r.context_v, lse=r.lse, qx=r.qx, kx=r.kx, scores=r.scores,
                pair_scores=r.pair_scores, peak=r.peak,
            ),
            False,
            count,
        )
        outs.append(move.start(r.context_v, r.context))
        out_weight.wait()
        add_and_normalize(r.x, r.context_v, r.out_weight, r.mid_v, r.mid_inverse)
        outs.append(move.start(r.mid_v, r.mid))
        for copy in adapters + ups:
            copy.wait()
        feed_forward(
            r.mid_v, r.up, r.down, r.a_down, r.a_up, r.total,
            lambda index: r.slopes_v.at[index], lambda slot: r.active.at[slot], r.narrow_v,
        )
        outs.append(move.start(r.slopes_v, r.slopes))
        outs.append(move.start(r.narrow_v, r.narrow))
        finish_forward(r.total, r.memory_v, r.memory_inverse)
        outs.append(move.start(r.memory_v, r.memory))
        pair_weight.wait()
        outs.pop(0).wait()
        memory_pairs = r.qkv_v.at[: 2 * width]
        project_wide(memory_pairs, r.pair_weight, r.memory_v[...], 0)
        outs.append(move.start(memory_pairs, r.memory_pairs))
        for own, remote in later:
            own.wait()
            for copy in remote:
                copy.wait()
        for copy in outs:
            copy.wait()

    return run_kernel(
        body,
        "encoder_forward",
        near=dict(marks=w.source_segments, enc_prefix=w.enc_prefix, dec_prefix=w.dec_prefix),
        far=dict(
            source=w.source, target=w.target, enc_qkv=w.enc_qkv,
            enc_out=w.enc_out, enc_up=w.enc_up, enc_down=w.enc_down,
            enc_adapter_down=w.enc_adapter_down, enc_adapter_up=w.enc_adapter_up,
            cross_kv=w.cross_kv, enc_prefix_in=w.enc_prefix_in, enc_prefix_out=w.enc_prefix_out,
            dec_prefix_in=w.dec_prefix_in, dec_prefix_out=w.dec_prefix_out,
        ),
        near_outs=dict(
            lse=((16, tokens), WIDE), mid_inverse=((tokens, 1), WIDE),
            memory_inverse=((tokens, 1), WIDE),
            enc_hidden=((PAD, units), WIDE), enc_pairs=((PAD, 2 * width), LOW),
            dec_hidden=((PAD, units), WIDE), dec_pairs=((PAD, 2 * width), LOW),
            dec_pairs_wide=((2 * width, PAD), LOW),
        ),
        far_outs=dict(
            qkv=((3 * width, tokens), LOW), context=((width, tokens), LOW), mid=((tokens, width), LOW),
            slopes=((blocks, tokens, INNER), LOW), narrow=((tokens, narrow), LOW),
            memory=((tokens, width), LOW), memory_pairs=((2 * width, tokens), LOW),
            target_rows=((later_tokens, width), LOW),
        ),
        scratch=dict(
            x=((tokens, width), LOW), qkv_weight=((width, 3 * width), LOW),
            own_target=((later_share, width), LOW),
            enc_pairs_wide=((2 * width, PAD), LOW),
            out_weight=((width, width), LOW), a_down=((width, narrow), LOW),
            a_up=((narrow, width), LOW), up=((width, inner), LOW), down=((inner, width), LOW),
            pair_weight=((width, 2 * width), LOW), qkv_v=((3 * width, tokens), LOW),
            context_v=((width, tokens), LOW), mid_v=((tokens, width), LOW),
            slopes_v=((blocks, tokens, INNER), LOW), narrow_v=((tokens, narrow), LOW),
            memory_v=((tokens, width), LOW),
            active=((2, CHUNK, inner + narrow), LOW), total=((tokens, width), WIDE), qx=((16, tokens), LOW), kx=((16, tokens), LOW),
            scores=((2, tokens, tokens), WIDE), pair_scores=((2, PAD, tokens), WIDE),
            peak=((2, 8, tokens), WIDE),
        ),
        flops=2 * tokens * width * 11776 + 4 * tokens * tokens * width,
        links=2 * (group - 1),
        collective=0,
    )


def decoder(forward, w, group, copies, replicas):
    tokens, width = forward.target_rows.shape
    share = tokens // group
    keys = forward.memory_pairs.shape[1]
    count = w.dec_prefix.shape[0]
    second, flat, part = flat_shapes(width, w.dec_adapter_down.shape[1], group, replicas)
    inner = w.dec_up.shape[1]
    narrow = w.dec_adapter_down.shape[1]
    blocks = 1 + inner // INNER
    heads = width // HEAD

    def body(r):
        move = Mover(r.semaphores)
        ins = [move.start(r.target, r.x), move.start(r.dec_qkv, r.qkv_weight)]
        links = Links(r.sent, r.arrived, {"seq": group, "dp": replicas})
        exchange = Exchange(move, links)
        for copy in ins:
            copy.wait()
        out_weight = move.start(r.dec_out, r.out_weight)
        crosses = [
            move.start(r.cross_q, r.query_weight),
            move.start(r.memory_pairs, r.pairs_v),
            move.start(r.cross_out, r.cross_out_weight),
        ]
        adapters = [
            move.start(r.dec_adapter_down, r.a_down),
            move.start(r.dec_adapter_up, r.a_up),
        ]
        ups = [move.start(r.dec_up, r.up), move.start(r.dec_down, r.down)]
        d_qkv = r.slopes.at[: 3 * width, :tokens]

        def slope_of(index):
            return r.slopes.at[rows_at(index, tokens), :]

        me = links.place["seq"]
        size = tokens // group
        mine = r.cotangent_v.at[pl.ds(pl.multiple_of(me * size, size), size), :]
        cotangents = links.scatter("seq", lambda peer: r.cotangent.at[peer // copies], mine)
        cotangents.append(move.start(r.cotangent.at[me // copies], mine))
        project_wide(r.qkv, r.qkv_weight, r.x[...], width)
        row = pl.ds(me // copies, 1)
        marks, source_marks = r.marks[row, :], r.source_marks[row, :]
        shared = dict(
            qx=r.qx, kx=r.kx, scores=r.scores, pair_scores=r.pair_scores, peak=r.peak, dx=r.dx,
            vx=r.vx, delta=r.delta, dq_sum=r.dq_sum, work=r.work,
            d_context=r.d_context,
        )
        self_part = SimpleNamespace(
            q=r.qkv, k=r.qkv, v=r.qkv, q0=0, k0=width, v0=2 * width,
            q_marks=marks, k_marks=marks, pair_keys=r.pairs_wide.at[:width],
            pair_values=r.pairs_wide.at[width:], pairs=r.pairs, context=r.context, lse=r.lse,
            dq=d_qkv, dk=d_qkv, dv=d_qkv, dq0=0, dk0=width, dv0=2 * width,
            d_pairs=r.d_pairs, factor=1.0 / copies, **shared,
        )
        attend(self_part, True, count)
        out_weight.wait()
        add_and_normalize(r.x, r.context, r.out_weight, r.mid, r.mid_inverse)
        for copy in crosses:
            copy.wait()
        project_wide(r.query, r.query_weight, r.mid[...], width)
        cross_part = SimpleNamespace(
            q=r.query, k=r.pairs_v, v=r.pairs_v, q0=0, k0=0, v0=width,
            q_marks=marks, k_marks=source_marks, context=r.cross_context, lse=r.cross_lse,
            dq=r.d_query, dk=r.d_pairs_v, dv=r.d_pairs_v, dq0=0, dk0=0, dv0=width, **shared,
        )
        attend(cross_part, False, 0)
        add_and_normalize(r.mid, r.cross_context, r.cross_out_weight, r.crossed, r.crossed_inverse)
        for copy in adapters + ups + cotangents:
            copy.wait()
        feed_forward(
            r.crossed, r.up, r.down, r.a_down, r.a_up, r.total,
            slope_of, lambda slot: r.work.at[slot], r.narrow,
        )
        finish_forward(r.total, r.out_v, r.out_inverse)
        exchange.start("out", "seq", rows_for(r.out_v, group), r.out_all)
        outs = []
        normalize_back_all(r.cotangent_v, r.out_v, r.out_inverse, r.total)
        feed_back(
            SimpleNamespace(
                grad=r.total, low=r.low, side=r.side, hidden=r.crossed, narrow=r.narrow, up=r.up,
                down=r.down, adapter_down=r.a_down, adapter_up=r.a_up,
                slopes=slope_of, flat=r.flat, second=second,
                d_narrow=r.d_narrow, factor=1.0 / copies, active=lambda slot: r.work.at[slot],
            )
        )
        exchange.start("flat", "dp", columns_for(r.flat, replicas), r.parts)
        normalize_back_all(r.total, r.crossed, r.crossed_inverse, r.total)
        context_back(r.d_context, r.cross_out_weight, r.total)
        attend_back(cross_part, False, 0)
        outs.append(move.start(r.d_pairs_v, r.memory_pairs_grad))
        exchange.end("flat")
        r.flat_sum[...] = sum_parts(r.parts).astype(LOW)
        exchange.start("flat", "seq", lambda peer: r.flat_sum.at[peer], r.flat_own)
        for cut in chunks(tokens, CHUNK):
            r.total[cut, :] += contract(r.d_query[:, cut], r.query_weight[...], 0, 1)
        normalize_back_all(r.total, r.mid, r.mid_inverse, r.total)
        context_back(r.d_context, r.out_weight, r.total)
        attend_back(self_part, True, count)
        for cut in chunks(tokens, CHUNK):
            r.x[cut, :] = (
                r.total[cut, :] + contract(d_qkv[:, cut], r.qkv_weight[...], 0, 1)
            ).astype(LOW)
        outs.append(move.start(r.x, r.target_grad))
        for copy in outs:
            copy.wait()
        exchange.end("out", "flat")

    return run_kernel(
        body,
        "decoder",
        near=dict(
            marks=w.target_segments, source_marks=w.source_segments,
            pairs_wide=forward.dec_pairs_wide, pairs=forward.dec_pairs,
        ),
        far=dict(
            target=forward.target_rows, cotangent=w.cotangent,
            memory_pairs=forward.memory_pairs, dec_qkv=w.dec_qkv,
            dec_out=w.dec_out, cross_q=w.cross_q, cross_out=w.cross_out, dec_up=w.dec_up,
            dec_down=w.dec_down, dec_adapter_down=w.dec_adapter_down,
            dec_adapter_up=w.dec_adapter_up,
        ),
        near_outs=dict(d_pairs=((PAD, 2 * width), WIDE)),
        far_outs=dict(
            out_all=((group, share, width), LOW), target_grad=((tokens, width), LOW),
            memory_pairs_grad=((2 * width, keys), LOW),
            flat_own=(part, LOW),
        ),
        scratch=dict(
            flat=(flat, LOW), parts=((replicas, *part), LOW), flat_sum=(part, LOW),
            x=((tokens, width), LOW), cotangent_v=((tokens, width), LOW),
            qkv_weight=((width, 3 * width), LOW), out_weight=((width, width), LOW),
            query_weight=((width, width), LOW), cross_out_weight=((width, width), LOW),
            pairs_v=((2 * width, keys), LOW), a_down=((width, narrow), LOW),
            a_up=((narrow, width), LOW), up=((width, inner), LOW), down=((inner, width), LOW),
            qkv=((3 * width, tokens), LOW), context=((width, tokens), LOW),
            mid=((tokens, width), LOW), mid_inverse=((tokens, 1), WIDE),
            query=((width, tokens), LOW), cross_context=((width, tokens), LOW),
            crossed=((tokens, width), LOW), crossed_inverse=((tokens, 1), WIDE),
            out_v=((tokens, width), LOW), out_inverse=((tokens, 1), WIDE),
            slopes=((blocks * tokens, INNER), LOW), narrow=((tokens, narrow), LOW),
            low=((tokens, width), LOW), side=((tokens, width), LOW), d_narrow=((tokens, narrow), LOW),
            total=((tokens, width), WIDE), lse=((16, tokens), WIDE), cross_lse=((16, tokens), WIDE),
            d_context=((width, tokens), LOW), d_query=((width, tokens), LOW),
            d_pairs_v=((2 * width, keys), LOW),
            qx=((heads * 16, tokens), LOW), kx=((16, keys), LOW),
            scores=((2, keys, tokens), WIDE), pair_scores=((2, PAD, tokens), WIDE),
            peak=((2, 8, tokens), WIDE), dx=((heads * 16, tokens), LOW), vx=((16, keys), LOW),
            delta=((16, tokens), WIDE), dq_sum=((width, tokens), WIDE),
            work=((2, TILE, 16 * TILE), LOW),
        ),
        flops=4 * tokens * width * 11776 + 14 * tokens * (keys + tokens) * width,
        links=3 * (group - 1) + replicas - 1,
        collective=3,
    )


def encoder_feed_back(dec, forward, w, group, copies, replicas):
    tokens, width = forward.memory.shape
    inner = w.enc_up.shape[1]
    narrow = w.enc_adapter_down.shape[1]
    blocks = 1 + inner // INNER
    second, flat, part = flat_shapes(width, narrow, group, replicas)
    later = dec.target_grad.shape[0] // group

    def body(r):
        move = Mover(r.semaphores)
        firsts = [
            move.start(r.memory_pairs_grad, r.d_pairs),
            move.start(r.cross_kv, r.pair_weight),
            move.start(r.memory, r.memory_v),
        ]
        adapters = [
            move.start(r.enc_adapter_up, r.a_up),
            move.start(r.slopes.at[0], r.slopes_v.at[0]),
            move.start(r.narrow, r.narrow_v),
            move.start(r.mid, r.mid_v),
        ]
        ups = [
            move.start(r.enc_adapter_down, r.a_down),
            move.start(r.slopes.at[1:], r.slopes_v.at[1:]),
            move.start(r.enc_down, r.down),
            move.start(r.enc_up, r.up),
            move.start(r.enc_out, r.out_weight),
        ]
        links = Links(r.sent, r.arrived, {"seq": group, "dp": replicas})
        exchange = Exchange(move, links)
        me, core = links.place["seq"], lax.rem(links.place["dp"], 2)
        targets = [
            links.plan("seq", links.peer("seq", shift), r.target_grad.at[links.peer("seq", shift)], r.target_grad_all.at[me])
            for shift in range(1, group)
        ]

        def send_targets():
            for copy in targets:
                copy.start()

        pl.when(core == 0)(send_targets)
        own_target = move.start(r.target_grad.at[me], r.own_target)
        for copy in firsts:
            copy.wait()
        for cut in chunks(tokens, CHUNK):
            grad = contract(r.d_pairs[:, cut], r.pair_weight[...], 0, 1)
            r.total[cut, :] = normalize_back(
                grad, r.memory_v[cut, :].astype(WIDE), r.memory_inverse[cut, :]
            )
        for copy in adapters:
            copy.wait()

        def send():
            exchange.start("flat", "dp", columns_for(r.flat, replicas), r.parts)
            pl.when(core == 1)(send_targets)
            own_target.wait()
            targets.append(move.start(r.own_target, r.target_grad_all.at[me]))
            for copy in ups:
                copy.wait()

        feed_back(
            SimpleNamespace(
                grad=r.total, low=r.low, side=r.side, hidden=r.mid_v, narrow=r.narrow_v, up=r.up,
                down=r.down, adapter_down=r.a_down, adapter_up=r.a_up,
                slopes=lambda index: r.slopes_v.at[index], flat=r.flat, second=second,
                d_narrow=r.d_narrow, factor=1.0 / copies, active=lambda slot: r.active.at[slot],
            ),
            send,
        )
        normalize_back_all(r.total, r.mid_v, r.mid_inverse, r.low)
        outs = [move.start(r.low, r.summed_grad)]
        context_back(r.d_context_v, r.out_weight, r.low)
        outs.append(move.start(r.d_context_v, r.d_context))
        for copy in outs:
            copy.wait()
        exchange.end("flat")
        for copy in targets:
            copy.wait()

    return run_kernel(
        body,
        "encoder_feed_back",
        near=dict(mid_inverse=forward.mid_inverse, memory_inverse=forward.memory_inverse),
        far=dict(
            target_grad=dec.target_grad.reshape(group, -1, width),
            memory_pairs_grad=dec.memory_pairs_grad, memory=forward.memory, mid=forward.mid,
            slopes=forward.slopes, narrow=forward.narrow, cross_kv=w.cross_kv,
            enc_out=w.enc_out, enc_up=w.enc_up, enc_down=w.enc_down,
            enc_adapter_down=w.enc_adapter_down, enc_adapter_up=w.enc_adapter_up,
        ),
        near_outs={},
        far_outs=dict(
            summed_grad=((tokens, width), LOW), d_context=((width, tokens), LOW),
            parts=((replicas, *part), LOW),
            target_grad_all=((group, later, width), LOW),
        ),
        scratch=dict(
            own_target=((later, width), LOW),
            flat=(flat, LOW), d_pairs=((2 * width, tokens), LOW), pair_weight=((width, 2 * width), LOW),
            memory_v=((tokens, width), LOW), mid_v=((tokens, width), LOW),
            slopes_v=((blocks, tokens, INNER), LOW), narrow_v=((tokens, narrow), LOW),
            out_weight=((width, width), LOW), a_down=((width, narrow), LOW),
            a_up=((narrow, width), LOW), up=((width, inner), LOW), down=((inner, width), LOW),
            low=((tokens, width), LOW), side=((tokens, width), LOW), d_narrow=((tokens, narrow), LOW),
            active=((2, CHUNK, inner), LOW), total=((tokens, width), WIDE), d_context_v=((width, tokens), LOW),
        ),
        flops=2 * tokens * width * 9728,
        links=group - 1 + replicas - 1,
        collective=1,
    )


def split_product(left, right, left_dim, right_dim):
    return total_of(
        [contract(part.astype(LOW), right, left_dim, right_dim) for part in split_three(left)]
    )


def prefix_back(p):
    count, group = p.prefix.shape[0], p.group
    d_pairs, hidden = p.d_pairs, p.hidden[...]
    units, width = hidden.shape[1], p.prefix.shape[1]
    p.tall_hidden[...] = hidden.T
    share = units // group
    own = p.tall_hidden[pl.ds(pl.multiple_of(p.place * share, share), share), :]
    parts = split_three(d_pairs)
    p.out_grad[...] = total_of(
        [split_product(own, part.astype(LOW), 1, 0) for part in parts]
    )
    d_hidden = split_product(d_pairs, p.second[...], 1, 1) * (1.0 - hidden * hidden)
    p.wide_prefix[...] = jnp.zeros(p.wide_prefix.shape, WIDE)
    p.wide_prefix[:count, :] = p.prefix[...].astype(WIDE)
    p.tall_prefix[...] = p.wide_prefix[...].T
    share = width // group
    own = p.tall_prefix[pl.ds(pl.multiple_of(p.place * share, share), share), :].astype(LOW)
    p.in_grad[...] = total_of([contract(own, part.astype(LOW), 1, 0) for part in split_three(d_hidden)])
    p.embed_grad[...] = split_product(d_hidden, p.first_share[...], 1, 1)[:count]


def block_order(place, count):
    if count == 4:
        half, odd = place // 2, lax.rem(place, 2)
        return [1 + 2 * odd - half, 3 - place, 2 + half - 2 * odd, place]
    return [lax.rem(place + step + 1, count) for step in range(count)]


def encoder_attend_back(feed, dec, forward, w, group, copies, replicas):
    tokens, width = feed.summed_grad.shape
    share = tokens // group
    count = w.enc_prefix.shape[0]
    narrow, units = w.enc_adapter_down.shape[1], w.enc_prefix_in.shape[1]
    second, _, part = flat_shapes(width, narrow, group, replicas)
    heads = width // HEAD
    tile = TILE
    blocks, per = tokens // tile, tile // share
    grains = [
        (layer, 8 * row, 128 * column)
        for layer in range(2) for column in range(2 * width // 128) for row in range(PAD // 8)
    ]
    depth = -(-len(grains) // (group * replicas))

    def grain_place(number):
        device, inside = number // depth, number % depth
        return (device // group, device % group, slice(8 * inside, 8 * inside + 8))
    layers = ("enc", "dec")

    def body(r):
        move = Mover(r.semaphores)
        me = lax.axis_index("seq")
        sums = move.start(r.enc_parts, r.enc_parts_v)
        order = [pl.multiple_of(block * tile, tile) for block in block_order(me // per, blocks)]
        firsts, lasts = [], []
        for stage, begin in enumerate(order):
            goal, origin = slice(stage * tile, (stage + 1) * tile), pl.ds(begin, tile)
            firsts.append(move.start(r.qkv.at[:, origin], r.qkv_v.at[:, goal]))
            firsts.append(move.start(r.d_context.at[:, origin], r.d_context_v.at[:, goal]))
            firsts.append(move.start(r.context.at[:, origin], r.context_v.at[:, goal]))
            lasts.append(move.start(r.summed_grad.at[origin, :], r.summed_v.at[goal, :]))
            r.lse_v[:, goal] = r.lse[:, origin]
        totals = move.start(r.dec_own, r.dec_own_v)
        row = pl.ds(me // copies, 1)
        marks = jnp.concatenate([r.marks[row, pl.ds(begin, tile)] for begin in order], 1)
        lasts += [
            move.start(r.enc_qkv, r.qkv_weight),
            move.start(r.enc_prefix_out, r.enc_second), move.start(r.dec_prefix_out, r.dec_second),
        ]
        size = width // group
        first_rows = pl.ds(pl.multiple_of(me * size, size), size)
        lasts.append(move.start(r.enc_prefix_in.at[first_rows, :], r.enc_first))
        lasts.append(move.start(r.dec_prefix_in.at[first_rows, :], r.dec_first))

        links = Links(r.sent, r.arrived, {"seq": group, "dp": replicas})
        exchange = Exchange(move, links)

        def send_total(name, own, mine, total):
            mine[...] = sum_parts(own).astype(LOW)
            exchange.start(name, "dp", lambda peer: mine, total)

        def ready(step):
            if step == 0:
                r.pair_out[...] = jnp.zeros(r.pair_out.shape, WIDE)
                for number, (layer, row, column) in enumerate(grains):
                    origin = (r.enc_d_pairs, r.dec_d_pairs)[layer]
                    r.pair_out[grain_place(number)] = origin[row : row + 8, column : column + 128]
                exchange.start("pairs", "dp", lambda peer: r.pair_out.at[peer], r.pair_parts)
                totals.wait()
                send_total("dec", r.dec_own_v, r.dec_mine, r.dec_total)
            elif step == 1:
                exchange.end("pairs")
                r.pair_sum[...] = sum_parts(r.pair_parts)
                exchange.start("pairs", "seq", lambda peer: r.pair_sum.at[peer], r.pair_own)
            else:
                exchange.end("pairs")
                r.pair_mine[...] = sum_parts(r.pair_own)
                exchange.start("pairs", "seq", lambda peer: r.pair_mine, r.pair_row)

        sent = []

        def staged(stage, cut):
            r.d_qkv[:width, :] = (r.dq_sum[:, cut] * SCALE).astype(LOW)
            r.d_qkv[width : 2 * width, :] = (r.dk_sum[:, cut] * (1.0 / LOG2E)).astype(LOW)
            r.d_qkv[2 * width :, :] = r.dv_sum[:, cut].astype(LOW)
            if stage == 0:
                for copy in lasts:
                    copy.wait()
            r.summed_v[cut, :] = (
                r.summed_v[cut, :].astype(WIDE) + contract(r.d_qkv[...], r.qkv_weight[...], 0, 1)
            ).astype(LOW)
            inside = lax.rem(me, per)
            last = stage == blocks - 1
            for turn in range(per):
                number = lax.rem(inside + turn, per)
                origin = r.summed_v.at[
                    pl.ds(pl.multiple_of(stage * tile + number * share, share), share), :
                ]
                if last and turn == 0:
                    sent.append(move.start(origin, r.source_grad.at[me]))
                else:
                    target = order[stage] // share + number
                    sent.append(links.start_to("seq", target, origin, r.source_grad.at[me]))
            if stage == 0:
                exchange.end("enc", "pairs")
                send_total("enc", r.enc_own, r.enc_mine, r.enc_total)
                exchange.start("pairs", "dp", lambda peer: r.pair_row, r.pair_total)

        sums.wait()
        r.enc_sum[...] = sum_parts(r.enc_parts_v).astype(LOW)
        exchange.start("enc", "seq", lambda peer: r.enc_sum.at[peer], r.enc_own)
        for copy in firsts:
            copy.wait()
        attend_back(
            SimpleNamespace(
                q=r.qkv_v, k=r.qkv_v, v=r.qkv_v, q0=0, k0=width, v0=2 * width,
                q_marks=marks, k_marks=marks, pairs=r.enc_pairs, context=r.context_v, lse=r.lse_v,
                d_context=r.d_context_v, d_pairs=r.enc_d_pairs, factor=1.0 / copies, qx=r.qx, kx=r.kx,
                dx=r.dx, vx=r.vx, delta=r.delta, dq_sum=r.dq_sum, dk_sum=r.dk_sum, dv_sum=r.dv_sum,
                work=r.work,
            ),
            False,
            count,
            ready,
            staged,
        )
        exchange.end("pairs")
        for number, (layer, row, column) in enumerate(grains):
            r.whole[layer, row : row + 8, column : column + 128] = r.pair_total[grain_place(number)]
        for number, layer in enumerate(layers):
            prefix_back(
                SimpleNamespace(
                    d_pairs=r.whole[number], group=group, place=me,
                    hidden=getattr(r, f"{layer}_hidden"), prefix=getattr(r, f"{layer}_prefix"),
                    second=getattr(r, f"{layer}_second"), first_share=getattr(r, f"{layer}_first"),
                    tall_hidden=r.tall_hidden, tall_prefix=r.tall_prefix, wide_prefix=r.wide_prefix,
                    embed_grad=getattr(r, f"{layer}_embed"), in_grad=getattr(r, f"{layer}_in"),
                    out_grad=getattr(r, f"{layer}_out_grad"),
                )
            )
            exchange.end(layer)
            total = getattr(r, f"{layer}_total")
            total = jnp.concatenate([total[place].astype(WIDE) for place in range(replicas)], 0)
            for kind, first in (("down", 0), ("up", second)):
                out = getattr(r, f"{layer}_{kind}_grad_all")
                out[...] = unpack(total, first, out.shape)
        for copy in sent:
            copy.wait()

    near_outs = {}
    for layer in layers:
        near_outs[f"{layer}_embed"] = ((count, width // group), WIDE)
        near_outs[f"{layer}_in"] = ((width // group, units), WIDE)
        near_outs[f"{layer}_out_grad"] = ((units // group, 2 * width), WIDE)
        near_outs[f"{layer}_down_grad_all"] = ((width // group, narrow), WIDE)
        near_outs[f"{layer}_up_grad_all"] = ((narrow // group, width), WIDE)
    scratch = {}
    scratch["enc_parts_v"] = ((replicas, *part), LOW)
    scratch["enc_sum"] = scratch["enc_own"] = scratch["dec_own_v"] = (part, LOW)
    for layer in layers:
        scratch[f"{layer}_mine"] = (part[1:], LOW)
        scratch[f"{layer}_total"] = ((replicas, *part[1:]), LOW)
        scratch[f"{layer}_second"] = ((units, 2 * width), LOW)
        scratch[f"{layer}_first"] = ((width // group, units), LOW)
    own = (group, 8 * depth, 128)
    for name in ("pair_out", "pair_parts", "pair_total"):
        scratch[name] = ((replicas, *own), WIDE)
    for name in ("pair_sum", "pair_own", "pair_row"):
        scratch[name] = (own, WIDE)
    scratch["pair_mine"] = (own[1:], WIDE)
    scratch["whole"] = ((2, PAD, 2 * width), WIDE)
    scratch["enc_d_pairs"] = ((PAD, 2 * width), WIDE)
    scratch["tall_hidden"] = ((units, PAD), WIDE)
    scratch["wide_prefix"] = ((PAD, width), WIDE)
    scratch["tall_prefix"] = ((width, PAD), WIDE)
    for name in ("dq_sum", "dk_sum", "dv_sum"):
        scratch[name] = ((width, tokens), WIDE)
    return run_kernel(
        body,
        "encoder_attend_back",
        near=dict(
            marks=w.source_segments, enc_pairs=forward.enc_pairs, lse=forward.lse,
            dec_d_pairs=dec.d_pairs, enc_hidden=forward.enc_hidden, dec_hidden=forward.dec_hidden,
            enc_prefix=w.enc_prefix, dec_prefix=w.dec_prefix,
        ),
        far=dict(
            qkv=forward.qkv, d_context=feed.d_context, context=forward.context,
            enc_qkv=w.enc_qkv, summed_grad=feed.summed_grad,
            enc_parts=feed.parts, dec_own=dec.flat_own,
            enc_prefix_in=w.enc_prefix_in, enc_prefix_out=w.enc_prefix_out,
            dec_prefix_in=w.dec_prefix_in, dec_prefix_out=w.dec_prefix_out,
        ),
        near_outs=near_outs,
        far_outs=dict(source_grad=((group, share, width), LOW)),
        scratch=dict(
            qkv_v=((3 * width, tokens), LOW), d_context_v=((width, tokens), LOW),
            context_v=((width, tokens), LOW), qkv_weight=((width, 3 * width), LOW),
            summed_v=((tokens, width), LOW), d_qkv=((3 * width, tile), LOW), lse_v=((16, tokens), WIDE),
            qx=((heads * 16, tokens), LOW), kx=((16, tokens), LOW),
            dx=((heads * 16, tokens), LOW), vx=((16, tokens), LOW), delta=((16, tokens), WIDE),
            work=((2, TILE, 14 * TILE), LOW), **scratch,
        ),
        flops=2 * tokens * width * 2304 + 20 * tokens * tokens * width,
        links=3 * (group - 1) + 4 * (replicas - 1) + group - 1,
        collective=2,
    )


def finish(attended, feed, dec, copies):
    small = [name for name in vars(attended) if name != "source_grad"]
    shape = attended.source_grad.shape
    later = dec.out_all.shape

    def body(r):
        move = Mover(r.semaphores)
        ins = [
            move.start(r.source_grad, r.source_v),
            move.start(r.target_grad, r.target_v),
        ]
        outs = []
        relays = [
            (move.start(r.out_all.at[place * copies], r.out_v.at[place]), r.out_v.at[place], r.out.at[place])
            for place in range(later[0] // copies)
        ]
        for name in small:
            via = getattr(r, name + "_v")
            relays.append((move.start(getattr(r, name + "_in"), via), via, getattr(r, name)))
        for copy, via, goal in relays:
            copy.wait()
            outs.append(move.start(via, goal))
        for copy, origin, wide, goal in (
            (ins[0], r.source_v, r.source_w, r.source_out), (ins[1], r.target_v, r.target_w, r.target_out)
        ):
            copy.wait()
            for place in range(wide.shape[0]):
                wide[place] = origin[place * copies].astype(WIDE)
                outs.append(move.start(wide.at[place], goal.at[place]))
        for copy in outs:
            copy.wait()

    rows = shape[0] // copies
    return run_kernel(
        body,
        "finish",
        near={},
        far=dict(
            source_grad=attended.source_grad, target_grad=feed.target_grad_all, out_all=dec.out_all,
            **{name + "_in": getattr(attended, name) for name in small},
        ),
        near_outs={},
        far_outs=dict(
            out=((rows, *later[1:]), LOW), source_out=((rows, *shape[1:]), WIDE),
            target_out=((rows, *later[1:]), WIDE),
            **{name: (getattr(attended, name).shape, WIDE) for name in small},
        ),
        scratch=dict(
            source_v=(shape, LOW), source_w=((rows, *shape[1:]), WIDE), target_v=(later, LOW),
            target_w=((rows, *later[1:]), WIDE), out_v=((rows, *later[1:]), LOW),
            **{name + "_v": (getattr(attended, name).shape, WIDE) for name in small},
        ),
        flops=0,
    )


NAMES = (
    "source",
    "target",
    "source_segments",
    "target_segments",
    "cotangent",
    "enc_qkv",
    "enc_out",
    "enc_up",
    "enc_down",
    "dec_qkv",
    "dec_out",
    "cross_q",
    "cross_kv",
    "cross_out",
    "dec_up",
    "dec_down",
    "enc_prefix",
    "enc_prefix_in",
    "enc_prefix_out",
    "enc_adapter_down",
    "enc_adapter_up",
    "dec_prefix",
    "dec_prefix_in",
    "dec_prefix_out",
    "dec_adapter_down",
    "dec_adapter_up",
)


def shards(*operands, group, replicas):
    w = SimpleNamespace(**dict(zip(NAMES, operands)))
    copies = group // w.source.shape[0]
    forward = encoder_forward(w, group, copies)
    dec = decoder(forward, w, group, copies, replicas)
    feed = encoder_feed_back(dec, forward, w, group, copies, replicas)
    attended = encoder_attend_back(feed, dec, forward, w, group, copies, replicas)
    done = finish(attended, feed, dec, copies)
    results = [done.out, done.source_out, done.target_out]
    for layer in ("enc", "dec"):
        for name in ("embed", "in", "out_grad", "down_grad_all", "up_grad_all"):
            results.append(getattr(done, f"{layer}_{name}"))
    return tuple(results)


def solution(mesh):
    rows = P("dp", "seq", None)
    marks = P("dp", None)
    in_specs = (rows, rows, marks, marks, rows) + (P(),) * 21
    across, down = P(None, "seq"), P("seq", None)
    layer = (across, down, down, down, down)
    return jax.shard_map(
        functools.partial(shards, group=mesh.shape["seq"], replicas=mesh.shape["dp"]),
        mesh=mesh,
        in_specs=in_specs,
        out_specs=(rows, rows, rows) + layer + layer,
        check_vma=False,
    )
```

```python
import functools
import math
from types import SimpleNamespace

import jax
import jax.numpy as jnp
from jax import lax
from jax.experimental import pallas as pl
from jax.experimental.pallas import tpu as pltpu
from jax.sharding import PartitionSpec as P

HEAD = 64
GROUP = 4
PAD = 32
BIG = 2.0**100
LOG2E = math.log2(math.e)
SCALE = 1.0 / math.sqrt(HEAD)
VMEM_BYTES = 60 * 2**20
CHUNK = 256
TILE = 256
COLUMNS = 512
INNER = 512
LOW = jnp.bfloat16
WIDE = jnp.float32


def contract(left, right, left_dim, right_dim):
    return lax.dot_general(
        left, right, (((left_dim,), (right_dim,)), ((), ())), preferred_element_type=WIDE
    )


def rows_at(index, size, base=0):
    return pl.ds(pl.multiple_of(base + index * size, size), size)


def chunks(size, step):
    step = min(step, size)
    return [slice(start, start + step) for start in range(0, size, step)]


def total_of(values):
    return functools.reduce(lambda left, right: left + right, values)


def normalize(value):
    centered = value - jnp.mean(value, axis=-1, keepdims=True)
    inverse = lax.rsqrt(jnp.mean(centered * centered, axis=-1, keepdims=True) + 1e-05)
    return (centered * inverse, inverse)


def normalize_back(gradient, normed, inverse):
    return (
        gradient
        - jnp.mean(gradient, axis=-1, keepdims=True)
        - normed * jnp.mean(gradient * normed, axis=-1, keepdims=True)
    ) * inverse


def gelu_both(value):
    scale = math.sqrt(2.0 / math.pi)
    square = value * value
    half = 0.5 + 0.5 * jnp.tanh(value * (scale + (scale * 0.044715) * square))
    active = value * half
    slope = half + active * (1.0 - half) * (2.0 * scale + (6.0 * scale * 0.044715) * square)
    return (active, slope)


class Mover:
    def __init__(self, semaphores):
        self.semaphores = semaphores
        self.used = 0

    def start(self, origin, goal):
        copy = pltpu.make_async_copy(origin, goal, self.semaphores.at[self.used])
        self.used += 1
        copy.start()
        return copy


def run_kernel(body, name, near, far, near_outs, far_outs, scratch, flops, links=0, collective=None):
    in_names = list(near) + list(far)
    out_names = list(near_outs) + list(far_outs)
    names = in_names + out_names + list(scratch) + ["semaphores"]
    link_scratch = []
    remote = {}
    if collective is not None:
        names += ["sent", "arrived"]
        link_scratch = [pltpu.SemaphoreType.DMA((links,)), pltpu.SemaphoreType.DMA((links,))]
        remote = dict(collective_id=collective, has_side_effects=True)

    def kernel(*refs):
        body(SimpleNamespace(**dict(zip(names, refs))))

    near_spec = pl.BlockSpec(memory_space=pltpu.VMEM)
    far_spec = pl.BlockSpec(memory_space=pl.ANY)
    results = pl.pallas_call(
        kernel,
        out_shape=tuple(
            jax.ShapeDtypeStruct(*out) for out in (*near_outs.values(), *far_outs.values())
        ),
        in_specs=[near_spec] * len(near) + [far_spec] * len(far),
        out_specs=tuple([near_spec] * len(near_outs) + [far_spec] * len(far_outs)),
        scratch_shapes=[pltpu.VMEM(*shape) for shape in scratch.values()]
        + [pltpu.SemaphoreType.DMA((80,))]
        + link_scratch,
        compiler_params=pltpu.CompilerParams(vmem_limit_bytes=VMEM_BYTES, **remote),
        cost_estimate=pl.CostEstimate(flops=flops, bytes_accessed=2**24, transcendentals=0),
        name=name,
    )(*near.values(), *far.values())
    return SimpleNamespace(**dict(zip(out_names, results)))


class Links:
    def __init__(self, sent, arrived, groups):
        self.sent, self.arrived = sent, arrived
        self.used = 0
        self.place = {axis: lax.axis_index(axis) for axis in ("dp", "seq")}
        self.sizes = groups
        barrier = pltpu.get_barrier_semaphore()
        peers = 0
        for axis, size in groups.items():
            for shift in range(1, size):
                pl.semaphore_signal(
                    barrier, inc=1, device_id=self.device(axis, shift), device_id_type=pl.DeviceIdType.MESH
                )
                peers += 1
        pl.semaphore_wait(barrier, peers)

    def peer(self, axis, shift):
        return lax.rem(self.place[axis] + shift, self.sizes[axis])

    def device(self, axis, shift):
        return self.device_at(axis, self.peer(axis, shift))

    def device_at(self, axis, index):
        return (index, self.place["seq"]) if axis == "dp" else (self.place["dp"], index)

    def start(self, axis, shift, origin, goal):
        return self.start_to(axis, self.peer(axis, shift), origin, goal)

    def start_to(self, axis, index, origin, goal):
        copy = self.plan(axis, index, origin, goal)
        copy.start()
        return copy

    def plan(self, axis, index, origin, goal):
        copy = pltpu.make_async_remote_copy(
            src_ref=origin,
            dst_ref=goal,
            send_sem=self.sent.at[self.used],
            recv_sem=self.arrived.at[self.used],
            device_id=self.device_at(axis, index),
            device_id_type=pl.DeviceIdType.MESH,
        )
        self.used += 1
        return copy

    def scatter(self, axis, pick, goal):
        return [
            self.start(axis, shift, pick(self.peer(axis, shift)), goal)
            for shift in range(1, self.sizes[axis])
        ]


class Exchange:
    def __init__(self, move, links):
        self.move, self.links = move, links
        self.place, self.sizes = links.place, links.sizes
        self.open = {}

    def start(self, name, axis, pick, goal, via=None):
        mine = self.place[axis]
        copies = self.links.scatter(axis, pick, goal.at[mine])
        if via is None:
            copies.append(self.move.start(pick(mine), goal.at[mine]))
        else:
            self.move.start(pick(mine), via).wait()
            copies.append(self.move.start(via, goal.at[mine]))
        self.open[name] = copies

    def end(self, *names):
        for name in names:
            for copy in self.open.pop(name):
                copy.wait()


def sum_parts(parts):
    return total_of([parts[part].astype(WIDE) for part in range(parts.shape[0])])


def rows_for(ref, count):
    size = ref.shape[0] // count
    return lambda place: ref.at[pl.ds(pl.multiple_of(place * size, size), size), :]


def split_three(value):
    high = value.astype(LOW).astype(WIDE)
    rest = value - high
    middle = rest.astype(LOW).astype(WIDE)
    return (high, middle, rest - middle)


def place_rows(parts, first, shape):
    row = lax.broadcasted_iota(jnp.int32, shape, 0)
    out = jnp.zeros(shape, WIDE)
    for offset, part in enumerate(parts):
        out = jnp.where(row == first + offset, part, out)
    return out


def document_rows(segments, tokens, is_key):
    row = lax.broadcasted_iota(jnp.int32, (16, tokens), 0)
    same = row == segments
    if is_key:
        return jnp.where(row < 4, jnp.where(same, 0.0, -BIG), 0.0)
    return jnp.where(same & (row < 4), 1.0, 0.0)


def column_peak(scores, peak):
    for start in range(0, scores.shape[0], 8):
        peak = jnp.maximum(peak, scores[start : start + 8])
    return peak


def from_column(value, low):
    if low == 0:
        return value
    return jnp.concatenate([jnp.zeros((value.shape[0], low), value.dtype), value], 1)


def attend(a, causal, prefix, entries=None):
    queries, keys = a.q.shape[1], a.k.shape[1]
    width = a.context.shape[0]
    heads = width // HEAD
    tile = min(256, keys)
    tiles = keys // tile
    a.qx[:16, :queries] = document_rows(a.q_marks, queries, False).astype(LOW)
    a.kx[:, :keys] = document_rows(a.k_marks, keys, True).astype(LOW)
    if entries is None:
        entries = [
            (own, [part for part in range(tiles) if not (causal and part * tile >= own.stop)], prefix > 0, "whole")
            for own in chunks(queries, COLUMNS)
        ]

    def front(head, slot, entry, work):
        own, parts, sees_prefix, _ = entry
        start = own.start
        query = jnp.concatenate([a.q[rows_at(head, HEAD, a.q0), own], a.qx[:16, own]], 0)
        peak = jnp.full((8, own.stop - start), -4.0 * BIG, WIDE)
        if sees_prefix:
            scores = contract(a.pair_keys[rows_at(head, HEAD), :], query[:HEAD], 0, 0)
            row = lax.broadcasted_iota(jnp.int32, scores.shape, 0)
            scores = jnp.where(row < prefix, scores, -BIG)
            a.pair_scores[slot, :, own] = scores
            peak = column_peak(scores, peak)
        for part in parts:
            cut = slice(part * tile, (part + 1) * tile)
            key = jnp.concatenate([a.k[rows_at(head, HEAD, a.k0), cut], a.kx[:, cut]], 0)
            scores = contract(key, query, 0, 0)
            if causal and cut.stop > start:
                place = lax.broadcasted_iota(jnp.int32, scores.shape, 0) + (cut.start - start)
                scores = jnp.where(
                    place <= lax.broadcasted_iota(jnp.int32, scores.shape, 1), scores, -BIG
                )
            a.scores[slot, cut, own] = scores
            peak = column_peak(scores, peak)
            work(part)
        a.peak[slot, :, own] = peak

    def step(head, following, slot):
        for entry in entries:
            own, _, sees_prefix, mode = entry
            peak = jnp.max(a.peak[slot, :, own], 0, keepdims=True)
            context = []
            if mode == "merge":
                before = a.lse[pl.ds(head, 1), own]
                peak = jnp.maximum(peak, before)
                context.append(a.partial[rows_at(head, HEAD + 16), own] * jnp.exp2(before - peak))
            if sees_prefix:
                weights = jnp.exp2(a.pair_scores[slot, :, own] - peak).astype(LOW)
                value = jnp.concatenate(
                    [a.pair_values[rows_at(head, HEAD), :], jnp.ones((16, PAD), LOW)], 0
                )
                context.append(contract(value, weights, 1, 0))

            def work(part):
                cut = slice(part * tile, (part + 1) * tile)
                weights = jnp.exp2(a.scores[slot, cut, own] - peak).astype(LOW)
                value = jnp.concatenate(
                    [a.v[rows_at(head, HEAD, a.v0), cut], jnp.ones((16, tile), LOW)], 0
                )
                context.append(contract(value, weights, 1, 0))

            front(following, 1 - slot, entry, work)
            summed = total_of(context)
            if mode == "save":
                a.partial[rows_at(head, HEAD + 16), own] = summed
                a.lse[pl.ds(head, 1), own] = peak
            else:
                total = summed[HEAD : HEAD + 1]
                a.context[rows_at(head, HEAD), own] = (summed[:HEAD] * (1.0 / total)).astype(LOW)
                a.lse[pl.ds(head, 1), own] = peak + jnp.log2(total)

    for entry in entries:
        front(0, 0, entry, lambda part: None)

    def pair(index, carry):
        step(2 * index, 2 * index + 1, 0)
        step(2 * index + 1, jnp.minimum(2 * index + 2, heads - 1), 1)
        return carry

    lax.fori_loop(0, heads // 2, pair, 0)


def block_diagonal(pairs, group, first):
    wide = GROUP * HEAD
    rows = pairs[:, first + group * wide : first + (group + 1) * wide]
    column = lax.broadcasted_iota(jnp.int32, rows.shape, 1)
    parts = [
        jnp.where((column >= member * HEAD) & (column < (member + 1) * HEAD), rows.astype(WIDE), 0.0)
        for member in range(GROUP)
    ]
    return jnp.concatenate(parts, 0).astype(LOW)


def own_columns(grads):
    column = lax.broadcasted_iota(jnp.int32, (PAD, GROUP * HEAD), 1)
    out = jnp.zeros((PAD, GROUP * HEAD), WIDE)
    for member in range(GROUP):
        own = (column >= member * HEAD) & (column < (member + 1) * HEAD)
        out = jnp.where(own, grads[member * PAD : (member + 1) * PAD], out)
    return out


def attend_back(a, causal, prefix, ready=None, staged=None):
    queries, keys = a.q.shape[1], a.k.shape[1]
    width = a.context.shape[0]
    heads = width // HEAD
    tiles = keys // TILE
    row = lax.broadcasted_iota(jnp.int32, (16, keys), 0)
    a.kx[:, :keys] = jnp.where(
        (row >= 4) & (row < 7), 1.0, document_rows(a.k_marks, keys, True)
    ).astype(LOW)
    a.vx[:, :keys] = jnp.where(row < 3, 1.0, 0.0).astype(LOW)
    documents = document_rows(a.q_marks, queries, False)

    def prepare(head, carry):
        rows = rows_at(head, HEAD)
        delta = jnp.sum(
            a.d_context[rows, :].astype(WIDE) * a.context[rows, :].astype(WIDE),
            axis=0,
            keepdims=True,
        )
        a.delta[pl.ds(head, 1), :queries] = delta
        a.dx[rows_at(head, 16), :queries] = place_rows(
            split_three(-delta), 0, (16, queries)
        ).astype(LOW)
        minus = split_three(-a.lse[pl.ds(head, 1), :])
        a.qx[rows_at(head, 16), :queries] = (
            documents + place_rows(minus, 4, (16, queries))
        ).astype(LOW)
        return carry

    lax.fori_loop(0, heads, prepare, 0)

    if prefix:
        for group in range(heads // GROUP):
            start = group * GROUP * HEAD
            own = slice(start, start + GROUP * HEAD)
            query = a.q[a.q0 + start : a.q0 + start + GROUP * HEAD, :]
            grad = a.d_context[own, :]
            pair_keys = block_diagonal(a.pairs[...], group, 0)
            pair_values = block_diagonal(a.pairs[...], group, width)
            scores = contract(pair_keys, query, 1, 0)
            gains = contract(pair_values, grad, 1, 0)
            chances, changes = [], []
            for member in range(GROUP):
                head = group * GROUP + member
                part = slice(member * PAD, (member + 1) * PAD)
                chance = jnp.exp2(scores[part] - a.lse[head : head + 1, :])
                place = lax.broadcasted_iota(jnp.int32, chance.shape, 0)
                chance = jnp.where(place < prefix, chance, 0.0)
                chances.append(chance)
                changes.append(chance * (gains[part] - a.delta[head : head + 1, :queries]))
            chances = jnp.concatenate(chances, 0).astype(LOW)
            changes = jnp.concatenate(changes, 0).astype(LOW)
            a.dq_sum[own, :queries] = contract(pair_keys, changes, 0, 0)
            a.d_pairs[:, own] = own_columns(contract(changes, query, 1, 1)) * (a.factor / LOG2E)
            a.d_pairs[:, width + start : width + start + GROUP * HEAD] = (
                own_columns(contract(chances, grad, 1, 1)) * a.factor
            )
    else:
        a.dq_sum[:, :queries] = jnp.zeros((width, queries), WIDE)
    if ready is not None:
        ready(0)


    def span(part):
        return slice(part * TILE, (part + 1) * TILE)

    def place_of(number, kind):
        return span(2 * number + kind)

    def front(head, own, cut, slot, number):
        query = jnp.concatenate([a.q[rows_at(head, HEAD, a.q0), own], a.qx[rows_at(head, 16), own]], 0)
        key = jnp.concatenate([a.k[rows_at(head, HEAD, a.k0), cut], a.kx[:, cut]], 0)
        scores = contract(query, key, 0, 0)
        if causal and own == cut:
            place = lax.broadcasted_iota(jnp.int32, scores.shape, 1)
            scores = jnp.where(place <= lax.broadcasted_iota(jnp.int32, scores.shape, 0), scores, -BIG)
        grad = jnp.concatenate([a.d_context[rows_at(head, HEAD), own], a.dx[rows_at(head, 16), own]], 0)
        value = jnp.concatenate([a.v[rows_at(head, HEAD, a.v0), cut], a.vx[:, cut]], 0)
        gains = contract(grad, value, 0, 0)
        chance = jnp.exp2(scores)
        a.work[slot, :, place_of(number, 0)] = chance.astype(LOW)
        a.work[slot, :, place_of(number, 1)] = (chance * gains).astype(LOW)

    def run(pieces, together, add):
        unit = [(offset, own, cut) for offset in range(together) for own, cut in pieces]

        def begin(index, slot, number):
            offset, own, cut = unit[number]
            front(index * together + offset, own, cut, slot, number)

        def mix(index, slot, following):
            by_key, by_query = {}, {}
            for number, (offset, own, cut) in enumerate(unit):
                head = index * together + offset
                rows = rows_at(head, HEAD)
                left = unit[number + 1 :]
                chances = a.work[slot, :, place_of(number, 0)]
                changes = a.work[slot, :, place_of(number, 1)]
                pair = by_key.setdefault((offset, cut.start), [])
                d_value = contract(a.d_context[rows, own], chances, 1, 0)
                pair.append((contract(a.q[rows_at(head, HEAD, a.q0), own], changes, 1, 0), d_value))
                begin(following, 1 - slot, number)
                d_query = by_query.setdefault((offset, own.start), [])
                d_query.append(contract(a.k[rows_at(head, HEAD, a.k0), cut], changes, 1, 1))
                if not any((other, keys_.start) == (offset, cut.start) for other, _, keys_ in left):
                    add(head, cut, *(total_of(parts) for parts in zip(*pair)))
                if not any((other, queries_.start) == (offset, own.start) for other, queries_, _ in left):
                    a.dq_sum[rows, own] += total_of(d_query)

        def two(index, carry):
            mix(2 * index, 0, 2 * index + 1)
            mix(2 * index + 1, 1, jnp.minimum(2 * index + 2, count - 1))
            return carry

        count = heads // together
        for number in range(len(unit)):
            begin(0, 0, number)
        return two, count // 2

    if staged is not None:
        for stage in range(tiles):
            pieces = [(span(other), span(stage)) for other in range(stage + 1, tiles)]
            pieces += [(span(stage), span(other)) for other in range(stage, tiles)]

            def add(head, cut, d_key, d_value):
                rows = rows_at(head, HEAD)
                if stage == 0:
                    a.dk_sum[rows, cut] = d_key
                    a.dv_sum[rows, cut] = d_value
                else:
                    a.dk_sum[rows, cut] += d_key
                    a.dv_sum[rows, cut] += d_value

            step, steps = run(pieces, {1: heads // 2, 3: 2}.get(len(pieces), 1), add)
            cuts = [0, steps // 3, 2 * steps // 3, steps] if stage == 0 else [0, steps]
            for number in range(len(cuts) - 1):
                lax.fori_loop(cuts[number], cuts[number + 1], step, 0)
                if number + 2 < len(cuts):
                    ready(number + 1)
            staged(stage, span(stage))
        return

    def add(head, cut, d_key, d_value):
        a.dk[rows_at(head, HEAD, a.dk0), cut] = (d_key * (1.0 / LOG2E)).astype(LOW)
        a.dv[rows_at(head, HEAD, a.dv0), cut] = d_value.astype(LOW)

    pieces = [
        (span(own), span(part))
        for part in range(tiles)
        for own in range(part if causal else 0, queries // TILE)
    ]
    step, steps = run(pieces, 2 if len(pieces) < 4 else 1, add)
    lax.fori_loop(0, steps, step, 0)
    a.dq[rows_at(0, width, a.dq0), :] = (a.dq_sum[:, :queries] * SCALE).astype(LOW)


def project_wide(out, weight, rows, scaled, place=slice(None)):
    for cut in chunks(weight.shape[1], 256):
        result = contract(weight[:, cut], rows, 0, 1)
        if cut.start < scaled:
            result = result * (SCALE * LOG2E)
        out[cut, place] = result.astype(LOW)


def add_and_normalize(hidden, context, weight, normed, inverse):
    for cut in chunks(hidden.shape[0], CHUNK):
        summed = hidden[cut, :].astype(WIDE) + contract(context[:, cut], weight[...], 0, 0)
        result, scale = normalize(summed)
        normed[cut, :] = result.astype(LOW)
        inverse[cut, :] = scale


def chunk_pipeline(tokens, make, use, steps, uses):
    count = tokens // CHUNK

    def rows_of(index):
        return rows_at(index, CHUNK)

    def body(index, slot, following):
        done = 0
        for step in range(steps):
            if following is not None:
                make(rows_of(following), 1 - slot, step)
            while done < uses and done * steps <= step * uses:
                use(rows_of(index), slot, done)
                done += 1
        while done < uses:
            use(rows_of(index), slot, done)
            done += 1

    def two(index, carry):
        body(2 * index, 0, 2 * index + 1)
        body(2 * index + 1, 1, 2 * index + 2)
        return carry

    for step in range(steps):
        make(rows_of(0), 0, step)
    if count > 2:
        lax.fori_loop(0, count // 2 - 1, two, 0)
    body(count - 2, 0, count - 1)
    body(count - 1, 1, None)


def feed_forward(hidden, up, down, adapter_down, adapter_up, total, slopes_of, active_of, narrow):
    inner = up.shape[1]
    count = inner // INNER

    def make(rows, slot, step):
        if step < count:
            cut = slice(step * INNER, (step + 1) * INNER)
            active, slope = gelu_both(contract(hidden[rows, :], up[:, cut], 1, 0))
            slopes_of(step + 1)[rows, :] = slope.astype(LOW)
        else:
            cut = slice(inner, inner + INNER)
            active, slope = gelu_both(contract(hidden[rows, :], adapter_down[...], 1, 0))
            slopes_of(0)[rows, :] = slope.astype(LOW)
            narrow[rows, :] = active.astype(LOW)
            active = 4.0 * active
        active_of(slot)[:, cut] = active.astype(LOW)

    def use(rows, slot, number):
        active = active_of(slot)
        total[rows, :] = (
            hidden[rows, :].astype(WIDE)
            + contract(active[:, :inner], down[...], 1, 0)
            + contract(active[:, inner : inner + INNER], adapter_up[...], 1, 0)
        )

    chunk_pipeline(hidden.shape[0], make, use, count + 1, 1)


def finish_forward(total, normed, inverse):
    for cut in chunks(total.shape[0], CHUNK):
        result, scale = normalize(total[cut, :])
        normed[cut, :] = result.astype(LOW)
        inverse[cut, :] = scale


def pack(flat, value, first):
    size = value.shape[0] // flat.shape[0]
    for place in range(flat.shape[0]):
        for block in range(value.shape[1] // 128):
            goal = slice(first + block * size, first + (block + 1) * size)
            flat[place, goal, :] = value[
                place * size : (place + 1) * size, block * 128 : (block + 1) * 128
            ].astype(flat.dtype)


def unpack(rows, first, shape):
    parts = [
        rows[first + block * shape[0] : first + (block + 1) * shape[0]] for block in range(shape[1] // 128)
    ]
    return jnp.concatenate(parts, 1)


def flat_shapes(width, narrow, group, replicas):
    second = width // group * (narrow // 128)
    rows = second + narrow // group * (width // 128)
    return second, (group, rows, 128), (group, rows // replicas, 128)


def columns_for(flat, replicas):
    size = flat.shape[1] // replicas
    return lambda place: flat.at[:, pl.ds(pl.multiple_of(place * size, size), size), :]


def feed_back(f, send=None):
    tokens = f.hidden.shape[0]
    cuts = chunks(tokens, CHUNK)
    for cut in cuts:
        value = f.grad[cut, :]
        f.low[cut, :] = value.astype(LOW)
        f.side[cut, :] = (4.0 * value).astype(LOW)

    for cut in cuts:
        change = contract(f.side[cut, :], f.adapter_up[...], 1, 1) * f.slopes(0)[cut, :].astype(WIDE)
        f.d_narrow[cut, :] = change.astype(LOW)
    pack(f.flat, contract(f.hidden[...], f.d_narrow[...], 0, 0) * f.factor, 0)
    pack(f.flat, contract(f.narrow[...], f.side[...], 0, 0) * f.factor, f.second)
    if send is not None:
        send()

    def make(rows, slot, step):
        cut = slice(step * INNER, (step + 1) * INNER)
        change = contract(f.low[rows, :], f.down[cut, :], 1, 1) * f.slopes(step + 1)[rows, :].astype(WIDE)
        f.active(slot)[:, cut] = change.astype(LOW)

    def use(rows, slot, number):
        f.grad[rows, :] += contract(f.active(slot)[:, : f.up.shape[1]], f.up[...], 1, 1) + contract(
            f.d_narrow[rows, :], f.adapter_down[...], 1, 1
        )

    chunk_pipeline(tokens, make, use, f.up.shape[1] // INNER, 1)


def normalize_back_all(grad, normed, inverse, out):
    for cut in chunks(grad.shape[0], CHUNK):
        out[cut, :] = normalize_back(
            grad[cut, :].astype(WIDE), normed[cut, :].astype(WIDE), inverse[cut, :]
        ).astype(out.dtype)


def context_back(out, weight, grad):
    value = grad[...].astype(LOW)
    for cut in chunks(weight.shape[0], 256):
        out[cut, :] = contract(weight[cut, :], value, 1, 1).astype(LOW)


def prefix_pairs(prefix, first, second, hidden, pairs, pairs_wide):
    count = prefix.shape[0]
    hidden[...] = jnp.zeros(hidden.shape, WIDE)
    hidden[:count, :] = jnp.tanh(contract(prefix[...], first[...], 1, 0))
    parts = [part.astype(LOW) for part in split_three(hidden[...])]
    pairs[...] = total_of([contract(part, second[...], 1, 0) for part in parts]).astype(LOW)
    pairs_wide[...] = total_of([contract(second[...], part, 0, 1) for part in parts]).astype(LOW)


def near_order(place):
    return [place, place + 1 - 2 * lax.rem(place, 2), lax.rem(place + 2, 4), 3 - place]


def is_inner(place):
    return lax.rem(place // 2 + lax.rem(place, 2), 2)


def encoder_forward(w, group, copies):
    width = w.source.shape[2]
    share, later_share = w.source.shape[1], w.target.shape[1]
    tokens, later_tokens = share * group, later_share * group
    per = TILE // share
    inner = w.enc_up.shape[1]
    narrow = w.enc_adapter_down.shape[1]
    units = w.enc_prefix_in.shape[1]
    count = w.enc_prefix.shape[0]
    blocks = 1 + inner // INNER

    def body(r):
        move = Mover(r.semaphores)
        weights = [move.start(r.enc_qkv, r.qkv_weight)]
        enc_first, dec_first = r.mid_v.at[:width, :units], r.memory_v.at[:width, :units]
        enc_second, dec_second = r.up.at[:units, : 2 * width], r.up.at[:units, 2 * width : 4 * width]
        weights.append(move.start(r.enc_prefix_in, enc_first))
        weights.append(move.start(r.enc_prefix_out, enc_second))
        weights.append(move.start(r.dec_prefix_in, dec_first))
        weights.append(move.start(r.dec_prefix_out, dec_second))
        links = Links(r.sent, r.arrived, {"seq": group})
        me = links.place["seq"]
        row = me // copies
        block, inside = me // per, lax.rem(me, per)
        others = near_order(block)
        arrivals = []
        for slot, other in enumerate(others):
            goal = r.x.at[pl.ds(pl.multiple_of(slot * TILE + inside * share, share), share), :]
            arrivals.append([])
            for turn in range(per):
                target = other * per + lax.rem(inside + turn, per)
                if slot == 0 and turn == 0:
                    here = move.start(r.source.at[row], goal)
                else:
                    arrivals[slot].append(links.plan("seq", target, r.source.at[target // copies], goal))

        def send(*slots):
            for slot in slots:
                for copy in arrivals[slot]:
                    copy.start()

        pl.when(is_inner(block) == 0)(lambda: send(1, 2))
        pl.when(is_inner(block) == 1)(lambda: send(2, 1))
        send(0, 3)

        def tokens_of(place, size):
            return pl.ds(pl.multiple_of(place * size, size), size)

        def bring(origin, goal, size, via=None):
            own = tokens_of(me, size)
            copies_out = links.scatter("seq", lambda peer: origin.at[peer // copies], goal.at[own, :])
            if via is None:
                return (move.start(origin.at[row], goal.at[own, :]), copies_out)
            move.start(origin.at[row], via).wait()
            return (move.start(via, goal.at[own, :]), copies_out)

        out_weight = move.start(r.enc_out, r.out_weight)
        adapters = [
            move.start(r.enc_adapter_down, r.a_down),
            move.start(r.enc_adapter_up, r.a_up),
        ]
        pair_weight = move.start(r.cross_kv, r.pair_weight)
        for copy in weights:
            copy.wait()
        prefix_pairs(r.enc_prefix, enc_first, enc_second, r.enc_hidden, r.enc_pairs, r.enc_pairs_wide)
        prefix_pairs(r.dec_prefix, dec_first, dec_second, r.dec_hidden, r.dec_pairs, r.dec_pairs_wide)
        ups = [move.start(r.enc_up, r.up), move.start(r.enc_down, r.down)]
        def project(slot):
            for copy in arrivals[slot]:
                copy.wait()
            cut = slice(slot * TILE, (slot + 1) * TILE)
            project_wide(r.qkv_v, r.qkv_weight, r.x[cut, :], width, cut)

        r.marks_out[...] = jnp.concatenate(
            [r.marks[pl.ds(row, 1), pl.ds(pl.multiple_of(other * TILE, TILE), TILE)] for other in others], 1
        )
        marks = r.marks_out[...]
        attention = SimpleNamespace(
            q=r.qkv_v, k=r.qkv_v, v=r.qkv_v, q0=0, k0=width, v0=2 * width,
            q_marks=marks, k_marks=marks, pair_keys=r.enc_pairs_wide.at[:width],
            pair_values=r.enc_pairs_wide.at[width:],
            context=r.context_v, lse=r.lse, qx=r.qx, kx=r.kx, scores=r.scores,
            pair_scores=r.pair_scores, peak=r.peak, partial=r.total,
        )
        here.wait()
        for slot in (1, 2, 0):
            project(slot)
        tiles = tokens // TILE
        most = (tiles - 1) * TILE
        early = [slice(0, most // 2), slice(most // 2, most)] if most // 2 % 128 == 0 else [slice(0, most)]
        attend(
            attention, False, count, [(own, list(range(tiles - 1)), True, "save") for own in early]
        )
        project(tiles - 1)
        later = [bring(r.target, r.target_rows, later_share, r.own_target)]
        outs = [move.start(r.qkv_v, r.qkv)]
        attend(
            attention,
            False,
            count,
            [(slice(most, tokens), list(range(tiles)), True, "whole")]
            + [(own, [tiles - 1], False, "merge") for own in early],
        )
        outs.append(move.start(r.context_v, r.context))
        out_weight.wait()
        add_and_normalize(r.x, r.context_v, r.out_weight, r.mid_v, r.mid_inverse)
        outs.append(move.start(r.mid_v, r.mid))
        for copy in adapters + ups:
            copy.wait()
        feed_forward(
            r.mid_v, r.up, r.down, r.a_down, r.a_up, r.total,
            lambda index: r.slopes_v.at[index], lambda slot: r.active.at[slot], r.narrow_v,
        )
        outs.append(move.start(r.slopes_v, r.slopes))
        outs.append(move.start(r.narrow_v, r.narrow))
        finish_forward(r.total, r.memory_v, r.memory_inverse)
        outs.append(move.start(r.memory_v, r.memory))
        pair_weight.wait()
        outs.pop(0).wait()
        memory_pairs = r.qkv_v.at[: 2 * width]
        project_wide(memory_pairs, r.pair_weight, r.memory_v[...], 0)
        outs.append(move.start(memory_pairs, r.memory_pairs))
        for own, remote in later:
            own.wait()
            for copy in remote:
                copy.wait()
        for copy in outs:
            copy.wait()

    return run_kernel(
        body,
        "encoder_forward",
        near=dict(marks=w.source_segments, enc_prefix=w.enc_prefix, dec_prefix=w.dec_prefix),
        far=dict(
            source=w.source, target=w.target, enc_qkv=w.enc_qkv,
            enc_out=w.enc_out, enc_up=w.enc_up, enc_down=w.enc_down,
            enc_adapter_down=w.enc_adapter_down, enc_adapter_up=w.enc_adapter_up,
            cross_kv=w.cross_kv, enc_prefix_in=w.enc_prefix_in, enc_prefix_out=w.enc_prefix_out,
            dec_prefix_in=w.dec_prefix_in, dec_prefix_out=w.dec_prefix_out,
        ),
        near_outs=dict(
            lse=((16, tokens), WIDE), mid_inverse=((tokens, 1), WIDE),
            memory_inverse=((tokens, 1), WIDE), marks_out=((1, tokens), jnp.int32),
            enc_hidden=((PAD, units), WIDE), enc_pairs=((PAD, 2 * width), LOW),
            dec_hidden=((PAD, units), WIDE), dec_pairs=((PAD, 2 * width), LOW),
            dec_pairs_wide=((2 * width, PAD), LOW),
        ),
        far_outs=dict(
            qkv=((3 * width, tokens), LOW), context=((width, tokens), LOW), mid=((tokens, width), LOW),
            slopes=((blocks, tokens, INNER), LOW), narrow=((tokens, narrow), LOW),
            memory=((tokens, width), LOW), memory_pairs=((2 * width, tokens), LOW),
            target_rows=((later_tokens, width), LOW),
        ),
        scratch=dict(
            x=((tokens, width), LOW), qkv_weight=((width, 3 * width), LOW),
            own_target=((later_share, width), LOW),
            enc_pairs_wide=((2 * width, PAD), LOW),
            out_weight=((width, width), LOW), a_down=((width, narrow), LOW),
            a_up=((narrow, width), LOW), up=((width, inner), LOW), down=((inner, width), LOW),
            pair_weight=((width, 2 * width), LOW), qkv_v=((3 * width, tokens), LOW),
            context_v=((width, tokens), LOW), mid_v=((tokens, width), LOW),
            slopes_v=((blocks, tokens, INNER), LOW), narrow_v=((tokens, narrow), LOW),
            memory_v=((tokens, width), LOW),
            active=((2, CHUNK, inner + narrow), LOW), total=((tokens, width), WIDE), qx=((16, tokens), LOW), kx=((16, tokens), LOW),
            scores=((2, tokens, tokens), WIDE), pair_scores=((2, PAD, tokens), WIDE),
            peak=((2, 8, tokens), WIDE),
        ),
        flops=2 * tokens * width * 11776 + 4 * tokens * tokens * width,
        links=2 * (group - 1),
        collective=0,
    )


def decoder(forward, w, group, copies, replicas):
    tokens, width = forward.target_rows.shape
    share = tokens // group
    keys = forward.memory_pairs.shape[1]
    count = w.dec_prefix.shape[0]
    second, flat, part = flat_shapes(width, w.dec_adapter_down.shape[1], group, replicas)
    inner = w.dec_up.shape[1]
    narrow = w.dec_adapter_down.shape[1]
    blocks = 1 + inner // INNER
    heads = width // HEAD

    def body(r):
        move = Mover(r.semaphores)
        ins = [move.start(r.target, r.x), move.start(r.dec_qkv, r.qkv_weight)]
        links = Links(r.sent, r.arrived, {"seq": group, "dp": replicas})
        exchange = Exchange(move, links)
        for copy in ins:
            copy.wait()
        out_weight = move.start(r.dec_out, r.out_weight)
        crosses = [
            move.start(r.cross_q, r.query_weight),
            move.start(r.memory_pairs, r.pairs_v),
            move.start(r.cross_out, r.cross_out_weight),
        ]
        adapters = [
            move.start(r.dec_adapter_down, r.a_down),
            move.start(r.dec_adapter_up, r.a_up),
        ]
        ups = [move.start(r.dec_up, r.up), move.start(r.dec_down, r.down)]
        d_qkv = r.slopes.at[: 3 * width, :tokens]

        def slope_of(index):
            return r.slopes.at[rows_at(index, tokens), :]

        me = links.place["seq"]
        size = tokens // group
        mine = r.cotangent_v.at[pl.ds(pl.multiple_of(me * size, size), size), :]
        cotangents = links.scatter("seq", lambda peer: r.cotangent.at[peer // copies], mine)
        cotangents.append(move.start(r.cotangent.at[me // copies], mine))
        project_wide(r.qkv, r.qkv_weight, r.x[...], width)
        row = pl.ds(me // copies, 1)
        marks, source_marks = r.marks[row, :], r.source_marks[...]
        shared = dict(
            qx=r.qx, kx=r.kx, scores=r.scores, pair_scores=r.pair_scores, peak=r.peak, dx=r.dx,
            vx=r.vx, delta=r.delta, dq_sum=r.dq_sum, work=r.work,
            d_context=r.d_context,
        )
        self_part = SimpleNamespace(
            q=r.qkv, k=r.qkv, v=r.qkv, q0=0, k0=width, v0=2 * width,
            q_marks=marks, k_marks=marks, pair_keys=r.pairs_wide.at[:width],
            pair_values=r.pairs_wide.at[width:], pairs=r.pairs, context=r.context, lse=r.lse,
            dq=d_qkv, dk=d_qkv, dv=d_qkv, dq0=0, dk0=width, dv0=2 * width,
            d_pairs=r.d_pairs, factor=1.0 / copies, **shared,
        )
        attend(self_part, True, count)
        out_weight.wait()
        add_and_normalize(r.x, r.context, r.out_weight, r.mid, r.mid_inverse)
        for copy in crosses:
            copy.wait()
        project_wide(r.query, r.query_weight, r.mid[...], width)
        cross_part = SimpleNamespace(
            q=r.query, k=r.pairs_v, v=r.pairs_v, q0=0, k0=0, v0=width,
            q_marks=marks, k_marks=source_marks, context=r.cross_context, lse=r.cross_lse,
            dq=r.d_query, dk=r.d_pairs_v, dv=r.d_pairs_v, dq0=0, dk0=0, dv0=width, **shared,
        )
        attend(cross_part, False, 0)
        add_and_normalize(r.mid, r.cross_context, r.cross_out_weight, r.crossed, r.crossed_inverse)
        for copy in adapters + ups + cotangents:
            copy.wait()
        feed_forward(
            r.crossed, r.up, r.down, r.a_down, r.a_up, r.total,
            slope_of, lambda slot: r.work.at[slot], r.narrow,
        )
        finish_forward(r.total, r.out_v, r.out_inverse)
        exchange.start("out", "seq", rows_for(r.out_v, group), r.out_all)
        outs = []
        normalize_back_all(r.cotangent_v, r.out_v, r.out_inverse, r.total)
        feed_back(
            SimpleNamespace(
                grad=r.total, low=r.low, side=r.side, hidden=r.crossed, narrow=r.narrow, up=r.up,
                down=r.down, adapter_down=r.a_down, adapter_up=r.a_up,
                slopes=slope_of, flat=r.flat, second=second,
                d_narrow=r.d_narrow, factor=1.0 / copies, active=lambda slot: r.work.at[slot],
            )
        )
        exchange.start("flat", "dp", columns_for(r.flat, replicas), r.parts)
        normalize_back_all(r.total, r.crossed, r.crossed_inverse, r.total)
        context_back(r.d_context, r.cross_out_weight, r.total)
        attend_back(cross_part, False, 0)
        outs.append(move.start(r.d_pairs_v, r.memory_pairs_grad))
        exchange.end("flat")
        r.flat_sum[...] = sum_parts(r.parts).astype(LOW)
        exchange.start("flat", "seq", lambda peer: r.flat_sum.at[peer], r.flat_own)
        for cut in chunks(tokens, CHUNK):
            r.total[cut, :] += contract(r.d_query[:, cut], r.query_weight[...], 0, 1)
        normalize_back_all(r.total, r.mid, r.mid_inverse, r.total)
        context_back(r.d_context, r.out_weight, r.total)
        attend_back(self_part, True, count)
        for cut in chunks(tokens, CHUNK):
            r.x[cut, :] = (
                r.total[cut, :] + contract(d_qkv[:, cut], r.qkv_weight[...], 0, 1)
            ).astype(LOW)
        outs.append(move.start(r.x, r.target_grad))
        for copy in outs:
            copy.wait()
        exchange.end("out", "flat")

    return run_kernel(
        body,
        "decoder",
        near=dict(
            marks=w.target_segments, source_marks=forward.marks_out,
            pairs_wide=forward.dec_pairs_wide, pairs=forward.dec_pairs,
        ),
        far=dict(
            target=forward.target_rows, cotangent=w.cotangent,
            memory_pairs=forward.memory_pairs, dec_qkv=w.dec_qkv,
            dec_out=w.dec_out, cross_q=w.cross_q, cross_out=w.cross_out, dec_up=w.dec_up,
            dec_down=w.dec_down, dec_adapter_down=w.dec_adapter_down,
            dec_adapter_up=w.dec_adapter_up,
        ),
        near_outs=dict(d_pairs=((PAD, 2 * width), WIDE)),
        far_outs=dict(
            out_all=((group, share, width), LOW), target_grad=((tokens, width), LOW),
            memory_pairs_grad=((2 * width, keys), LOW),
            flat_own=(part, LOW),
        ),
        scratch=dict(
            flat=(flat, LOW), parts=((replicas, *part), LOW), flat_sum=(part, LOW),
            x=((tokens, width), LOW), cotangent_v=((tokens, width), LOW),
            qkv_weight=((width, 3 * width), LOW), out_weight=((width, width), LOW),
            query_weight=((width, width), LOW), cross_out_weight=((width, width), LOW),
            pairs_v=((2 * width, keys), LOW), a_down=((width, narrow), LOW),
            a_up=((narrow, width), LOW), up=((width, inner), LOW), down=((inner, width), LOW),
            qkv=((3 * width, tokens), LOW), context=((width, tokens), LOW),
            mid=((tokens, width), LOW), mid_inverse=((tokens, 1), WIDE),
            query=((width, tokens), LOW), cross_context=((width, tokens), LOW),
            crossed=((tokens, width), LOW), crossed_inverse=((tokens, 1), WIDE),
            out_v=((tokens, width), LOW), out_inverse=((tokens, 1), WIDE),
            slopes=((blocks * tokens, INNER), LOW), narrow=((tokens, narrow), LOW),
            low=((tokens, width), LOW), side=((tokens, width), LOW), d_narrow=((tokens, narrow), LOW),
            total=((tokens, width), WIDE), lse=((16, tokens), WIDE), cross_lse=((16, tokens), WIDE),
            d_context=((width, tokens), LOW), d_query=((width, tokens), LOW),
            d_pairs_v=((2 * width, keys), LOW),
            qx=((heads * 16, tokens), LOW), kx=((16, keys), LOW),
            scores=((2, keys, tokens), WIDE), pair_scores=((2, PAD, tokens), WIDE),
            peak=((2, 8, tokens), WIDE), dx=((heads * 16, tokens), LOW), vx=((16, keys), LOW),
            delta=((16, tokens), WIDE), dq_sum=((width, tokens), WIDE),
            work=((2, TILE, 16 * TILE), LOW),
        ),
        flops=4 * tokens * width * 11776 + 14 * tokens * (keys + tokens) * width,
        links=3 * (group - 1) + replicas - 1,
        collective=3,
    )


def encoder_feed_back(dec, forward, w, group, copies, replicas):
    tokens, width = forward.memory.shape
    inner = w.enc_up.shape[1]
    narrow = w.enc_adapter_down.shape[1]
    blocks = 1 + inner // INNER
    second, flat, part = flat_shapes(width, narrow, group, replicas)
    later = dec.target_grad.shape[0] // group

    def body(r):
        move = Mover(r.semaphores)
        firsts = [
            move.start(r.memory_pairs_grad, r.d_pairs),
            move.start(r.cross_kv, r.pair_weight),
            move.start(r.memory, r.memory_v),
        ]
        adapters = [
            move.start(r.enc_adapter_up, r.a_up),
            move.start(r.slopes.at[0], r.slopes_v.at[0]),
            move.start(r.narrow, r.narrow_v),
            move.start(r.mid, r.mid_v),
        ]
        ups = [
            move.start(r.enc_adapter_down, r.a_down),
            move.start(r.slopes.at[1:], r.slopes_v.at[1:]),
            move.start(r.enc_down, r.down),
            move.start(r.enc_up, r.up),
            move.start(r.enc_out, r.out_weight),
        ]
        links = Links(r.sent, r.arrived, {"seq": group, "dp": replicas})
        exchange = Exchange(move, links)
        me, core = links.place["seq"], lax.rem(links.place["dp"], 2)
        targets = [
            links.plan("seq", links.peer("seq", shift), r.target_grad.at[links.peer("seq", shift)], r.target_grad_all.at[me])
            for shift in range(1, group)
        ]

        def send_targets():
            for copy in targets:
                copy.start()

        pl.when(core == 0)(send_targets)
        own_target = move.start(r.target_grad.at[me], r.own_target)
        for copy in firsts:
            copy.wait()
        for cut in chunks(tokens, CHUNK):
            grad = contract(r.d_pairs[:, cut], r.pair_weight[...], 0, 1)
            r.total[cut, :] = normalize_back(
                grad, r.memory_v[cut, :].astype(WIDE), r.memory_inverse[cut, :]
            )
        for copy in adapters:
            copy.wait()

        def send():
            exchange.start("flat", "dp", columns_for(r.flat, replicas), r.parts)
            pl.when(core == 1)(send_targets)
            own_target.wait()
            targets.append(move.start(r.own_target, r.target_grad_all.at[me]))
            for copy in ups:
                copy.wait()

        feed_back(
            SimpleNamespace(
                grad=r.total, low=r.low, side=r.side, hidden=r.mid_v, narrow=r.narrow_v, up=r.up,
                down=r.down, adapter_down=r.a_down, adapter_up=r.a_up,
                slopes=lambda index: r.slopes_v.at[index], flat=r.flat, second=second,
                d_narrow=r.d_narrow, factor=1.0 / copies, active=lambda slot: r.active.at[slot],
            ),
            send,
        )
        normalize_back_all(r.total, r.mid_v, r.mid_inverse, r.low)
        outs = [move.start(r.low, r.summed_grad)]
        context_back(r.d_context_v, r.out_weight, r.low)
        outs.append(move.start(r.d_context_v, r.d_context))
        for copy in outs:
            copy.wait()
        exchange.end("flat")
        for copy in targets:
            copy.wait()

    return run_kernel(
        body,
        "encoder_feed_back",
        near=dict(mid_inverse=forward.mid_inverse, memory_inverse=forward.memory_inverse),
        far=dict(
            target_grad=dec.target_grad.reshape(group, -1, width),
            memory_pairs_grad=dec.memory_pairs_grad, memory=forward.memory, mid=forward.mid,
            slopes=forward.slopes, narrow=forward.narrow, cross_kv=w.cross_kv,
            enc_out=w.enc_out, enc_up=w.enc_up, enc_down=w.enc_down,
            enc_adapter_down=w.enc_adapter_down, enc_adapter_up=w.enc_adapter_up,
        ),
        near_outs={},
        far_outs=dict(
            summed_grad=((tokens, width), LOW), d_context=((width, tokens), LOW),
            parts=((replicas, *part), LOW),
            target_grad_all=((group, later, width), LOW),
        ),
        scratch=dict(
            own_target=((later, width), LOW),
            flat=(flat, LOW), d_pairs=((2 * width, tokens), LOW), pair_weight=((width, 2 * width), LOW),
            memory_v=((tokens, width), LOW), mid_v=((tokens, width), LOW),
            slopes_v=((blocks, tokens, INNER), LOW), narrow_v=((tokens, narrow), LOW),
            out_weight=((width, width), LOW), a_down=((width, narrow), LOW),
            a_up=((narrow, width), LOW), up=((width, inner), LOW), down=((inner, width), LOW),
            low=((tokens, width), LOW), side=((tokens, width), LOW), d_narrow=((tokens, narrow), LOW),
            active=((2, CHUNK, inner), LOW), total=((tokens, width), WIDE), d_context_v=((width, tokens), LOW),
        ),
        flops=2 * tokens * width * 9728,
        links=group - 1 + replicas - 1,
        collective=1,
    )


def split_product(left, right, left_dim, right_dim):
    return total_of(
        [contract(part.astype(LOW), right, left_dim, right_dim) for part in split_three(left)]
    )


def prefix_back(p):
    count, group = p.prefix.shape[0], p.group
    d_pairs, hidden = p.d_pairs, p.hidden[...]
    units, width = hidden.shape[1], p.prefix.shape[1]
    p.tall_hidden[...] = hidden.T
    share = units // group
    own = p.tall_hidden[pl.ds(pl.multiple_of(p.place * share, share), share), :]
    parts = split_three(d_pairs)
    p.out_grad[...] = total_of(
        [split_product(own, part.astype(LOW), 1, 0) for part in parts]
    )
    d_hidden = split_product(d_pairs, p.second[...], 1, 1) * (1.0 - hidden * hidden)
    p.wide_prefix[...] = jnp.zeros(p.wide_prefix.shape, WIDE)
    p.wide_prefix[:count, :] = p.prefix[...].astype(WIDE)
    p.tall_prefix[...] = p.wide_prefix[...].T
    share = width // group
    own = p.tall_prefix[pl.ds(pl.multiple_of(p.place * share, share), share), :].astype(LOW)
    p.in_grad[...] = total_of([contract(own, part.astype(LOW), 1, 0) for part in split_three(d_hidden)])
    p.embed_grad[...] = split_product(d_hidden, p.first_share[...], 1, 1)[:count]


def block_order(place):
    return [1 + is_inner(place), 3, 2 - is_inner(place), 0]


def encoder_attend_back(feed, dec, forward, w, group, copies, replicas):
    tokens, width = feed.summed_grad.shape
    share = tokens // group
    count = w.enc_prefix.shape[0]
    narrow, units = w.enc_adapter_down.shape[1], w.enc_prefix_in.shape[1]
    second, _, part = flat_shapes(width, narrow, group, replicas)
    heads = width // HEAD
    tile = TILE
    blocks, per = tokens // tile, tile // share
    grains = [
        (layer, 8 * row, 128 * column)
        for layer in range(2) for column in range(2 * width // 128) for row in range(PAD // 8)
    ]
    depth = -(-len(grains) // (group * replicas))

    def grain_place(number):
        device, inside = number // depth, number % depth
        return (device // group, device % group, slice(8 * inside, 8 * inside + 8))
    layers = ("enc", "dec")

    def body(r):
        move = Mover(r.semaphores)
        me = lax.axis_index("seq")
        sums = move.start(r.enc_parts, r.enc_parts_v)
        slots = block_order(me // per)
        near = near_order(me // per)
        begins = [pl.multiple_of(slot * tile, tile) for slot in slots]
        inner = is_inner(me // per)
        goals = [near[1] + inner * (near[2] - near[1]), near[3], near[2] + inner * (near[1] - near[2]), near[0]]
        firsts, lasts = [], []
        for stage, begin in enumerate(begins):
            goal, origin = slice(stage * tile, (stage + 1) * tile), pl.ds(begin, tile)
            firsts.append(move.start(r.qkv.at[:, origin], r.qkv_v.at[:, goal]))
            firsts.append(move.start(r.d_context.at[:, origin], r.d_context_v.at[:, goal]))
            firsts.append(move.start(r.context.at[:, origin], r.context_v.at[:, goal]))
            lasts.append(move.start(r.summed_grad.at[origin, :], r.summed_v.at[goal, :]))
            r.lse_v[:, goal] = r.lse[:, origin]
        totals = move.start(r.dec_own, r.dec_own_v)
        marks = jnp.concatenate([r.marks[:, pl.ds(begin, tile)] for begin in begins], 1)
        lasts += [
            move.start(r.enc_qkv, r.qkv_weight),
            move.start(r.enc_prefix_out, r.enc_second), move.start(r.dec_prefix_out, r.dec_second),
        ]
        size = width // group
        first_rows = pl.ds(pl.multiple_of(me * size, size), size)
        lasts.append(move.start(r.enc_prefix_in.at[first_rows, :], r.enc_first))
        lasts.append(move.start(r.dec_prefix_in.at[first_rows, :], r.dec_first))

        links = Links(r.sent, r.arrived, {"seq": group, "dp": replicas})
        exchange = Exchange(move, links)

        def send_total(name, own, mine, total):
            mine[...] = sum_parts(own).astype(LOW)
            exchange.start(name, "dp", lambda peer: mine, total)

        def ready(step):
            if step == 0:
                r.pair_out[...] = jnp.zeros(r.pair_out.shape, WIDE)
                for number, (layer, row, column) in enumerate(grains):
                    origin = (r.enc_d_pairs, r.dec_d_pairs)[layer]
                    r.pair_out[grain_place(number)] = origin[row : row + 8, column : column + 128]
                exchange.start("pairs", "dp", lambda peer: r.pair_out.at[peer], r.pair_parts)
                totals.wait()
                send_total("dec", r.dec_own_v, r.dec_mine, r.dec_total)
            elif step == 1:
                exchange.end("pairs")
                r.pair_sum[...] = sum_parts(r.pair_parts)
                exchange.start("pairs", "seq", lambda peer: r.pair_sum.at[peer], r.pair_own)
            else:
                exchange.end("pairs")
                r.pair_mine[...] = sum_parts(r.pair_own)
                exchange.start("pairs", "seq", lambda peer: r.pair_mine, r.pair_row)

        sent = []

        def staged(stage, cut):
            r.d_qkv[:width, :] = (r.dq_sum[:, cut] * SCALE).astype(LOW)
            r.d_qkv[width : 2 * width, :] = (r.dk_sum[:, cut] * (1.0 / LOG2E)).astype(LOW)
            r.d_qkv[2 * width :, :] = r.dv_sum[:, cut].astype(LOW)
            if stage == 0:
                for copy in lasts:
                    copy.wait()
            r.summed_v[cut, :] = (
                r.summed_v[cut, :].astype(WIDE) + contract(r.d_qkv[...], r.qkv_weight[...], 0, 1)
            ).astype(LOW)
            inside = lax.rem(me, per)
            last = stage == blocks - 1
            for turn in range(per):
                number = lax.rem(inside + turn, per)
                origin = r.summed_v.at[
                    pl.ds(pl.multiple_of(stage * tile + number * share, share), share), :
                ]
                if last and turn == 0:
                    sent.append(move.start(origin, r.source_grad.at[me]))
                else:
                    target = goals[stage] * per + number
                    sent.append(links.start_to("seq", target, origin, r.source_grad.at[me]))
            if stage == 0:
                exchange.end("enc", "pairs")
                send_total("enc", r.enc_own, r.enc_mine, r.enc_total)
                exchange.start("pairs", "dp", lambda peer: r.pair_row, r.pair_total)

        sums.wait()
        r.enc_sum[...] = sum_parts(r.enc_parts_v).astype(LOW)
        exchange.start("enc", "seq", lambda peer: r.enc_sum.at[peer], r.enc_own)
        for copy in firsts:
            copy.wait()
        attend_back(
            SimpleNamespace(
                q=r.qkv_v, k=r.qkv_v, v=r.qkv_v, q0=0, k0=width, v0=2 * width,
                q_marks=marks, k_marks=marks, pairs=r.enc_pairs, context=r.context_v, lse=r.lse_v,
                d_context=r.d_context_v, d_pairs=r.enc_d_pairs, factor=1.0 / copies, qx=r.qx, kx=r.kx,
                dx=r.dx, vx=r.vx, delta=r.delta, dq_sum=r.dq_sum, dk_sum=r.dk_sum, dv_sum=r.dv_sum,
                work=r.work,
            ),
            False,
            count,
            ready,
            staged,
        )
        exchange.end("pairs")
        for number, (layer, row, column) in enumerate(grains):
            r.whole[layer, row : row + 8, column : column + 128] = r.pair_total[grain_place(number)]
        for number, layer in enumerate(layers):
            prefix_back(
                SimpleNamespace(
                    d_pairs=r.whole[number], group=group, place=me,
                    hidden=getattr(r, f"{layer}_hidden"), prefix=getattr(r, f"{layer}_prefix"),
                    second=getattr(r, f"{layer}_second"), first_share=getattr(r, f"{layer}_first"),
                    tall_hidden=r.tall_hidden, tall_prefix=r.tall_prefix, wide_prefix=r.wide_prefix,
                    embed_grad=getattr(r, f"{layer}_embed"), in_grad=getattr(r, f"{layer}_in"),
                    out_grad=getattr(r, f"{layer}_out_grad"),
                )
            )
            exchange.end(layer)
            total = getattr(r, f"{layer}_total")
            total = jnp.concatenate([total[place].astype(WIDE) for place in range(replicas)], 0)
            for kind, first in (("down", 0), ("up", second)):
                out = getattr(r, f"{layer}_{kind}_grad_all")
                out[...] = unpack(total, first, out.shape)
        for copy in sent:
            copy.wait()

    near_outs = {}
    for layer in layers:
        near_outs[f"{layer}_embed"] = ((count, width // group), WIDE)
        near_outs[f"{layer}_in"] = ((width // group, units), WIDE)
        near_outs[f"{layer}_out_grad"] = ((units // group, 2 * width), WIDE)
        near_outs[f"{layer}_down_grad_all"] = ((width // group, narrow), WIDE)
        near_outs[f"{layer}_up_grad_all"] = ((narrow // group, width), WIDE)
    scratch = {}
    scratch["enc_parts_v"] = ((replicas, *part), LOW)
    scratch["enc_sum"] = scratch["enc_own"] = scratch["dec_own_v"] = (part, LOW)
    for layer in layers:
        scratch[f"{layer}_mine"] = (part[1:], LOW)
        scratch[f"{layer}_total"] = ((replicas, *part[1:]), LOW)
        scratch[f"{layer}_second"] = ((units, 2 * width), LOW)
        scratch[f"{layer}_first"] = ((width // group, units), LOW)
    own = (group, 8 * depth, 128)
    for name in ("pair_out", "pair_parts", "pair_total"):
        scratch[name] = ((replicas, *own), WIDE)
    for name in ("pair_sum", "pair_own", "pair_row"):
        scratch[name] = (own, WIDE)
    scratch["pair_mine"] = (own[1:], WIDE)
    scratch["whole"] = ((2, PAD, 2 * width), WIDE)
    scratch["enc_d_pairs"] = ((PAD, 2 * width), WIDE)
    scratch["tall_hidden"] = ((units, PAD), WIDE)
    scratch["wide_prefix"] = ((PAD, width), WIDE)
    scratch["tall_prefix"] = ((width, PAD), WIDE)
    for name in ("dq_sum", "dk_sum", "dv_sum"):
        scratch[name] = ((width, tokens), WIDE)
    return run_kernel(
        body,
        "encoder_attend_back",
        near=dict(
            marks=forward.marks_out, enc_pairs=forward.enc_pairs, lse=forward.lse,
            dec_d_pairs=dec.d_pairs, enc_hidden=forward.enc_hidden, dec_hidden=forward.dec_hidden,
            enc_prefix=w.enc_prefix, dec_prefix=w.dec_prefix,
        ),
        far=dict(
            qkv=forward.qkv, d_context=feed.d_context, context=forward.context,
            enc_qkv=w.enc_qkv, summed_grad=feed.summed_grad,
            enc_parts=feed.parts, dec_own=dec.flat_own,
            enc_prefix_in=w.enc_prefix_in, enc_prefix_out=w.enc_prefix_out,
            dec_prefix_in=w.dec_prefix_in, dec_prefix_out=w.dec_prefix_out,
        ),
        near_outs=near_outs,
        far_outs=dict(source_grad=((group, share, width), LOW)),
        scratch=dict(
            qkv_v=((3 * width, tokens), LOW), d_context_v=((width, tokens), LOW),
            context_v=((width, tokens), LOW), qkv_weight=((width, 3 * width), LOW),
            summed_v=((tokens, width), LOW), d_qkv=((3 * width, tile), LOW), lse_v=((16, tokens), WIDE),
            qx=((heads * 16, tokens), LOW), kx=((16, tokens), LOW),
            dx=((heads * 16, tokens), LOW), vx=((16, tokens), LOW), delta=((16, tokens), WIDE),
            work=((2, TILE, 14 * TILE), LOW), **scratch,
        ),
        flops=2 * tokens * width * 2304 + 20 * tokens * tokens * width,
        links=3 * (group - 1) + 4 * (replicas - 1) + group - 1,
        collective=2,
    )


def finish(attended, feed, dec, copies):
    small = [name for name in vars(attended) if name != "source_grad"]
    shape = attended.source_grad.shape
    later = dec.out_all.shape

    def body(r):
        move = Mover(r.semaphores)
        ins = [
            move.start(r.source_grad, r.source_v),
            move.start(r.target_grad, r.target_v),
        ]
        outs = []
        relays = [
            (move.start(r.out_all.at[place * copies], r.out_v.at[place]), r.out_v.at[place], r.out.at[place])
            for place in range(later[0] // copies)
        ]
        for name in small:
            via = getattr(r, name + "_v")
            relays.append((move.start(getattr(r, name + "_in"), via), via, getattr(r, name)))
        for copy, via, goal in relays:
            copy.wait()
            outs.append(move.start(via, goal))
        for copy, origin, wide, goal in (
            (ins[0], r.source_v, r.source_w, r.source_out), (ins[1], r.target_v, r.target_w, r.target_out)
        ):
            copy.wait()
            for place in range(wide.shape[0]):
                wide[place] = origin[place * copies].astype(WIDE)
                outs.append(move.start(wide.at[place], goal.at[place]))
        for copy in outs:
            copy.wait()

    rows = shape[0] // copies
    return run_kernel(
        body,
        "finish",
        near={},
        far=dict(
            source_grad=attended.source_grad, target_grad=feed.target_grad_all, out_all=dec.out_all,
            **{name + "_in": getattr(attended, name) for name in small},
        ),
        near_outs={},
        far_outs=dict(
            out=((rows, *later[1:]), LOW), source_out=((rows, *shape[1:]), WIDE),
            target_out=((rows, *later[1:]), WIDE),
            **{name: (getattr(attended, name).shape, WIDE) for name in small},
        ),
        scratch=dict(
            source_v=(shape, LOW), source_w=((rows, *shape[1:]), WIDE), target_v=(later, LOW),
            target_w=((rows, *later[1:]), WIDE), out_v=((rows, *later[1:]), LOW),
            **{name + "_v": (getattr(attended, name).shape, WIDE) for name in small},
        ),
        flops=0,
    )


NAMES = (
    "source",
    "target",
    "source_segments",
    "target_segments",
    "cotangent",
    "enc_qkv",
    "enc_out",
    "enc_up",
    "enc_down",
    "dec_qkv",
    "dec_out",
    "cross_q",
    "cross_kv",
    "cross_out",
    "dec_up",
    "dec_down",
    "enc_prefix",
    "enc_prefix_in",
    "enc_prefix_out",
    "enc_adapter_down",
    "enc_adapter_up",
    "dec_prefix",
    "dec_prefix_in",
    "dec_prefix_out",
    "dec_adapter_down",
    "dec_adapter_up",
)


def shards(*operands, group, replicas):
    w = SimpleNamespace(**dict(zip(NAMES, operands)))
    copies = group // w.source.shape[0]
    forward = encoder_forward(w, group, copies)
    dec = decoder(forward, w, group, copies, replicas)
    feed = encoder_feed_back(dec, forward, w, group, copies, replicas)
    attended = encoder_attend_back(feed, dec, forward, w, group, copies, replicas)
    done = finish(attended, feed, dec, copies)
    results = [done.out, done.source_out, done.target_out]
    for layer in ("enc", "dec"):
        for name in ("embed", "in", "out_grad", "down_grad_all", "up_grad_all"):
            results.append(getattr(done, f"{layer}_{name}"))
    return tuple(results)


def solution(mesh):
    rows = P("dp", "seq", None)
    marks = P("dp", None)
    in_specs = (rows, rows, marks, marks, rows) + (P(),) * 21
    across, down = P(None, "seq"), P("seq", None)
    layer = (across, down, down, down, down)
    return jax.shard_map(
        functools.partial(shards, group=mesh.shape["seq"], replicas=mesh.shape["dp"]),
        mesh=mesh,
        in_specs=in_specs,
        out_specs=(rows, rows, rows) + layer + layer,
        check_vma=False,
    )
```

```python
import functools
import math
from types import SimpleNamespace

import jax
import jax.numpy as jnp
from jax import lax
from jax.experimental import pallas as pl
from jax.experimental.pallas import tpu as pltpu
from jax.sharding import PartitionSpec as P

HEAD = 64
GROUP = 4
PAD = 32
BIG = 2.0**100
LOG2E = math.log2(math.e)
SCALE = 1.0 / math.sqrt(HEAD)
VMEM_BYTES = 60 * 2**20
CHUNK = 256
TILE = 256
COLUMNS = 512
TOGETHER = 6
UNITS = 4
INNER = 512
LOW = jnp.bfloat16
WIDE = jnp.float32


def contract(left, right, left_dim, right_dim):
    return lax.dot_general(
        left, right, (((left_dim,), (right_dim,)), ((), ())), preferred_element_type=WIDE
    )


def rows_at(index, size, base=0):
    return pl.ds(pl.multiple_of(base + index * size, size), size)


def chunks(size, step):
    step = min(step, size)
    return [slice(start, start + step) for start in range(0, size, step)]


def total_of(values):
    return functools.reduce(lambda left, right: left + right, values)


def normalize(value):
    centered = value - jnp.mean(value, axis=-1, keepdims=True)
    inverse = lax.rsqrt(jnp.mean(centered * centered, axis=-1, keepdims=True) + 1e-05)
    return (centered * inverse, inverse)


def normalize_back(gradient, normed, inverse):
    return (
        gradient
        - jnp.mean(gradient, axis=-1, keepdims=True)
        - normed * jnp.mean(gradient * normed, axis=-1, keepdims=True)
    ) * inverse


def gelu_both(value):
    scale = math.sqrt(2.0 / math.pi)
    square = value * value
    half = 0.5 + 0.5 * jnp.tanh(value * (scale + (scale * 0.044715) * square))
    active = value * half
    slope = half + active * (1.0 - half) * (2.0 * scale + (6.0 * scale * 0.044715) * square)
    return (active, slope)


class Mover:
    def __init__(self, semaphores):
        self.semaphores = semaphores
        self.used = 0

    def start(self, origin, goal):
        copy = pltpu.make_async_copy(origin, goal, self.semaphores.at[self.used])
        self.used += 1
        copy.start()
        return copy


def run_kernel(body, name, near, far, near_outs, far_outs, scratch, flops, links=0, collective=None):
    in_names = list(near) + list(far)
    out_names = list(near_outs) + list(far_outs)
    names = in_names + out_names + list(scratch) + ["semaphores"]
    link_scratch = []
    remote = {}
    if collective is not None:
        names += ["sent", "arrived"]
        link_scratch = [pltpu.SemaphoreType.DMA((links,)), pltpu.SemaphoreType.DMA((links,))]
        remote = dict(collective_id=collective, has_side_effects=True)

    def kernel(*refs):
        body(SimpleNamespace(**dict(zip(names, refs))))

    near_spec = pl.BlockSpec(memory_space=pltpu.VMEM)
    far_spec = pl.BlockSpec(memory_space=pl.ANY)
    results = pl.pallas_call(
        kernel,
        out_shape=tuple(
            jax.ShapeDtypeStruct(*out) for out in (*near_outs.values(), *far_outs.values())
        ),
        in_specs=[near_spec] * len(near) + [far_spec] * len(far),
        out_specs=tuple([near_spec] * len(near_outs) + [far_spec] * len(far_outs)),
        scratch_shapes=[pltpu.VMEM(*shape) for shape in scratch.values()]
        + [pltpu.SemaphoreType.DMA((80,))]
        + link_scratch,
        compiler_params=pltpu.CompilerParams(vmem_limit_bytes=VMEM_BYTES, **remote),
        cost_estimate=pl.CostEstimate(flops=flops, bytes_accessed=2**24, transcendentals=0),
        name=name,
    )(*near.values(), *far.values())
    return SimpleNamespace(**dict(zip(out_names, results)))


class Links:
    def __init__(self, sent, arrived, groups):
        self.sent, self.arrived = sent, arrived
        self.used = 0
        self.place = {axis: lax.axis_index(axis) for axis in ("dp", "seq")}
        self.sizes = groups
        barrier = pltpu.get_barrier_semaphore()
        peers = 0
        for axis, size in groups.items():
            for shift in range(1, size):
                pl.semaphore_signal(
                    barrier, inc=1, device_id=self.device(axis, shift), device_id_type=pl.DeviceIdType.MESH
                )
                peers += 1
        pl.semaphore_wait(barrier, peers)

    def peer(self, axis, shift):
        return lax.rem(self.place[axis] + shift, self.sizes[axis])

    def device(self, axis, shift):
        return self.device_at(axis, self.peer(axis, shift))

    def device_at(self, axis, index):
        return (index, self.place["seq"]) if axis == "dp" else (self.place["dp"], index)

    def start(self, axis, shift, origin, goal):
        return self.start_to(axis, self.peer(axis, shift), origin, goal)

    def start_to(self, axis, index, origin, goal):
        copy = self.plan(axis, index, origin, goal)
        copy.start()
        return copy

    def plan(self, axis, index, origin, goal):
        copy = pltpu.make_async_remote_copy(
            src_ref=origin,
            dst_ref=goal,
            send_sem=self.sent.at[self.used],
            recv_sem=self.arrived.at[self.used],
            device_id=self.device_at(axis, index),
            device_id_type=pl.DeviceIdType.MESH,
        )
        self.used += 1
        return copy

    def scatter(self, axis, pick, goal):
        return [
            self.start(axis, shift, pick(self.peer(axis, shift)), goal)
            for shift in range(1, self.sizes[axis])
        ]


class Exchange:
    def __init__(self, move, links):
        self.move, self.links = move, links
        self.place, self.sizes = links.place, links.sizes
        self.open = {}

    def start(self, name, axis, pick, goal, via=None):
        mine = self.place[axis]
        copies = self.links.scatter(axis, pick, goal.at[mine])
        if via is None:
            copies.append(self.move.start(pick(mine), goal.at[mine]))
        else:
            self.move.start(pick(mine), via).wait()
            copies.append(self.move.start(via, goal.at[mine]))
        self.open[name] = copies

    def end(self, *names):
        for name in names:
            for copy in self.open.pop(name):
                copy.wait()


def sum_parts(parts):
    return total_of([parts[part].astype(WIDE) for part in range(parts.shape[0])])


def rows_for(ref, count):
    size = ref.shape[0] // count
    return lambda place: ref.at[pl.ds(pl.multiple_of(place * size, size), size), :]


def split_three(value):
    high = value.astype(LOW).astype(WIDE)
    rest = value - high
    middle = rest.astype(LOW).astype(WIDE)
    return (high, middle, rest - middle)


def place_rows(parts, first, shape):
    row = lax.broadcasted_iota(jnp.int32, shape, 0)
    out = jnp.zeros(shape, WIDE)
    for offset, part in enumerate(parts):
        out = jnp.where(row == first + offset, part, out)
    return out


def document_rows(segments, tokens, is_key):
    row = lax.broadcasted_iota(jnp.int32, (16, tokens), 0)
    same = row == segments
    if is_key:
        return jnp.where(row < 4, jnp.where(same, 0.0, -BIG), 0.0)
    return jnp.where(same & (row < 4), 1.0, 0.0)


def column_peak(scores, peak):
    for start in range(0, scores.shape[0], 8):
        peak = jnp.maximum(peak, scores[start : start + 8])
    return peak


def from_column(value, low):
    if low == 0:
        return value
    return jnp.concatenate([jnp.zeros((value.shape[0], low), value.dtype), value], 1)


def attend(a, causal, prefix, entries=None):
    queries, keys = a.q.shape[1], a.k.shape[1]
    width = a.context.shape[0]
    heads = width // HEAD
    tile = min(256, keys)
    tiles = keys // tile
    a.qx[:16, :queries] = document_rows(a.q_marks, queries, False).astype(LOW)
    a.kx[:, :keys] = document_rows(a.k_marks, keys, True).astype(LOW)
    if entries is None:
        entries = [
            (own, [part for part in range(tiles) if not (causal and part * tile >= own.stop)], prefix > 0, "whole")
            for own in chunks(queries, COLUMNS)
        ]

    def front(head, slot, entry, work):
        own, parts, sees_prefix, _ = entry
        start = own.start
        query = jnp.concatenate([a.q[rows_at(head, HEAD, a.q0), own], a.qx[:16, own]], 0)
        peak = jnp.full((8, own.stop - start), -4.0 * BIG, WIDE)
        if sees_prefix:
            scores = contract(a.pair_keys[rows_at(head, HEAD), :], query[:HEAD], 0, 0)
            row = lax.broadcasted_iota(jnp.int32, scores.shape, 0)
            scores = jnp.where(row < prefix, scores, -BIG)
            a.pair_scores[slot, :, own] = scores
            peak = column_peak(scores, peak)
        for part in parts:
            cut = slice(part * tile, (part + 1) * tile)
            key = jnp.concatenate([a.k[rows_at(head, HEAD, a.k0), cut], a.kx[:, cut]], 0)
            scores = contract(key, query, 0, 0)
            if causal and cut.stop > start:
                place = lax.broadcasted_iota(jnp.int32, scores.shape, 0) + (cut.start - start)
                scores = jnp.where(
                    place <= lax.broadcasted_iota(jnp.int32, scores.shape, 1), scores, -BIG
                )
            a.scores[slot, cut, own] = scores
            peak = column_peak(scores, peak)
            work(part)
        a.peak[slot, :, own] = peak

    def step(head, following, slot):
        for entry in entries:
            own, _, sees_prefix, mode = entry
            peak = jnp.max(a.peak[slot, :, own], 0, keepdims=True)
            context = []
            if mode == "merge":
                before = a.lse[pl.ds(head, 1), own]
                peak = jnp.maximum(peak, before)
                context.append(a.partial[rows_at(head, HEAD + 16), own] * jnp.exp2(before - peak))
            if sees_prefix:
                weights = jnp.exp2(a.pair_scores[slot, :, own] - peak).astype(LOW)
                value = jnp.concatenate(
                    [a.pair_values[rows_at(head, HEAD), :], jnp.ones((16, PAD), LOW)], 0
                )
                context.append(contract(value, weights, 1, 0))

            def work(part):
                cut = slice(part * tile, (part + 1) * tile)
                weights = jnp.exp2(a.scores[slot, cut, own] - peak).astype(LOW)
                value = jnp.concatenate(
                    [a.v[rows_at(head, HEAD, a.v0), cut], jnp.ones((16, tile), LOW)], 0
                )
                context.append(contract(value, weights, 1, 0))

            front(following, 1 - slot, entry, work)
            summed = total_of(context)
            if mode == "save":
                a.partial[rows_at(head, HEAD + 16), own] = summed
                a.lse[pl.ds(head, 1), own] = peak
            else:
                total = summed[HEAD : HEAD + 1]
                a.context[rows_at(head, HEAD), own] = (summed[:HEAD] * (1.0 / total)).astype(LOW)
                a.lse[pl.ds(head, 1), own] = peak + jnp.log2(total)

    for entry in entries:
        front(0, 0, entry, lambda part: None)

    def several(index, carry):
        for number in range(TOGETHER):
            head = TOGETHER * index + number
            step(head, jnp.minimum(head + 1, heads - 1), number % 2)
        return carry

    lax.fori_loop(0, heads // TOGETHER, several, 0)


def block_diagonal(pairs, group, first):
    wide = GROUP * HEAD
    rows = pairs[:, first + group * wide : first + (group + 1) * wide]
    column = lax.broadcasted_iota(jnp.int32, rows.shape, 1)
    parts = [
        jnp.where((column >= member * HEAD) & (column < (member + 1) * HEAD), rows.astype(WIDE), 0.0)
        for member in range(GROUP)
    ]
    return jnp.concatenate(parts, 0).astype(LOW)


def own_columns(grads):
    column = lax.broadcasted_iota(jnp.int32, (PAD, GROUP * HEAD), 1)
    out = jnp.zeros((PAD, GROUP * HEAD), WIDE)
    for member in range(GROUP):
        own = (column >= member * HEAD) & (column < (member + 1) * HEAD)
        out = jnp.where(own, grads[member * PAD : (member + 1) * PAD], out)
    return out


def attend_back(a, causal, prefix, ready=None, staged=None):
    queries, keys = a.q.shape[1], a.k.shape[1]
    width = a.context.shape[0]
    heads = width // HEAD
    tiles = keys // TILE
    row = lax.broadcasted_iota(jnp.int32, (16, keys), 0)
    a.kx[:, :keys] = jnp.where(
        (row >= 4) & (row < 7), 1.0, document_rows(a.k_marks, keys, True)
    ).astype(LOW)
    a.vx[:, :keys] = jnp.where(row < 3, 1.0, 0.0).astype(LOW)
    documents = document_rows(a.q_marks, queries, False)

    def prepare(head, carry):
        rows = rows_at(head, HEAD)
        delta = jnp.sum(
            a.d_context[rows, :].astype(WIDE) * a.context[rows, :].astype(WIDE),
            axis=0,
            keepdims=True,
        )
        a.delta[pl.ds(head, 1), :queries] = delta
        a.dx[rows_at(head, 16), :queries] = place_rows(
            split_three(-delta), 0, (16, queries)
        ).astype(LOW)
        minus = split_three(-a.lse[pl.ds(head, 1), :])
        a.qx[rows_at(head, 16), :queries] = (
            documents + place_rows(minus, 4, (16, queries))
        ).astype(LOW)
        return carry

    lax.fori_loop(0, heads, prepare, 0)

    if prefix:
        for group in range(heads // GROUP):
            start = group * GROUP * HEAD
            own = slice(start, start + GROUP * HEAD)
            query = a.q[a.q0 + start : a.q0 + start + GROUP * HEAD, :]
            grad = a.d_context[own, :]
            pair_keys = block_diagonal(a.pairs[...], group, 0)
            pair_values = block_diagonal(a.pairs[...], group, width)
            scores = contract(pair_keys, query, 1, 0)
            gains = contract(pair_values, grad, 1, 0)
            chances, changes = [], []
            for member in range(GROUP):
                head = group * GROUP + member
                part = slice(member * PAD, (member + 1) * PAD)
                chance = jnp.exp2(scores[part] - a.lse[head : head + 1, :])
                place = lax.broadcasted_iota(jnp.int32, chance.shape, 0)
                chance = jnp.where(place < prefix, chance, 0.0)
                chances.append(chance)
                changes.append(chance * (gains[part] - a.delta[head : head + 1, :queries]))
            chances = jnp.concatenate(chances, 0).astype(LOW)
            changes = jnp.concatenate(changes, 0).astype(LOW)
            a.dq_sum[own, :queries] = contract(pair_keys, changes, 0, 0)
            a.d_pairs[:, own] = own_columns(contract(changes, query, 1, 1)) * (a.factor / LOG2E)
            a.d_pairs[:, width + start : width + start + GROUP * HEAD] = (
                own_columns(contract(chances, grad, 1, 1)) * a.factor
            )
    else:
        a.dq_sum[:, :queries] = jnp.zeros((width, queries), WIDE)
    if ready is not None:
        ready(0)


    def span(part):
        return slice(part * TILE, (part + 1) * TILE)

    def place_of(number, kind):
        return span(2 * number + kind)

    def front(head, own, cut, slot, number):
        query = jnp.concatenate([a.q[rows_at(head, HEAD, a.q0), own], a.qx[rows_at(head, 16), own]], 0)
        key = jnp.concatenate([a.k[rows_at(head, HEAD, a.k0), cut], a.kx[:, cut]], 0)
        scores = contract(query, key, 0, 0)
        if causal and own == cut:
            place = lax.broadcasted_iota(jnp.int32, scores.shape, 1)
            scores = jnp.where(place <= lax.broadcasted_iota(jnp.int32, scores.shape, 0), scores, -BIG)
        grad = jnp.concatenate([a.d_context[rows_at(head, HEAD), own], a.dx[rows_at(head, 16), own]], 0)
        value = jnp.concatenate([a.v[rows_at(head, HEAD, a.v0), cut], a.vx[:, cut]], 0)
        gains = contract(grad, value, 0, 0)
        chance = jnp.exp2(scores)
        a.work[slot, :, place_of(number, 0)] = chance.astype(LOW)
        a.work[slot, :, place_of(number, 1)] = (chance * gains).astype(LOW)

    def run(pieces, together, add):
        unit = [(offset, own, cut) for offset in range(together) for own, cut in pieces]

        def begin(index, slot, number):
            offset, own, cut = unit[number]
            front(index * together + offset, own, cut, slot, number)

        def mix(index, slot, following):
            by_key, by_query = {}, {}
            for number, (offset, own, cut) in enumerate(unit):
                head = index * together + offset
                rows = rows_at(head, HEAD)
                left = unit[number + 1 :]
                chances = a.work[slot, :, place_of(number, 0)]
                changes = a.work[slot, :, place_of(number, 1)]
                pair = by_key.setdefault((offset, cut.start), [])
                d_value = contract(a.d_context[rows, own], chances, 1, 0)
                pair.append((contract(a.q[rows_at(head, HEAD, a.q0), own], changes, 1, 0), d_value))
                begin(following, 1 - slot, number)
                d_query = by_query.setdefault((offset, own.start), [])
                d_query.append(contract(a.k[rows_at(head, HEAD, a.k0), cut], changes, 1, 1))
                if not any((other, keys_.start) == (offset, cut.start) for other, _, keys_ in left):
                    add(head, cut, *(total_of(parts) for parts in zip(*pair)))
                if not any((other, queries_.start) == (offset, own.start) for other, queries_, _ in left):
                    a.dq_sum[rows, own] += total_of(d_query)

        count = heads // together
        turn = next(size for size in (UNITS, 6, 4, 2) if count % size == 0)

        def several(index, carry):
            for number in range(turn):
                place = turn * index + number
                mix(place, number % 2, jnp.minimum(place + 1, count - 1))
            return carry

        for number in range(len(unit)):
            begin(0, 0, number)
        return several, count // turn

    if staged is not None:
        for stage in range(tiles):
            pieces = [(span(other), span(stage)) for other in range(stage + 1, tiles)]
            pieces += [(span(stage), span(other)) for other in range(stage, tiles)]

            def add(head, cut, d_key, d_value):
                rows = rows_at(head, HEAD)
                if stage == 0:
                    a.dk_sum[rows, cut] = d_key
                    a.dv_sum[rows, cut] = d_value
                else:
                    a.dk_sum[rows, cut] += d_key
                    a.dv_sum[rows, cut] += d_value

            step, steps = run(pieces, {1: heads // 2, 3: 2}.get(len(pieces), 1), add)
            cuts = [0, steps // 3, 2 * steps // 3, steps] if stage == 0 else [0, steps]
            for number in range(len(cuts) - 1):
                lax.fori_loop(cuts[number], cuts[number + 1], step, 0)
                if number + 2 < len(cuts):
                    ready(number + 1)
            staged(stage, span(stage))
        return

    def add(head, cut, d_key, d_value):
        a.dk[rows_at(head, HEAD, a.dk0), cut] = (d_key * (1.0 / LOG2E)).astype(LOW)
        a.dv[rows_at(head, HEAD, a.dv0), cut] = d_value.astype(LOW)

    pieces = [
        (span(own), span(part))
        for part in range(tiles)
        for own in range(part if causal else 0, queries // TILE)
    ]
    step, steps = run(pieces, 2 if len(pieces) < 4 else 1, add)
    lax.fori_loop(0, steps, step, 0)
    a.dq[rows_at(0, width, a.dq0), :] = (a.dq_sum[:, :queries] * SCALE).astype(LOW)


def project_wide(out, weight, rows, scaled, place=slice(None)):
    for cut in chunks(weight.shape[1], 256):
        result = contract(weight[:, cut], rows, 0, 1)
        if cut.start < scaled:
            result = result * (SCALE * LOG2E)
        out[cut, place] = result.astype(LOW)


def add_and_normalize(hidden, context, weight, normed, inverse):
    for cut in chunks(hidden.shape[0], CHUNK):
        summed = hidden[cut, :].astype(WIDE) + contract(context[:, cut], weight[...], 0, 0)
        result, scale = normalize(summed)
        normed[cut, :] = result.astype(LOW)
        inverse[cut, :] = scale


def chunk_pipeline(tokens, make, use, steps, uses):
    count = tokens // CHUNK

    def rows_of(index):
        return rows_at(index, CHUNK)

    def body(index, slot, following):
        done = 0
        for step in range(steps):
            if following is not None:
                make(rows_of(following), 1 - slot, step)
            while done < uses and done * steps <= step * uses:
                use(rows_of(index), slot, done)
                done += 1
        while done < uses:
            use(rows_of(index), slot, done)
            done += 1

    def two(index, carry):
        body(2 * index, 0, 2 * index + 1)
        body(2 * index + 1, 1, 2 * index + 2)
        return carry

    for step in range(steps):
        make(rows_of(0), 0, step)
    if count > 2:
        lax.fori_loop(0, count // 2 - 1, two, 0)
    body(count - 2, 0, count - 1)
    body(count - 1, 1, None)


def feed_forward(hidden, up, down, adapter_down, adapter_up, total, slopes_of, active_of, narrow):
    inner = up.shape[1]
    count = inner // INNER

    def make(rows, slot, step):
        if step < count:
            cut = slice(step * INNER, (step + 1) * INNER)
            active, slope = gelu_both(contract(hidden[rows, :], up[:, cut], 1, 0))
            slopes_of(step + 1)[rows, :] = slope.astype(LOW)
        else:
            cut = slice(inner, inner + INNER)
            active, slope = gelu_both(contract(hidden[rows, :], adapter_down[...], 1, 0))
            slopes_of(0)[rows, :] = slope.astype(LOW)
            narrow[rows, :] = active.astype(LOW)
            active = 4.0 * active
        active_of(slot)[:, cut] = active.astype(LOW)

    def use(rows, slot, number):
        active = active_of(slot)
        total[rows, :] = (
            hidden[rows, :].astype(WIDE)
            + contract(active[:, :inner], down[...], 1, 0)
            + contract(active[:, inner : inner + INNER], adapter_up[...], 1, 0)
        )

    chunk_pipeline(hidden.shape[0], make, use, count + 1, 1)


def finish_forward(total, normed, inverse):
    for cut in chunks(total.shape[0], CHUNK):
        result, scale = normalize(total[cut, :])
        normed[cut, :] = result.astype(LOW)
        inverse[cut, :] = scale


def pack(flat, value, first):
    size = value.shape[0] // flat.shape[0]
    for place in range(flat.shape[0]):
        for block in range(value.shape[1] // 128):
            goal = slice(first + block * size, first + (block + 1) * size)
            flat[place, goal, :] = value[
                place * size : (place + 1) * size, block * 128 : (block + 1) * 128
            ].astype(flat.dtype)


def unpack(rows, first, shape):
    parts = [
        rows[first + block * shape[0] : first + (block + 1) * shape[0]] for block in range(shape[1] // 128)
    ]
    return jnp.concatenate(parts, 1)


def flat_shapes(width, narrow, group, replicas):
    second = width // group * (narrow // 128)
    rows = second + narrow // group * (width // 128)
    return second, (group, rows, 128), (group, rows // replicas, 128)


def columns_for(flat, replicas):
    size = flat.shape[1] // replicas
    return lambda place: flat.at[:, pl.ds(pl.multiple_of(place * size, size), size), :]


def feed_back(f, send=None):
    tokens = f.hidden.shape[0]
    cuts = chunks(tokens, CHUNK)
    for cut in cuts:
        value = f.grad[cut, :]
        f.low[cut, :] = value.astype(LOW)
        f.side[cut, :] = (4.0 * value).astype(LOW)

    for cut in cuts:
        change = contract(f.side[cut, :], f.adapter_up[...], 1, 1) * f.slopes(0)[cut, :].astype(WIDE)
        f.d_narrow[cut, :] = change.astype(LOW)
    pack(f.flat, contract(f.hidden[...], f.d_narrow[...], 0, 0) * f.factor, 0)
    pack(f.flat, contract(f.narrow[...], f.side[...], 0, 0) * f.factor, f.second)
    if send is not None:
        send()

    def make(rows, slot, step):
        cut = slice(step * INNER, (step + 1) * INNER)
        change = contract(f.low[rows, :], f.down[cut, :], 1, 1) * f.slopes(step + 1)[rows, :].astype(WIDE)
        f.active(slot)[:, cut] = change.astype(LOW)

    def use(rows, slot, number):
        f.grad[rows, :] += contract(f.active(slot)[:, : f.up.shape[1]], f.up[...], 1, 1) + contract(
            f.d_narrow[rows, :], f.adapter_down[...], 1, 1
        )

    chunk_pipeline(tokens, make, use, f.up.shape[1] // INNER, 1)


def normalize_back_all(grad, normed, inverse, out):
    for cut in chunks(grad.shape[0], CHUNK):
        out[cut, :] = normalize_back(
            grad[cut, :].astype(WIDE), normed[cut, :].astype(WIDE), inverse[cut, :]
        ).astype(out.dtype)


def context_back(out, weight, grad):
    value = grad[...].astype(LOW)
    for cut in chunks(weight.shape[0], 256):
        out[cut, :] = contract(weight[cut, :], value, 1, 1).astype(LOW)


def prefix_pairs(prefix, first, second, hidden, pairs, pairs_wide):
    count = prefix.shape[0]
    hidden[...] = jnp.zeros(hidden.shape, WIDE)
    hidden[:count, :] = jnp.tanh(contract(prefix[...], first[...], 1, 0))
    parts = [part.astype(LOW) for part in split_three(hidden[...])]
    pairs[...] = total_of([contract(part, second[...], 1, 0) for part in parts]).astype(LOW)
    pairs_wide[...] = total_of([contract(second[...], part, 0, 1) for part in parts]).astype(LOW)


def near_order(place):
    return [place, place + 1 - 2 * lax.rem(place, 2), lax.rem(place + 2, 4), 3 - place]


def is_inner(place):
    return lax.rem(place // 2 + lax.rem(place, 2), 2)


def encoder_forward(w, group, copies):
    width = w.source.shape[2]
    share, later_share = w.source.shape[1], w.target.shape[1]
    tokens, later_tokens = share * group, later_share * group
    per = TILE // share
    inner = w.enc_up.shape[1]
    narrow = w.enc_adapter_down.shape[1]
    units = w.enc_prefix_in.shape[1]
    count = w.enc_prefix.shape[0]
    blocks = 1 + inner // INNER

    def body(r):
        move = Mover(r.semaphores)
        weights = [move.start(r.enc_qkv, r.qkv_weight)]
        enc_first, dec_first = r.mid_v.at[:width, :units], r.memory_v.at[:width, :units]
        enc_second, dec_second = r.up.at[:units, : 2 * width], r.up.at[:units, 2 * width : 4 * width]
        weights.append(move.start(r.enc_prefix_in, enc_first))
        weights.append(move.start(r.enc_prefix_out, enc_second))
        weights.append(move.start(r.dec_prefix_in, dec_first))
        weights.append(move.start(r.dec_prefix_out, dec_second))
        links = Links(r.sent, r.arrived, {"seq": group})
        me = links.place["seq"]
        row = me // copies
        block, inside = me // per, lax.rem(me, per)
        others = near_order(block)
        arrivals = []
        for slot, other in enumerate(others):
            goal = r.x.at[pl.ds(pl.multiple_of(slot * TILE + inside * share, share), share), :]
            arrivals.append([])
            for turn in range(per):
                target = other * per + lax.rem(inside + turn, per)
                if slot == 0 and turn == 0:
                    here = move.start(r.source.at[row], goal)
                else:
                    arrivals[slot].append(links.plan("seq", target, r.source.at[target // copies], goal))

        def send(*slots):
            for slot in slots:
                for copy in arrivals[slot]:
                    copy.start()

        pl.when(is_inner(block) == 0)(lambda: send(1, 2))
        pl.when(is_inner(block) == 1)(lambda: send(2, 1))
        send(0, 3)

        def tokens_of(place, size):
            return pl.ds(pl.multiple_of(place * size, size), size)

        def bring(origin, goal, size, via=None):
            own = tokens_of(me, size)
            copies_out = links.scatter("seq", lambda peer: origin.at[peer // copies], goal.at[own, :])
            if via is None:
                return (move.start(origin.at[row], goal.at[own, :]), copies_out)
            move.start(origin.at[row], via).wait()
            return (move.start(via, goal.at[own, :]), copies_out)

        out_weight = move.start(r.enc_out, r.out_weight)
        adapters = [
            move.start(r.enc_adapter_down, r.a_down),
            move.start(r.enc_adapter_up, r.a_up),
        ]
        pair_weight = move.start(r.cross_kv, r.pair_weight)
        for copy in weights:
            copy.wait()
        prefix_pairs(r.enc_prefix, enc_first, enc_second, r.enc_hidden, r.enc_pairs, r.enc_pairs_wide)
        prefix_pairs(r.dec_prefix, dec_first, dec_second, r.dec_hidden, r.dec_pairs, r.dec_pairs_wide)
        ups = [move.start(r.enc_up, r.up), move.start(r.enc_down, r.down)]
        def project(slot):
            for copy in arrivals[slot]:
                copy.wait()
            cut = slice(slot * TILE, (slot + 1) * TILE)
            project_wide(r.qkv_v, r.qkv_weight, r.x[cut, :], width, cut)

        r.marks_out[...] = jnp.concatenate(
            [r.marks[pl.ds(row, 1), pl.ds(pl.multiple_of(other * TILE, TILE), TILE)] for other in others], 1
        )
        marks = r.marks_out[...]
        attention = SimpleNamespace(
            q=r.qkv_v, k=r.qkv_v, v=r.qkv_v, q0=0, k0=width, v0=2 * width,
            q_marks=marks, k_marks=marks, pair_keys=r.enc_pairs_wide.at[:width],
            pair_values=r.enc_pairs_wide.at[width:],
            context=r.context_v, lse=r.lse, qx=r.qx, kx=r.kx, scores=r.scores,
            pair_scores=r.pair_scores, peak=r.peak, partial=r.total,
        )
        here.wait()
        for slot in (1, 2, 0):
            project(slot)
        tiles = tokens // TILE
        most = (tiles - 1) * TILE
        early = [slice(0, most // 2), slice(most // 2, most)] if most // 2 % 128 == 0 else [slice(0, most)]
        attend(
            attention, False, count, [(own, list(range(tiles - 1)), True, "save") for own in early]
        )
        project(tiles - 1)
        later = [bring(r.target, r.target_rows, later_share, r.own_target)]
        outs = [move.start(r.qkv_v, r.qkv)]
        attend(
            attention,
            False,
            count,
            [(slice(most, tokens), list(range(tiles)), True, "whole")]
            + [(own, [tiles - 1], False, "merge") for own in early],
        )
        outs.append(move.start(r.context_v, r.context))
        out_weight.wait()
        add_and_normalize(r.x, r.context_v, r.out_weight, r.mid_v, r.mid_inverse)
        outs.append(move.start(r.mid_v, r.mid))
        for copy in adapters + ups:
            copy.wait()
        feed_forward(
            r.mid_v, r.up, r.down, r.a_down, r.a_up, r.total,
            lambda index: r.slopes_v.at[index], lambda slot: r.active.at[slot], r.narrow_v,
        )
        outs.append(move.start(r.slopes_v, r.slopes))
        outs.append(move.start(r.narrow_v, r.narrow))
        finish_forward(r.total, r.memory_v, r.memory_inverse)
        outs.append(move.start(r.memory_v, r.memory))
        pair_weight.wait()
        outs.pop(0).wait()
        memory_pairs = r.qkv_v.at[: 2 * width]
        project_wide(memory_pairs, r.pair_weight, r.memory_v[...], 0)
        outs.append(move.start(memory_pairs, r.memory_pairs))
        for own, remote in later:
            own.wait()
            for copy in remote:
                copy.wait()
        for copy in outs:
            copy.wait()

    return run_kernel(
        body,
        "encoder_forward",
        near=dict(marks=w.source_segments, enc_prefix=w.enc_prefix, dec_prefix=w.dec_prefix),
        far=dict(
            source=w.source, target=w.target, enc_qkv=w.enc_qkv,
            enc_out=w.enc_out, enc_up=w.enc_up, enc_down=w.enc_down,
            enc_adapter_down=w.enc_adapter_down, enc_adapter_up=w.enc_adapter_up,
            cross_kv=w.cross_kv, enc_prefix_in=w.enc_prefix_in, enc_prefix_out=w.enc_prefix_out,
            dec_prefix_in=w.dec_prefix_in, dec_prefix_out=w.dec_prefix_out,
        ),
        near_outs=dict(
            lse=((16, tokens), WIDE), mid_inverse=((tokens, 1), WIDE),
            memory_inverse=((tokens, 1), WIDE), marks_out=((1, tokens), jnp.int32),
            enc_hidden=((PAD, units), WIDE), enc_pairs=((PAD, 2 * width), LOW),
            dec_hidden=((PAD, units), WIDE), dec_pairs=((PAD, 2 * width), LOW),
            dec_pairs_wide=((2 * width, PAD), LOW),
        ),
        far_outs=dict(
            qkv=((3 * width, tokens), LOW), context=((width, tokens), LOW), mid=((tokens, width), LOW),
            slopes=((blocks, tokens, INNER), LOW), narrow=((tokens, narrow), LOW),
            memory=((tokens, width), LOW), memory_pairs=((2 * width, tokens), LOW),
            target_rows=((later_tokens, width), LOW),
        ),
        scratch=dict(
            x=((tokens, width), LOW), qkv_weight=((width, 3 * width), LOW),
            own_target=((later_share, width), LOW),
            enc_pairs_wide=((2 * width, PAD), LOW),
            out_weight=((width, width), LOW), a_down=((width, narrow), LOW),
            a_up=((narrow, width), LOW), up=((width, inner), LOW), down=((inner, width), LOW),
            pair_weight=((width, 2 * width), LOW), qkv_v=((3 * width, tokens), LOW),
            context_v=((width, tokens), LOW), mid_v=((tokens, width), LOW),
            slopes_v=((blocks, tokens, INNER), LOW), narrow_v=((tokens, narrow), LOW),
            memory_v=((tokens, width), LOW),
            active=((2, CHUNK, inner + narrow), LOW), total=((tokens, width), WIDE), qx=((16, tokens), LOW), kx=((16, tokens), LOW),
            scores=((2, tokens, tokens), WIDE), pair_scores=((2, PAD, tokens), WIDE),
            peak=((2, 8, tokens), WIDE),
        ),
        flops=2 * tokens * width * 11776 + 4 * tokens * tokens * width,
        links=2 * (group - 1),
        collective=0,
    )


def decoder(forward, w, group, copies, replicas):
    tokens, width = forward.target_rows.shape
    share = tokens // group
    keys = forward.memory_pairs.shape[1]
    count = w.dec_prefix.shape[0]
    second, flat, part = flat_shapes(width, w.dec_adapter_down.shape[1], group, replicas)
    inner = w.dec_up.shape[1]
    narrow = w.dec_adapter_down.shape[1]
    blocks = 1 + inner // INNER
    heads = width // HEAD

    def body(r):
        move = Mover(r.semaphores)
        ins = [move.start(r.target, r.x), move.start(r.dec_qkv, r.qkv_weight)]
        links = Links(r.sent, r.arrived, {"seq": group, "dp": replicas})
        exchange = Exchange(move, links)
        for copy in ins:
            copy.wait()
        out_weight = move.start(r.dec_out, r.out_weight)
        crosses = [
            move.start(r.cross_q, r.query_weight),
            move.start(r.memory_pairs, r.pairs_v),
            move.start(r.cross_out, r.cross_out_weight),
        ]
        adapters = [
            move.start(r.dec_adapter_down, r.a_down),
            move.start(r.dec_adapter_up, r.a_up),
        ]
        ups = [move.start(r.dec_up, r.up), move.start(r.dec_down, r.down)]
        d_qkv = r.slopes.at[: 3 * width, :tokens]

        def slope_of(index):
            return r.slopes.at[rows_at(index, tokens), :]

        me = links.place["seq"]
        size = tokens // group
        mine = r.cotangent_v.at[pl.ds(pl.multiple_of(me * size, size), size), :]
        cotangents = links.scatter("seq", lambda peer: r.cotangent.at[peer // copies], mine)
        cotangents.append(move.start(r.cotangent.at[me // copies], mine))
        project_wide(r.qkv, r.qkv_weight, r.x[...], width)
        row = pl.ds(me // copies, 1)
        marks, source_marks = r.marks[row, :], r.source_marks[...]
        shared = dict(
            qx=r.qx, kx=r.kx, scores=r.scores, pair_scores=r.pair_scores, peak=r.peak, dx=r.dx,
            vx=r.vx, delta=r.delta, dq_sum=r.dq_sum, work=r.work,
            d_context=r.d_context,
        )
        self_part = SimpleNamespace(
            q=r.qkv, k=r.qkv, v=r.qkv, q0=0, k0=width, v0=2 * width,
            q_marks=marks, k_marks=marks, pair_keys=r.pairs_wide.at[:width],
            pair_values=r.pairs_wide.at[width:], pairs=r.pairs, context=r.context, lse=r.lse,
            dq=d_qkv, dk=d_qkv, dv=d_qkv, dq0=0, dk0=width, dv0=2 * width,
            d_pairs=r.d_pairs, factor=1.0 / copies, **shared,
        )
        attend(self_part, True, count)
        out_weight.wait()
        add_and_normalize(r.x, r.context, r.out_weight, r.mid, r.mid_inverse)
        for copy in crosses:
            copy.wait()
        project_wide(r.query, r.query_weight, r.mid[...], width)
        cross_part = SimpleNamespace(
            q=r.query, k=r.pairs_v, v=r.pairs_v, q0=0, k0=0, v0=width,
            q_marks=marks, k_marks=source_marks, context=r.cross_context, lse=r.cross_lse,
            dq=r.d_query, dk=r.d_pairs_v, dv=r.d_pairs_v, dq0=0, dk0=0, dv0=width, **shared,
        )
        attend(cross_part, False, 0)
        add_and_normalize(r.mid, r.cross_context, r.cross_out_weight, r.crossed, r.crossed_inverse)
        for copy in adapters + ups + cotangents:
            copy.wait()
        feed_forward(
            r.crossed, r.up, r.down, r.a_down, r.a_up, r.total,
            slope_of, lambda slot: r.work.at[slot], r.narrow,
        )
        finish_forward(r.total, r.out_v, r.out_inverse)
        core, part_of = lax.rem(links.place["dp"], 2), rows_for(r.out_v, group)
        outputs = [
            links.plan("seq", links.peer("seq", shift), part_of(links.peer("seq", shift)), r.out_all.at[me])
            for shift in range(1, group)
        ]

        def send_outputs():
            for copy in outputs:
                copy.start()

        pl.when(core == 0)(send_outputs)
        outs = [move.start(part_of(me), r.out_all.at[me])]
        normalize_back_all(r.cotangent_v, r.out_v, r.out_inverse, r.total)
        feed_back(
            SimpleNamespace(
                grad=r.total, low=r.low, side=r.side, hidden=r.crossed, narrow=r.narrow, up=r.up,
                down=r.down, adapter_down=r.a_down, adapter_up=r.a_up,
                slopes=slope_of, flat=r.flat, second=second,
                d_narrow=r.d_narrow, factor=1.0 / copies, active=lambda slot: r.work.at[slot],
            )
        )
        exchange.start("flat", "dp", columns_for(r.flat, replicas), r.parts)
        pl.when(core == 1)(send_outputs)
        normalize_back_all(r.total, r.crossed, r.crossed_inverse, r.total)
        context_back(r.d_context, r.cross_out_weight, r.total)
        attend_back(cross_part, False, 0)
        outs.append(move.start(r.d_pairs_v, r.memory_pairs_grad))
        for cut in chunks(tokens, CHUNK):
            r.total[cut, :] += contract(r.d_query[:, cut], r.query_weight[...], 0, 1)
        normalize_back_all(r.total, r.mid, r.mid_inverse, r.total)
        context_back(r.d_context, r.out_weight, r.total)

        def pass_on(step):
            exchange.end("flat")
            r.flat_sum[...] = sum_parts(r.parts).astype(LOW)
            exchange.start("flat", "seq", lambda peer: r.flat_sum.at[peer], r.flat_own)

        attend_back(self_part, True, count, pass_on)
        for cut in chunks(tokens, CHUNK):
            r.x[cut, :] = (
                r.total[cut, :] + contract(d_qkv[:, cut], r.qkv_weight[...], 0, 1)
            ).astype(LOW)
        outs.append(move.start(r.x, r.target_grad))
        for copy in outs:
            copy.wait()
        exchange.end("flat")
        for copy in outputs:
            copy.wait()

    return run_kernel(
        body,
        "decoder",
        near=dict(
            marks=w.target_segments, source_marks=forward.marks_out,
            pairs_wide=forward.dec_pairs_wide, pairs=forward.dec_pairs,
        ),
        far=dict(
            target=forward.target_rows, cotangent=w.cotangent,
            memory_pairs=forward.memory_pairs, dec_qkv=w.dec_qkv,
            dec_out=w.dec_out, cross_q=w.cross_q, cross_out=w.cross_out, dec_up=w.dec_up,
            dec_down=w.dec_down, dec_adapter_down=w.dec_adapter_down,
            dec_adapter_up=w.dec_adapter_up,
        ),
        near_outs=dict(d_pairs=((PAD, 2 * width), WIDE)),
        far_outs=dict(
            out_all=((group, share, width), LOW), target_grad=((tokens, width), LOW),
            memory_pairs_grad=((2 * width, keys), LOW),
            flat_own=(part, LOW),
        ),
        scratch=dict(
            flat=(flat, LOW), parts=((replicas, *part), LOW), flat_sum=(part, LOW),
            x=((tokens, width), LOW), cotangent_v=((tokens, width), LOW),
            qkv_weight=((width, 3 * width), LOW), out_weight=((width, width), LOW),
            query_weight=((width, width), LOW), cross_out_weight=((width, width), LOW),
            pairs_v=((2 * width, keys), LOW), a_down=((width, narrow), LOW),
            a_up=((narrow, width), LOW), up=((width, inner), LOW), down=((inner, width), LOW),
            qkv=((3 * width, tokens), LOW), context=((width, tokens), LOW),
            mid=((tokens, width), LOW), mid_inverse=((tokens, 1), WIDE),
            query=((width, tokens), LOW), cross_context=((width, tokens), LOW),
            crossed=((tokens, width), LOW), crossed_inverse=((tokens, 1), WIDE),
            out_v=((tokens, width), LOW), out_inverse=((tokens, 1), WIDE),
            slopes=((blocks * tokens, INNER), LOW), narrow=((tokens, narrow), LOW),
            low=((tokens, width), LOW), side=((tokens, width), LOW), d_narrow=((tokens, narrow), LOW),
            total=((tokens, width), WIDE), lse=((16, tokens), WIDE), cross_lse=((16, tokens), WIDE),
            d_context=((width, tokens), LOW), d_query=((width, tokens), LOW),
            d_pairs_v=((2 * width, keys), LOW),
            qx=((heads * 16, tokens), LOW), kx=((16, keys), LOW),
            scores=((2, keys, tokens), WIDE), pair_scores=((2, PAD, tokens), WIDE),
            peak=((2, 8, tokens), WIDE), dx=((heads * 16, tokens), LOW), vx=((16, keys), LOW),
            delta=((16, tokens), WIDE), dq_sum=((width, tokens), WIDE),
            work=((2, TILE, 16 * TILE), LOW),
        ),
        flops=4 * tokens * width * 11776 + 14 * tokens * (keys + tokens) * width,
        links=3 * (group - 1) + replicas - 1,
        collective=3,
    )


def encoder_feed_back(dec, forward, w, group, copies, replicas):
    tokens, width = forward.memory.shape
    inner = w.enc_up.shape[1]
    narrow = w.enc_adapter_down.shape[1]
    blocks = 1 + inner // INNER
    second, flat, part = flat_shapes(width, narrow, group, replicas)
    later = dec.target_grad.shape[0] // group

    def body(r):
        move = Mover(r.semaphores)
        firsts = [
            move.start(r.memory_pairs_grad, r.d_pairs),
            move.start(r.cross_kv, r.pair_weight),
            move.start(r.memory, r.memory_v),
        ]
        adapters = [
            move.start(r.enc_adapter_up, r.a_up),
            move.start(r.slopes.at[0], r.slopes_v.at[0]),
            move.start(r.narrow, r.narrow_v),
            move.start(r.mid, r.mid_v),
        ]
        ups = [
            move.start(r.enc_adapter_down, r.a_down),
            move.start(r.slopes.at[1:], r.slopes_v.at[1:]),
            move.start(r.enc_down, r.down),
            move.start(r.enc_up, r.up),
            move.start(r.enc_out, r.out_weight),
        ]
        links = Links(r.sent, r.arrived, {"seq": group, "dp": replicas})
        exchange = Exchange(move, links)
        me, core = links.place["seq"], lax.rem(links.place["dp"], 2)
        targets = [
            links.plan("seq", links.peer("seq", shift), r.target_grad.at[links.peer("seq", shift)], r.target_grad_all.at[me])
            for shift in range(1, group)
        ]

        def send_targets():
            for copy in targets:
                copy.start()

        pl.when(core == 0)(send_targets)
        own_target = move.start(r.target_grad.at[me], r.own_target)
        for copy in firsts:
            copy.wait()
        for cut in chunks(tokens, CHUNK):
            grad = contract(r.d_pairs[:, cut], r.pair_weight[...], 0, 1)
            r.total[cut, :] = normalize_back(
                grad, r.memory_v[cut, :].astype(WIDE), r.memory_inverse[cut, :]
            )
        for copy in adapters:
            copy.wait()

        def send():
            exchange.start("flat", "dp", columns_for(r.flat, replicas), r.parts)
            pl.when(core == 1)(send_targets)
            own_target.wait()
            targets.append(move.start(r.own_target, r.target_grad_all.at[me]))
            for copy in ups:
                copy.wait()

        feed_back(
            SimpleNamespace(
                grad=r.total, low=r.low, side=r.side, hidden=r.mid_v, narrow=r.narrow_v, up=r.up,
                down=r.down, adapter_down=r.a_down, adapter_up=r.a_up,
                slopes=lambda index: r.slopes_v.at[index], flat=r.flat, second=second,
                d_narrow=r.d_narrow, factor=1.0 / copies, active=lambda slot: r.active.at[slot],
            ),
            send,
        )
        normalize_back_all(r.total, r.mid_v, r.mid_inverse, r.low)
        outs = [move.start(r.low, r.summed_grad)]
        context_back(r.d_context_v, r.out_weight, r.low)
        outs.append(move.start(r.d_context_v, r.d_context))
        for copy in outs:
            copy.wait()
        exchange.end("flat")
        for copy in targets:
            copy.wait()

    return run_kernel(
        body,
        "encoder_feed_back",
        near=dict(mid_inverse=forward.mid_inverse, memory_inverse=forward.memory_inverse),
        far=dict(
            target_grad=dec.target_grad.reshape(group, -1, width),
            memory_pairs_grad=dec.memory_pairs_grad, memory=forward.memory, mid=forward.mid,
            slopes=forward.slopes, narrow=forward.narrow, cross_kv=w.cross_kv,
            enc_out=w.enc_out, enc_up=w.enc_up, enc_down=w.enc_down,
            enc_adapter_down=w.enc_adapter_down, enc_adapter_up=w.enc_adapter_up,
        ),
        near_outs={},
        far_outs=dict(
            summed_grad=((tokens, width), LOW), d_context=((width, tokens), LOW),
            parts=((replicas, *part), LOW),
            target_grad_all=((group, later, width), LOW),
        ),
        scratch=dict(
            own_target=((later, width), LOW),
            flat=(flat, LOW), d_pairs=((2 * width, tokens), LOW), pair_weight=((width, 2 * width), LOW),
            memory_v=((tokens, width), LOW), mid_v=((tokens, width), LOW),
            slopes_v=((blocks, tokens, INNER), LOW), narrow_v=((tokens, narrow), LOW),
            out_weight=((width, width), LOW), a_down=((width, narrow), LOW),
            a_up=((narrow, width), LOW), up=((width, inner), LOW), down=((inner, width), LOW),
            low=((tokens, width), LOW), side=((tokens, width), LOW), d_narrow=((tokens, narrow), LOW),
            active=((2, CHUNK, inner), LOW), total=((tokens, width), WIDE), d_context_v=((width, tokens), LOW),
        ),
        flops=2 * tokens * width * 9728,
        links=group - 1 + replicas - 1,
        collective=1,
    )


def split_product(left, right, left_dim, right_dim):
    return total_of(
        [contract(part.astype(LOW), right, left_dim, right_dim) for part in split_three(left)]
    )


def prefix_back(p):
    count, group = p.prefix.shape[0], p.group
    d_pairs, hidden = p.d_pairs, p.hidden[...]
    units, width = hidden.shape[1], p.prefix.shape[1]
    p.tall_hidden[...] = hidden.T
    share = units // group
    own = p.tall_hidden[pl.ds(pl.multiple_of(p.place * share, share), share), :]
    parts = split_three(d_pairs)
    p.out_grad[...] = total_of(
        [split_product(own, part.astype(LOW), 1, 0) for part in parts]
    )
    d_hidden = split_product(d_pairs, p.second[...], 1, 1) * (1.0 - hidden * hidden)
    p.wide_prefix[...] = jnp.zeros(p.wide_prefix.shape, WIDE)
    p.wide_prefix[:count, :] = p.prefix[...].astype(WIDE)
    p.tall_prefix[...] = p.wide_prefix[...].T
    share = width // group
    own = p.tall_prefix[pl.ds(pl.multiple_of(p.place * share, share), share), :].astype(LOW)
    p.in_grad[...] = total_of([contract(own, part.astype(LOW), 1, 0) for part in split_three(d_hidden)])
    p.embed_grad[...] = split_product(d_hidden, p.first_share[...], 1, 1)[:count]


def block_order(place):
    return [1 + is_inner(place), 3, 2 - is_inner(place), 0]


def encoder_attend_back(feed, dec, forward, w, group, copies, replicas):
    tokens, width = feed.summed_grad.shape
    share = tokens // group
    count = w.enc_prefix.shape[0]
    narrow, units = w.enc_adapter_down.shape[1], w.enc_prefix_in.shape[1]
    second, _, part = flat_shapes(width, narrow, group, replicas)
    heads = width // HEAD
    tile = TILE
    blocks, per = tokens // tile, tile // share
    grains = [
        (layer, 8 * row, 128 * column)
        for layer in range(2) for column in range(2 * width // 128) for row in range(PAD // 8)
    ]
    depth = -(-len(grains) // (group * replicas))

    def grain_place(number):
        device, inside = number // depth, number % depth
        return (device // group, device % group, slice(8 * inside, 8 * inside + 8))
    layers = ("enc", "dec")

    def body(r):
        move = Mover(r.semaphores)
        me = lax.axis_index("seq")
        sums = move.start(r.enc_parts, r.enc_parts_v)
        slots = block_order(me // per)
        near = near_order(me // per)
        begins = [pl.multiple_of(slot * tile, tile) for slot in slots]
        inner = is_inner(me // per)
        goals = [near[1] + inner * (near[2] - near[1]), near[3], near[2] + inner * (near[1] - near[2]), near[0]]
        firsts, lasts = [], []
        for stage, begin in enumerate(begins):
            goal, origin = slice(stage * tile, (stage + 1) * tile), pl.ds(begin, tile)
            firsts.append(move.start(r.qkv.at[:, origin], r.qkv_v.at[:, goal]))
            firsts.append(move.start(r.d_context.at[:, origin], r.d_context_v.at[:, goal]))
            firsts.append(move.start(r.context.at[:, origin], r.context_v.at[:, goal]))
            lasts.append(move.start(r.summed_grad.at[origin, :], r.summed_v.at[goal, :]))
            r.lse_v[:, goal] = r.lse[:, origin]
        totals = move.start(r.dec_own, r.dec_own_v)
        marks = jnp.concatenate([r.marks[:, pl.ds(begin, tile)] for begin in begins], 1)
        lasts += [
            move.start(r.enc_qkv, r.qkv_weight),
            move.start(r.enc_prefix_out, r.enc_second), move.start(r.dec_prefix_out, r.dec_second),
        ]
        size = width // group
        first_rows = pl.ds(pl.multiple_of(me * size, size), size)
        lasts.append(move.start(r.enc_prefix_in.at[first_rows, :], r.enc_first))
        lasts.append(move.start(r.dec_prefix_in.at[first_rows, :], r.dec_first))

        links = Links(r.sent, r.arrived, {"seq": group, "dp": replicas})
        exchange = Exchange(move, links)

        def send_total(name, own, mine, total):
            mine[...] = sum_parts(own).astype(LOW)
            exchange.start(name, "dp", lambda peer: mine, total)

        def ready(step):
            if step == 0:
                r.pair_out[...] = jnp.zeros(r.pair_out.shape, WIDE)
                for number, (layer, row, column) in enumerate(grains):
                    origin = (r.enc_d_pairs, r.dec_d_pairs)[layer]
                    r.pair_out[grain_place(number)] = origin[row : row + 8, column : column + 128]
                exchange.start("pairs", "dp", lambda peer: r.pair_out.at[peer], r.pair_parts)
                totals.wait()
                send_total("dec", r.dec_own_v, r.dec_mine, r.dec_total)
            elif step == 1:
                exchange.end("pairs")
                r.pair_sum[...] = sum_parts(r.pair_parts)
                exchange.start("pairs", "seq", lambda peer: r.pair_sum.at[peer], r.pair_own)
            else:
                exchange.end("pairs")
                r.pair_mine[...] = sum_parts(r.pair_own)
                exchange.start("pairs", "seq", lambda peer: r.pair_mine, r.pair_row)

        sent = []

        def staged(stage, cut):
            r.d_qkv[:width, :] = (r.dq_sum[:, cut] * SCALE).astype(LOW)
            r.d_qkv[width : 2 * width, :] = (r.dk_sum[:, cut] * (1.0 / LOG2E)).astype(LOW)
            r.d_qkv[2 * width :, :] = r.dv_sum[:, cut].astype(LOW)
            if stage == 0:
                for copy in lasts:
                    copy.wait()
            r.summed_v[cut, :] = (
                r.summed_v[cut, :].astype(WIDE) + contract(r.d_qkv[...], r.qkv_weight[...], 0, 1)
            ).astype(LOW)
            inside = lax.rem(me, per)
            last = stage == blocks - 1
            for turn in range(per):
                number = lax.rem(inside + turn, per)
                origin = r.summed_v.at[
                    pl.ds(pl.multiple_of(stage * tile + number * share, share), share), :
                ]
                if last and turn == 0:
                    sent.append(move.start(origin, r.source_grad.at[me]))
                else:
                    target = goals[stage] * per + number
                    sent.append(links.start_to("seq", target, origin, r.source_grad.at[me]))
            if stage == 0:
                exchange.end("enc", "pairs")
                send_total("enc", r.enc_own, r.enc_mine, r.enc_total)
                exchange.start("pairs", "dp", lambda peer: r.pair_row, r.pair_total)

        sums.wait()
        r.enc_sum[...] = sum_parts(r.enc_parts_v).astype(LOW)
        exchange.start("enc", "seq", lambda peer: r.enc_sum.at[peer], r.enc_own)
        for copy in firsts:
            copy.wait()
        attend_back(
            SimpleNamespace(
                q=r.qkv_v, k=r.qkv_v, v=r.qkv_v, q0=0, k0=width, v0=2 * width,
                q_marks=marks, k_marks=marks, pairs=r.enc_pairs, context=r.context_v, lse=r.lse_v,
                d_context=r.d_context_v, d_pairs=r.enc_d_pairs, factor=1.0 / copies, qx=r.qx, kx=r.kx,
                dx=r.dx, vx=r.vx, delta=r.delta, dq_sum=r.dq_sum, dk_sum=r.dk_sum, dv_sum=r.dv_sum,
                work=r.work,
            ),
            False,
            count,
            ready,
            staged,
        )
        exchange.end("pairs")
        for number, (layer, row, column) in enumerate(grains):
            r.whole[layer, row : row + 8, column : column + 128] = r.pair_total[grain_place(number)]
        for number, layer in enumerate(layers):
            prefix_back(
                SimpleNamespace(
                    d_pairs=r.whole[number], group=group, place=me,
                    hidden=getattr(r, f"{layer}_hidden"), prefix=getattr(r, f"{layer}_prefix"),
                    second=getattr(r, f"{layer}_second"), first_share=getattr(r, f"{layer}_first"),
                    tall_hidden=r.tall_hidden, tall_prefix=r.tall_prefix, wide_prefix=r.wide_prefix,
                    embed_grad=getattr(r, f"{layer}_embed"), in_grad=getattr(r, f"{layer}_in"),
                    out_grad=getattr(r, f"{layer}_out_grad"),
                )
            )
            exchange.end(layer)
            total = getattr(r, f"{layer}_total")
            total = jnp.concatenate([total[place].astype(WIDE) for place in range(replicas)], 0)
            for kind, first in (("down", 0), ("up", second)):
                out = getattr(r, f"{layer}_{kind}_grad_all")
                out[...] = unpack(total, first, out.shape)
        for copy in sent:
            copy.wait()

    near_outs = {}
    for layer in layers:
        near_outs[f"{layer}_embed"] = ((count, width // group), WIDE)
        near_outs[f"{layer}_in"] = ((width // group, units), WIDE)
        near_outs[f"{layer}_out_grad"] = ((units // group, 2 * width), WIDE)
        near_outs[f"{layer}_down_grad_all"] = ((width // group, narrow), WIDE)
        near_outs[f"{layer}_up_grad_all"] = ((narrow // group, width), WIDE)
    scratch = {}
    scratch["enc_parts_v"] = ((replicas, *part), LOW)
    scratch["enc_sum"] = scratch["enc_own"] = scratch["dec_own_v"] = (part, LOW)
    for layer in layers:
        scratch[f"{layer}_mine"] = (part[1:], LOW)
        scratch[f"{layer}_total"] = ((replicas, *part[1:]), LOW)
        scratch[f"{layer}_second"] = ((units, 2 * width), LOW)
        scratch[f"{layer}_first"] = ((width // group, units), LOW)
    own = (group, 8 * depth, 128)
    for name in ("pair_out", "pair_parts", "pair_total"):
        scratch[name] = ((replicas, *own), WIDE)
    for name in ("pair_sum", "pair_own", "pair_row"):
        scratch[name] = (own, WIDE)
    scratch["pair_mine"] = (own[1:], WIDE)
    scratch["whole"] = ((2, PAD, 2 * width), WIDE)
    scratch["enc_d_pairs"] = ((PAD, 2 * width), WIDE)
    scratch["tall_hidden"] = ((units, PAD), WIDE)
    scratch["wide_prefix"] = ((PAD, width), WIDE)
    scratch["tall_prefix"] = ((width, PAD), WIDE)
    for name in ("dq_sum", "dk_sum", "dv_sum"):
        scratch[name] = ((width, tokens), WIDE)
    return run_kernel(
        body,
        "encoder_attend_back",
        near=dict(
            marks=forward.marks_out, enc_pairs=forward.enc_pairs, lse=forward.lse,
            dec_d_pairs=dec.d_pairs, enc_hidden=forward.enc_hidden, dec_hidden=forward.dec_hidden,
            enc_prefix=w.enc_prefix, dec_prefix=w.dec_prefix,
        ),
        far=dict(
            qkv=forward.qkv, d_context=feed.d_context, context=forward.context,
            enc_qkv=w.enc_qkv, summed_grad=feed.summed_grad,
            enc_parts=feed.parts, dec_own=dec.flat_own,
            enc_prefix_in=w.enc_prefix_in, enc_prefix_out=w.enc_prefix_out,
            dec_prefix_in=w.dec_prefix_in, dec_prefix_out=w.dec_prefix_out,
        ),
        near_outs=near_outs,
        far_outs=dict(source_grad=((group, share, width), LOW)),
        scratch=dict(
            qkv_v=((3 * width, tokens), LOW), d_context_v=((width, tokens), LOW),
            context_v=((width, tokens), LOW), qkv_weight=((width, 3 * width), LOW),
            summed_v=((tokens, width), LOW), d_qkv=((3 * width, tile), LOW), lse_v=((16, tokens), WIDE),
            qx=((heads * 16, tokens), LOW), kx=((16, tokens), LOW),
            dx=((heads * 16, tokens), LOW), vx=((16, tokens), LOW), delta=((16, tokens), WIDE),
            work=((2, TILE, 14 * TILE), LOW), **scratch,
        ),
        flops=2 * tokens * width * 2304 + 20 * tokens * tokens * width,
        links=3 * (group - 1) + 4 * (replicas - 1) + group - 1,
        collective=2,
    )


def finish(attended, feed, dec, copies):
    small = [name for name in vars(attended) if name != "source_grad"]
    shape = attended.source_grad.shape
    later = dec.out_all.shape

    def body(r):
        move = Mover(r.semaphores)
        ins = [
            move.start(r.source_grad, r.source_v),
            move.start(r.target_grad, r.target_v),
        ]
        outs = []
        relays = [
            (move.start(r.out_all.at[place * copies], r.out_v.at[place]), r.out_v.at[place], r.out.at[place])
            for place in range(later[0] // copies)
        ]
        for name in small:
            via = getattr(r, name + "_v")
            relays.append((move.start(getattr(r, name + "_in"), via), via, getattr(r, name)))
        for copy, via, goal in relays:
            copy.wait()
            outs.append(move.start(via, goal))
        for copy, origin, wide, goal in (
            (ins[0], r.source_v, r.source_w, r.source_out), (ins[1], r.target_v, r.target_w, r.target_out)
        ):
            copy.wait()
            for place in range(wide.shape[0]):
                wide[place] = origin[place * copies].astype(WIDE)
                outs.append(move.start(wide.at[place], goal.at[place]))
        for copy in outs:
            copy.wait()

    rows = shape[0] // copies
    return run_kernel(
        body,
        "finish",
        near={},
        far=dict(
            source_grad=attended.source_grad, target_grad=feed.target_grad_all, out_all=dec.out_all,
            **{name + "_in": getattr(attended, name) for name in small},
        ),
        near_outs={},
        far_outs=dict(
            out=((rows, *later[1:]), LOW), source_out=((rows, *shape[1:]), WIDE),
            target_out=((rows, *later[1:]), WIDE),
            **{name: (getattr(attended, name).shape, WIDE) for name in small},
        ),
        scratch=dict(
            source_v=(shape, LOW), source_w=((rows, *shape[1:]), WIDE), target_v=(later, LOW),
            target_w=((rows, *later[1:]), WIDE), out_v=((rows, *later[1:]), LOW),
            **{name + "_v": (getattr(attended, name).shape, WIDE) for name in small},
        ),
        flops=0,
    )


NAMES = (
    "source",
    "target",
    "source_segments",
    "target_segments",
    "cotangent",
    "enc_qkv",
    "enc_out",
    "enc_up",
    "enc_down",
    "dec_qkv",
    "dec_out",
    "cross_q",
    "cross_kv",
    "cross_out",
    "dec_up",
    "dec_down",
    "enc_prefix",
    "enc_prefix_in",
    "enc_prefix_out",
    "enc_adapter_down",
    "enc_adapter_up",
    "dec_prefix",
    "dec_prefix_in",
    "dec_prefix_out",
    "dec_adapter_down",
    "dec_adapter_up",
)


def shards(*operands, group, replicas):
    w = SimpleNamespace(**dict(zip(NAMES, operands)))
    copies = group // w.source.shape[0]
    forward = encoder_forward(w, group, copies)
    dec = decoder(forward, w, group, copies, replicas)
    feed = encoder_feed_back(dec, forward, w, group, copies, replicas)
    attended = encoder_attend_back(feed, dec, forward, w, group, copies, replicas)
    done = finish(attended, feed, dec, copies)
    results = [done.out, done.source_out, done.target_out]
    for layer in ("enc", "dec"):
        for name in ("embed", "in", "out_grad", "down_grad_all", "up_grad_all"):
            results.append(getattr(done, f"{layer}_{name}"))
    return tuple(results)


def solution(mesh):
    rows = P("dp", "seq", None)
    marks = P("dp", None)
    in_specs = (rows, rows, marks, marks, rows) + (P(),) * 21
    across, down = P(None, "seq"), P("seq", None)
    layer = (across, down, down, down, down)
    return jax.shard_map(
        functools.partial(shards, group=mesh.shape["seq"], replicas=mesh.shape["dp"]),
        mesh=mesh,
        in_specs=in_specs,
        out_specs=(rows, rows, rows) + layer + layer,
        check_vma=False,
    )
```

```python
import functools
import math
from types import SimpleNamespace

import jax
import jax.numpy as jnp
from jax import lax
from jax.experimental import pallas as pl
from jax.experimental.pallas import tpu as pltpu
from jax.sharding import PartitionSpec as P

HEAD = 64
GROUP = 4
PAD = 32
BIG = 2.0**100
LOG2E = math.log2(math.e)
SCALE = 1.0 / math.sqrt(HEAD)
VMEM_BYTES = 60 * 2**20
CHUNK = 256
TILE = 256
COLUMNS = 512
TOGETHER = 6
UNITS = 4
INNER = 512
LOW = jnp.bfloat16
WIDE = jnp.float32


def contract(left, right, left_dim, right_dim):
    return lax.dot_general(
        left, right, (((left_dim,), (right_dim,)), ((), ())), preferred_element_type=WIDE
    )


def rows_at(index, size, base=0):
    return pl.ds(pl.multiple_of(base + index * size, size), size)


def chunks(size, step):
    step = min(step, size)
    return [slice(start, start + step) for start in range(0, size, step)]


def total_of(values):
    return functools.reduce(lambda left, right: left + right, values)


def normalize(value):
    centered = value - jnp.mean(value, axis=-1, keepdims=True)
    inverse = lax.rsqrt(jnp.mean(centered * centered, axis=-1, keepdims=True) + 1e-05)
    return (centered * inverse, inverse)


def normalize_back(gradient, normed, inverse):
    return (
        gradient
        - jnp.mean(gradient, axis=-1, keepdims=True)
        - normed * jnp.mean(gradient * normed, axis=-1, keepdims=True)
    ) * inverse


def gelu_both(value):
    scale = math.sqrt(2.0 / math.pi)
    square = value * value
    half = 0.5 + 0.5 * jnp.tanh(value * (scale + (scale * 0.044715) * square))
    active = value * half
    slope = half + active * (1.0 - half) * (2.0 * scale + (6.0 * scale * 0.044715) * square)
    return (active, slope)


class Mover:
    def __init__(self, semaphores):
        self.semaphores = semaphores
        self.used = 0

    def start(self, origin, goal):
        copy = pltpu.make_async_copy(origin, goal, self.semaphores.at[self.used])
        self.used += 1
        copy.start()
        return copy


def run_kernel(body, name, near, far, near_outs, far_outs, scratch, flops, links=0, collective=None):
    in_names = list(near) + list(far)
    out_names = list(near_outs) + list(far_outs)
    names = in_names + out_names + list(scratch) + ["semaphores"]
    link_scratch = []
    remote = {}
    if collective is not None:
        names += ["sent", "arrived"]
        link_scratch = [pltpu.SemaphoreType.DMA((links,)), pltpu.SemaphoreType.DMA((links,))]
        remote = dict(collective_id=collective, has_side_effects=True)

    def kernel(*refs):
        body(SimpleNamespace(**dict(zip(names, refs))))

    near_spec = pl.BlockSpec(memory_space=pltpu.VMEM)
    far_spec = pl.BlockSpec(memory_space=pl.ANY)
    results = pl.pallas_call(
        kernel,
        out_shape=tuple(
            jax.ShapeDtypeStruct(*out) for out in (*near_outs.values(), *far_outs.values())
        ),
        in_specs=[near_spec] * len(near) + [far_spec] * len(far),
        out_specs=tuple([near_spec] * len(near_outs) + [far_spec] * len(far_outs)),
        scratch_shapes=[pltpu.VMEM(*shape) for shape in scratch.values()]
        + [pltpu.SemaphoreType.DMA((80,))]
        + link_scratch,
        compiler_params=pltpu.CompilerParams(vmem_limit_bytes=VMEM_BYTES, **remote),
        cost_estimate=pl.CostEstimate(flops=flops, bytes_accessed=2**24, transcendentals=0),
        name=name,
    )(*near.values(), *far.values())
    return SimpleNamespace(**dict(zip(out_names, results)))


class Links:
    def __init__(self, sent, arrived, groups):
        self.sent, self.arrived = sent, arrived
        self.used = 0
        self.place = {axis: lax.axis_index(axis) for axis in ("dp", "seq")}
        self.sizes = groups
        barrier = pltpu.get_barrier_semaphore()
        peers = 0
        for axis, size in groups.items():
            for shift in range(1, size):
                pl.semaphore_signal(
                    barrier, inc=1, device_id=self.device(axis, shift), device_id_type=pl.DeviceIdType.MESH
                )
                peers += 1
        pl.semaphore_wait(barrier, peers)

    def peer(self, axis, shift):
        return lax.rem(self.place[axis] + shift, self.sizes[axis])

    def device(self, axis, shift):
        return self.device_at(axis, self.peer(axis, shift))

    def device_at(self, axis, index):
        return (index, self.place["seq"]) if axis == "dp" else (self.place["dp"], index)

    def start(self, axis, shift, origin, goal):
        return self.start_to(axis, self.peer(axis, shift), origin, goal)

    def start_to(self, axis, index, origin, goal):
        copy = self.plan(axis, index, origin, goal)
        copy.start()
        return copy

    def plan(self, axis, index, origin, goal):
        copy = pltpu.make_async_remote_copy(
            src_ref=origin,
            dst_ref=goal,
            send_sem=self.sent.at[self.used],
            recv_sem=self.arrived.at[self.used],
            device_id=self.device_at(axis, index),
            device_id_type=pl.DeviceIdType.MESH,
        )
        self.used += 1
        return copy

    def scatter(self, axis, pick, goal):
        return [
            self.start(axis, shift, pick(self.peer(axis, shift)), goal)
            for shift in range(1, self.sizes[axis])
        ]


class Exchange:
    def __init__(self, move, links):
        self.move, self.links = move, links
        self.place, self.sizes = links.place, links.sizes
        self.open = {}

    def start(self, name, axis, pick, goal, via=None):
        mine = self.place[axis]
        copies = self.links.scatter(axis, pick, goal.at[mine])
        if via is None:
            copies.append(self.move.start(pick(mine), goal.at[mine]))
        else:
            self.move.start(pick(mine), via).wait()
            copies.append(self.move.start(via, goal.at[mine]))
        self.open[name] = copies

    def end(self, *names):
        for name in names:
            for copy in self.open.pop(name):
                copy.wait()


def sum_parts(parts):
    return total_of([parts[part].astype(WIDE) for part in range(parts.shape[0])])


def rows_for(ref, count):
    size = ref.shape[0] // count
    return lambda place: ref.at[pl.ds(pl.multiple_of(place * size, size), size), :]


def split_three(value):
    high = value.astype(LOW).astype(WIDE)
    rest = value - high
    middle = rest.astype(LOW).astype(WIDE)
    return (high, middle, rest - middle)


def place_rows(parts, first, shape):
    row = lax.broadcasted_iota(jnp.int32, shape, 0)
    out = jnp.zeros(shape, WIDE)
    for offset, part in enumerate(parts):
        out = jnp.where(row == first + offset, part, out)
    return out


def document_rows(segments, tokens, is_key):
    row = lax.broadcasted_iota(jnp.int32, (16, tokens), 0)
    same = row == segments
    if is_key:
        return jnp.where(row < 4, jnp.where(same, 0.0, -BIG), 0.0)
    return jnp.where(same & (row < 4), 1.0, 0.0)


def column_peak(scores, peak):
    for start in range(0, scores.shape[0], 8):
        peak = jnp.maximum(peak, scores[start : start + 8])
    return peak


def from_column(value, low):
    if low == 0:
        return value
    return jnp.concatenate([jnp.zeros((value.shape[0], low), value.dtype), value], 1)


def attend(a, causal, prefix, entries=None):
    queries, keys = a.q.shape[1], a.k.shape[1]
    width = a.context.shape[0]
    heads = width // HEAD
    tile = min(256, keys)
    tiles = keys // tile
    a.qx[:16, :queries] = document_rows(a.q_marks, queries, False).astype(LOW)
    a.kx[:, :keys] = document_rows(a.k_marks, keys, True).astype(LOW)
    if entries is None:
        entries = [
            (own, [part for part in range(tiles) if not (causal and part * tile >= own.stop)], prefix > 0, "whole")
            for own in chunks(queries, COLUMNS)
        ]

    def front(head, slot, entry, work):
        own, parts, sees_prefix, _ = entry
        start = own.start
        query = jnp.concatenate([a.q[rows_at(head, HEAD, a.q0), own], a.qx[:16, own]], 0)
        peak = jnp.full((8, own.stop - start), -4.0 * BIG, WIDE)
        if sees_prefix:
            scores = contract(a.pair_keys[rows_at(head, HEAD), :], query[:HEAD], 0, 0)
            row = lax.broadcasted_iota(jnp.int32, scores.shape, 0)
            scores = jnp.where(row < prefix, scores, -BIG)
            a.pair_scores[slot, :, own] = scores
            peak = column_peak(scores, peak)
        for part in parts:
            cut = slice(part * tile, (part + 1) * tile)
            key = jnp.concatenate([a.k[rows_at(head, HEAD, a.k0), cut], a.kx[:, cut]], 0)
            scores = contract(key, query, 0, 0)
            if causal and cut.stop > start:
                place = lax.broadcasted_iota(jnp.int32, scores.shape, 0) + (cut.start - start)
                scores = jnp.where(
                    place <= lax.broadcasted_iota(jnp.int32, scores.shape, 1), scores, -BIG
                )
            a.scores[slot, cut, own] = scores
            peak = column_peak(scores, peak)
            work(part)
        a.peak[slot, :, own] = peak

    def step(head, following, slot):
        for entry in entries:
            own, _, sees_prefix, mode = entry
            peak = jnp.max(a.peak[slot, :, own], 0, keepdims=True)
            context = []
            if mode == "merge":
                before = a.lse[pl.ds(head, 1), own]
                peak = jnp.maximum(peak, before)
                context.append(a.partial[rows_at(head, HEAD + 16), own] * jnp.exp2(before - peak))
            if sees_prefix:
                weights = jnp.exp2(a.pair_scores[slot, :, own] - peak).astype(LOW)
                value = jnp.concatenate(
                    [a.pair_values[rows_at(head, HEAD), :], jnp.ones((16, PAD), LOW)], 0
                )
                context.append(contract(value, weights, 1, 0))

            def work(part):
                cut = slice(part * tile, (part + 1) * tile)
                weights = jnp.exp2(a.scores[slot, cut, own] - peak).astype(LOW)
                value = jnp.concatenate(
                    [a.v[rows_at(head, HEAD, a.v0), cut], jnp.ones((16, tile), LOW)], 0
                )
                context.append(contract(value, weights, 1, 0))

            front(following, 1 - slot, entry, work)
            summed = total_of(context)
            if mode == "save":
                a.partial[rows_at(head, HEAD + 16), own] = summed
                a.lse[pl.ds(head, 1), own] = peak
            else:
                total = summed[HEAD : HEAD + 1]
                a.context[rows_at(head, HEAD), own] = (summed[:HEAD] * (1.0 / total)).astype(LOW)
                a.lse[pl.ds(head, 1), own] = peak + jnp.log2(total)

    for entry in entries:
        front(0, 0, entry, lambda part: None)

    def several(index, carry):
        for number in range(TOGETHER):
            head = TOGETHER * index + number
            step(head, jnp.minimum(head + 1, heads - 1), number % 2)
        return carry

    lax.fori_loop(0, heads // TOGETHER, several, 0)


def block_diagonal(pairs, group, first):
    wide = GROUP * HEAD
    rows = pairs[:, first + group * wide : first + (group + 1) * wide]
    column = lax.broadcasted_iota(jnp.int32, rows.shape, 1)
    parts = [
        jnp.where((column >= member * HEAD) & (column < (member + 1) * HEAD), rows.astype(WIDE), 0.0)
        for member in range(GROUP)
    ]
    return jnp.concatenate(parts, 0).astype(LOW)


def own_columns(grads):
    column = lax.broadcasted_iota(jnp.int32, (PAD, GROUP * HEAD), 1)
    out = jnp.zeros((PAD, GROUP * HEAD), WIDE)
    for member in range(GROUP):
        own = (column >= member * HEAD) & (column < (member + 1) * HEAD)
        out = jnp.where(own, grads[member * PAD : (member + 1) * PAD], out)
    return out


def attend_back(a, causal, prefix, ready=None, staged=None):
    queries, keys = a.q.shape[1], a.k.shape[1]
    width = a.context.shape[0]
    heads = width // HEAD
    tiles = keys // TILE
    row = lax.broadcasted_iota(jnp.int32, (16, keys), 0)
    a.kx[:, :keys] = jnp.where(
        (row >= 4) & (row < 7), 1.0, document_rows(a.k_marks, keys, True)
    ).astype(LOW)
    a.vx[:, :keys] = jnp.where(row < 3, 1.0, 0.0).astype(LOW)
    documents = document_rows(a.q_marks, queries, False)

    def prepare(head, carry):
        rows = rows_at(head, HEAD)
        delta = jnp.sum(
            a.d_context[rows, :].astype(WIDE) * a.context[rows, :].astype(WIDE),
            axis=0,
            keepdims=True,
        )
        a.delta[pl.ds(head, 1), :queries] = delta
        a.dx[rows_at(head, 16), :queries] = place_rows(
            split_three(-delta), 0, (16, queries)
        ).astype(LOW)
        minus = split_three(-a.lse[pl.ds(head, 1), :])
        a.qx[rows_at(head, 16), :queries] = (
            documents + place_rows(minus, 4, (16, queries))
        ).astype(LOW)
        return carry

    lax.fori_loop(0, heads, prepare, 0)

    if prefix:
        for group in range(heads // GROUP):
            start = group * GROUP * HEAD
            own = slice(start, start + GROUP * HEAD)
            query = a.q[a.q0 + start : a.q0 + start + GROUP * HEAD, :]
            grad = a.d_context[own, :]
            pair_keys = block_diagonal(a.pairs[...], group, 0)
            pair_values = block_diagonal(a.pairs[...], group, width)
            scores = contract(pair_keys, query, 1, 0)
            gains = contract(pair_values, grad, 1, 0)
            chances, changes = [], []
            for member in range(GROUP):
                head = group * GROUP + member
                part = slice(member * PAD, (member + 1) * PAD)
                chance = jnp.exp2(scores[part] - a.lse[head : head + 1, :])
                place = lax.broadcasted_iota(jnp.int32, chance.shape, 0)
                chance = jnp.where(place < prefix, chance, 0.0)
                chances.append(chance)
                changes.append(chance * (gains[part] - a.delta[head : head + 1, :queries]))
            chances = jnp.concatenate(chances, 0).astype(LOW)
            changes = jnp.concatenate(changes, 0).astype(LOW)
            a.dq_sum[own, :queries] = contract(pair_keys, changes, 0, 0)
            a.d_pairs[:, own] = own_columns(contract(changes, query, 1, 1)) * (a.factor / LOG2E)
            a.d_pairs[:, width + start : width + start + GROUP * HEAD] = (
                own_columns(contract(chances, grad, 1, 1)) * a.factor
            )
    else:
        a.dq_sum[:, :queries] = jnp.zeros((width, queries), WIDE)
    if ready is not None:
        ready(0)


    def span(part):
        return slice(part * TILE, (part + 1) * TILE)

    def place_of(number, kind):
        return span(2 * number + kind)

    def front(head, own, cut, slot, number):
        query = jnp.concatenate([a.q[rows_at(head, HEAD, a.q0), own], a.qx[rows_at(head, 16), own]], 0)
        key = jnp.concatenate([a.k[rows_at(head, HEAD, a.k0), cut], a.kx[:, cut]], 0)
        scores = contract(query, key, 0, 0)
        if causal and own == cut:
            place = lax.broadcasted_iota(jnp.int32, scores.shape, 1)
            scores = jnp.where(place <= lax.broadcasted_iota(jnp.int32, scores.shape, 0), scores, -BIG)
        grad = jnp.concatenate([a.d_context[rows_at(head, HEAD), own], a.dx[rows_at(head, 16), own]], 0)
        value = jnp.concatenate([a.v[rows_at(head, HEAD, a.v0), cut], a.vx[:, cut]], 0)
        gains = contract(grad, value, 0, 0)
        chance = jnp.exp2(scores)
        a.work[slot, :, place_of(number, 0)] = chance.astype(LOW)
        a.work[slot, :, place_of(number, 1)] = (chance * gains).astype(LOW)

    def run(pieces, together, add):
        unit = [(offset, own, cut) for offset in range(together) for own, cut in pieces]

        def begin(index, slot, number):
            offset, own, cut = unit[number]
            front(index * together + offset, own, cut, slot, number)

        def mix(index, slot, following):
            by_key, by_query = {}, {}
            for number, (offset, own, cut) in enumerate(unit):
                head = index * together + offset
                rows = rows_at(head, HEAD)
                left = unit[number + 1 :]
                chances = a.work[slot, :, place_of(number, 0)]
                changes = a.work[slot, :, place_of(number, 1)]
                pair = by_key.setdefault((offset, cut.start), [])
                d_value = contract(a.d_context[rows, own], chances, 1, 0)
                pair.append((contract(a.q[rows_at(head, HEAD, a.q0), own], changes, 1, 0), d_value))
                begin(following, 1 - slot, number)
                d_query = by_query.setdefault((offset, own.start), [])
                d_query.append(contract(a.k[rows_at(head, HEAD, a.k0), cut], changes, 1, 1))
                if not any((other, keys_.start) == (offset, cut.start) for other, _, keys_ in left):
                    add(head, cut, *(total_of(parts) for parts in zip(*pair)))
                if not any((other, queries_.start) == (offset, own.start) for other, queries_, _ in left):
                    a.dq_sum[rows, own] += total_of(d_query)

        count = heads // together
        turn = next(size for size in (UNITS, 6, 4, 2) if count % size == 0)

        def several(index, carry):
            for number in range(turn):
                place = turn * index + number
                mix(place, number % 2, jnp.minimum(place + 1, count - 1))
            return carry

        for number in range(len(unit)):
            begin(0, 0, number)
        return several, count // turn

    if staged is not None:
        for stage in range(tiles):
            pieces = [(span(other), span(stage)) for other in range(stage + 1, tiles)]
            pieces += [(span(stage), span(other)) for other in range(stage, tiles)]

            def add(head, cut, d_key, d_value):
                rows = rows_at(head, HEAD)
                if stage == 0:
                    a.dk_sum[rows, cut] = d_key
                    a.dv_sum[rows, cut] = d_value
                else:
                    a.dk_sum[rows, cut] += d_key
                    a.dv_sum[rows, cut] += d_value

            step, steps = run(pieces, {1: heads // 2, 3: 2}.get(len(pieces), 1), add)
            cuts = [0, steps // 3, 2 * steps // 3, steps] if stage == 0 else [0, steps]
            for number in range(len(cuts) - 1):
                lax.fori_loop(cuts[number], cuts[number + 1], step, 0)
                if number + 2 < len(cuts):
                    ready(number + 1)
            staged(stage, span(stage))
        return

    def add(head, cut, d_key, d_value):
        a.dk[rows_at(head, HEAD, a.dk0), cut] = (d_key * (1.0 / LOG2E)).astype(LOW)
        a.dv[rows_at(head, HEAD, a.dv0), cut] = d_value.astype(LOW)

    pieces = [
        (span(own), span(part))
        for part in range(tiles)
        for own in range(part if causal else 0, queries // TILE)
    ]
    step, steps = run(pieces, 2 if len(pieces) < 4 else 1, add)
    lax.fori_loop(0, steps, step, 0)
    a.dq[rows_at(0, width, a.dq0), :] = (a.dq_sum[:, :queries] * SCALE).astype(LOW)


def project_wide(out, weight, rows, scaled, place=slice(None)):
    for cut in chunks(weight.shape[1], 256):
        result = contract(weight[:, cut], rows, 0, 1)
        if cut.start < scaled:
            result = result * (SCALE * LOG2E)
        out[cut, place] = result.astype(LOW)


def add_and_normalize(hidden, context, weight, normed, inverse):
    for cut in chunks(hidden.shape[0], CHUNK):
        summed = hidden[cut, :].astype(WIDE) + contract(context[:, cut], weight[...], 0, 0)
        result, scale = normalize(summed)
        normed[cut, :] = result.astype(LOW)
        inverse[cut, :] = scale


def chunk_pipeline(tokens, make, use, steps, uses):
    count = tokens // CHUNK

    def rows_of(index):
        return rows_at(index, CHUNK)

    def body(index, slot, following):
        done = 0
        for step in range(steps):
            if following is not None:
                make(rows_of(following), 1 - slot, step)
            while done < uses and done * steps <= step * uses:
                use(rows_of(index), slot, done)
                done += 1
        while done < uses:
            use(rows_of(index), slot, done)
            done += 1

    def two(index, carry):
        body(2 * index, 0, 2 * index + 1)
        body(2 * index + 1, 1, 2 * index + 2)
        return carry

    for step in range(steps):
        make(rows_of(0), 0, step)
    if count > 2:
        lax.fori_loop(0, count // 2 - 1, two, 0)
    body(count - 2, 0, count - 1)
    body(count - 1, 1, None)


def feed_forward(hidden, up, down, adapter_down, adapter_up, total, slopes_of, active_of, narrow):
    inner = up.shape[1]
    count = inner // INNER

    def make(rows, slot, step):
        if step < count:
            cut = slice(step * INNER, (step + 1) * INNER)
            active, slope = gelu_both(contract(hidden[rows, :], up[:, cut], 1, 0))
            slopes_of(step + 1)[rows, :] = slope.astype(LOW)
        else:
            cut = slice(inner, inner + INNER)
            active, slope = gelu_both(contract(hidden[rows, :], adapter_down[...], 1, 0))
            slopes_of(0)[rows, :] = slope.astype(LOW)
            narrow[rows, :] = active.astype(LOW)
            active = 4.0 * active
        active_of(slot)[:, cut] = active.astype(LOW)

    def use(rows, slot, number):
        active = active_of(slot)
        total[rows, :] = (
            hidden[rows, :].astype(WIDE)
            + contract(active[:, :inner], down[...], 1, 0)
            + contract(active[:, inner : inner + INNER], adapter_up[...], 1, 0)
        )

    chunk_pipeline(hidden.shape[0], make, use, count + 1, 1)


def finish_forward(total, normed, inverse):
    for cut in chunks(total.shape[0], CHUNK):
        result, scale = normalize(total[cut, :])
        normed[cut, :] = result.astype(LOW)
        inverse[cut, :] = scale


def pack(flat, value, first):
    size = value.shape[0] // flat.shape[0]
    for place in range(flat.shape[0]):
        for block in range(value.shape[1] // 128):
            goal = slice(first + block * size, first + (block + 1) * size)
            flat[place, goal, :] = value[
                place * size : (place + 1) * size, block * 128 : (block + 1) * 128
            ].astype(flat.dtype)


def unpack(rows, first, shape):
    parts = [
        rows[first + block * shape[0] : first + (block + 1) * shape[0]] for block in range(shape[1] // 128)
    ]
    return jnp.concatenate(parts, 1)


def flat_shapes(width, narrow, group, replicas):
    second = width // group * (narrow // 128)
    rows = second + narrow // group * (width // 128)
    return second, (group, rows, 128), (group, rows // replicas, 128)


def columns_for(flat, replicas):
    size = flat.shape[1] // replicas
    return lambda place: flat.at[:, pl.ds(pl.multiple_of(place * size, size), size), :]


def feed_back(f, send=None):
    tokens = f.hidden.shape[0]
    cuts = chunks(tokens, CHUNK)
    for cut in cuts:
        value = f.grad[cut, :]
        f.low[cut, :] = value.astype(LOW)
        f.side[cut, :] = (4.0 * value).astype(LOW)

    for cut in cuts:
        change = contract(f.side[cut, :], f.adapter_up[...], 1, 1) * f.slopes(0)[cut, :].astype(WIDE)
        f.d_narrow[cut, :] = change.astype(LOW)
    pack(f.flat, contract(f.hidden[...], f.d_narrow[...], 0, 0) * f.factor, 0)
    pack(f.flat, contract(f.narrow[...], f.side[...], 0, 0) * f.factor, f.second)
    if send is not None:
        send()

    def make(rows, slot, step):
        cut = slice(step * INNER, (step + 1) * INNER)
        change = contract(f.low[rows, :], f.down[cut, :], 1, 1) * f.slopes(step + 1)[rows, :].astype(WIDE)
        f.active(slot)[:, cut] = change.astype(LOW)

    def use(rows, slot, number):
        f.grad[rows, :] += contract(f.active(slot)[:, : f.up.shape[1]], f.up[...], 1, 1) + contract(
            f.d_narrow[rows, :], f.adapter_down[...], 1, 1
        )

    chunk_pipeline(tokens, make, use, f.up.shape[1] // INNER, 1)


def normalize_back_all(grad, normed, inverse, out):
    for cut in chunks(grad.shape[0], CHUNK):
        out[cut, :] = normalize_back(
            grad[cut, :].astype(WIDE), normed[cut, :].astype(WIDE), inverse[cut, :]
        ).astype(out.dtype)


def context_back(out, weight, grad):
    value = grad[...].astype(LOW)
    for cut in chunks(weight.shape[0], 256):
        out[cut, :] = contract(weight[cut, :], value, 1, 1).astype(LOW)


def prefix_pairs(prefix, first, second, hidden, pairs, pairs_wide):
    count = prefix.shape[0]
    hidden[...] = jnp.zeros(hidden.shape, WIDE)
    hidden[:count, :] = jnp.tanh(contract(prefix[...], first[...], 1, 0))
    parts = [part.astype(LOW) for part in split_three(hidden[...])]
    pairs[...] = total_of([contract(part, second[...], 1, 0) for part in parts]).astype(LOW)
    pairs_wide[...] = total_of([contract(second[...], part, 0, 1) for part in parts]).astype(LOW)


def near_order(place):
    return [place, place + 1 - 2 * lax.rem(place, 2), lax.rem(place + 2, 4), 3 - place]


def is_inner(place):
    return lax.rem(place // 2 + lax.rem(place, 2), 2)


def encoder_forward(w, group, copies):
    width = w.source.shape[2]
    share, later_share = w.source.shape[1], w.target.shape[1]
    tokens, later_tokens = share * group, later_share * group
    per = TILE // share
    inner = w.enc_up.shape[1]
    narrow = w.enc_adapter_down.shape[1]
    units = w.enc_prefix_in.shape[1]
    count = w.enc_prefix.shape[0]
    blocks = 1 + inner // INNER

    def body(r):
        move = Mover(r.semaphores)
        weights = [move.start(r.enc_qkv, r.qkv_weight)]
        enc_first, dec_first = r.mid_v.at[:width, :units], r.memory_v.at[:width, :units]
        enc_second, dec_second = r.up.at[:units, : 2 * width], r.up.at[:units, 2 * width : 4 * width]
        weights.append(move.start(r.enc_prefix_in, enc_first))
        weights.append(move.start(r.enc_prefix_out, enc_second))
        weights.append(move.start(r.dec_prefix_in, dec_first))
        weights.append(move.start(r.dec_prefix_out, dec_second))
        links = Links(r.sent, r.arrived, {"seq": group})
        me = links.place["seq"]
        row = me // copies
        block, inside = me // per, lax.rem(me, per)
        others = near_order(block)
        arrivals = []
        for slot, other in enumerate(others):
            goal = r.x.at[pl.ds(pl.multiple_of(slot * TILE + inside * share, share), share), :]
            arrivals.append([])
            for turn in range(per):
                target = other * per + lax.rem(inside + turn, per)
                if slot == 0 and turn == 0:
                    here = move.start(r.source.at[row], goal)
                else:
                    arrivals[slot].append(links.plan("seq", target, r.source.at[target // copies], goal))

        def send(*slots):
            for slot in slots:
                for copy in arrivals[slot]:
                    copy.start()

        pl.when(is_inner(block) == 0)(lambda: send(1, 2))
        pl.when(is_inner(block) == 1)(lambda: send(2, 1))
        send(0, 3)

        def tokens_of(place, size):
            return pl.ds(pl.multiple_of(place * size, size), size)

        def bring(origin, goal, size, via=None):
            own = tokens_of(me, size)
            copies_out = links.scatter("seq", lambda peer: origin.at[peer // copies], goal.at[own, :])
            if via is None:
                return (move.start(origin.at[row], goal.at[own, :]), copies_out)
            move.start(origin.at[row], via).wait()
            return (move.start(via, goal.at[own, :]), copies_out)

        out_weight = move.start(r.enc_out, r.out_weight)
        adapters = [
            move.start(r.enc_adapter_down, r.a_down),
            move.start(r.enc_adapter_up, r.a_up),
        ]
        pair_weight = move.start(r.cross_kv, r.pair_weight)
        for copy in weights:
            copy.wait()
        prefix_pairs(r.enc_prefix, enc_first, enc_second, r.enc_hidden, r.enc_pairs, r.enc_pairs_wide)
        prefix_pairs(r.dec_prefix, dec_first, dec_second, r.dec_hidden, r.dec_pairs, r.dec_pairs_wide)
        ups = [move.start(r.enc_up, r.up), move.start(r.enc_down, r.down)]
        def project(slot):
            for copy in arrivals[slot]:
                copy.wait()
            cut = slice(slot * TILE, (slot + 1) * TILE)
            project_wide(r.qkv_v, r.qkv_weight, r.x[cut, :], width, cut)

        r.marks_out[...] = jnp.concatenate(
            [r.marks[pl.ds(row, 1), pl.ds(pl.multiple_of(other * TILE, TILE), TILE)] for other in others], 1
        )
        marks = r.marks_out[...]
        attention = SimpleNamespace(
            q=r.qkv_v, k=r.qkv_v, v=r.qkv_v, q0=0, k0=width, v0=2 * width,
            q_marks=marks, k_marks=marks, pair_keys=r.enc_pairs_wide.at[:width],
            pair_values=r.enc_pairs_wide.at[width:],
            context=r.context_v, lse=r.lse, qx=r.qx, kx=r.kx, scores=r.scores,
            pair_scores=r.pair_scores, peak=r.peak, partial=r.total,
        )
        here.wait()
        for slot in (1, 2, 0):
            project(slot)
        tiles = tokens // TILE
        most = (tiles - 1) * TILE
        early = [slice(0, most // 2), slice(most // 2, most)] if most // 2 % 128 == 0 else [slice(0, most)]
        attend(
            attention, False, count, [(own, list(range(tiles - 1)), True, "save") for own in early]
        )
        project(tiles - 1)
        later = [bring(r.target, r.target_rows, later_share, r.own_target)]
        outs = [move.start(r.qkv_v, r.qkv)]
        attend(
            attention,
            False,
            count,
            [(slice(most, tokens), list(range(tiles)), True, "whole")]
            + [(own, [tiles - 1], False, "merge") for own in early],
        )
        outs.append(move.start(r.context_v, r.context))
        out_weight.wait()
        add_and_normalize(r.x, r.context_v, r.out_weight, r.mid_v, r.mid_inverse)
        outs.append(move.start(r.mid_v, r.mid))
        for copy in adapters + ups:
            copy.wait()
        feed_forward(
            r.mid_v, r.up, r.down, r.a_down, r.a_up, r.total,
            lambda index: r.slopes_v.at[index], lambda slot: r.active.at[slot], r.narrow_v,
        )
        outs.append(move.start(r.slopes_v, r.slopes))
        outs.append(move.start(r.narrow_v, r.narrow))
        finish_forward(r.total, r.memory_v, r.memory_inverse)
        outs.append(move.start(r.memory_v, r.memory))
        pair_weight.wait()
        outs.pop(0).wait()
        memory_pairs = r.qkv_v.at[: 2 * width]
        project_wide(memory_pairs, r.pair_weight, r.memory_v[...], 0)
        outs.append(move.start(memory_pairs, r.memory_pairs))
        for own, remote in later:
            own.wait()
            for copy in remote:
                copy.wait()
        for copy in outs:
            copy.wait()

    return run_kernel(
        body,
        "encoder_forward",
        near=dict(marks=w.source_segments, enc_prefix=w.enc_prefix, dec_prefix=w.dec_prefix),
        far=dict(
            source=w.source, target=w.target, enc_qkv=w.enc_qkv,
            enc_out=w.enc_out, enc_up=w.enc_up, enc_down=w.enc_down,
            enc_adapter_down=w.enc_adapter_down, enc_adapter_up=w.enc_adapter_up,
            cross_kv=w.cross_kv, enc_prefix_in=w.enc_prefix_in, enc_prefix_out=w.enc_prefix_out,
            dec_prefix_in=w.dec_prefix_in, dec_prefix_out=w.dec_prefix_out,
        ),
        near_outs=dict(
            lse=((16, tokens), WIDE), mid_inverse=((tokens, 1), WIDE),
            memory_inverse=((tokens, 1), WIDE), marks_out=((1, tokens), jnp.int32),
            enc_hidden=((PAD, units), WIDE), enc_pairs=((PAD, 2 * width), LOW),
            dec_hidden=((PAD, units), WIDE), dec_pairs=((PAD, 2 * width), LOW),
            dec_pairs_wide=((2 * width, PAD), LOW),
        ),
        far_outs=dict(
            qkv=((3 * width, tokens), LOW), context=((width, tokens), LOW), mid=((tokens, width), LOW),
            slopes=((blocks, tokens, INNER), LOW), narrow=((tokens, narrow), LOW),
            memory=((tokens, width), LOW), memory_pairs=((2 * width, tokens), LOW),
            target_rows=((later_tokens, width), LOW),
        ),
        scratch=dict(
            x=((tokens, width), LOW), qkv_weight=((width, 3 * width), LOW),
            own_target=((later_share, width), LOW),
            enc_pairs_wide=((2 * width, PAD), LOW),
            out_weight=((width, width), LOW), a_down=((width, narrow), LOW),
            a_up=((narrow, width), LOW), up=((width, inner), LOW), down=((inner, width), LOW),
            pair_weight=((width, 2 * width), LOW), qkv_v=((3 * width, tokens), LOW),
            context_v=((width, tokens), LOW), mid_v=((tokens, width), LOW),
            slopes_v=((blocks, tokens, INNER), LOW), narrow_v=((tokens, narrow), LOW),
            memory_v=((tokens, width), LOW),
            active=((2, CHUNK, inner + narrow), LOW), total=((tokens, width), WIDE), qx=((16, tokens), LOW), kx=((16, tokens), LOW),
            scores=((2, tokens, tokens), WIDE), pair_scores=((2, PAD, tokens), WIDE),
            peak=((2, 8, tokens), WIDE),
        ),
        flops=2 * tokens * width * 11776 + 4 * tokens * tokens * width,
        links=2 * (group - 1),
        collective=0,
    )


def decoder(forward, w, group, copies, replicas):
    tokens, width = forward.target_rows.shape
    share = tokens // group
    keys = forward.memory_pairs.shape[1]
    count = w.dec_prefix.shape[0]
    second, flat, part = flat_shapes(width, w.dec_adapter_down.shape[1], group, replicas)
    inner = w.dec_up.shape[1]
    narrow = w.dec_adapter_down.shape[1]
    blocks = 1 + inner // INNER
    heads = width // HEAD

    def body(r):
        move = Mover(r.semaphores)
        ins = [move.start(r.target, r.x), move.start(r.dec_qkv, r.qkv_weight)]
        links = Links(r.sent, r.arrived, {"seq": group, "dp": replicas})
        exchange = Exchange(move, links)
        for copy in ins:
            copy.wait()
        out_weight = move.start(r.dec_out, r.out_weight)
        crosses = [
            move.start(r.cross_q, r.query_weight),
            move.start(r.memory_pairs, r.pairs_v),
            move.start(r.cross_out, r.cross_out_weight),
        ]
        adapters = [
            move.start(r.dec_adapter_down, r.a_down),
            move.start(r.dec_adapter_up, r.a_up),
        ]
        ups = [move.start(r.dec_up, r.up), move.start(r.dec_down, r.down)]
        d_qkv = r.slopes.at[: 3 * width, :tokens]

        def slope_of(index):
            return r.slopes.at[rows_at(index, tokens), :]

        me = links.place["seq"]
        size = tokens // group
        mine = r.cotangent_v.at[pl.ds(pl.multiple_of(me * size, size), size), :]
        cotangents = links.scatter("seq", lambda peer: r.cotangent.at[peer // copies], mine)
        cotangents.append(move.start(r.cotangent.at[me // copies], mine))
        project_wide(r.qkv, r.qkv_weight, r.x[...], width)
        row = pl.ds(me // copies, 1)
        marks, source_marks = r.marks[row, :], r.source_marks[...]
        shared = dict(
            qx=r.qx, kx=r.kx, scores=r.scores, pair_scores=r.pair_scores, peak=r.peak, dx=r.dx,
            vx=r.vx, delta=r.delta, dq_sum=r.dq_sum, work=r.work,
            d_context=r.d_context,
        )
        self_part = SimpleNamespace(
            q=r.qkv, k=r.qkv, v=r.qkv, q0=0, k0=width, v0=2 * width,
            q_marks=marks, k_marks=marks, pair_keys=r.pairs_wide.at[:width],
            pair_values=r.pairs_wide.at[width:], pairs=r.pairs, context=r.context, lse=r.lse,
            dq=d_qkv, dk=d_qkv, dv=d_qkv, dq0=0, dk0=width, dv0=2 * width,
            d_pairs=r.d_pairs, factor=1.0 / copies, **shared,
        )
        attend(self_part, True, count)
        out_weight.wait()
        add_and_normalize(r.x, r.context, r.out_weight, r.mid, r.mid_inverse)
        for copy in crosses:
            copy.wait()
        project_wide(r.query, r.query_weight, r.mid[...], width)
        cross_part = SimpleNamespace(
            q=r.query, k=r.pairs_v, v=r.pairs_v, q0=0, k0=0, v0=width,
            q_marks=marks, k_marks=source_marks, context=r.cross_context, lse=r.cross_lse,
            dq=r.d_query, dk=r.d_pairs_v, dv=r.d_pairs_v, dq0=0, dk0=0, dv0=width, **shared,
        )
        attend(cross_part, False, 0)
        add_and_normalize(r.mid, r.cross_context, r.cross_out_weight, r.crossed, r.crossed_inverse)
        for copy in adapters + ups + cotangents:
            copy.wait()
        feed_forward(
            r.crossed, r.up, r.down, r.a_down, r.a_up, r.total,
            slope_of, lambda slot: r.work.at[slot], r.narrow,
        )
        finish_forward(r.total, r.out_v, r.out_inverse)
        core, part_of = lax.rem(links.place["dp"], 2), rows_for(r.out_v, group)
        outputs = [
            links.plan("seq", links.peer("seq", shift), part_of(links.peer("seq", shift)), r.out_all.at[me])
            for shift in range(1, group)
        ]

        def send_outputs():
            for copy in outputs:
                copy.start()

        pl.when(core == 0)(send_outputs)
        outs = [move.start(part_of(me), r.out_all.at[me])]
        normalize_back_all(r.cotangent_v, r.out_v, r.out_inverse, r.total)
        feed_back(
            SimpleNamespace(
                grad=r.total, low=r.low, side=r.side, hidden=r.crossed, narrow=r.narrow, up=r.up,
                down=r.down, adapter_down=r.a_down, adapter_up=r.a_up,
                slopes=slope_of, flat=r.flat, second=second,
                d_narrow=r.d_narrow, factor=1.0 / copies, active=lambda slot: r.work.at[slot],
            )
        )
        exchange.start("flat", "dp", columns_for(r.flat, replicas), r.parts)
        pl.when(core == 1)(send_outputs)
        normalize_back_all(r.total, r.crossed, r.crossed_inverse, r.total)
        context_back(r.d_context, r.cross_out_weight, r.total)
        attend_back(cross_part, False, 0)
        outs.append(move.start(r.d_pairs_v, r.memory_pairs_grad))
        for cut in chunks(tokens, CHUNK):
            r.total[cut, :] += contract(r.d_query[:, cut], r.query_weight[...], 0, 1)
        normalize_back_all(r.total, r.mid, r.mid_inverse, r.total)
        context_back(r.d_context, r.out_weight, r.total)

        def pass_on(step):
            exchange.end("flat")
            r.flat_sum[...] = sum_parts(r.parts).astype(LOW)
            exchange.start("flat", "seq", lambda peer: r.flat_sum.at[peer], r.flat_own)

        attend_back(self_part, True, count, pass_on)
        for cut in chunks(tokens, CHUNK):
            r.x[cut, :] = (
                r.total[cut, :] + contract(d_qkv[:, cut], r.qkv_weight[...], 0, 1)
            ).astype(LOW)
        outs.append(move.start(r.x, r.target_grad))
        for copy in outs:
            copy.wait()
        exchange.end("flat")
        for copy in outputs:
            copy.wait()

    return run_kernel(
        body,
        "decoder",
        near=dict(
            marks=w.target_segments, source_marks=forward.marks_out,
            pairs_wide=forward.dec_pairs_wide, pairs=forward.dec_pairs,
        ),
        far=dict(
            target=forward.target_rows, cotangent=w.cotangent,
            memory_pairs=forward.memory_pairs, dec_qkv=w.dec_qkv,
            dec_out=w.dec_out, cross_q=w.cross_q, cross_out=w.cross_out, dec_up=w.dec_up,
            dec_down=w.dec_down, dec_adapter_down=w.dec_adapter_down,
            dec_adapter_up=w.dec_adapter_up,
        ),
        near_outs=dict(d_pairs=((PAD, 2 * width), WIDE)),
        far_outs=dict(
            out_all=((group, share, width), LOW), target_grad=((tokens, width), LOW),
            memory_pairs_grad=((2 * width, keys), LOW),
            flat_own=(part, LOW),
        ),
        scratch=dict(
            flat=(flat, LOW), parts=((replicas, *part), LOW), flat_sum=(part, LOW),
            x=((tokens, width), LOW), cotangent_v=((tokens, width), LOW),
            qkv_weight=((width, 3 * width), LOW), out_weight=((width, width), LOW),
            query_weight=((width, width), LOW), cross_out_weight=((width, width), LOW),
            pairs_v=((2 * width, keys), LOW), a_down=((width, narrow), LOW),
            a_up=((narrow, width), LOW), up=((width, inner), LOW), down=((inner, width), LOW),
            qkv=((3 * width, tokens), LOW), context=((width, tokens), LOW),
            mid=((tokens, width), LOW), mid_inverse=((tokens, 1), WIDE),
            query=((width, tokens), LOW), cross_context=((width, tokens), LOW),
            crossed=((tokens, width), LOW), crossed_inverse=((tokens, 1), WIDE),
            out_v=((tokens, width), LOW), out_inverse=((tokens, 1), WIDE),
            slopes=((blocks * tokens, INNER), LOW), narrow=((tokens, narrow), LOW),
            low=((tokens, width), LOW), side=((tokens, width), LOW), d_narrow=((tokens, narrow), LOW),
            total=((tokens, width), WIDE), lse=((16, tokens), WIDE), cross_lse=((16, tokens), WIDE),
            d_context=((width, tokens), LOW), d_query=((width, tokens), LOW),
            d_pairs_v=((2 * width, keys), LOW),
            qx=((heads * 16, tokens), LOW), kx=((16, keys), LOW),
            scores=((2, keys, tokens), WIDE), pair_scores=((2, PAD, tokens), WIDE),
            peak=((2, 8, tokens), WIDE), dx=((heads * 16, tokens), LOW), vx=((16, keys), LOW),
            delta=((16, tokens), WIDE), dq_sum=((width, tokens), WIDE),
            work=((2, TILE, 16 * TILE), LOW),
        ),
        flops=4 * tokens * width * 11776 + 14 * tokens * (keys + tokens) * width,
        links=3 * (group - 1) + replicas - 1,
        collective=3,
    )


def encoder_feed_back(dec, forward, w, group, copies, replicas):
    tokens, width = forward.memory.shape
    inner = w.enc_up.shape[1]
    narrow = w.enc_adapter_down.shape[1]
    blocks = 1 + inner // INNER
    second, flat, part = flat_shapes(width, narrow, group, replicas)
    later = dec.target_grad.shape[0] // group

    def body(r):
        move = Mover(r.semaphores)
        firsts = [
            move.start(r.memory_pairs_grad, r.d_pairs),
            move.start(r.cross_kv, r.pair_weight),
            move.start(r.memory, r.memory_v),
        ]
        adapters = [
            move.start(r.enc_adapter_up, r.a_up),
            move.start(r.slopes.at[0], r.slopes_v.at[0]),
            move.start(r.narrow, r.narrow_v),
            move.start(r.mid, r.mid_v),
        ]
        ups = [
            move.start(r.enc_adapter_down, r.a_down),
            move.start(r.slopes.at[1:], r.slopes_v.at[1:]),
            move.start(r.enc_down, r.down),
            move.start(r.enc_up, r.up),
            move.start(r.enc_out, r.out_weight),
        ]
        links = Links(r.sent, r.arrived, {"seq": group, "dp": replicas})
        exchange = Exchange(move, links)
        me, core = links.place["seq"], lax.rem(links.place["dp"], 2)
        targets = [
            links.plan("seq", links.peer("seq", shift), r.target_grad.at[links.peer("seq", shift)], r.target_grad_all.at[me])
            for shift in range(1, group)
        ]

        def send_targets():
            for copy in targets:
                copy.start()

        pl.when(core == 0)(send_targets)
        own_target = move.start(r.target_grad.at[me], r.own_target)
        for copy in firsts:
            copy.wait()
        for cut in chunks(tokens, CHUNK):
            grad = contract(r.d_pairs[:, cut], r.pair_weight[...], 0, 1)
            r.total[cut, :] = normalize_back(
                grad, r.memory_v[cut, :].astype(WIDE), r.memory_inverse[cut, :]
            )
        for copy in adapters:
            copy.wait()

        def send():
            exchange.start("flat", "dp", columns_for(r.flat, replicas), r.parts)
            pl.when(core == 1)(send_targets)
            own_target.wait()
            targets.append(move.start(r.own_target, r.target_grad_all.at[me]))
            for copy in ups:
                copy.wait()

        feed_back(
            SimpleNamespace(
                grad=r.total, low=r.low, side=r.side, hidden=r.mid_v, narrow=r.narrow_v, up=r.up,
                down=r.down, adapter_down=r.a_down, adapter_up=r.a_up,
                slopes=lambda index: r.slopes_v.at[index], flat=r.flat, second=second,
                d_narrow=r.d_narrow, factor=1.0 / copies, active=lambda slot: r.active.at[slot],
            ),
            send,
        )
        normalize_back_all(r.total, r.mid_v, r.mid_inverse, r.low)
        outs = [move.start(r.low, r.summed_grad)]
        context_back(r.d_context_v, r.out_weight, r.low)
        outs.append(move.start(r.d_context_v, r.d_context))
        for copy in outs:
            copy.wait()
        exchange.end("flat")
        for copy in targets:
            copy.wait()

    return run_kernel(
        body,
        "encoder_feed_back",
        near=dict(mid_inverse=forward.mid_inverse, memory_inverse=forward.memory_inverse),
        far=dict(
            target_grad=dec.target_grad.reshape(group, -1, width),
            memory_pairs_grad=dec.memory_pairs_grad, memory=forward.memory, mid=forward.mid,
            slopes=forward.slopes, narrow=forward.narrow, cross_kv=w.cross_kv,
            enc_out=w.enc_out, enc_up=w.enc_up, enc_down=w.enc_down,
            enc_adapter_down=w.enc_adapter_down, enc_adapter_up=w.enc_adapter_up,
        ),
        near_outs={},
        far_outs=dict(
            summed_grad=((tokens, width), LOW), d_context=((width, tokens), LOW),
            parts=((replicas, *part), LOW),
            target_grad_all=((group, later, width), LOW),
        ),
        scratch=dict(
            own_target=((later, width), LOW),
            flat=(flat, LOW), d_pairs=((2 * width, tokens), LOW), pair_weight=((width, 2 * width), LOW),
            memory_v=((tokens, width), LOW), mid_v=((tokens, width), LOW),
            slopes_v=((blocks, tokens, INNER), LOW), narrow_v=((tokens, narrow), LOW),
            out_weight=((width, width), LOW), a_down=((width, narrow), LOW),
            a_up=((narrow, width), LOW), up=((width, inner), LOW), down=((inner, width), LOW),
            low=((tokens, width), LOW), side=((tokens, width), LOW), d_narrow=((tokens, narrow), LOW),
            active=((2, CHUNK, inner), LOW), total=((tokens, width), WIDE), d_context_v=((width, tokens), LOW),
        ),
        flops=2 * tokens * width * 9728,
        links=group - 1 + replicas - 1,
        collective=1,
    )


def split_product(left, right, left_dim, right_dim):
    return total_of(
        [contract(part.astype(LOW), right, left_dim, right_dim) for part in split_three(left)]
    )


def prefix_back(p):
    count, group = p.prefix.shape[0], p.group
    d_pairs, hidden = p.d_pairs, p.hidden[...]
    units, width = hidden.shape[1], p.prefix.shape[1]
    p.tall_hidden[...] = hidden.T
    share = units // group
    own = p.tall_hidden[pl.ds(pl.multiple_of(p.place * share, share), share), :]
    parts = split_three(d_pairs)
    p.out_grad[...] = total_of(
        [split_product(own, part.astype(LOW), 1, 0) for part in parts]
    )
    d_hidden = split_product(d_pairs, p.second[...], 1, 1) * (1.0 - hidden * hidden)
    p.wide_prefix[...] = jnp.zeros(p.wide_prefix.shape, WIDE)
    p.wide_prefix[:count, :] = p.prefix[...].astype(WIDE)
    p.tall_prefix[...] = p.wide_prefix[...].T
    share = width // group
    own = p.tall_prefix[pl.ds(pl.multiple_of(p.place * share, share), share), :].astype(LOW)
    p.in_grad[...] = total_of([contract(own, part.astype(LOW), 1, 0) for part in split_three(d_hidden)])
    p.embed_grad[...] = split_product(d_hidden, p.first_share[...], 1, 1)[:count]


def block_order(place):
    return [1 + is_inner(place), 3, 2 - is_inner(place), 0]


def encoder_attend_back(feed, dec, forward, w, group, copies, replicas):
    tokens, width = feed.summed_grad.shape
    share = tokens // group
    count = w.enc_prefix.shape[0]
    narrow, units = w.enc_adapter_down.shape[1], w.enc_prefix_in.shape[1]
    second, _, part = flat_shapes(width, narrow, group, replicas)
    heads = width // HEAD
    tile = TILE
    blocks, per = tokens // tile, tile // share
    grains = [
        (layer, 8 * row, 128 * column)
        for layer in range(2) for column in range(2 * width // 128) for row in range(PAD // 8)
    ]
    depth = -(-len(grains) // (group * replicas))

    def grain_place(number):
        device, inside = number // depth, number % depth
        return (device // group, device % group, slice(8 * inside, 8 * inside + 8))
    layers = ("enc", "dec")

    def body(r):
        move = Mover(r.semaphores)
        me = lax.axis_index("seq")
        sums = move.start(r.enc_parts, r.enc_parts_v)
        slots = block_order(me // per)
        near = near_order(me // per)
        begins = [pl.multiple_of(slot * tile, tile) for slot in slots]
        inner = is_inner(me // per)
        goals = [near[1] + inner * (near[2] - near[1]), near[3], near[2] + inner * (near[1] - near[2]), near[0]]
        firsts, lasts = [], []
        for stage, begin in enumerate(begins):
            goal, origin = slice(stage * tile, (stage + 1) * tile), pl.ds(begin, tile)
            firsts.append(move.start(r.qkv.at[:, origin], r.qkv_v.at[:, goal]))
            firsts.append(move.start(r.d_context.at[:, origin], r.d_context_v.at[:, goal]))
            firsts.append(move.start(r.context.at[:, origin], r.context_v.at[:, goal]))
            lasts.append(move.start(r.summed_grad.at[origin, :], r.summed_v.at[goal, :]))
            r.lse_v[:, goal] = r.lse[:, origin]
        totals = move.start(r.dec_own, r.dec_own_v)
        marks = jnp.concatenate([r.marks[:, pl.ds(begin, tile)] for begin in begins], 1)
        lasts += [
            move.start(r.enc_qkv, r.qkv_weight),
            move.start(r.enc_prefix_out, r.enc_second), move.start(r.dec_prefix_out, r.dec_second),
        ]
        size = width // group
        first_rows = pl.ds(pl.multiple_of(me * size, size), size)
        lasts.append(move.start(r.enc_prefix_in.at[first_rows, :], r.enc_first))
        lasts.append(move.start(r.dec_prefix_in.at[first_rows, :], r.dec_first))

        links = Links(r.sent, r.arrived, {"seq": group, "dp": replicas})
        exchange = Exchange(move, links)

        def send_total(name, own, mine, total):
            mine[...] = sum_parts(own).astype(LOW)
            exchange.start(name, "dp", lambda peer: mine, total)

        def ready(step):
            if step == 0:
                r.pair_out[...] = jnp.zeros(r.pair_out.shape, WIDE)
                for number, (layer, row, column) in enumerate(grains):
                    origin = (r.enc_d_pairs, r.dec_d_pairs)[layer]
                    r.pair_out[grain_place(number)] = origin[row : row + 8, column : column + 128]
                exchange.start("pairs", "dp", lambda peer: r.pair_out.at[peer], r.pair_parts)
            elif step == 1:
                exchange.end("pairs")
                r.pair_sum[...] = sum_parts(r.pair_parts)
                exchange.start("pairs", "seq", lambda peer: r.pair_sum.at[peer], r.pair_own)
            else:
                exchange.end("pairs")
                r.pair_mine[...] = sum_parts(r.pair_own)
                exchange.start("pairs", "seq", lambda peer: r.pair_mine, r.pair_row)

        sent = []

        def staged(stage, cut):
            r.d_qkv[:width, :] = (r.dq_sum[:, cut] * SCALE).astype(LOW)
            r.d_qkv[width : 2 * width, :] = (r.dk_sum[:, cut] * (1.0 / LOG2E)).astype(LOW)
            r.d_qkv[2 * width :, :] = r.dv_sum[:, cut].astype(LOW)
            if stage == 0:
                for copy in lasts:
                    copy.wait()
            r.summed_v[cut, :] = (
                r.summed_v[cut, :].astype(WIDE) + contract(r.d_qkv[...], r.qkv_weight[...], 0, 1)
            ).astype(LOW)
            inside = lax.rem(me, per)
            last = stage == blocks - 1
            for turn in range(per):
                number = lax.rem(inside + turn, per)
                origin = r.summed_v.at[
                    pl.ds(pl.multiple_of(stage * tile + number * share, share), share), :
                ]
                if last and turn == 0:
                    sent.append(move.start(origin, r.source_grad.at[me]))
                else:
                    target = goals[stage] * per + number
                    sent.append(links.start_to("seq", target, origin, r.source_grad.at[me]))
            if stage == 0:
                totals.wait()
                send_total("dec", r.dec_own_v, r.dec_mine, r.dec_total)
                exchange.end("enc", "pairs")
                send_total("enc", r.enc_own, r.enc_mine, r.enc_total)
                exchange.start("pairs", "dp", lambda peer: r.pair_row, r.pair_total)

        sums.wait()
        r.enc_sum[...] = sum_parts(r.enc_parts_v).astype(LOW)
        exchange.start("enc", "seq", lambda peer: r.enc_sum.at[peer], r.enc_own)
        for copy in firsts:
            copy.wait()
        attend_back(
            SimpleNamespace(
                q=r.qkv_v, k=r.qkv_v, v=r.qkv_v, q0=0, k0=width, v0=2 * width,
                q_marks=marks, k_marks=marks, pairs=r.enc_pairs, context=r.context_v, lse=r.lse_v,
                d_context=r.d_context_v, d_pairs=r.enc_d_pairs, factor=1.0 / copies, qx=r.qx, kx=r.kx,
                dx=r.dx, vx=r.vx, delta=r.delta, dq_sum=r.dq_sum, dk_sum=r.dk_sum, dv_sum=r.dv_sum,
                work=r.work,
            ),
            False,
            count,
            ready,
            staged,
        )
        exchange.end("pairs")
        for number, (layer, row, column) in enumerate(grains):
            r.whole[layer, row : row + 8, column : column + 128] = r.pair_total[grain_place(number)]
        for number, layer in enumerate(layers):
            prefix_back(
                SimpleNamespace(
                    d_pairs=r.whole[number], group=group, place=me,
                    hidden=getattr(r, f"{layer}_hidden"), prefix=getattr(r, f"{layer}_prefix"),
                    second=getattr(r, f"{layer}_second"), first_share=getattr(r, f"{layer}_first"),
                    tall_hidden=r.tall_hidden, tall_prefix=r.tall_prefix, wide_prefix=r.wide_prefix,
                    embed_grad=getattr(r, f"{layer}_embed"), in_grad=getattr(r, f"{layer}_in"),
                    out_grad=getattr(r, f"{layer}_out_grad"),
                )
            )
            exchange.end(layer)
            total = getattr(r, f"{layer}_total")
            total = jnp.concatenate([total[place].astype(WIDE) for place in range(replicas)], 0)
            for kind, first in (("down", 0), ("up", second)):
                out = getattr(r, f"{layer}_{kind}_grad_all")
                out[...] = unpack(total, first, out.shape)
        for copy in sent:
            copy.wait()

    near_outs = {}
    for layer in layers:
        near_outs[f"{layer}_embed"] = ((count, width // group), WIDE)
        near_outs[f"{layer}_in"] = ((width // group, units), WIDE)
        near_outs[f"{layer}_out_grad"] = ((units // group, 2 * width), WIDE)
        near_outs[f"{layer}_down_grad_all"] = ((width // group, narrow), WIDE)
        near_outs[f"{layer}_up_grad_all"] = ((narrow // group, width), WIDE)
    scratch = {}
    scratch["enc_parts_v"] = ((replicas, *part), LOW)
    scratch["enc_sum"] = scratch["enc_own"] = scratch["dec_own_v"] = (part, LOW)
    for layer in layers:
        scratch[f"{layer}_mine"] = (part[1:], LOW)
        scratch[f"{layer}_total"] = ((replicas, *part[1:]), LOW)
        scratch[f"{layer}_second"] = ((units, 2 * width), LOW)
        scratch[f"{layer}_first"] = ((width // group, units), LOW)
    own = (group, 8 * depth, 128)
    for name in ("pair_out", "pair_parts", "pair_total"):
        scratch[name] = ((replicas, *own), WIDE)
    for name in ("pair_sum", "pair_own", "pair_row"):
        scratch[name] = (own, WIDE)
    scratch["pair_mine"] = (own[1:], WIDE)
    scratch["whole"] = ((2, PAD, 2 * width), WIDE)
    scratch["enc_d_pairs"] = ((PAD, 2 * width), WIDE)
    scratch["tall_hidden"] = ((units, PAD), WIDE)
    scratch["wide_prefix"] = ((PAD, width), WIDE)
    scratch["tall_prefix"] = ((width, PAD), WIDE)
    for name in ("dq_sum", "dk_sum", "dv_sum"):
        scratch[name] = ((width, tokens), WIDE)
    return run_kernel(
        body,
        "encoder_attend_back",
        near=dict(
            marks=forward.marks_out, enc_pairs=forward.enc_pairs, lse=forward.lse,
            dec_d_pairs=dec.d_pairs, enc_hidden=forward.enc_hidden, dec_hidden=forward.dec_hidden,
            enc_prefix=w.enc_prefix, dec_prefix=w.dec_prefix,
        ),
        far=dict(
            qkv=forward.qkv, d_context=feed.d_context, context=forward.context,
            enc_qkv=w.enc_qkv, summed_grad=feed.summed_grad,
            enc_parts=feed.parts, dec_own=dec.flat_own,
            enc_prefix_in=w.enc_prefix_in, enc_prefix_out=w.enc_prefix_out,
            dec_prefix_in=w.dec_prefix_in, dec_prefix_out=w.dec_prefix_out,
        ),
        near_outs=near_outs,
        far_outs=dict(source_grad=((group, share, width), LOW)),
        scratch=dict(
            qkv_v=((3 * width, tokens), LOW), d_context_v=((width, tokens), LOW),
            context_v=((width, tokens), LOW), qkv_weight=((width, 3 * width), LOW),
            summed_v=((tokens, width), LOW), d_qkv=((3 * width, tile), LOW), lse_v=((16, tokens), WIDE),
            qx=((heads * 16, tokens), LOW), kx=((16, tokens), LOW),
            dx=((heads * 16, tokens), LOW), vx=((16, tokens), LOW), delta=((16, tokens), WIDE),
            work=((2, TILE, 14 * TILE), LOW), **scratch,
        ),
        flops=2 * tokens * width * 2304 + 20 * tokens * tokens * width,
        links=3 * (group - 1) + 4 * (replicas - 1) + group - 1,
        collective=2,
    )


def finish(attended, feed, dec, copies):
    small = [name for name in vars(attended) if name != "source_grad"]
    shape = attended.source_grad.shape
    later = dec.out_all.shape

    def body(r):
        move = Mover(r.semaphores)
        ins = [
            move.start(r.source_grad, r.source_v),
            move.start(r.target_grad, r.target_v),
        ]
        outs = []
        relays = [
            (move.start(r.out_all.at[place * copies], r.out_v.at[place]), r.out_v.at[place], r.out.at[place])
            for place in range(later[0] // copies)
        ]
        for name in small:
            via = getattr(r, name + "_v")
            relays.append((move.start(getattr(r, name + "_in"), via), via, getattr(r, name)))
        for copy, via, goal in relays:
            copy.wait()
            outs.append(move.start(via, goal))
        for copy, origin, wide, goal in (
            (ins[0], r.source_v, r.source_w, r.source_out), (ins[1], r.target_v, r.target_w, r.target_out)
        ):
            copy.wait()
            for place in range(wide.shape[0]):
                wide[place] = origin[place * copies].astype(WIDE)
                outs.append(move.start(wide.at[place], goal.at[place]))
        for copy in outs:
            copy.wait()

    rows = shape[0] // copies
    return run_kernel(
        body,
        "finish",
        near={},
        far=dict(
            source_grad=attended.source_grad, target_grad=feed.target_grad_all, out_all=dec.out_all,
            **{name + "_in": getattr(attended, name) for name in small},
        ),
        near_outs={},
        far_outs=dict(
            out=((rows, *later[1:]), LOW), source_out=((rows, *shape[1:]), WIDE),
            target_out=((rows, *later[1:]), WIDE),
            **{name: (getattr(attended, name).shape, WIDE) for name in small},
        ),
        scratch=dict(
            source_v=(shape, LOW), source_w=((rows, *shape[1:]), WIDE), target_v=(later, LOW),
            target_w=((rows, *later[1:]), WIDE), out_v=((rows, *later[1:]), LOW),
            **{name + "_v": (getattr(attended, name).shape, WIDE) for name in small},
        ),
        flops=0,
    )


NAMES = (
    "source",
    "target",
    "source_segments",
    "target_segments",
    "cotangent",
    "enc_qkv",
    "enc_out",
    "enc_up",
    "enc_down",
    "dec_qkv",
    "dec_out",
    "cross_q",
    "cross_kv",
    "cross_out",
    "dec_up",
    "dec_down",
    "enc_prefix",
    "enc_prefix_in",
    "enc_prefix_out",
    "enc_adapter_down",
    "enc_adapter_up",
    "dec_prefix",
    "dec_prefix_in",
    "dec_prefix_out",
    "dec_adapter_down",
    "dec_adapter_up",
)


def shards(*operands, group, replicas):
    w = SimpleNamespace(**dict(zip(NAMES, operands)))
    copies = group // w.source.shape[0]
    forward = encoder_forward(w, group, copies)
    dec = decoder(forward, w, group, copies, replicas)
    feed = encoder_feed_back(dec, forward, w, group, copies, replicas)
    attended = encoder_attend_back(feed, dec, forward, w, group, copies, replicas)
    done = finish(attended, feed, dec, copies)
    results = [done.out, done.source_out, done.target_out]
    for layer in ("enc", "dec"):
        for name in ("embed", "in", "out_grad", "down_grad_all", "up_grad_all"):
            results.append(getattr(done, f"{layer}_{name}"))
    return tuple(results)


def solution(mesh):
    rows = P("dp", "seq", None)
    marks = P("dp", None)
    in_specs = (rows, rows, marks, marks, rows) + (P(),) * 21
    across, down = P(None, "seq"), P("seq", None)
    layer = (across, down, down, down, down)
    return jax.shard_map(
        functools.partial(shards, group=mesh.shape["seq"], replicas=mesh.shape["dp"]),
        mesh=mesh,
        in_specs=in_specs,
        out_specs=(rows, rows, rows) + layer + layer,
        check_vma=False,
    )
```
